32 devices in a mesh: shard: 4 (over y, x), rep: 8 (over z, core).
Axes of the slice: x: 2, y: 2, z: 4, core: 2. Of those that a mesh axis runs over, the one named last changes fastest.
Arguments:
- tokens: bfloat16 [8, 1024, 1600], P('rep', 'shard'), may hold values from -6 to 6
- cotangent: bfloat16 [8, 1024, 1600], P('rep', 'shard'), may hold values from -6 to 6
- lengths: int32 [8, 3], P('rep'), may hold values from 1 to 4, 8 in all within a row
- attn_weight: bfloat16 [1600, 4800], P('shard'), may hold values from -0.15625 to 0.15625
- query_bias: bfloat16 [1600], P('shard'), may hold values from -1.75 to 1.75
- value_bias: bfloat16 [1600], P('shard'), may hold values from -0.125 to 0.125
- proj_weight: bfloat16 [1600, 1600], P('shard'), may hold values from -2.5 to 2.5
- proj_bias: bfloat16 [1600], P('shard'), may hold values from -1.75 to 1.75
- ln1_gain: bfloat16 [1600], P('shard'), may hold values from 0.25 to 1.75
- ln1_bias: bfloat16 [1600], P('shard'), may hold values from -1.75 to 1.75
- ln2_gain: bfloat16 [1600], P('shard'), may hold values from 0.25 to 1.75
- ln2_bias: bfloat16 [1600], P('shard'), may hold values from -1.75 to 1.75
- fc_weight: bfloat16 [1600, 6400], P('shard'), may hold values from -0.15625 to 0.15625
- fc_bias: bfloat16 [6400], P('shard'), may hold values from -3 to 3
- out_weight: bfloat16 [6400, 1600], P('shard'), may hold values from -0.109375 to 0.109375
- out_bias: bfloat16 [1600], P('shard'), may hold values from -1.75 to 1.75
Outputs:
- output: bfloat16 [8, 1024, 1600], P('rep', 'shard')
- input_grad: bfloat16 [8, 1024, 1600], P('rep', 'shard')
- grad_attn_weight: float32 [1600, 4800], P('shard')
- grad_query_bias: float32 [1600], P('shard')
- grad_value_bias: float32 [1600], P('shard')
- grad_proj_weight: float32 [1600, 1600], P('shard')
- grad_proj_bias: float32 [1600], P('shard')
- grad_ln1_gain: float32 [1600], P('shard')
- grad_ln1_bias: float32 [1600], P('shard')
- grad_ln2_gain: float32 [1600], P('shard')
- grad_ln2_bias: float32 [1600], P('shard')
- grad_fc_weight: float32 [1600, 6400], P('shard')
- grad_fc_bias: float32 [6400], P('shard')
- grad_out_weight: float32 [6400, 1600], P('shard')
- grad_out_bias: float32 [1600], P('shard')
The draws below stay inside these ranges and needn't reach their ends.
Inputs may be any that keep to these rules, and one draw needn't show every extreme that they name: Each row of lengths sums to 8; a sequence holds 4 * 32 times its entry in tokens, an equal share on each device of its group; the largest entry of every row is reached.
All inputs are finite; a program needn't handle non-finite values.
Results may differ from the reference program's by a relative error of at most 0.02.
Values may be sent and summed in bfloat16 or wider, within the bound.
No kernel may reach another device: no remote copies, remote signals or barrier semaphores. Data moves between devices by JAX's collectives and lax.ppermute only.
A program may use at most 384 MiB of HBM per device.

```python
import math
import jax
import jax.numpy as jnp
import numpy as np
from jax import lax

D = 1600
HEADS = 25
HD = 64
FF = 6400
TOK_DEV = 256
UNIT = 32
NSEQ = 3
GROUP = 1024
N_SHARD = 4
N_REP = 8


def steps_of(rng, extent, cuts, smallest, largest):
    level = 1.0
    for axis_at, parts in cuts:
        steps = jax.random.uniform(jax.random.fold_in(jax.random.fold_in(rng, 6), axis_at), (parts,), jnp.float32, smallest / len(cuts), largest / len(cuts))
        level = level * jnp.repeat(jnp.exp(steps), extent[axis_at] // parts).reshape((-1,) + (1,) * (len(extent) - 1 - axis_at))
    return level


def length_profile(number_of, total, most, lean):
    weights = [(1 << 20) // math.isqrt(grade ** lean) + 1 for grade in range(2, number_of + 1)]
    rest, holding = total - most - (number_of - 1), [1] * (number_of - 1)
    while rest > 0:
        movable = [i for i in range(number_of - 1) if holding[i] < most]
        pool, budget = sum([weights[i] for i in movable]), rest
        for i in movable:
            more = min(most - holding[i], max(1, budget * weights[i] // pool), rest)
            holding[i] = holding[i] + more
            rest = rest - more
    return np.array([most] + holding)


def uneven(key, count, total, bound, skew):
    if count == 2:
        one = jax.random.randint(key, (), max(1, total - bound), min(bound, total - 1) + 1)
        return jnp.stack([one, total - one])
    tallies = jnp.asarray(length_profile(count, total, bound, skew), jnp.int32)
    pairs = (count - 1) // 2
    giver, receiver = tallies[1:1 + 2 * pairs:2], tallies[2:2 + 2 * pairs:2]
    room = jnp.minimum(giver - 1, bound - receiver)
    passed = jax.random.randint(jax.random.fold_in(key, 1), (pairs,), 0, 1 << 20) % (room + 1)
    tallies = tallies.at[1:1 + 2 * pairs:2].set(giver - passed).at[2:2 + 2 * pairs:2].set(receiver + passed)
    return tallies[jax.random.permutation(jax.random.fold_in(key, 2), count)]


def centred(key, dims, width, limit, shards=(), held_as=jnp.bfloat16):
    loudness = steps_of(key, dims, shards, -0.22, 0.18) if shards else 1.0
    drawn = jax.random.normal(key, dims, jnp.float32) * width * loudness
    return jnp.minimum(jnp.maximum(drawn, -limit), limit).astype(held_as)


def setup_inputs(seed: int = 0) -> dict:
    seeds = jax.random.split(jax.random.key(seed), 17)
    return {
        "tokens": centred(seeds[0], (N_REP, GROUP, D), 1.0, 6.0, ((0, 8), (1, 4))),
        "cotangent": centred(seeds[1], (N_REP, GROUP, D), 1.0, 6.0, ((0, 8), (1, 4))),
        "lengths": jax.vmap(lambda own: uneven(own, NSEQ, TOK_DEV // UNIT, TOK_DEV // UNIT // 2, 2))(jax.random.split(seeds[2], N_REP)).reshape((N_REP, NSEQ)).astype(jnp.int32),
        "attn_weight": centred(seeds[3], (D, 3 * D), D ** -0.5, 0.15625, ((0, 4),)),
        "query_bias": centred(seeds[4], (D,), 0.3, 1.75, ((0, 4),)),
        "value_bias": centred(seeds[5], (D,), 0.02, 0.125, ((0, 4),)),
        "proj_weight": centred(seeds[6], (D, D), (max(D // 256, 1)) ** -0.5, 2.5, ((0, 4),)),
        "proj_bias": centred(seeds[7], (D,), 0.3, 1.75, ((0, 4),)),
        "ln1_gain": jnp.clip(1.0 + 0.15 * jax.random.normal(seeds[8], (D,), jnp.float32), 0.25, 1.75).astype(jnp.bfloat16),
        "ln1_bias": centred(seeds[9], (D,), 0.3, 1.75, ((0, 4),)),
        "ln2_gain": jnp.clip(1.0 + 0.15 * jax.random.normal(seeds[10], (D,), jnp.float32), 0.25, 1.75).astype(jnp.bfloat16),
        "ln2_bias": centred(seeds[11], (D,), 0.3, 1.75, ((0, 4),)),
        "fc_weight": centred(seeds[12], (D, FF), D ** -0.5, 0.15625, ((0, 4),)),
        "fc_bias": centred(seeds[13], (FF,), 0.5, 3.0, ((0, 4),)),
        "out_weight": centred(seeds[14], (FF, D), (FF // 2) ** -0.5, 0.109375, ((0, 4),)),
        "out_bias": centred(seeds[15], (D,), 0.3, 1.75, ((0, 4),)),
    }


@jax.custom_vjp
def low(v):
    return lax.optimization_barrier(v.astype(jnp.bfloat16)).astype(jnp.float32)

@jax.custom_vjp
def low_back(v):
    return v

def low_keep(v):
    return (low(v), None)

def low_pass(kept, grad):
    return (grad,)

def back_keep(v):
    return (v, None)

def back_low(kept, grad):
    return (low(grad),)
low.defvjp(low_keep, low_pass)
low_back.defvjp(back_keep, back_low)
precision_high = lax.Precision.HIGHEST

def positions(unit_counts, row_ids, rows_device, unit_rows):
    seq_ends = jnp.cumsum(unit_counts).astype(jnp.int32)
    seq_starts = seq_ends - unit_counts
    local_row = row_ids % rows_device
    device_row = row_ids // rows_device
    block_index = local_row // unit_rows
    seq_index = lax.optimization_barrier(jnp.sum((block_index[:, None] >= seq_ends[None, :]).astype(jnp.int32), axis=1))
    picked = (seq_index[:, None] == jnp.arange(unit_counts.shape[0], dtype=jnp.int32)[None, :]).astype(jnp.int32)
    first_row = lax.optimization_barrier(jnp.sum(picked * seq_starts[None, :], axis=1)) * unit_rows
    span_rows = lax.optimization_barrier(jnp.sum(picked * unit_counts[None, :], axis=1)) * unit_rows
    return (seq_index, device_row * span_rows + local_row - first_row)

def layer_norm(values, gain, offset):
    center = values - lax.optimization_barrier(jnp.mean(values, axis=-1, keepdims=True))
    spread = lax.optimization_barrier(jnp.mean(center * center, axis=-1, keepdims=True))
    return center * lax.rsqrt(spread + 1e-05) * gain + offset

def gelu_tanh(values):
    return 0.5 * values * (1.0 + jnp.tanh(0.7978845608028654 * (values + 0.044715 * values * values * values)))

def matmul(left, right):
    return jnp.dot(left, right, precision=precision_high, preferred_element_type=jnp.float32)

def forward(tokens, params, seq_index, seq_pos):
    attn_weight, query_bias, value_bias, proj_weight, proj_bias, ln1_gain, ln1_bias, ln2_gain, ln2_bias, fc_weight, fc_bias, out_weight, out_bias = params
    scale = 1.0 / math.sqrt(HD)
    rows = tokens.shape[0]
    normed = low(layer_norm(tokens, ln1_gain, ln1_bias))
    qkv_bias = jnp.concatenate([query_bias, jnp.zeros_like(query_bias), value_bias])
    qkv = low_back(low(matmul(normed, attn_weight) + qkv_bias))
    queries = qkv[:, :D].reshape(rows, HEADS, HD)
    keys = qkv[:, D:2 * D].reshape(rows, HEADS, HD)
    values = qkv[:, 2 * D:].reshape(rows, HEADS, HD)
    query_blocks = queries.reshape(N_SHARD, rows // N_SHARD, HEADS, HD)
    seq_blocks = seq_index.reshape(N_SHARD, rows // N_SHARD)
    pos_blocks = seq_pos.reshape(N_SHARD, rows // N_SHARD)

    @jax.checkpoint
    def attend(block):
        query_part, seq_part, pos_part = block
        scores = low_back(jnp.einsum('qhd,khd->hqk', query_part, keys, precision=precision_high) * scale)
        allowed = (seq_part[:, None] == seq_index[None, :]) & (seq_pos[None, :] <= pos_part[:, None])
        scores = jnp.where(allowed[None], scores, -1e+30)
        probs = low(jax.nn.softmax(scores, axis=-1))
        return jnp.einsum('hqk,khd->qhd', probs, values, precision=precision_high)
    mixed = lax.map(attend, (query_blocks, seq_blocks, pos_blocks)).reshape(rows, D)
    mixed = low_back(low(mixed))
    middle = tokens + low_back(matmul(mixed, proj_weight) + proj_bias)
    normed_two = low(layer_norm(middle, ln2_gain, ln2_bias))
    hidden = low_back(matmul(normed_two, fc_weight) + fc_bias)
    active = low(gelu_tanh(hidden))
    return middle + low_back(matmul(active, out_weight) + out_bias)

def reference(tokens, cotangent, lengths, attn_weight, query_bias, value_bias, proj_weight, proj_bias, ln1_gain, ln1_bias, ln2_gain, ln2_bias, fc_weight, fc_bias, out_weight, out_bias):
    params = tuple((weight.astype(jnp.float32) for weight in (attn_weight, query_bias, value_bias, proj_weight, proj_bias, ln1_gain, ln1_bias, ln2_gain, ln2_bias, fc_weight, fc_bias, out_weight, out_bias)))
    group_rows = TOK_DEV * N_SHARD
    row_ids = jnp.arange(group_rows, dtype=jnp.int32)

    def group_step(totals, inputs):
        group_tokens, group_cot, group_lengths = inputs
        seq_index, seq_pos = positions(group_lengths, row_ids, TOK_DEV, UNIT)

        def closed(token_values, param_values):
            return forward(token_values, param_values, seq_index, seq_pos)
        result, pull = jax.vjp(closed, group_tokens.astype(jnp.float32), params)
        token_grad, param_grads = pull(group_cot.astype(jnp.float32))
        totals = tuple((running + update for running, update in zip(totals, param_grads)))
        return (totals, (result.astype(jnp.bfloat16), token_grad.astype(jnp.bfloat16)))
    start = tuple((jnp.zeros_like(weight) for weight in params))
    totals, (output, input_grad) = lax.scan(group_step, start, (tokens, cotangent, lengths))
    return (output, input_grad, totals[0], totals[1], totals[2], totals[3], totals[4], totals[5], totals[6], totals[7], totals[8], totals[9], totals[10], totals[11], totals[12])
```

```python
import functools
import math

import jax
import jax.numpy as jnp
from jax import lax
from jax.experimental import pallas as pl
from jax.experimental.pallas import tpu as pltpu
from jax.sharding import PartitionSpec as P

D = 1600
HEADS = 25
HD = 64
UNIT = 32
LANES = 128
NEG = -1e30
BF = jnp.bfloat16
F32 = jnp.float32


def gelu_tanh(values):
    return (
        0.5
        * values
        * (1.0 + jnp.tanh(0.7978845608028654 * (values + 0.044715 * values * values * values)))
    )


def dot(left, right, dims):
    return lax.dot_general(left, right, (dims, ((), ())), preferred_element_type=F32)


def rows_dot(left, right):
    return dot(left, right, ((0,), (0,)))


def cols_dot(left, right):
    return dot(left, right, ((1,), (1,)))


def normalize(values):
    center = values - jnp.mean(values, axis=-1, keepdims=True)
    spread = jnp.mean(center * center, axis=-1, keepdims=True)
    inv = lax.rsqrt(spread + 1e-05)
    return center * inv, inv


def place_blocks(info_ref, shards, units):
    b0, b1, b2, me = info_ref[0], info_ref[1], info_ref[2], info_ref[3]
    e0, e1 = b0, b0 + b1
    places = []
    for d in range(shards):
        s = jnp.bitwise_xor(me, d)
        for u in range(units):
            first = jnp.where(u < e0, 0, jnp.where(u < e1, e0, e1))
            span = jnp.where(u < e0, b0, jnp.where(u < e1, b1, b2))
            places.append((d * units + u, first * shards + s * span + (u - first)))
    return places, e0, e1


def head_lanes(tile_rows, half):
    lane = lax.broadcasted_iota(jnp.int32, (tile_rows, LANES), 1)
    return (lane < HD) if half == 0 else (lane >= HD)


def window_scores(q, k, rows, width):
    scores = cols_dot(q, k)
    row = lax.broadcasted_iota(jnp.int32, (rows, width * rows), 0)
    col = lax.broadcasted_iota(jnp.int32, (rows, width * rows), 1)
    return jnp.where(col <= row + (width - 1) * rows, scores, NEG)


def fwd_kernel(shards, units, heads, info_ref, qkv_ref, out_ref, perm, mixed):
    block = UNIT
    rows = shards * block
    main = heads * HD
    places, e0, e1 = place_blocks(info_ref, shards, units)
    for src, dst in places:
        at = pl.ds(pl.multiple_of(dst * block, block), block)
        perm[at, :] = qkv_ref[src * block : (src + 1) * block, :]

    def unit(i, carry):
        first = jnp.where(i < e0, 0, jnp.where(i < e1, e0, e1))
        q_at = pl.ds(pl.multiple_of(i * rows, rows), rows)
        for width in range(1, 5):

            @pl.when(i - first + 1 == width)
            def _():
                k_at = pl.ds(pl.multiple_of(first * rows, rows), width * rows)

                def attend(q, k, v):
                    scores = window_scores(q * BF(0.125), k, rows, width)
                    top = jnp.max(scores, axis=1, keepdims=True)
                    probs = jnp.exp(scores - top)
                    total = jnp.sum(probs, axis=1, keepdims=True)
                    return dot(probs.astype(BF), v, ((1,), (0,))) / total

                for tile in range(main // LANES):
                    lanes = slice(tile * LANES, (tile + 1) * LANES)
                    k_lanes = slice(main + lanes.start, main + lanes.stop)
                    v_lanes = slice(2 * main + lanes.start, 2 * main + lanes.stop)
                    q, k, v = perm[q_at, lanes], perm[k_at, k_lanes], perm[k_at, v_lanes]
                    low = head_lanes(rows, 0)
                    zero = jnp.zeros_like(q)
                    left = attend(jnp.where(low, q, zero), k, v)
                    right = attend(jnp.where(low, zero, q), k, v)
                    mixed[q_at, lanes] = jnp.where(low, left, right).astype(BF)
                if main % LANES:
                    lanes = main - HD
                    mixed[q_at, lanes:main] = attend(
                        perm[q_at, lanes:main],
                        perm[k_at, main + lanes : 2 * main],
                        perm[k_at, 2 * main + lanes : 3 * main],
                    ).astype(BF)
                base = 3 * main
                mixed[q_at, main : main + HD] = attend(
                    perm[q_at, base : base + HD],
                    perm[k_at, base + HD : base + 2 * HD],
                    perm[k_at, base + 2 * HD : base + 3 * HD],
                ).astype(BF)

        return carry

    lax.fori_loop(0, units, unit, 0)
    for src, dst in places:
        at = pl.ds(pl.multiple_of(dst * block, block), block)
        out_ref[src * block : (src + 1) * block, :] = mixed[at, :]


def bwd_kernel(
    shards, units, heads, info_ref, qkv_ref, dmix_ref, out_ref, perm, dperm, dq_acc, dk_acc, dv_acc
):
    block = UNIT
    rows = shards * block
    main = heads * HD
    places, e0, e1 = place_blocks(info_ref, shards, units)
    for src, dst in places:
        at = pl.ds(pl.multiple_of(dst * block, block), block)
        perm[at, :] = qkv_ref[src * block : (src + 1) * block, :]
        dperm[at, :] = dmix_ref[src * block : (src + 1) * block, :]
    dk_acc[...] = jnp.zeros_like(dk_acc)
    dv_acc[...] = jnp.zeros_like(dv_acc)

    def unit(i, carry):
        first = jnp.where(i < e0, 0, jnp.where(i < e1, e0, e1))
        q_at = pl.ds(pl.multiple_of(i * rows, rows), rows)
        for width in range(1, 5):

            @pl.when(i - first + 1 == width)
            def _():
                k_at = pl.ds(pl.multiple_of(first * rows, rows), width * rows)

                def pull(q, k, v, g):
                    q = q * BF(0.125)
                    scores = window_scores(q, k, rows, width)
                    top = jnp.max(scores, axis=1, keepdims=True)
                    probs = jnp.exp(scores - top)
                    total = jnp.sum(probs, axis=1, keepdims=True)
                    probs = probs * (1.0 / total)
                    d_probs = cols_dot(g, v)
                    delta = jnp.sum(probs * d_probs, axis=1, keepdims=True)
                    d_scores = (probs * (d_probs - delta)).astype(BF)
                    d_q = dot(d_scores, k, ((1,), (0,))) * 0.125
                    return d_q, rows_dot(d_scores, q), rows_dot(probs.astype(BF), g)

                for tile in range(main // LANES):
                    lanes = slice(tile * LANES, (tile + 1) * LANES)
                    k_lanes = slice(main + lanes.start, main + lanes.stop)
                    v_lanes = slice(2 * main + lanes.start, 2 * main + lanes.stop)
                    q, k, v = perm[q_at, lanes], perm[k_at, k_lanes], perm[k_at, v_lanes]
                    g = dperm[q_at, lanes]
                    low = head_lanes(rows, 0)
                    zero = jnp.zeros_like(q)
                    dq0, dk0, dv0 = pull(jnp.where(low, q, zero), k, v, jnp.where(low, g, zero))
                    dq1, dk1, dv1 = pull(jnp.where(low, zero, q), k, v, jnp.where(low, zero, g))
                    dq_acc[q_at, lanes] = jnp.where(low, dq0, dq1).astype(BF)
                    dk_acc[k_at, lanes] += dk0 + dk1
                    dv_acc[k_at, lanes] += dv0 + dv1
                extra = [(main, 3 * main, 3 * main + HD, 3 * main + 2 * HD)]
                if main % LANES:
                    extra.append((main - HD, main - HD, 2 * main - HD, 3 * main - HD))
                for own, q_lane, k_lane, v_lane in extra:
                    dq0, dk0, dv0 = pull(
                        perm[q_at, q_lane : q_lane + HD],
                        perm[k_at, k_lane : k_lane + HD],
                        perm[k_at, v_lane : v_lane + HD],
                        dperm[q_at, own : own + HD],
                    )
                    dq_acc[q_at, own : own + HD] = dq0.astype(BF)
                    dk_acc[k_at, own : own + HD] += dk0
                    dv_acc[k_at, own : own + HD] += dv0

        return carry

    lax.fori_loop(0, units, unit, 0)
    for src, dst in places:
        at = pl.ds(pl.multiple_of(dst * block, block), block)
        to = slice(src * block, (src + 1) * block)
        for part, acc in enumerate((dq_acc, dk_acc, dv_acc)):
            got = acc[at, :].astype(BF)
            out_ref[to, part * main : (part + 1) * main] = got[:, :main]
            lane = 3 * main + part * HD
            out_ref[to, lane : lane + HD] = got[:, main:]


def vmem_call(kernel, out_shape, scratch, cost, inputs):
    return pl.pallas_call(
        kernel,
        out_shape=out_shape,
        in_specs=[pl.BlockSpec(memory_space=pltpu.SMEM)]
        + [pl.BlockSpec(memory_space=pltpu.VMEM)] * (len(inputs) - 1),
        out_specs=pl.BlockSpec(memory_space=pltpu.VMEM),
        scratch_shapes=scratch,
        compiler_params=pltpu.CompilerParams(vmem_limit_bytes=48 << 20),
        cost_estimate=cost,
    )(*inputs)


def attention_fwd(info, qkv, shards, heads):
    total, width = qkv.shape
    units = total // (shards * UNIT)
    own = (heads + 1) * HD
    return vmem_call(
        functools.partial(fwd_kernel, shards, units, heads),
        jax.ShapeDtypeStruct((total, own), BF),
        [pltpu.VMEM((total, width), BF), pltpu.VMEM((total, own), BF)],
        pl.CostEstimate(flops=10**10, bytes_accessed=total * width * 3, transcendentals=0),
        (info, qkv),
    )


def attention_bwd(info, qkv, d_mixed, shards, heads):
    total, width = qkv.shape
    units = total // (shards * UNIT)
    own = (heads + 1) * HD
    return vmem_call(
        functools.partial(bwd_kernel, shards, units, heads),
        jax.ShapeDtypeStruct((total, width), BF),
        [
            pltpu.VMEM((total, width), BF),
            pltpu.VMEM((total, own), BF),
            pltpu.VMEM((total, own), BF),
            pltpu.VMEM((total, own), F32),
            pltpu.VMEM((total, own), F32),
        ],
        pl.CostEstimate(flops=2 * 10**10, bytes_accessed=total * width * 5, transcendentals=0),
        (info, qkv, d_mixed),
    )


def body(
    tokens,
    cotangent,
    lengths,
    attn_weight,
    query_bias,
    value_bias,
    proj_weight,
    proj_bias,
    ln1_gain,
    ln1_bias,
    ln2_gain,
    ln2_bias,
    fc_weight,
    fc_bias,
    out_weight,
    out_bias,
):
    n = lax.axis_size("shard")
    reps = lax.axis_size("rep")
    me = lax.axis_index("shard")
    core = lax.axis_index("rep") % 2
    heads = (HEADS - 1) // n
    main = heads * HD
    spare = D - n * main
    own_rows = attn_weight.shape[0]

    def swap(value, d):
        return lax.ppermute(value, "shard", [(i, i ^ d) for i in range(n)])

    def swap_core(value):
        return lax.ppermute(value, "rep", [(i, i ^ 1) for i in range(reps)])

    def gather(value):
        return [value] + [swap(value, d) for d in range(1, n)]

    def pick(stacked, index):
        return lax.dynamic_index_in_dim(stacked, index, 0, keepdims=False)

    def natural(pieces):
        stacked = jnp.stack(pieces)
        return [pick(stacked, me ^ j) for j in range(n)]

    half_rows = -(-own_rows // 32) * 16
    half_step = own_rows - half_rows

    def share(pieces):
        mine = jnp.stack(pieces)
        other = swap_core(mine)
        low = jnp.where(core == 0, mine, other)
        high = jnp.where(core == 0, other, mine)
        whole = jnp.concatenate([low[:, :half_step], high], axis=1)
        return whole.reshape(n * own_rows, whole.shape[2])

    def own_half(value):
        return lax.dynamic_slice_in_dim(value, core * half_step, half_rows, value.ndim - 2)

    def scatter_weight(parts):
        parts = own_half(parts)
        got = [pick(parts, me)] + [swap(pick(parts, me ^ d), d) for d in range(1, n)]
        return share(natural(got))

    def reduce_rows(parts):
        total = parts[0]
        for d in range(1, n):
            total = total + swap(parts[d].astype(BF), d).astype(F32)
        return total

    group_tokens = jnp.concatenate(gather(tokens[0]), axis=0)
    small = jnp.stack(
        [query_bias, value_bias, proj_bias, ln1_gain, ln1_bias, ln2_gain, ln2_bias, out_bias]
    )
    small = jnp.stack(natural(gather(small)), axis=1).reshape(8, D).astype(F32)
    b_query, b_value, b_proj, gain_one, bias_one, gain_two, bias_two, b_out = [
        small[i] for i in range(8)
    ]
    by_part = attn_weight.reshape(own_rows, 3, D)
    for_dest = jnp.stack(
        [by_part[:, :, j * main : (j + 1) * main].reshape(own_rows, 3 * main) for j in range(n)]
    )
    for_all = by_part[:, :, n * main :].reshape(own_rows, 3 * spare)
    w_attn = scatter_weight(
        jnp.concatenate(
            [for_dest, jnp.broadcast_to(for_all[None], (n, own_rows, 3 * spare))], axis=2
        )
    )
    w_proj = share(natural(gather(own_half(proj_weight))))
    own_ff = fc_bias.shape[0]
    w_fc = scatter_weight(fc_weight.reshape(own_rows, n, own_ff).transpose(1, 0, 2))
    group_cot = jnp.concatenate(gather(cotangent[0]), axis=0)
    own_cot = cotangent[0]

    def my_columns(vector):
        return jnp.concatenate(
            [lax.dynamic_slice_in_dim(vector, me * main, main, 0)], axis=0
        ), vector[n * main :]

    q_main, q_spare = my_columns(b_query)
    v_main, v_spare = my_columns(b_value)
    qkv_bias = jnp.concatenate(
        [q_main, jnp.zeros_like(q_main), v_main, q_spare, jnp.zeros_like(q_spare), v_spare]
    )

    rows = tokens.shape[1]
    xhat_one, _ = normalize(group_tokens.astype(F32))
    normed = (xhat_one * gain_one + bias_one).astype(BF)
    qkv = (jnp.dot(normed, w_attn, preferred_element_type=F32) + qkv_bias).astype(BF)
    info = jnp.concatenate([lengths[0], me.astype(jnp.int32)[None]])
    mixed_heads = attention_fwd(info, qkv, n, heads)

    def block(value, d):
        return value[d * rows : (d + 1) * rows]

    got = [block(mixed_heads, 0)[:, :main]] + [
        swap(block(mixed_heads, d)[:, :main], d) for d in range(1, n)
    ]
    mixed_low = jnp.concatenate(natural(got) + [block(mixed_heads, 0)[:, main:]], axis=1)
    own_tokens = tokens[0].astype(F32)
    middle = own_tokens + jnp.dot(mixed_low, w_proj, preferred_element_type=F32) + b_proj
    xhat_two, inv_two = normalize(middle)
    own_normed_two = (xhat_two * gain_two + bias_two).astype(BF)
    normed_two = jnp.concatenate(gather(own_normed_two), axis=0)
    hidden = jnp.dot(normed_two, w_fc, preferred_element_type=F32) + fc_bias.astype(F32)
    active, gelu_pull = jax.vjp(gelu_tanh, hidden)
    active = active.astype(BF)

    grad_out_weight = rows_dot(active, group_cot).astype(BF)
    sum_out_weight = lax.psum(grad_out_weight, "rep").astype(F32)
    d_active = cols_dot(group_cot, out_weight)
    d_hidden = gelu_pull(d_active)[0].astype(BF)
    e_parts = [cols_dot(block(d_hidden, d), w_fc) for d in range(n)]
    e = reduce_rows(e_parts)
    out_parts = [
        jnp.dot(block(active, d), out_weight, preferred_element_type=F32) for d in range(n)
    ]
    output = (middle + reduce_rows(out_parts) + b_out).astype(BF)[None]
    grad_fc = rows_dot(normed_two, d_hidden).astype(BF).reshape(n, own_rows, own_ff)
    got = [pick(grad_fc, me)] + [swap(pick(grad_fc, me ^ d), d) for d in range(1, n)]
    grad_fc_weight = jnp.stack(natural(got), axis=1).reshape(own_rows, n * own_ff)
    sum_fc_weight = lax.psum(grad_fc_weight, "rep").astype(F32)
    grad_fc_bias = jnp.sum(d_hidden.astype(F32), axis=0)
    e_gain = e * gain_two
    d_middle = own_cot.astype(F32) + inv_two * (
        e_gain
        - jnp.mean(e_gain, axis=-1, keepdims=True)
        - xhat_two * jnp.mean(e_gain * xhat_two, axis=-1, keepdims=True)
    )

    d_branch = d_middle.astype(BF)
    d_mixed = cols_dot(d_branch, w_proj).astype(BF)
    for_heads = jnp.stack([d_mixed[:, j * main : (j + 1) * main] for j in range(n)])
    last = d_mixed[:, n * main :]
    got = [jnp.concatenate([pick(for_heads, me), last], axis=1)] + [
        swap(jnp.concatenate([pick(for_heads, me ^ d), last], axis=1), d) for d in range(1, n)
    ]
    d_qkv = attention_bwd(info, qkv, jnp.concatenate(got, axis=0), n, heads)
    counted = (lax.broadcasted_iota(jnp.int32, (n * rows, 1), 0) < rows) | (
        lax.broadcasted_iota(jnp.int32, (1, d_qkv.shape[1]), 1) < 3 * main
    )
    d_once = jnp.where(counted, d_qkv, BF(0))
    f_parts = [cols_dot(block(d_once, d), w_attn) for d in range(n)]
    f = reduce_rows(f_parts)
    xhat_own, inv_own = normalize(own_tokens)
    f_gain = f * gain_one
    d_tokens = inv_own * (
        f_gain
        - jnp.mean(f_gain, axis=-1, keepdims=True)
        - xhat_own * jnp.mean(f_gain * xhat_own, axis=-1, keepdims=True)
    )
    input_grad = (d_middle + d_tokens).astype(BF)[None]

    grad_proj = rows_dot(mixed_low, d_branch).reshape(n, own_rows, D)
    grad_proj_weight = reduce_rows([pick(grad_proj, me ^ d) for d in range(n)]).astype(BF)

    grad_attn = rows_dot(normed, d_qkv).astype(BF).reshape(n, own_rows, d_qkv.shape[1])
    got = [pick(grad_attn, me)[:, : 3 * main]] + [
        swap(pick(grad_attn, me ^ d)[:, : 3 * main], d) for d in range(1, n)
    ]
    got = natural(got)
    last = pick(grad_attn, me)[:, 3 * main :]
    grad_attn_weight = jnp.concatenate(
        [
            piece
            for part in range(3)
            for piece in [g[:, part * main : (part + 1) * main] for g in got]
            + [last[:, part * spare : (part + 1) * spare]]
        ],
        axis=1,
    )
    sum_attn_weight = lax.psum(grad_attn_weight, "rep").astype(F32)
    sum_proj_weight = lax.psum(grad_proj_weight, "rep").astype(F32)

    d_once_sum = jnp.sum(d_once.astype(F32), axis=0)

    def vector_of(part):
        whole = jnp.zeros((D,), F32)
        whole = lax.dynamic_update_slice_in_dim(
            whole, d_once_sum[part * main : (part + 1) * main], me * main, 0
        )
        lane = 3 * main + part * spare
        return jnp.concatenate([whole[: n * main], d_once_sum[lane : lane + spare]])

    small_grads = jnp.stack(
        [
            vector_of(0),
            vector_of(2),
            jnp.sum(d_branch.astype(F32), axis=0),
            jnp.sum(f * xhat_own, axis=0),
            jnp.sum(f, axis=0),
            jnp.sum(e * xhat_two, axis=0),
            jnp.sum(e, axis=0),
            jnp.sum(own_cot.astype(F32), axis=0),
        ]
    )
    small_grads = small_grads.reshape(8, n, own_rows).transpose(1, 0, 2)
    small_own = pick(small_grads, me)
    for d in range(1, n):
        small_own = small_own + swap(pick(small_grads, me ^ d), d)
    small_sum = lax.psum(
        jnp.concatenate([small_own.reshape(-1), grad_fc_bias]), "rep"
    )
    s = small_sum[: 8 * own_rows].reshape(8, own_rows)
    sum_fc_bias = small_sum[8 * own_rows :]
    return (
        output,
        input_grad,
        sum_attn_weight,
        s[0],
        s[1],
        sum_proj_weight,
        s[2],
        s[3],
        s[4],
        s[5],
        s[6],
        sum_fc_weight,
        sum_fc_bias,
        sum_out_weight,
        s[7],
    )


def solution(mesh):
    return jax.shard_map(
        body,
        mesh=mesh,
        in_specs=(
            P("rep", "shard", None),
            P("rep", "shard", None),
            P("rep", None),
            P("shard", None),
            P("shard"),
            P("shard"),
            P("shard", None),
            P("shard"),
            P("shard"),
            P("shard"),
            P("shard"),
            P("shard"),
            P("shard", None),
            P("shard"),
            P("shard", None),
            P("shard"),
        ),
        out_specs=(
            P("rep", "shard", None),
            P("rep", "shard", None),
            P("shard", None),
            P("shard"),
            P("shard"),
            P("shard", None),
            P("shard"),
            P("shard"),
            P("shard"),
            P("shard"),
            P("shard"),
            P("shard", None),
            P("shard"),
            P("shard", None),
            P("shard"),
        ),
        check_vma=False,
    )
```

```python
import functools
import math

import jax
import jax.numpy as jnp
from jax import lax
from jax.experimental import pallas as pl
from jax.experimental.pallas import tpu as pltpu
from jax.sharding import PartitionSpec as P

D = 1600
HEADS = 25
HD = 64
UNIT = 32
LANES = 128
NEG = -1e30
BF = jnp.bfloat16
F32 = jnp.float32


def dot(left, right, dims):
    return lax.dot_general(left, right, (dims, ((), ())), preferred_element_type=F32)


def rows_dot(left, right):
    return dot(left, right, ((0,), (0,)))


def cols_dot(left, right):
    return dot(left, right, ((1,), (1,)))


def normalize(values):
    center = values - jnp.mean(values, axis=-1, keepdims=True)
    spread = jnp.mean(center * center, axis=-1, keepdims=True)
    inv = lax.rsqrt(spread + 1e-05)
    return center * inv, inv


def place_blocks(info_ref, shards, units):
    b0, b1, b2, me = info_ref[0], info_ref[1], info_ref[2], info_ref[3]
    e0, e1 = b0, b0 + b1
    places = []
    for d in range(shards):
        s = jnp.bitwise_xor(me, d)
        for u in range(units):
            first = jnp.where(u < e0, 0, jnp.where(u < e1, e0, e1))
            span = jnp.where(u < e0, b0, jnp.where(u < e1, b1, b2))
            places.append((d * units + u, first * shards + s * span + (u - first)))
    return places, e0, e1


def head_lanes(tile_rows, half):
    lane = lax.broadcasted_iota(jnp.int32, (tile_rows, LANES), 1)
    return (lane < HD) if half == 0 else (lane >= HD)


def window_scores(q, k, rows, width):
    scores = cols_dot(q, k)
    row = lax.broadcasted_iota(jnp.int32, (rows, width * rows), 0)
    col = lax.broadcasted_iota(jnp.int32, (rows, width * rows), 1)
    return jnp.where(col <= row + (width - 1) * rows, scores, NEG)


def fwd_kernel(shards, units, heads, info_ref, qkv_ref, out_ref, perm, mixed):
    block = UNIT
    rows = shards * block
    main = heads * HD
    places, e0, e1 = place_blocks(info_ref, shards, units)
    for src, dst in places:
        at = pl.ds(pl.multiple_of(dst * block, block), block)
        perm[at, :] = qkv_ref[src * block : (src + 1) * block, :]

    def unit(i, carry):
        first = jnp.where(i < e0, 0, jnp.where(i < e1, e0, e1))
        q_at = pl.ds(pl.multiple_of(i * rows, rows), rows)
        for width in range(1, 5):

            @pl.when(i - first + 1 == width)
            def _():
                k_at = pl.ds(pl.multiple_of(first * rows, rows), width * rows)

                def attend(q, k, v):
                    scores = window_scores(q * BF(0.125), k, rows, width)
                    top = jnp.max(scores, axis=1, keepdims=True)
                    probs = jnp.exp(scores - top)
                    total = jnp.sum(probs, axis=1, keepdims=True)
                    return dot(probs.astype(BF), v, ((1,), (0,))) / total

                for tile in range(main // LANES):
                    lanes = slice(tile * LANES, (tile + 1) * LANES)
                    k_lanes = slice(main + lanes.start, main + lanes.stop)
                    v_lanes = slice(2 * main + lanes.start, 2 * main + lanes.stop)
                    q, k, v = perm[q_at, lanes], perm[k_at, k_lanes], perm[k_at, v_lanes]
                    low = head_lanes(rows, 0)
                    zero = jnp.zeros_like(q)
                    left = attend(jnp.where(low, q, zero), k, v)
                    right = attend(jnp.where(low, zero, q), k, v)
                    mixed[q_at, lanes] = jnp.where(low, left, right).astype(BF)
                if main % LANES:
                    lanes = main - HD
                    mixed[q_at, lanes:main] = attend(
                        perm[q_at, lanes:main],
                        perm[k_at, main + lanes : 2 * main],
                        perm[k_at, 2 * main + lanes : 3 * main],
                    ).astype(BF)
                base = 3 * main
                mixed[q_at, main : main + HD] = attend(
                    perm[q_at, base : base + HD],
                    perm[k_at, base + HD : base + 2 * HD],
                    perm[k_at, base + 2 * HD : base + 3 * HD],
                ).astype(BF)

        return carry

    lax.fori_loop(0, units, unit, 0)
    for src, dst in places:
        at = pl.ds(pl.multiple_of(dst * block, block), block)
        out_ref[src * block : (src + 1) * block, :] = mixed[at, :]


def bwd_kernel(
    shards, units, heads, info_ref, qkv_ref, dmix_ref, out_ref, perm, dperm, dq_acc, dk_acc, dv_acc
):
    block = UNIT
    rows = shards * block
    main = heads * HD
    places, e0, e1 = place_blocks(info_ref, shards, units)
    for src, dst in places:
        at = pl.ds(pl.multiple_of(dst * block, block), block)
        perm[at, :] = qkv_ref[src * block : (src + 1) * block, :]
        dperm[at, :] = dmix_ref[src * block : (src + 1) * block, :]
    dk_acc[...] = jnp.zeros_like(dk_acc)
    dv_acc[...] = jnp.zeros_like(dv_acc)

    def unit(i, carry):
        first = jnp.where(i < e0, 0, jnp.where(i < e1, e0, e1))
        q_at = pl.ds(pl.multiple_of(i * rows, rows), rows)
        for width in range(1, 5):

            @pl.when(i - first + 1 == width)
            def _():
                k_at = pl.ds(pl.multiple_of(first * rows, rows), width * rows)

                def pull(q, k, v, g):
                    q = q * BF(0.125)
                    scores = window_scores(q, k, rows, width)
                    top = jnp.max(scores, axis=1, keepdims=True)
                    probs = jnp.exp(scores - top)
                    total = jnp.sum(probs, axis=1, keepdims=True)
                    probs = probs * (1.0 / total)
                    d_probs = cols_dot(g, v)
                    delta = jnp.sum(probs * d_probs, axis=1, keepdims=True)
                    d_scores = (probs * (d_probs - delta)).astype(BF)
                    d_q = dot(d_scores, k, ((1,), (0,))) * 0.125
                    return d_q, rows_dot(d_scores, q), rows_dot(probs.astype(BF), g)

                for tile in range(main // LANES):
                    lanes = slice(tile * LANES, (tile + 1) * LANES)
                    k_lanes = slice(main + lanes.start, main + lanes.stop)
                    v_lanes = slice(2 * main + lanes.start, 2 * main + lanes.stop)
                    q, k, v = perm[q_at, lanes], perm[k_at, k_lanes], perm[k_at, v_lanes]
                    g = dperm[q_at, lanes]
                    low = head_lanes(rows, 0)
                    zero = jnp.zeros_like(q)
                    dq0, dk0, dv0 = pull(jnp.where(low, q, zero), k, v, jnp.where(low, g, zero))
                    dq1, dk1, dv1 = pull(jnp.where(low, zero, q), k, v, jnp.where(low, zero, g))
                    dq_acc[q_at, lanes] = jnp.where(low, dq0, dq1).astype(BF)
                    dk_acc[k_at, lanes] += dk0 + dk1
                    dv_acc[k_at, lanes] += dv0 + dv1
                extra = [(main, 3 * main, 3 * main + HD, 3 * main + 2 * HD)]
                if main % LANES:
                    extra.append((main - HD, main - HD, 2 * main - HD, 3 * main - HD))
                for own, q_lane, k_lane, v_lane in extra:
                    dq0, dk0, dv0 = pull(
                        perm[q_at, q_lane : q_lane + HD],
                        perm[k_at, k_lane : k_lane + HD],
                        perm[k_at, v_lane : v_lane + HD],
                        dperm[q_at, own : own + HD],
                    )
                    dq_acc[q_at, own : own + HD] = dq0.astype(BF)
                    dk_acc[k_at, own : own + HD] += dk0
                    dv_acc[k_at, own : own + HD] += dv0

        return carry

    lax.fori_loop(0, units, unit, 0)
    for src, dst in places:
        at = pl.ds(pl.multiple_of(dst * block, block), block)
        to = slice(src * block, (src + 1) * block)
        for part, acc in enumerate((dq_acc, dk_acc, dv_acc)):
            got = acc[at, :].astype(BF)
            out_ref[to, part * main : (part + 1) * main] = got[:, :main]
            lane = 3 * main + part * HD
            out_ref[to, lane : lane + HD] = got[:, main:]


def vmem_call(kernel, out_shape, scratch, cost, inputs):
    return pl.pallas_call(
        kernel,
        out_shape=out_shape,
        in_specs=[pl.BlockSpec(memory_space=pltpu.SMEM)]
        + [pl.BlockSpec(memory_space=pltpu.VMEM)] * (len(inputs) - 1),
        out_specs=pl.BlockSpec(memory_space=pltpu.VMEM),
        scratch_shapes=scratch,
        compiler_params=pltpu.CompilerParams(vmem_limit_bytes=48 << 20),
        cost_estimate=cost,
    )(*inputs)


def attention_fwd(info, qkv, shards, heads):
    total, width = qkv.shape
    units = total // (shards * UNIT)
    own = (heads + 1) * HD
    return vmem_call(
        functools.partial(fwd_kernel, shards, units, heads),
        jax.ShapeDtypeStruct((total, own), BF),
        [pltpu.VMEM((total, width), BF), pltpu.VMEM((total, own), BF)],
        pl.CostEstimate(flops=10**10, bytes_accessed=total * width * 3, transcendentals=0),
        (info, qkv),
    )


def attention_bwd(info, qkv, d_mixed, shards, heads):
    total, width = qkv.shape
    units = total // (shards * UNIT)
    own = (heads + 1) * HD
    return vmem_call(
        functools.partial(bwd_kernel, shards, units, heads),
        jax.ShapeDtypeStruct((total, width), BF),
        [
            pltpu.VMEM((total, width), BF),
            pltpu.VMEM((total, own), BF),
            pltpu.VMEM((total, own), BF),
            pltpu.VMEM((total, own), F32),
            pltpu.VMEM((total, own), F32),
        ],
        pl.CostEstimate(flops=2 * 10**10, bytes_accessed=total * width * 5, transcendentals=0),
        (info, qkv, d_mixed),
    )


def on_place(me, core, shards, run):
    for m in range(shards):
        for c in range(2):

            @pl.when((me == m) & (core == c))
            def _():
                run(m, c)


def attn_columns(value, j, heads):
    main = heads * HD
    first = D // main * main
    parts = [value[:, p * D + j * main : p * D + (j + 1) * main] for p in range(3)]
    parts += [value[:, p * D + first : (p + 1) * D] for p in range(3)]
    return jnp.concatenate(parts, axis=1)


def fc_columns(value, j, width):
    return value[:, j * width : (j + 1) * width]


def pack_kernel(shards, half, step, columns, at_ref, dep_ref, weight_ref, *outs):
    del dep_ref

    def run(m, c):
        outs[0][...] = columns(weight_ref, m)
        for d in range(1, shards):
            piece = columns(weight_ref.at[c * step : c * step + half], m ^ d)
            outs[d][...] = piece

    on_place(at_ref[0], at_ref[1], shards, run)


def place_kernel(shards, half, step, rows, at_ref, *refs):
    own, mine, other, out = refs[0], refs[1:shards], refs[shards], refs[shards + 1]

    def run(m, c):
        out[m * rows : (m + 1) * rows, :] = own[...]
        for d in range(1, shards):
            base = (m ^ d) * rows
            low, high = (mine[d - 1][...], other[d - 1]) if c == 0 else (other[d - 1], mine[d - 1][...])
            out[base : base + step, :] = low[:step]
            out[base + step : base + rows, :] = high

    on_place(at_ref[0], at_ref[1], shards, run)


def unpack_kernel(shards, half, step, columns, at_ref, *refs):
    mine, other, out = refs[:shards], refs[shards], refs[shards + 1]

    def run(m, c):
        for d in range(shards):
            for where, low, high in columns(m, d):
                width = high - low
                a = mine[d][:, low:high]
                b = other[d, :, low:high]
                first, second = (a, b) if c == 0 else (b, a)
                out[:step, where : where + width] = first[:step].astype(F32)
                out[step:, where : where + width] = second.astype(F32)

    on_place(at_ref[0], at_ref[1], shards, run)


def local_call(kernel, out_shape, cost_bytes, at, *inputs, anywhere=()):
    vmem = pl.BlockSpec(memory_space=pltpu.VMEM)
    specs = [pl.BlockSpec(memory_space=pl.ANY) if i in anywhere else vmem for i in range(len(inputs))]
    return pl.pallas_call(
        kernel,
        out_shape=out_shape,
        in_specs=[pl.BlockSpec(memory_space=pltpu.SMEM)] + specs,
        out_specs=jax.tree.map(lambda _: vmem, out_shape),
        compiler_params=pltpu.CompilerParams(vmem_limit_bytes=48 << 20),
        cost_estimate=pl.CostEstimate(flops=0, bytes_accessed=cost_bytes, transcendentals=0),
    )(at, *inputs)


def body(
    tokens,
    cotangent,
    lengths,
    attn_weight,
    query_bias,
    value_bias,
    proj_weight,
    proj_bias,
    ln1_gain,
    ln1_bias,
    ln2_gain,
    ln2_bias,
    fc_weight,
    fc_bias,
    out_weight,
    out_bias,
):
    n = lax.axis_size("shard")
    planes = lax.axis_size("plane")
    me = lax.axis_index("shard")
    core = lax.axis_index("core")
    heads = (HEADS - 1) // n
    main = heads * HD
    spare = D - n * main
    own_rows = attn_weight.shape[0]
    own_ff = fc_bias.shape[0]
    rows = tokens.shape[1]
    half = -(-own_rows // 32) * 16
    step = own_rows - half
    at = jnp.stack([me, core]).astype(jnp.int32)

    def swap(value, d):
        return lax.ppermute(value, "shard", [(i, i ^ d) for i in range(n)])

    def swap_core(value):
        return lax.ppermute(value, "core", [(0, 1), (1, 0)])

    def gather(value):
        if n != 4:
            return [value] + [swap(value, d) for d in range(1, n)]
        cut = value.shape[0] // 32 * 16
        one, two = swap(value, 1), swap(value, 2)
        three = jnp.concatenate([swap(one[:cut], 2), swap(two[cut:], 1)], axis=0)
        return [value, one, two, three]

    def pick(stacked, index):
        return lax.dynamic_index_in_dim(stacked, index, 0, keepdims=False)

    def natural(pieces):
        stacked = jnp.stack(pieces)
        return [pick(stacked, me ^ j) for j in range(n)]

    def after(value, *deps):
        return lax.optimization_barrier((value, deps))[0]

    def block(value, d):
        return value[d * rows : (d + 1) * rows]

    def place(own, mine):
        other = swap_core(jnp.stack(mine))
        return local_call(
            functools.partial(place_kernel, n, half, step, own_rows),
            jax.ShapeDtypeStruct((n * own_rows, own.shape[1]), BF),
            n * own.size * 4,
            at,
            own,
            *mine,
            other,
        )

    def pack(weight, columns, width, dep):
        shapes = [jax.ShapeDtypeStruct((own_rows, width), BF)]
        shapes += [jax.ShapeDtypeStruct((half, width), BF)] * (n - 1)
        return local_call(
            functools.partial(pack_kernel, n, half, step, columns),
            shapes,
            weight.size * 2,
            at,
            dep,
            weight,
            anywhere=(0,),
        )

    def reduce_rows(parts):
        total = parts[0].astype(F32)
        for d in range(1, n):
            total = total + swap(parts[d].astype(BF), d).astype(F32)
        return total

    def core_halves(parts):
        keep = lax.dynamic_slice_in_dim(parts, core * step, half, 1)
        give = lax.dynamic_slice_in_dim(parts, (1 - core) * step, half, 1)
        return (keep.astype(F32) + swap_core(give).astype(F32)).astype(BF)

    small = jnp.stack(
        [query_bias, value_bias, proj_bias, ln1_gain, ln1_bias, ln2_gain, ln2_bias, out_bias]
    )
    tokens_parts = gather(tokens[0])
    attn_width = 3 * (main + spare)
    attn_sent = pack(
        attn_weight, lambda ref, j: attn_columns(ref, j, heads), attn_width, lengths
    )
    attn_got = [swap(attn_sent[d], d) for d in range(1, n)]
    small = jnp.stack(natural([small] + [swap(small, d) for d in range(1, n)]), axis=1)
    small = small.reshape(8, D).astype(F32)
    b_query, b_value, b_proj, gain_one, bias_one, gain_two, bias_two, b_out = [
        small[i] for i in range(8)
    ]
    w_attn = place(attn_sent[0], attn_got)

    def my_columns(vector):
        return lax.dynamic_slice_in_dim(vector, me * main, main, 0), vector[n * main :]

    q_main, q_spare = my_columns(b_query)
    v_main, v_spare = my_columns(b_value)
    qkv_bias = jnp.concatenate(
        [q_main, jnp.zeros_like(q_main), v_main, q_spare, jnp.zeros_like(q_spare), v_spare]
    )

    fc_sent = pack(fc_weight, lambda ref, j: fc_columns(ref, j, own_ff), own_ff, attn_got[0])
    fc_got = [swap(fc_sent[d], d) for d in range(1, n)]
    w_fc = place(fc_sent[0], fc_got)
    proj_half = lax.dynamic_slice_in_dim(after(proj_weight, attn_got[0]), core * step, half, 0)
    proj_mine = lax.all_gather(proj_half, "shard", axis=0, tiled=False)
    proj_other = swap_core(proj_mine)
    proj_low = jnp.where(core == 0, proj_mine, proj_other)
    proj_high = jnp.where(core == 0, proj_other, proj_mine)
    w_proj = jnp.concatenate([proj_low[:, :step], proj_high], axis=1).reshape(D, D)
    own_cot = cotangent[0]
    cot_all = lax.all_gather(after(own_cot, proj_mine), "shard", axis=0, tiled=False)
    group_cot = jnp.concatenate([pick(cot_all, me ^ d) for d in range(n)], axis=0)

    group_tokens = jnp.concatenate(tokens_parts, axis=0)
    xhat_one, _ = normalize(group_tokens.astype(F32))
    normed = (xhat_one * gain_one + bias_one).astype(BF)
    qkv = (jnp.dot(normed, w_attn, preferred_element_type=F32) + qkv_bias).astype(BF)
    info = jnp.concatenate([lengths[0], me.astype(jnp.int32)[None]])
    mixed_heads = attention_fwd(info, qkv, n, heads)
    got = [block(mixed_heads, 0)[:, :main]] + [
        swap(block(mixed_heads, d)[:, :main], d) for d in range(1, n)
    ]
    mixed_low = jnp.concatenate(natural(got) + [block(mixed_heads, 0)[:, main:]], axis=1)
    own_tokens = tokens[0].astype(F32)
    middle = own_tokens + jnp.dot(mixed_low, w_proj, preferred_element_type=F32) + b_proj
    xhat_two, inv_two = normalize(middle)
    own_normed_two = (xhat_two * gain_two + bias_two).astype(BF)
    normed_two = jnp.concatenate(gather(own_normed_two), axis=0)
    hidden = jnp.dot(normed_two, w_fc, preferred_element_type=F32) + fc_bias.astype(F32)
    inner = jnp.tanh(0.7978845608028654 * (hidden + 0.044715 * hidden * hidden * hidden))
    active = (0.5 * hidden * (1.0 + inner)).astype(BF)
    slope = 0.5 * (1.0 + inner) + 0.5 * hidden * (1.0 - inner * inner) * (
        0.7978845608028654 * (1.0 + 3 * 0.044715 * hidden * hidden)
    )
    slope = slope.astype(BF)

    grad_out_weight = rows_dot(active, group_cot).astype(BF)
    sum_out_weight = lax.psum(grad_out_weight, ("plane", "core"))
    d_active = after(cols_dot(group_cot, out_weight))
    d_hidden = (d_active * slope.astype(F32)).astype(BF)
    e = reduce_rows([cols_dot(block(d_hidden, d), w_fc) for d in range(n)])
    e_gain = e * gain_two
    d_middle = own_cot.astype(F32) + inv_two * (
        e_gain
        - jnp.mean(e_gain, axis=-1, keepdims=True)
        - xhat_two * jnp.mean(e_gain * xhat_two, axis=-1, keepdims=True)
    )
    d_branch = d_middle.astype(BF)
    d_mixed = cols_dot(d_branch, w_proj).astype(BF)
    for_heads = jnp.stack([d_mixed[:, j * main : (j + 1) * main] for j in range(n)])
    last = d_mixed[:, n * main :]
    dmix_parts = [jnp.concatenate([pick(for_heads, me), last], axis=1)] + [
        swap(jnp.concatenate([pick(for_heads, me ^ d), last], axis=1), d) for d in range(1, n)
    ]

    grad_fc = rows_dot(normed_two, d_hidden).astype(BF).reshape(n, own_rows, own_ff)
    fc_halves = after(core_halves(grad_fc), dmix_parts)
    fc_parts = [pick(fc_halves, me)] + [swap(pick(fc_halves, me ^ d), d) for d in range(1, n)]
    fc_parts = after(fc_parts, sum_out_weight)
    fc_parts = lax.psum(tuple(fc_parts), "plane")
    grad_fc_bias = jnp.sum(d_hidden.astype(F32), axis=0)

    d_qkv = attention_bwd(info, qkv, jnp.concatenate(dmix_parts, axis=0), n, heads)

    grad_proj = rows_dot(mixed_low, d_branch).astype(BF).reshape(n, own_rows, D)
    proj_halves = core_halves(grad_proj)
    proj_sum = reduce_rows([pick(proj_halves, me ^ d) for d in range(n)]).astype(BF)

    grad_main = rows_dot(normed, d_qkv[:, : 3 * main]).astype(BF).reshape(n, own_rows, 3 * main)
    grad_spare = rows_dot(normed, d_qkv[:, 3 * main :]).astype(BF).reshape(n, own_rows, 3 * spare)
    main_halves = core_halves(grad_main)
    spare_halves = core_halves(pick(grad_spare, me)[None])[0]
    attn_parts = [jnp.concatenate([pick(main_halves, me), spare_halves], axis=1)]
    attn_parts += [swap(pick(main_halves, me ^ d), d) for d in range(1, n)]
    attn_parts = after(attn_parts, fc_parts)
    sums = lax.psum(tuple(attn_parts) + (proj_sum,), "plane")
    attn_parts, proj_sum = sums[:n], sums[n]

    counted = (lax.broadcasted_iota(jnp.int32, (n * rows, 1), 0) < rows) | (
        lax.broadcasted_iota(jnp.int32, (1, d_qkv.shape[1]), 1) < 3 * main
    )
    d_once = jnp.where(counted, d_qkv, BF(0))
    f = reduce_rows([cols_dot(block(d_once, d), w_attn) for d in range(n)])
    xhat_own, inv_own = normalize(own_tokens)
    f_gain = f * gain_one
    d_tokens = inv_own * (
        f_gain
        - jnp.mean(f_gain, axis=-1, keepdims=True)
        - xhat_own * jnp.mean(f_gain * xhat_own, axis=-1, keepdims=True)
    )
    input_grad = (d_middle + d_tokens).astype(BF)[None]

    out_parts = [
        jnp.dot(block(active, d), out_weight, preferred_element_type=F32) for d in range(n)
    ]
    output = (middle + reduce_rows(out_parts) + b_out).astype(BF)[None]

    sum_fc_weight = local_call(
        functools.partial(
            unpack_kernel, n, half, step, lambda m, d: [((m ^ d) * own_ff, 0, own_ff)]
        ),
        jax.ShapeDtypeStruct((own_rows, n * own_ff), F32),
        own_rows * n * own_ff * 8,
        at,
        *fc_parts,
        swap_core(jnp.stack(fc_parts)),
    )

    def attn_places(m, d):
        places = [(p * D + (m ^ d) * main, p * main, (p + 1) * main) for p in range(3)]
        if d == 0:
            places += [
                (p * D + n * main, 3 * main + p * spare, 3 * main + (p + 1) * spare)
                for p in range(3)
            ]
        return places

    padded = [attn_parts[0]] + [
        jnp.pad(part, ((0, 0), (0, 3 * spare))) for part in attn_parts[1:]
    ]
    sum_attn_weight = local_call(
        functools.partial(unpack_kernel, n, half, step, attn_places),
        jax.ShapeDtypeStruct((own_rows, 3 * D), F32),
        own_rows * 3 * D * 8,
        at,
        *attn_parts,
        swap_core(jnp.stack(padded)),
    )
    proj_other = swap_core(proj_sum)
    proj_low = jnp.where(core == 0, proj_sum, proj_other)
    proj_high = jnp.where(core == 0, proj_other, proj_sum)
    sum_proj_weight = jnp.concatenate([proj_low[:step], proj_high], axis=0).astype(F32)

    d_once_sum = jnp.sum(d_once.astype(F32), axis=0)

    def vector_of(part):
        whole = jnp.zeros((D,), F32)
        whole = lax.dynamic_update_slice_in_dim(
            whole, d_once_sum[part * main : (part + 1) * main], me * main, 0
        )
        lane = 3 * main + part * spare
        return jnp.concatenate([whole[: n * main], d_once_sum[lane : lane + spare]])

    small_grads = jnp.stack(
        [
            vector_of(0),
            vector_of(2),
            jnp.sum(d_branch.astype(F32), axis=0),
            jnp.sum(f * xhat_own, axis=0),
            jnp.sum(f, axis=0),
            jnp.sum(e * xhat_two, axis=0),
            jnp.sum(e, axis=0),
            jnp.sum(own_cot.astype(F32), axis=0),
        ]
    )
    small_grads = small_grads.reshape(8, n, own_rows).transpose(1, 0, 2)
    small_own = pick(small_grads, me)
    for d in range(1, n):
        small_own = small_own + swap(pick(small_grads, me ^ d), d)
    small_own = jnp.concatenate([small_own, grad_fc_bias.reshape(-1, own_rows)], axis=0)
    small_own = small_own + swap_core(small_own)
    hop = 1
    while hop < planes:
        small_own = small_own + lax.ppermute(
            small_own, "plane", [(i, i ^ hop) for i in range(planes)]
        )
        hop *= 2
    s = small_own[:8]
    sum_fc_bias = small_own[8:].reshape(-1)
    return (
        output,
        input_grad,
        sum_attn_weight,
        s[0],
        s[1],
        sum_proj_weight,
        s[2],
        s[3],
        s[4],
        s[5],
        s[6],
        sum_fc_weight,
        sum_fc_bias,
        sum_out_weight.astype(F32),
        s[7],
    )


def solution(mesh):
    shards, reps = mesh.devices.shape
    split = jax.sharding.Mesh(
        mesh.devices.reshape(shards, reps // 2, 2), ("shard", "plane", "core")
    )
    rep = ("plane", "core")
    batch = P(rep, "shard", None)
    row, vec = P("shard", None), P("shard")
    return jax.shard_map(
        body,
        mesh=split,
        in_specs=(batch, batch, P(rep, None), row, vec, vec, row)
        + (vec,) * 5
        + (row, vec, row, vec),
        out_specs=(batch, batch, row, vec, vec, row) + (vec,) * 5 + (row, vec, row, vec),
        check_vma=False,
    )
```

```python
import functools
import math

import jax
import jax.numpy as jnp
from jax import lax
from jax.experimental import pallas as pl
from jax.experimental.pallas import tpu as pltpu
from jax.sharding import PartitionSpec as P

D = 1600
HEADS = 25
HD = 64
UNIT = 32
LANES = 128
NEG = -1e30
VEC_ROWS = 16
BF = jnp.bfloat16
F32 = jnp.float32


def dot(left, right, dims):
    return lax.dot_general(left, right, (dims, ((), ())), preferred_element_type=F32)


def rows_dot(left, right):
    return dot(left, right, ((0,), (0,)))


def cols_dot(left, right):
    return dot(left, right, ((1,), (1,)))


def normalize(values):
    center = values - jnp.mean(values, axis=-1, keepdims=True)
    spread = jnp.mean(center * center, axis=-1, keepdims=True)
    inv = lax.rsqrt(spread + 1e-05)
    return center * inv, inv


def place_blocks(info_ref, shards, units):
    b0, b1, b2, me = info_ref[0], info_ref[1], info_ref[2], info_ref[3]
    e0, e1 = b0, b0 + b1
    places = []
    for d in range(shards):
        s = jnp.bitwise_xor(me, d)
        for u in range(units):
            first = jnp.where(u < e0, 0, jnp.where(u < e1, e0, e1))
            span = jnp.where(u < e0, b0, jnp.where(u < e1, b1, b2))
            places.append((d * units + u, first * shards + s * span + (u - first)))
    return places, e0, e1


def head_lanes(tile_rows, half):
    lane = lax.broadcasted_iota(jnp.int32, (tile_rows, LANES), 1)
    return (lane < HD) if half == 0 else (lane >= HD)


def window_scores(q, k, rows, width):
    scores = cols_dot(q, k)
    row = lax.broadcasted_iota(jnp.int32, (rows, width * rows), 0)
    col = lax.broadcasted_iota(jnp.int32, (rows, width * rows), 1)
    return jnp.where(col <= row + (width - 1) * rows, scores, NEG)


def fwd_kernel(shards, units, heads, info_ref, qkv_ref, out_ref, perm, mixed):
    block = UNIT
    rows = shards * block
    main = heads * HD
    places, e0, e1 = place_blocks(info_ref, shards, units)
    for src, dst in places:
        at = pl.ds(pl.multiple_of(dst * block, block), block)
        perm[at, :] = qkv_ref[src * block : (src + 1) * block, :]

    def unit(i, carry):
        first = jnp.where(i < e0, 0, jnp.where(i < e1, e0, e1))
        q_at = pl.ds(pl.multiple_of(i * rows, rows), rows)
        for width in range(1, 5):

            @pl.when(i - first + 1 == width)
            def _():
                k_at = pl.ds(pl.multiple_of(first * rows, rows), width * rows)

                def attend(q, k, v):
                    scores = window_scores(q * BF(0.125), k, rows, width)
                    top = jnp.max(scores, axis=1, keepdims=True)
                    probs = jnp.exp(scores - top)
                    total = jnp.sum(probs, axis=1, keepdims=True)
                    return dot(probs.astype(BF), v, ((1,), (0,))) / total

                for tile in range(main // LANES):
                    lanes = slice(tile * LANES, (tile + 1) * LANES)
                    k_lanes = slice(main + lanes.start, main + lanes.stop)
                    v_lanes = slice(2 * main + lanes.start, 2 * main + lanes.stop)
                    q, k, v = perm[q_at, lanes], perm[k_at, k_lanes], perm[k_at, v_lanes]
                    low = head_lanes(rows, 0)
                    zero = jnp.zeros_like(q)
                    left = attend(jnp.where(low, q, zero), k, v)
                    right = attend(jnp.where(low, zero, q), k, v)
                    mixed[q_at, lanes] = jnp.where(low, left, right).astype(BF)
                if main % LANES:
                    lanes = main - HD
                    mixed[q_at, lanes:main] = attend(
                        perm[q_at, lanes:main],
                        perm[k_at, main + lanes : 2 * main],
                        perm[k_at, 2 * main + lanes : 3 * main],
                    ).astype(BF)
                base = 3 * main
                mixed[q_at, main : main + HD] = attend(
                    perm[q_at, base : base + HD],
                    perm[k_at, base + HD : base + 2 * HD],
                    perm[k_at, base + 2 * HD : base + 3 * HD],
                ).astype(BF)

        return carry

    lax.fori_loop(0, units, unit, 0)
    for src, dst in places:
        at = pl.ds(pl.multiple_of(dst * block, block), block)
        out_ref[src * block : (src + 1) * block, :] = mixed[at, :]


def bwd_kernel(
    shards, units, heads, info_ref, qkv_ref, dmix_ref, out_ref, perm, dperm, dq_acc, dk_acc, dv_acc
):
    block = UNIT
    rows = shards * block
    main = heads * HD
    places, e0, e1 = place_blocks(info_ref, shards, units)
    for src, dst in places:
        at = pl.ds(pl.multiple_of(dst * block, block), block)
        perm[at, :] = qkv_ref[src * block : (src + 1) * block, :]
        dperm[at, :] = dmix_ref[src * block : (src + 1) * block, :]
    dk_acc[...] = jnp.zeros_like(dk_acc)
    dv_acc[...] = jnp.zeros_like(dv_acc)

    def unit(i, carry):
        first = jnp.where(i < e0, 0, jnp.where(i < e1, e0, e1))
        q_at = pl.ds(pl.multiple_of(i * rows, rows), rows)
        for width in range(1, 5):

            @pl.when(i - first + 1 == width)
            def _():
                k_at = pl.ds(pl.multiple_of(first * rows, rows), width * rows)

                def pull(q, k, v, g):
                    q = q * BF(0.125)
                    scores = window_scores(q, k, rows, width)
                    top = jnp.max(scores, axis=1, keepdims=True)
                    probs = jnp.exp(scores - top)
                    total = jnp.sum(probs, axis=1, keepdims=True)
                    probs = probs * (1.0 / total)
                    d_probs = cols_dot(g, v)
                    delta = jnp.sum(probs * d_probs, axis=1, keepdims=True)
                    d_scores = (probs * (d_probs - delta)).astype(BF)
                    d_q = dot(d_scores, k, ((1,), (0,))) * 0.125
                    return d_q, rows_dot(d_scores, q), rows_dot(probs.astype(BF), g)

                for tile in range(main // LANES):
                    lanes = slice(tile * LANES, (tile + 1) * LANES)
                    k_lanes = slice(main + lanes.start, main + lanes.stop)
                    v_lanes = slice(2 * main + lanes.start, 2 * main + lanes.stop)
                    q, k, v = perm[q_at, lanes], perm[k_at, k_lanes], perm[k_at, v_lanes]
                    g = dperm[q_at, lanes]
                    low = head_lanes(rows, 0)
                    zero = jnp.zeros_like(q)
                    dq0, dk0, dv0 = pull(jnp.where(low, q, zero), k, v, jnp.where(low, g, zero))
                    dq1, dk1, dv1 = pull(jnp.where(low, zero, q), k, v, jnp.where(low, zero, g))
                    dq_acc[q_at, lanes] = jnp.where(low, dq0, dq1).astype(BF)
                    dk_acc[k_at, lanes] += dk0 + dk1
                    dv_acc[k_at, lanes] += dv0 + dv1
                extra = [(main, 3 * main, 3 * main + HD, 3 * main + 2 * HD)]
                if main % LANES:
                    extra.append((main - HD, main - HD, 2 * main - HD, 3 * main - HD))
                for own, q_lane, k_lane, v_lane in extra:
                    dq0, dk0, dv0 = pull(
                        perm[q_at, q_lane : q_lane + HD],
                        perm[k_at, k_lane : k_lane + HD],
                        perm[k_at, v_lane : v_lane + HD],
                        dperm[q_at, own : own + HD],
                    )
                    dq_acc[q_at, own : own + HD] = dq0.astype(BF)
                    dk_acc[k_at, own : own + HD] += dk0
                    dv_acc[k_at, own : own + HD] += dv0

        return carry

    lax.fori_loop(0, units, unit, 0)
    for src, dst in places:
        at = pl.ds(pl.multiple_of(dst * block, block), block)
        to = slice(src * block, (src + 1) * block)
        for part, acc in enumerate((dq_acc, dk_acc, dv_acc)):
            got = acc[at, :].astype(BF)
            out_ref[to, part * main : (part + 1) * main] = got[:, :main]
            lane = 3 * main + part * HD
            out_ref[to, lane : lane + HD] = got[:, main:]


def vmem_call(kernel, out_shape, scratch, cost, inputs):
    return pl.pallas_call(
        kernel,
        out_shape=out_shape,
        in_specs=[pl.BlockSpec(memory_space=pltpu.SMEM)]
        + [pl.BlockSpec(memory_space=pltpu.VMEM)] * (len(inputs) - 1),
        out_specs=pl.BlockSpec(memory_space=pltpu.VMEM),
        scratch_shapes=scratch,
        compiler_params=pltpu.CompilerParams(vmem_limit_bytes=48 << 20),
        cost_estimate=cost,
    )(*inputs)


def attention_fwd(info, qkv, shards, heads):
    total, width = qkv.shape
    units = total // (shards * UNIT)
    own = (heads + 1) * HD
    return vmem_call(
        functools.partial(fwd_kernel, shards, units, heads),
        jax.ShapeDtypeStruct((total, own), BF),
        [pltpu.VMEM((total, width), BF), pltpu.VMEM((total, own), BF)],
        pl.CostEstimate(flops=10**10, bytes_accessed=total * width * 3, transcendentals=0),
        (info, qkv),
    )


def attention_bwd(info, qkv, d_mixed, shards, heads):
    total, width = qkv.shape
    units = total // (shards * UNIT)
    own = (heads + 1) * HD
    return vmem_call(
        functools.partial(bwd_kernel, shards, units, heads),
        jax.ShapeDtypeStruct((total, width), BF),
        [
            pltpu.VMEM((total, width), BF),
            pltpu.VMEM((total, own), BF),
            pltpu.VMEM((total, own), BF),
            pltpu.VMEM((total, own), F32),
            pltpu.VMEM((total, own), F32),
        ],
        pl.CostEstimate(flops=2 * 10**10, bytes_accessed=total * width * 5, transcendentals=0),
        (info, qkv, d_mixed),
    )


def on_place(me, core, shards, run):
    for m in range(shards):
        for c in range(2):

            @pl.when((me == m) & (core == c))
            def _():
                run(m, c)


def attn_columns(value, j, heads):
    main = heads * HD
    first = D // main * main
    parts = [value[:, p * D + j * main : p * D + (j + 1) * main] for p in range(3)]
    parts += [value[:, p * D + first : (p + 1) * D] for p in range(3)]
    return jnp.concatenate(parts, axis=1)


def fc_columns(value, j, width):
    return value[:, j * width : (j + 1) * width]


def pack_kernel(shards, half, step, columns, at_ref, dep_ref, weight_ref, *outs):
    del dep_ref

    def run(m, c):
        outs[0][...] = columns(weight_ref, m)
        for d in range(1, shards):
            piece = columns(weight_ref.at[c * step : c * step + half], m ^ d)
            outs[d][...] = piece

    on_place(at_ref[0], at_ref[1], shards, run)


def pack_attn_kernel(shards, half, step, heads, at_ref, weight_ref, *refs):
    vectors, outs = refs[: len(refs) - shards], refs[len(refs) - shards :]
    count = len(vectors)

    def run(m, c):
        outs[0][: shards_rows(outs[0]), :] = attn_columns(weight_ref, m, heads)
        for d in range(1, shards):
            outs[d][:half, :] = attn_columns(weight_ref.at[c * step : c * step + half], m ^ d, heads)

    def shards_rows(ref):
        return ref.shape[0] - VEC_ROWS

    on_place(at_ref[0], at_ref[1], shards, run)
    width = outs[0].shape[1]
    block = jnp.concatenate(
        [v[...].astype(F32).reshape(1, -1) for v in vectors]
        + [jnp.zeros((VEC_ROWS - count, vectors[0].shape[0]), F32)],
        axis=0,
    )
    block = jnp.concatenate(
        [block, jnp.zeros((VEC_ROWS, width - block.shape[1]), F32)], axis=1
    ).astype(BF)
    for out in outs:
        out[out.shape[0] - VEC_ROWS :, :] = block


def place_attn_kernel(shards, half, step, rows, count, at_ref, *refs):
    own, mine, other = refs[0], refs[1:shards], refs[shards]
    out, vec = refs[shards + 1 :]

    def run(m, c):
        out[m * rows : (m + 1) * rows, :] = own[:rows]
        for d in range(1, shards):
            base = (m ^ d) * rows
            a, b = mine[d - 1][:half], other[d - 1]
            low, high = (a, b) if c == 0 else (b, a)
            out[base : base + step, :] = low[:step]
            out[base + step : base + rows, :] = high
        for j in range(shards):
            ref, at = (own, rows) if j == m else (mine[(j ^ m) - 1], half)
            vec[:, j * rows : (j + 1) * rows] = ref[at : at + VEC_ROWS, :rows].astype(F32)[:count]

    on_place(at_ref[0], at_ref[1], shards, run)


def place_kernel(shards, half, step, rows, at_ref, *refs):
    own, mine, other, out = refs[0], refs[1:shards], refs[shards], refs[shards + 1]

    def run(m, c):
        out[m * rows : (m + 1) * rows, :] = own[...]
        for d in range(1, shards):
            base = (m ^ d) * rows
            low, high = (mine[d - 1][...], other[d - 1]) if c == 0 else (other[d - 1], mine[d - 1][...])
            out[base : base + step, :] = low[:step]
            out[base + step : base + rows, :] = high

    on_place(at_ref[0], at_ref[1], shards, run)


def unpack_kernel(shards, half, step, places, at_ref, mine, other, *outs):
    def run(m, c):
        for d in range(shards):
            for index, where, row, low, high in places(m, d):
                out, width = outs[index], high - low
                a = mine[row : row + half, low:high]
                b = other[row : row + half, low:high]
                first, second = (a, b) if c == 0 else (b, a)
                out[:step, where : where + width] = first[:step].astype(F32)
                out[step:, where : where + width] = second.astype(F32)

    on_place(at_ref[0], at_ref[1], shards, run)


def local_call(kernel, out_shape, cost_bytes, at, *inputs, anywhere=()):
    vmem = pl.BlockSpec(memory_space=pltpu.VMEM)
    specs = [pl.BlockSpec(memory_space=pl.ANY) if i in anywhere else vmem for i in range(len(inputs))]
    return pl.pallas_call(
        kernel,
        out_shape=out_shape,
        in_specs=[pl.BlockSpec(memory_space=pltpu.SMEM)] + specs,
        out_specs=jax.tree.map(lambda _: vmem, out_shape),
        compiler_params=pltpu.CompilerParams(vmem_limit_bytes=48 << 20),
        cost_estimate=pl.CostEstimate(flops=0, bytes_accessed=cost_bytes, transcendentals=0),
    )(at, *inputs)


def body(
    tokens,
    cotangent,
    lengths,
    attn_weight,
    query_bias,
    value_bias,
    proj_weight,
    proj_bias,
    ln1_gain,
    ln1_bias,
    ln2_gain,
    ln2_bias,
    fc_weight,
    fc_bias,
    out_weight,
    out_bias,
):
    n = lax.axis_size("shard")
    planes = lax.axis_size("plane")
    me = lax.axis_index("shard")
    core = lax.axis_index("core")
    heads = (HEADS - 1) // n
    main = heads * HD
    spare = D - n * main
    own_rows = attn_weight.shape[0]
    own_ff = fc_bias.shape[0]
    rows = tokens.shape[1]
    half = -(-own_rows // 32) * 16
    step = own_rows - half
    at = jnp.stack([me, core]).astype(jnp.int32)

    def swap(value, d):
        return lax.ppermute(value, "shard", [(i, i ^ d) for i in range(n)])

    def swap_core(value):
        return lax.ppermute(value, "core", [(0, 1), (1, 0)])

    def gather(value):
        if n != 4:
            return [value] + [swap(value, d) for d in range(1, n)]
        cut = value.shape[0] // 32 * 16
        one, two = swap(value, 1), swap(value, 2)
        three = jnp.concatenate([swap(one[:cut], 2), swap(two[cut:], 1)], axis=0)
        return [value, one, two, three]

    def pick(stacked, index):
        return lax.dynamic_index_in_dim(stacked, index, 0, keepdims=False)

    def natural(pieces):
        stacked = jnp.stack(pieces)
        return [pick(stacked, me ^ j) for j in range(n)]

    def after(value, *deps):
        return lax.optimization_barrier((value, deps))[0]

    def block(value, d):
        return value[d * rows : (d + 1) * rows]

    def place(own, mine):
        other = swap_core(jnp.stack(mine))
        return local_call(
            functools.partial(place_kernel, n, half, step, own_rows),
            jax.ShapeDtypeStruct((n * own_rows, own.shape[1]), BF),
            n * own.size * 4,
            at,
            own,
            *mine,
            other,
        )

    def pack(weight, columns, width, dep):
        shapes = [jax.ShapeDtypeStruct((own_rows, width), BF)]
        shapes += [jax.ShapeDtypeStruct((half, width), BF)] * (n - 1)
        return local_call(
            functools.partial(pack_kernel, n, half, step, columns),
            shapes,
            weight.size * 2,
            at,
            dep,
            weight,
            anywhere=(0,),
        )

    def reduce_rows(parts):
        total = parts[0].astype(F32)
        for d in range(1, n):
            total = total + swap(parts[d].astype(BF), d).astype(F32)
        return total

    def core_halves(parts):
        keep = lax.dynamic_slice_in_dim(parts, core * step, half, 1)
        give = lax.dynamic_slice_in_dim(parts, (1 - core) * step, half, 1)
        return (keep.astype(F32) + swap_core(give).astype(F32)).astype(BF)

    vectors = (
        query_bias, value_bias, proj_bias, ln1_gain, ln1_bias, ln2_gain, ln2_bias, out_bias
    )
    tokens_parts = gather(tokens[0])
    attn_width = 3 * (main + spare)
    attn_sent = local_call(
        functools.partial(pack_attn_kernel, n, half, step, heads),
        [jax.ShapeDtypeStruct((own_rows + VEC_ROWS, attn_width), BF)]
        + [jax.ShapeDtypeStruct((half + VEC_ROWS, attn_width), BF)] * (n - 1),
        attn_weight.size * 2,
        at,
        attn_weight,
        *vectors,
    )
    attn_got = [swap(attn_sent[d], d) for d in range(1, n)]
    attn_other = swap_core(jnp.stack([piece[:half] for piece in attn_got]))
    w_attn, small = local_call(
        functools.partial(place_attn_kernel, n, half, step, own_rows, len(vectors)),
        [
            jax.ShapeDtypeStruct((D, attn_width), BF),
            jax.ShapeDtypeStruct((len(vectors), D), F32),
        ],
        D * attn_width * 4,
        at,
        attn_sent[0],
        *attn_got,
        attn_other,
    )
    b_query, b_value, b_proj, gain_one, bias_one, gain_two, bias_two, b_out = [
        small[i] for i in range(8)
    ]

    def my_columns(vector):
        return lax.dynamic_slice_in_dim(vector, me * main, main, 0), vector[n * main :]

    q_main, q_spare = my_columns(b_query)
    v_main, v_spare = my_columns(b_value)
    qkv_bias = jnp.concatenate(
        [q_main, jnp.zeros_like(q_main), v_main, q_spare, jnp.zeros_like(q_spare), v_spare]
    )

    group_tokens = jnp.concatenate(tokens_parts, axis=0)
    fc_sent = pack(fc_weight, lambda ref, j: fc_columns(ref, j, own_ff), own_ff, attn_other)
    fc_got = [swap(fc_sent[d], d) for d in range(1, n)]
    w_fc = place(fc_sent[0], fc_got)
    proj_half = lax.dynamic_slice_in_dim(
        after(proj_weight, attn_other, tokens_parts[1:]), core * step, half, 0
    )
    proj_mine = lax.all_gather(proj_half, "shard", axis=0, tiled=False)
    proj_other = swap_core(proj_mine)
    proj_low = jnp.where(core == 0, proj_mine, proj_other)
    proj_high = jnp.where(core == 0, proj_other, proj_mine)
    w_proj = jnp.concatenate([proj_low[:, :step], proj_high], axis=1).reshape(D, D)
    own_cot = cotangent[0]
    cot_all = lax.all_gather(after(own_cot, proj_mine), "shard", axis=0, tiled=True)
    cot_parts = [own_cot] + [
        lax.dynamic_slice_in_dim(cot_all, (me ^ d) * rows, rows, 0) for d in range(1, n)
    ]
    group_cot = jnp.concatenate(cot_parts, axis=0)

    xhat_one, _ = normalize(group_tokens.astype(F32))
    normed = (xhat_one * gain_one + bias_one).astype(BF)
    qkv = (jnp.dot(normed, w_attn, preferred_element_type=F32) + qkv_bias).astype(BF)
    info = jnp.concatenate([lengths[0], me.astype(jnp.int32)[None]])
    mixed_heads = attention_fwd(info, qkv, n, heads)
    got = [block(mixed_heads, 0)[:, :main]] + [
        swap(block(mixed_heads, d)[:, :main], d) for d in range(1, n)
    ]
    mixed_low = jnp.concatenate(natural(got) + [block(mixed_heads, 0)[:, main:]], axis=1)
    own_tokens = tokens[0].astype(F32)
    middle = own_tokens + jnp.dot(mixed_low, w_proj, preferred_element_type=F32) + b_proj
    xhat_two, inv_two = normalize(middle)
    own_normed_two = (xhat_two * gain_two + bias_two).astype(BF)
    normed_parts = gather(own_normed_two)
    normed_two = jnp.concatenate(normed_parts, axis=0)

    def feed(part):
        hidden = jnp.dot(part, w_fc, preferred_element_type=F32) + fc_bias.astype(F32)
        inner = jnp.tanh(0.7978845608028654 * (hidden + 0.044715 * hidden * hidden * hidden))
        slope = 0.5 * (1.0 + inner) + 0.5 * hidden * (1.0 - inner * inner) * (
            0.7978845608028654 * (1.0 + 3 * 0.044715 * hidden * hidden)
        )
        return (0.5 * hidden * (1.0 + inner)).astype(BF), slope.astype(BF)

    fed = [feed(part) for part in normed_parts]
    active_parts = [a for a, _ in fed]
    active = jnp.concatenate(active_parts, axis=0)

    d_active = after(cols_dot(group_cot, out_weight))
    grad_out_weight = rows_dot(active, group_cot).astype(BF)
    sum_out_weight = lax.psum(grad_out_weight, ("plane", "core"))
    d_active = after(d_active, grad_out_weight)
    d_hidden_parts = [
        (block(d_active, d) * slope.astype(F32)).astype(BF) for d, (_, slope) in enumerate(fed)
    ]
    d_hidden = jnp.concatenate(d_hidden_parts, axis=0)
    e = reduce_rows([cols_dot(part, w_fc) for part in d_hidden_parts])
    e_gain = e * gain_two
    d_middle = own_cot.astype(F32) + inv_two * (
        e_gain
        - jnp.mean(e_gain, axis=-1, keepdims=True)
        - xhat_two * jnp.mean(e_gain * xhat_two, axis=-1, keepdims=True)
    )
    d_branch = d_middle.astype(BF)
    d_mixed = cols_dot(d_branch, w_proj).astype(BF)
    for_heads = jnp.stack([d_mixed[:, j * main : (j + 1) * main] for j in range(n)])
    last = d_mixed[:, n * main :]
    dmix_parts = [jnp.concatenate([pick(for_heads, me), last], axis=1)] + [
        swap(jnp.concatenate([pick(for_heads, me ^ d), last], axis=1), d) for d in range(1, n)
    ]

    grad_fc = rows_dot(normed_two, d_hidden).astype(BF).reshape(n, own_rows, own_ff)
    fc_halves = after(core_halves(grad_fc), dmix_parts)
    fc_parts = jnp.concatenate(
        [pick(fc_halves, me)] + [swap(pick(fc_halves, me ^ d), d) for d in range(1, n)]
    )
    fc_sum = lax.psum(after(fc_parts, sum_out_weight), "plane")
    grad_fc_bias = jnp.sum(d_hidden.astype(F32), axis=0)

    d_qkv = attention_bwd(info, qkv, jnp.concatenate(dmix_parts, axis=0), n, heads)

    grad_proj = rows_dot(mixed_low, d_branch).astype(BF).reshape(n, own_rows, D)
    proj_halves = after(core_halves(grad_proj), fc_parts)
    proj_part = reduce_rows([pick(proj_halves, me ^ d) for d in range(n)]).astype(BF)

    grad_main = rows_dot(normed, d_qkv[:, : 3 * main]).astype(BF).reshape(n, own_rows, 3 * main)
    grad_spare = rows_dot(normed, d_qkv[:, 3 * main :]).astype(BF).reshape(n, own_rows, 3 * spare)
    main_halves = core_halves(grad_main)
    spare_halves = core_halves(pick(grad_spare, me)[None])[0]
    attn_parts = jnp.concatenate(
        [pick(main_halves, me)]
        + [swap(pick(main_halves, me ^ d), d) for d in range(1, n)]
        + [spare_halves, proj_part],
        axis=1,
    )
    attn_sum = lax.psum(after(attn_parts, fc_sum), "plane")

    counted = (lax.broadcasted_iota(jnp.int32, (n * rows, 1), 0) < rows) | (
        lax.broadcasted_iota(jnp.int32, (1, d_qkv.shape[1]), 1) < 3 * main
    )
    d_once = after(jnp.where(counted, d_qkv, BF(0)), attn_parts)
    f = reduce_rows([cols_dot(block(d_once, d), w_attn) for d in range(n)])
    xhat_own, inv_own = normalize(own_tokens)
    f_gain = f * gain_one
    d_tokens = inv_own * (
        f_gain
        - jnp.mean(f_gain, axis=-1, keepdims=True)
        - xhat_own * jnp.mean(f_gain * xhat_own, axis=-1, keepdims=True)
    )
    input_grad = (d_middle + d_tokens).astype(BF)[None]

    late_active = after(active, attn_parts)
    out_parts = [
        jnp.dot(block(late_active, d), out_weight, preferred_element_type=F32) for d in range(n)
    ]
    output = (middle + reduce_rows(out_parts) + b_out).astype(BF)[None]

    sum_fc_weight = local_call(
        functools.partial(
            unpack_kernel,
            n,
            half,
            step,
            lambda m, d: [(0, (m ^ d) * own_ff, d * half, 0, own_ff)],
        ),
        [jax.ShapeDtypeStruct((own_rows, n * own_ff), F32)],
        own_rows * n * own_ff * 8,
        at,
        fc_sum,
        swap_core(fc_sum),
    )[0]

    def attn_places(m, d):
        base = d * 3 * main
        places = [
            (0, p * D + (m ^ d) * main, 0, base + p * main, base + (p + 1) * main)
            for p in range(3)
        ]
        if d == 0:
            base = n * 3 * main
            places += [
                (0, p * D + n * main, 0, base + p * spare, base + (p + 1) * spare)
                for p in range(3)
            ]
            places.append((1, 0, 0, 3 * D, 4 * D))
        return places

    sum_attn_weight, sum_proj_weight = local_call(
        functools.partial(unpack_kernel, n, half, step, attn_places),
        [
            jax.ShapeDtypeStruct((own_rows, 3 * D), F32),
            jax.ShapeDtypeStruct((own_rows, D), F32),
        ],
        own_rows * 4 * D * 8,
        at,
        attn_sum,
        swap_core(attn_sum),
    )

    d_once_sum = jnp.sum(d_once.astype(F32), axis=0)

    def vector_of(part):
        whole = jnp.zeros((D,), F32)
        whole = lax.dynamic_update_slice_in_dim(
            whole, d_once_sum[part * main : (part + 1) * main], me * main, 0
        )
        lane = 3 * main + part * spare
        return jnp.concatenate([whole[: n * main], d_once_sum[lane : lane + spare]])

    small_grads = jnp.stack(
        [
            vector_of(0),
            vector_of(2),
            jnp.sum(d_branch.astype(F32), axis=0),
            jnp.sum(f * xhat_own, axis=0),
            jnp.sum(f, axis=0),
            jnp.sum(e * xhat_two, axis=0),
            jnp.sum(e, axis=0),
            jnp.sum(own_cot.astype(F32), axis=0),
        ]
    )
    small_grads = small_grads.reshape(8, n, own_rows).transpose(1, 0, 2)
    small_own = pick(small_grads, me)
    for d in range(1, n):
        small_own = small_own + swap(pick(small_grads, me ^ d), d)
    small_own = jnp.concatenate([small_own, grad_fc_bias.reshape(-1, own_rows)], axis=0)
    small_own = small_own + swap_core(small_own)
    hop = 1
    while hop < planes:
        small_own = small_own + lax.ppermute(
            small_own, "plane", [(i, i ^ hop) for i in range(planes)]
        )
        hop *= 2
    s = small_own[:8]
    sum_fc_bias = small_own[8:].reshape(-1)
    return (
        output,
        input_grad,
        sum_attn_weight,
        s[0],
        s[1],
        sum_proj_weight,
        s[2],
        s[3],
        s[4],
        s[5],
        s[6],
        sum_fc_weight,
        sum_fc_bias,
        sum_out_weight.astype(F32),
        s[7],
    )


def solution(mesh):
    shards, reps = mesh.devices.shape
    split = jax.sharding.Mesh(
        mesh.devices.reshape(shards, reps // 2, 2), ("shard", "plane", "core")
    )
    rep = ("plane", "core")
    batch = P(rep, "shard", None)
    row, vec = P("shard", None), P("shard")
    return jax.shard_map(
        body,
        mesh=split,
        in_specs=(batch, batch, P(rep, None), row, vec, vec, row)
        + (vec,) * 5
        + (row, vec, row, vec),
        out_specs=(batch, batch, row, vec, vec, row) + (vec,) * 5 + (row, vec, row, vec),
        check_vma=False,
    )
```

```python
import functools
import math

import jax
import jax.numpy as jnp
from jax import lax
from jax.experimental import pallas as pl
from jax.experimental.pallas import tpu as pltpu
from jax.sharding import PartitionSpec as P

D = 1600
HEADS = 25
HD = 64
UNIT = 32
LANES = 128
NEG = -1e30
VEC_ROWS = 16
BF = jnp.bfloat16
F32 = jnp.float32


def dot(left, right, dims):
    return lax.dot_general(left, right, (dims, ((), ())), preferred_element_type=F32)


def rows_dot(left, right):
    return dot(left, right, ((0,), (0,)))


def cols_dot(left, right):
    return dot(left, right, ((1,), (1,)))


def normalize(values):
    center = values - jnp.mean(values, axis=-1, keepdims=True)
    spread = jnp.mean(center * center, axis=-1, keepdims=True)
    inv = lax.rsqrt(spread + 1e-05)
    return center * inv, inv


def place_blocks(info_ref, shards, units):
    b0, b1, b2, me = info_ref[0], info_ref[1], info_ref[2], info_ref[3]
    e0, e1 = b0, b0 + b1
    places = []
    for d in range(shards):
        s = jnp.bitwise_xor(me, d)
        for u in range(units):
            first = jnp.where(u < e0, 0, jnp.where(u < e1, e0, e1))
            span = jnp.where(u < e0, b0, jnp.where(u < e1, b1, b2))
            places.append((d * units + u, first * shards + s * span + (u - first)))
    return places, e0, e1


def head_lanes(tile_rows, half):
    lane = lax.broadcasted_iota(jnp.int32, (tile_rows, LANES), 1)
    return (lane < HD) if half == 0 else (lane >= HD)


def window_scores(q, k, rows, width):
    scores = cols_dot(q, k)
    row = lax.broadcasted_iota(jnp.int32, (rows, width * rows), 0)
    col = lax.broadcasted_iota(jnp.int32, (rows, width * rows), 1)
    return jnp.where(col <= row + (width - 1) * rows, scores, NEG)


def fwd_kernel(shards, units, heads, info_ref, qkv_ref, out_ref, perm, mixed):
    block = UNIT
    rows = shards * block
    main = heads * HD
    places, e0, e1 = place_blocks(info_ref, shards, units)
    for src, dst in places:
        at = pl.ds(pl.multiple_of(dst * block, block), block)
        perm[at, :] = qkv_ref[src * block : (src + 1) * block, :]

    def unit(i, carry):
        first = jnp.where(i < e0, 0, jnp.where(i < e1, e0, e1))
        q_at = pl.ds(pl.multiple_of(i * rows, rows), rows)
        for width in range(1, 5):

            @pl.when(i - first + 1 == width)
            def _():
                k_at = pl.ds(pl.multiple_of(first * rows, rows), width * rows)

                def attend(q, k, v):
                    scores = window_scores(q * BF(0.125), k, rows, width)
                    top = jnp.max(scores, axis=1, keepdims=True)
                    probs = jnp.exp(scores - top)
                    total = jnp.sum(probs, axis=1, keepdims=True)
                    return dot(probs.astype(BF), v, ((1,), (0,))) / total

                for tile in range(main // LANES):
                    lanes = slice(tile * LANES, (tile + 1) * LANES)
                    k_lanes = slice(main + lanes.start, main + lanes.stop)
                    v_lanes = slice(2 * main + lanes.start, 2 * main + lanes.stop)
                    q, k, v = perm[q_at, lanes], perm[k_at, k_lanes], perm[k_at, v_lanes]
                    low = head_lanes(rows, 0)
                    zero = jnp.zeros_like(q)
                    left = attend(jnp.where(low, q, zero), k, v)
                    right = attend(jnp.where(low, zero, q), k, v)
                    mixed[q_at, lanes] = jnp.where(low, left, right).astype(BF)
                if main % LANES:
                    lanes = main - HD
                    mixed[q_at, lanes:main] = attend(
                        perm[q_at, lanes:main],
                        perm[k_at, main + lanes : 2 * main],
                        perm[k_at, 2 * main + lanes : 3 * main],
                    ).astype(BF)
                base = 3 * main
                mixed[q_at, main : main + HD] = attend(
                    perm[q_at, base : base + HD],
                    perm[k_at, base + HD : base + 2 * HD],
                    perm[k_at, base + 2 * HD : base + 3 * HD],
                ).astype(BF)

        return carry

    lax.fori_loop(0, units, unit, 0)
    for src, dst in places:
        at = pl.ds(pl.multiple_of(dst * block, block), block)
        out_ref[src * block : (src + 1) * block, :] = mixed[at, :]


def bwd_kernel(
    shards, units, heads, info_ref, qkv_ref, dmix_ref, out_ref, perm, dperm, dq_acc, dk_acc, dv_acc
):
    block = UNIT
    rows = shards * block
    main = heads * HD
    places, e0, e1 = place_blocks(info_ref, shards, units)
    for src, dst in places:
        at = pl.ds(pl.multiple_of(dst * block, block), block)
        perm[at, :] = qkv_ref[src * block : (src + 1) * block, :]
        dperm[at, :] = dmix_ref[src * block : (src + 1) * block, :]
    dk_acc[...] = jnp.zeros_like(dk_acc)
    dv_acc[...] = jnp.zeros_like(dv_acc)

    def unit(i, carry):
        first = jnp.where(i < e0, 0, jnp.where(i < e1, e0, e1))
        q_at = pl.ds(pl.multiple_of(i * rows, rows), rows)
        for width in range(1, 5):

            @pl.when(i - first + 1 == width)
            def _():
                k_at = pl.ds(pl.multiple_of(first * rows, rows), width * rows)

                def pull(q, k, v, g):
                    q = q * BF(0.125)
                    scores = window_scores(q, k, rows, width)
                    top = jnp.max(scores, axis=1, keepdims=True)
                    probs = jnp.exp(scores - top)
                    total = jnp.sum(probs, axis=1, keepdims=True)
                    probs = probs * (1.0 / total)
                    d_probs = cols_dot(g, v)
                    delta = jnp.sum(probs * d_probs, axis=1, keepdims=True)
                    d_scores = (probs * (d_probs - delta)).astype(BF)
                    d_q = dot(d_scores, k, ((1,), (0,))) * 0.125
                    return d_q, rows_dot(d_scores, q), rows_dot(probs.astype(BF), g)

                for tile in range(main // LANES):
                    lanes = slice(tile * LANES, (tile + 1) * LANES)
                    k_lanes = slice(main + lanes.start, main + lanes.stop)
                    v_lanes = slice(2 * main + lanes.start, 2 * main + lanes.stop)
                    q, k, v = perm[q_at, lanes], perm[k_at, k_lanes], perm[k_at, v_lanes]
                    g = dperm[q_at, lanes]
                    low = head_lanes(rows, 0)
                    zero = jnp.zeros_like(q)
                    dq0, dk0, dv0 = pull(jnp.where(low, q, zero), k, v, jnp.where(low, g, zero))
                    dq1, dk1, dv1 = pull(jnp.where(low, zero, q), k, v, jnp.where(low, zero, g))
                    dq_acc[q_at, lanes] = jnp.where(low, dq0, dq1).astype(BF)
                    dk_acc[k_at, lanes] += dk0 + dk1
                    dv_acc[k_at, lanes] += dv0 + dv1
                extra = [(main, 3 * main, 3 * main + HD, 3 * main + 2 * HD)]
                if main % LANES:
                    extra.append((main - HD, main - HD, 2 * main - HD, 3 * main - HD))
                for own, q_lane, k_lane, v_lane in extra:
                    dq0, dk0, dv0 = pull(
                        perm[q_at, q_lane : q_lane + HD],
                        perm[k_at, k_lane : k_lane + HD],
                        perm[k_at, v_lane : v_lane + HD],
                        dperm[q_at, own : own + HD],
                    )
                    dq_acc[q_at, own : own + HD] = dq0.astype(BF)
                    dk_acc[k_at, own : own + HD] += dk0
                    dv_acc[k_at, own : own + HD] += dv0

        return carry

    lax.fori_loop(0, units, unit, 0)
    for src, dst in places:
        at = pl.ds(pl.multiple_of(dst * block, block), block)
        to = slice(src * block, (src + 1) * block)
        for part, acc in enumerate((dq_acc, dk_acc, dv_acc)):
            got = acc[at, :].astype(BF)
            out_ref[to, part * main : (part + 1) * main] = got[:, :main]
            lane = 3 * main + part * HD
            out_ref[to, lane : lane + HD] = got[:, main:]


def vmem_call(kernel, out_shape, scratch, cost, inputs):
    return pl.pallas_call(
        kernel,
        out_shape=out_shape,
        in_specs=[pl.BlockSpec(memory_space=pltpu.SMEM)]
        + [pl.BlockSpec(memory_space=pltpu.VMEM)] * (len(inputs) - 1),
        out_specs=pl.BlockSpec(memory_space=pltpu.VMEM),
        scratch_shapes=scratch,
        compiler_params=pltpu.CompilerParams(vmem_limit_bytes=48 << 20),
        cost_estimate=cost,
    )(*inputs)


def attention_fwd(info, qkv, shards, heads):
    total, width = qkv.shape
    units = total // (shards * UNIT)
    own = (heads + 1) * HD
    return vmem_call(
        functools.partial(fwd_kernel, shards, units, heads),
        jax.ShapeDtypeStruct((total, own), BF),
        [pltpu.VMEM((total, width), BF), pltpu.VMEM((total, own), BF)],
        pl.CostEstimate(flops=1, bytes_accessed=1, transcendentals=0),
        (info, qkv),
    )


def attention_bwd(info, qkv, d_mixed, shards, heads):
    total, width = qkv.shape
    units = total // (shards * UNIT)
    own = (heads + 1) * HD
    return vmem_call(
        functools.partial(bwd_kernel, shards, units, heads),
        jax.ShapeDtypeStruct((total, width), BF),
        [
            pltpu.VMEM((total, width), BF),
            pltpu.VMEM((total, own), BF),
            pltpu.VMEM((total, own), BF),
            pltpu.VMEM((total, own), F32),
            pltpu.VMEM((total, own), F32),
        ],
        pl.CostEstimate(flops=1, bytes_accessed=1, transcendentals=0),
        (info, qkv, d_mixed),
    )


def on_place(me, core, shards, run):
    for m in range(shards):
        for c in range(2):

            @pl.when((me == m) & (core == c))
            def _():
                run(m, c)


def attn_columns(value, j, heads):
    main = heads * HD
    first = D // main * main
    parts = [value[:, p * D + j * main : p * D + (j + 1) * main] for p in range(3)]
    parts += [value[:, p * D + first : (p + 1) * D] for p in range(3)]
    return jnp.concatenate(parts, axis=1)


def fc_columns(value, j, width):
    return value[:, j * width : (j + 1) * width]


def pack_kernel(shards, half, step, columns, at_ref, dep_ref, weight_ref, *outs):
    del dep_ref

    def run(m, c):
        outs[0][...] = columns(weight_ref, m)
        for d in range(1, shards):
            piece = columns(weight_ref.at[c * step : c * step + half], m ^ d)
            outs[d][...] = piece

    on_place(at_ref[0], at_ref[1], shards, run)


def pack_attn_kernel(shards, half, step, heads, at_ref, weight_ref, *refs):
    vectors, outs = refs[: len(refs) - shards], refs[len(refs) - shards :]
    count = len(vectors)

    def run(m, c):
        outs[0][: shards_rows(outs[0]), :] = attn_columns(weight_ref, m, heads)
        for d in range(1, shards):
            outs[d][:half, :] = attn_columns(weight_ref.at[c * step : c * step + half], m ^ d, heads)

    def shards_rows(ref):
        return ref.shape[0] - VEC_ROWS

    on_place(at_ref[0], at_ref[1], shards, run)
    width = outs[0].shape[1]
    block = jnp.concatenate(
        [v[...].astype(F32).reshape(1, -1) for v in vectors]
        + [jnp.zeros((VEC_ROWS - count, vectors[0].shape[0]), F32)],
        axis=0,
    )
    block = jnp.concatenate(
        [block, jnp.zeros((VEC_ROWS, width - block.shape[1]), F32)], axis=1
    ).astype(BF)
    for out in outs:
        out[out.shape[0] - VEC_ROWS :, :] = block


def place_attn_kernel(shards, half, step, rows, count, at_ref, *refs):
    own, mine, other = refs[0], refs[1:shards], refs[shards]
    out, vec = refs[shards + 1 :]

    def run(m, c):
        out[m * rows : (m + 1) * rows, :] = own[:rows]
        for d in range(1, shards):
            base = (m ^ d) * rows
            a, b = mine[d - 1][:half], other[d - 1]
            low, high = (a, b) if c == 0 else (b, a)
            out[base : base + step, :] = low[:step]
            out[base + step : base + rows, :] = high
        for j in range(shards):
            ref, at = (own, rows) if j == m else (mine[(j ^ m) - 1], half)
            vec[:, j * rows : (j + 1) * rows] = ref[at : at + VEC_ROWS, :rows].astype(F32)[:count]

    on_place(at_ref[0], at_ref[1], shards, run)


def place_kernel(shards, half, step, rows, at_ref, *refs):
    own, mine, other, out = refs[0], refs[1:shards], refs[shards], refs[shards + 1]

    def run(m, c):
        out[m * rows : (m + 1) * rows, :] = own[...]
        for d in range(1, shards):
            base = (m ^ d) * rows
            low, high = (mine[d - 1][...], other[d - 1]) if c == 0 else (other[d - 1], mine[d - 1][...])
            out[base : base + step, :] = low[:step]
            out[base + step : base + rows, :] = high

    on_place(at_ref[0], at_ref[1], shards, run)


def pack_part_kernel(shards, length, stride, columns, at_ref, weight_ref, *outs):
    part = pl.ds(pl.multiple_of(at_ref[2] * stride, 16), length)
    for m in range(shards):

        @pl.when(at_ref[0] == m)
        def _():
            outs[0][...] = columns(weight_ref, m)
            for d in range(1, shards):
                outs[d][...] = columns(weight_ref.at[part], m ^ d)


def place_part_kernel(shards, length, stride, rows, at_ref, own, mine, near, across, out):
    me, q = at_ref[0], at_ref[2]
    out[pl.ds(pl.multiple_of(me * rows, 16), rows), :] = own[...]
    size = (shards - 1) * length
    for d in range(1, shards):
        base = jnp.bitwise_xor(me, d) * rows
        for flip, ref, first in ((0, mine, 0), (2, near, 0), (1, across, 0), (3, across, size)):
            to = base + jnp.bitwise_xor(q, flip) * stride
            row = first + (d - 1) * length
            out[pl.ds(pl.multiple_of(to, 16), length), :] = ref[row : row + length, :]


def unpack_kernel(shards, half, step, places, at_ref, mine, other, *outs):
    def run(m, c):
        for d in range(shards):
            for index, where, row, low, high in places(m, d):
                out, width = outs[index], high - low
                a = mine[row : row + half, low:high]
                b = other[row : row + half, low:high]
                first, second = (a, b) if c == 0 else (b, a)
                out[:step, where : where + width] = first[:step].astype(F32)
                out[step:, where : where + width] = second.astype(F32)

    on_place(at_ref[0], at_ref[1], shards, run)


def local_call(kernel, out_shape, cost_bytes, at, *inputs, anywhere=()):
    vmem = pl.BlockSpec(memory_space=pltpu.VMEM)
    specs = [pl.BlockSpec(memory_space=pl.ANY) if i in anywhere else vmem for i in range(len(inputs))]
    return pl.pallas_call(
        kernel,
        out_shape=out_shape,
        in_specs=[pl.BlockSpec(memory_space=pltpu.SMEM)] + specs,
        out_specs=jax.tree.map(lambda _: vmem, out_shape),
        compiler_params=pltpu.CompilerParams(vmem_limit_bytes=48 << 20),
        cost_estimate=pl.CostEstimate(flops=1, bytes_accessed=1, transcendentals=0),
    )(at, *inputs)


def body(
    tokens,
    cotangent,
    lengths,
    attn_weight,
    query_bias,
    value_bias,
    proj_weight,
    proj_bias,
    ln1_gain,
    ln1_bias,
    ln2_gain,
    ln2_bias,
    fc_weight,
    fc_bias,
    out_weight,
    out_bias,
):
    n = lax.axis_size("shard")
    planes = lax.axis_size("plane")
    me = lax.axis_index("shard")
    core = lax.axis_index("core")
    heads = (HEADS - 1) // n
    main = heads * HD
    spare = D - n * main
    own_rows = attn_weight.shape[0]
    own_ff = fc_bias.shape[0]
    rows = tokens.shape[1]
    half = -(-own_rows // 32) * 16
    step = own_rows - half
    quarter = lax.axis_index("plane") % 2 * 2 + core
    at = jnp.stack([me, core, quarter]).astype(jnp.int32)

    def swap(value, d):
        return lax.ppermute(value, "shard", [(i, i ^ d) for i in range(n)])

    def swap_plane(value):
        return lax.ppermute(value, "plane", [(i, i ^ 1) for i in range(planes)])

    def swap_core(value):
        return lax.ppermute(value, "core", [(0, 1), (1, 0)])

    def gather_near(value):
        if n != 4:
            return [swap(value, d) for d in range(1, n)]
        return [swap(value, 1), swap(value, 2)]

    def gather_far(value, near):
        if n != 4:
            return [value] + near
        one, two = near
        cut = value.shape[0] // 32 * 16
        three = jnp.concatenate([swap(one[:cut], 2), swap(two[cut:], 1)], axis=0)
        return [value, one, two, three]

    def gather(value):
        return gather_far(value, gather_near(value))

    def pick(stacked, index):
        return lax.dynamic_index_in_dim(stacked, index, 0, keepdims=False)

    def natural(pieces):
        stacked = jnp.stack(pieces)
        return [pick(stacked, me ^ j) for j in range(n)]

    def after(value, *deps):
        return lax.optimization_barrier((value, deps))[0]

    def block(value, d):
        return value[d * rows : (d + 1) * rows]

    def place(own, mine):
        other = swap_core(jnp.stack(mine))
        return local_call(
            functools.partial(place_kernel, n, half, step, own_rows),
            jax.ShapeDtypeStruct((n * own_rows, own.shape[1]), BF),
            n * own.size * 4,
            at,
            own,
            *mine,
            other,
        )

    def pack(weight, columns, width, dep):
        shapes = [jax.ShapeDtypeStruct((own_rows, width), BF)]
        shapes += [jax.ShapeDtypeStruct((half, width), BF)] * (n - 1)
        return local_call(
            functools.partial(pack_kernel, n, half, step, columns),
            shapes,
            weight.size * 2,
            at,
            dep,
            weight,
            anywhere=(0,),
        )

    def reduce_rows(parts):
        total = parts[0].astype(F32)
        for d in range(1, n):
            total = total + swap(parts[d].astype(BF), d).astype(F32)
        return total

    def core_halves(parts):
        keep = lax.dynamic_slice_in_dim(parts, core * step, half, 1)
        give = lax.dynamic_slice_in_dim(parts, (1 - core) * step, half, 1)
        return (keep.astype(F32) + swap_core(give).astype(F32)).astype(BF)

    vectors = (
        query_bias, value_bias, proj_bias, ln1_gain, ln1_bias, ln2_gain, ln2_bias, out_bias
    )
    tokens_near = gather_near(tokens[0])
    attn_width = 3 * (main + spare)
    attn_sent = local_call(
        functools.partial(pack_attn_kernel, n, half, step, heads),
        [jax.ShapeDtypeStruct((own_rows + VEC_ROWS, attn_width), BF)]
        + [jax.ShapeDtypeStruct((half + VEC_ROWS, attn_width), BF)] * (n - 1),
        attn_weight.size * 2,
        at,
        attn_weight,
        *vectors,
    )
    attn_got = [swap(attn_sent[d], d) for d in range(1, n)]
    attn_got, tokens_near = after((attn_got, tokens_near))
    attn_other = swap_core(jnp.stack([piece[:half] for piece in attn_got]))
    tokens_parts = gather_far(tokens[0], tokens_near)
    w_attn, small = local_call(
        functools.partial(place_attn_kernel, n, half, step, own_rows, len(vectors)),
        [
            jax.ShapeDtypeStruct((D, attn_width), BF),
            jax.ShapeDtypeStruct((len(vectors), D), F32),
        ],
        D * attn_width * 4,
        at,
        attn_sent[0],
        *attn_got,
        attn_other,
    )
    b_query, b_value, b_proj, gain_one, bias_one, gain_two, bias_two, b_out = [
        small[i] for i in range(8)
    ]

    def my_columns(vector):
        return lax.dynamic_slice_in_dim(vector, me * main, main, 0), vector[n * main :]

    q_main, q_spare = my_columns(b_query)
    v_main, v_spare = my_columns(b_value)
    qkv_bias = jnp.concatenate(
        [q_main, jnp.zeros_like(q_main), v_main, q_spare, jnp.zeros_like(q_spare), v_spare]
    )

    group_tokens = jnp.concatenate(tokens_parts, axis=0)
    proj_half = lax.dynamic_slice_in_dim(after(proj_weight, attn_got), core * step, half, 0)
    proj_near = gather_near(proj_half)
    late_fc = after(fc_weight, attn_got)
    stride = own_rows // 64 * 16
    length = own_rows - 3 * stride
    by_parts = own_rows % 16 == 0 and stride > 0 and planes % 2 == 0
    if by_parts:
        fc_sent = local_call(
            functools.partial(
                pack_part_kernel, n, length, stride, lambda ref, j: fc_columns(ref, j, own_ff)
            ),
            [jax.ShapeDtypeStruct((own_rows, own_ff), BF)]
            + [jax.ShapeDtypeStruct((length, own_ff), BF)] * (n - 1),
            fc_weight.size * 2,
            at,
            late_fc,
        )
    else:
        fc_sent = pack(late_fc, lambda ref, j: fc_columns(ref, j, own_ff), own_ff, lengths)
    xhat_one, _ = normalize(group_tokens.astype(F32))
    normed = (xhat_one * gain_one + bias_one).astype(BF)
    qkv = (jnp.dot(normed, w_attn, preferred_element_type=F32) + qkv_bias).astype(BF)
    qkv, proj_near, fc_sent = after((qkv, proj_near, fc_sent))
    proj_parts = gather_far(proj_half, proj_near)
    fc_got = [swap(fc_sent[d], d) for d in range(1, n)]
    info = jnp.concatenate([lengths[0], me.astype(jnp.int32)[None]])
    mixed_heads = attention_fwd(info, qkv, n, heads)
    mixed_heads, proj_parts, fc_got = after((mixed_heads, proj_parts, fc_got))
    got = [block(mixed_heads, 0)[:, :main]] + [
        swap(block(mixed_heads, d)[:, :main], d) for d in range(1, n)
    ]
    if by_parts:
        fc_mine = jnp.concatenate(fc_got)
        fc_near = swap_plane(fc_mine)
    w_proj = place(proj_weight, proj_parts[1:])
    got, w_proj = after((got, w_proj))
    own_cot = cotangent[0]
    cot_near = gather_near(after(own_cot, got))
    mixed_low = jnp.concatenate(natural(got) + [block(mixed_heads, 0)[:, main:]], axis=1)
    own_tokens = tokens[0].astype(F32)
    middle = own_tokens + jnp.dot(mixed_low, w_proj, preferred_element_type=F32) + b_proj
    xhat_two, inv_two = normalize(middle)
    own_normed_two = (xhat_two * gain_two + bias_two).astype(BF)
    normed_near = gather_near(own_normed_two)
    if by_parts:
        w_fc = local_call(
            functools.partial(place_part_kernel, n, length, stride, own_rows),
            jax.ShapeDtypeStruct((D, own_ff), BF),
            D * own_ff * 4,
            at,
            fc_sent[0],
            fc_mine,
            fc_near,
            swap_core(jnp.concatenate([fc_mine, fc_near])),
        )
    else:
        w_fc = place(fc_sent[0], fc_got)
    cot_near, normed_near = after((cot_near, normed_near))
    normed_parts = gather_far(own_normed_two, normed_near)
    cot_parts = gather_far(own_cot, cot_near)
    group_cot = jnp.concatenate(cot_parts, axis=0)
    normed_two = jnp.concatenate(normed_parts, axis=0)

    def feed(part):
        hidden = jnp.dot(part, w_fc, preferred_element_type=F32) + fc_bias.astype(F32)
        inner = jnp.tanh(0.7978845608028654 * (hidden + 0.044715 * hidden * hidden * hidden))
        slope = 0.5 * (1.0 + inner) + 0.5 * hidden * (1.0 - inner * inner) * (
            0.7978845608028654 * (1.0 + 3 * 0.044715 * hidden * hidden)
        )
        return (0.5 * hidden * (1.0 + inner)).astype(BF), slope.astype(BF)

    fed = [feed(part) for part in normed_parts]
    active_parts = [a for a, _ in fed]
    active = jnp.concatenate(active_parts, axis=0)

    d_active = after(cols_dot(group_cot, out_weight))
    grad_out_weight = rows_dot(active, group_cot).astype(BF)
    sum_out_weight = lax.psum(grad_out_weight, ("plane", "core"))
    d_active = after(d_active, grad_out_weight)
    d_hidden_parts = [
        (block(d_active, d) * slope.astype(F32)).astype(BF) for d, (_, slope) in enumerate(fed)
    ]
    d_hidden = jnp.concatenate(d_hidden_parts, axis=0)
    e = reduce_rows([cols_dot(part, w_fc) for part in d_hidden_parts])
    e_gain = e * gain_two
    d_middle = own_cot.astype(F32) + inv_two * (
        e_gain
        - jnp.mean(e_gain, axis=-1, keepdims=True)
        - xhat_two * jnp.mean(e_gain * xhat_two, axis=-1, keepdims=True)
    )
    d_branch = d_middle.astype(BF)
    d_mixed = cols_dot(d_branch, w_proj).astype(BF)
    for_heads = jnp.stack([d_mixed[:, j * main : (j + 1) * main] for j in range(n)])
    last = d_mixed[:, n * main :]
    dmix_parts = [jnp.concatenate([pick(for_heads, me), last], axis=1)] + [
        swap(jnp.concatenate([pick(for_heads, me ^ d), last], axis=1), d) for d in range(1, n)
    ]

    grad_fc = rows_dot(normed_two, d_hidden).astype(BF).reshape(n, own_rows, own_ff)
    fc_halves = after(core_halves(grad_fc), dmix_parts)
    fc_parts = jnp.concatenate(
        [pick(fc_halves, me)] + [swap(pick(fc_halves, me ^ d), d) for d in range(1, n)]
    )
    fc_sum = lax.psum(fc_parts, "plane")
    grad_fc_bias = jnp.sum(d_hidden.astype(F32), axis=0)

    d_qkv = attention_bwd(info, qkv, jnp.concatenate(dmix_parts, axis=0), n, heads)
    d_qkv, fc_parts = after((d_qkv, fc_parts))

    grad_proj = rows_dot(mixed_low, d_branch).astype(BF).reshape(n, own_rows, D)
    proj_halves = after(core_halves(grad_proj), fc_parts)
    proj_part = reduce_rows([pick(proj_halves, me ^ d) for d in range(n)]).astype(BF)

    grad_main = rows_dot(normed, d_qkv[:, : 3 * main]).astype(BF).reshape(n, own_rows, 3 * main)
    grad_spare = rows_dot(normed, d_qkv[:, 3 * main :]).astype(BF).reshape(n, own_rows, 3 * spare)
    main_halves = core_halves(grad_main)
    spare_halves = core_halves(pick(grad_spare, me)[None])[0]
    attn_parts = jnp.concatenate(
        [pick(main_halves, me)]
        + [swap(pick(main_halves, me ^ d), d) for d in range(1, n)]
        + [spare_halves, proj_part],
        axis=1,
    )
    attn_sum = lax.psum(after(attn_parts, fc_sum), "plane")

    counted = (lax.broadcasted_iota(jnp.int32, (n * rows, 1), 0) < rows) | (
        lax.broadcasted_iota(jnp.int32, (1, d_qkv.shape[1]), 1) < 3 * main
    )
    d_once = after(jnp.where(counted, d_qkv, BF(0)), attn_parts)
    f = reduce_rows([cols_dot(block(d_once, d), w_attn) for d in range(n)])
    xhat_own, inv_own = normalize(own_tokens)
    f_gain = f * gain_one
    d_tokens = inv_own * (
        f_gain
        - jnp.mean(f_gain, axis=-1, keepdims=True)
        - xhat_own * jnp.mean(f_gain * xhat_own, axis=-1, keepdims=True)
    )
    input_grad = (d_middle + d_tokens).astype(BF)[None]

    late_active = after(active, attn_parts)
    out_parts = [
        jnp.dot(block(late_active, d), out_weight, preferred_element_type=F32) for d in range(n)
    ]
    output = (middle + reduce_rows(out_parts) + b_out).astype(BF)[None]

    sum_fc_weight = local_call(
        functools.partial(
            unpack_kernel,
            n,
            half,
            step,
            lambda m, d: [(0, (m ^ d) * own_ff, d * half, 0, own_ff)],
        ),
        [jax.ShapeDtypeStruct((own_rows, n * own_ff), F32)],
        own_rows * n * own_ff * 8,
        at,
        fc_sum,
        swap_core(fc_sum),
    )[0]

    def attn_places(m, d):
        base = d * 3 * main
        places = [
            (0, p * D + (m ^ d) * main, 0, base + p * main, base + (p + 1) * main)
            for p in range(3)
        ]
        if d == 0:
            base = n * 3 * main
            places += [
                (0, p * D + n * main, 0, base + p * spare, base + (p + 1) * spare)
                for p in range(3)
            ]
            places.append((1, 0, 0, 3 * D, 4 * D))
        return places

    sum_attn_weight, sum_proj_weight = local_call(
        functools.partial(unpack_kernel, n, half, step, attn_places),
        [
            jax.ShapeDtypeStruct((own_rows, 3 * D), F32),
            jax.ShapeDtypeStruct((own_rows, D), F32),
        ],
        own_rows * 4 * D * 8,
        at,
        attn_sum,
        swap_core(attn_sum),
    )

    d_once_sum = jnp.sum(d_once.astype(F32), axis=0)

    def vector_of(part):
        whole = jnp.zeros((D,), F32)
        whole = lax.dynamic_update_slice_in_dim(
            whole, d_once_sum[part * main : (part + 1) * main], me * main, 0
        )
        lane = 3 * main + part * spare
        return jnp.concatenate([whole[: n * main], d_once_sum[lane : lane + spare]])

    small_grads = jnp.stack(
        [
            vector_of(0),
            vector_of(2),
            jnp.sum(d_branch.astype(F32), axis=0),
            jnp.sum(f * xhat_own, axis=0),
            jnp.sum(f, axis=0),
            jnp.sum(e * xhat_two, axis=0),
            jnp.sum(e, axis=0),
            jnp.sum(own_cot.astype(F32), axis=0),
        ]
    )
    small_grads = small_grads.reshape(8, n, own_rows).transpose(1, 0, 2)
    small_own = pick(small_grads, me)
    for d in range(1, n):
        small_own = small_own + swap(pick(small_grads, me ^ d), d)
    small_own = jnp.concatenate([small_own, grad_fc_bias.reshape(-1, own_rows)], axis=0)
    small_own = small_own + swap_core(small_own)
    hop = 1
    while hop < planes:
        small_own = small_own + lax.ppermute(
            small_own, "plane", [(i, i ^ hop) for i in range(planes)]
        )
        hop *= 2
    s = small_own[:8]
    sum_fc_bias = small_own[8:].reshape(-1)
    return (
        output,
        input_grad,
        sum_attn_weight,
        s[0],
        s[1],
        sum_proj_weight,
        s[2],
        s[3],
        s[4],
        s[5],
        s[6],
        sum_fc_weight,
        sum_fc_bias,
        sum_out_weight.astype(F32),
        s[7],
    )


def solution(mesh):
    shards, reps = mesh.devices.shape
    split = jax.sharding.Mesh(
        mesh.devices.reshape(shards, reps // 2, 2), ("shard", "plane", "core")
    )
    rep = ("plane", "core")
    batch = P(rep, "shard", None)
    row, vec = P("shard", None), P("shard")
    return jax.shard_map(
        body,
        mesh=split,
        in_specs=(batch, batch, P(rep, None), row, vec, vec, row)
        + (vec,) * 5
        + (row, vec, row, vec),
        out_specs=(batch, batch, row, vec, vec, row) + (vec,) * 5 + (row, vec, row, vec),
        check_vma=False,
    )
```

```python
import functools
import math

import jax
import jax.numpy as jnp
from jax import lax
from jax.experimental import pallas as pl
from jax.experimental.pallas import tpu as pltpu
from jax.sharding import PartitionSpec as P

D = 1600
HEADS = 25
HD = 64
UNIT = 32
LANES = 128
NEG = -1e30
VEC_ROWS = 16
BF = jnp.bfloat16
F32 = jnp.float32


def dot(left, right, dims):
    return lax.dot_general(left, right, (dims, ((), ())), preferred_element_type=F32)


def rows_dot(left, right):
    return dot(left, right, ((0,), (0,)))


def cols_dot(left, right):
    return dot(left, right, ((1,), (1,)))


def normalize(values):
    center = values - jnp.mean(values, axis=-1, keepdims=True)
    spread = jnp.mean(center * center, axis=-1, keepdims=True)
    inv = lax.rsqrt(spread + 1e-05)
    return center * inv, inv


def place_blocks(info_ref, shards, units):
    b0, b1, b2, me = info_ref[0], info_ref[1], info_ref[2], info_ref[3]
    e0, e1 = b0, b0 + b1
    places = []
    for d in range(shards):
        s = jnp.bitwise_xor(me, d)
        for u in range(units):
            first = jnp.where(u < e0, 0, jnp.where(u < e1, e0, e1))
            span = jnp.where(u < e0, b0, jnp.where(u < e1, b1, b2))
            places.append((d * units + u, first * shards + s * span + (u - first)))
    return places, e0, e1


def head_lanes(tile_rows, half):
    lane = lax.broadcasted_iota(jnp.int32, (tile_rows, LANES), 1)
    return (lane < HD) if half == 0 else (lane >= HD)


def window_scores(q, k, rows, width):
    scores = cols_dot(q, k)
    row = lax.broadcasted_iota(jnp.int32, (rows, width * rows), 0)
    col = lax.broadcasted_iota(jnp.int32, (rows, width * rows), 1)
    return jnp.where(col <= row + (width - 1) * rows, scores, NEG)


def fwd_kernel(shards, units, heads, info_ref, qkv_ref, out_ref, perm, mixed):
    block = UNIT
    rows = shards * block
    main = heads * HD
    places, e0, e1 = place_blocks(info_ref, shards, units)
    for src, dst in places:
        at = pl.ds(pl.multiple_of(dst * block, block), block)
        perm[at, :] = qkv_ref[src * block : (src + 1) * block, :]

    def unit(i, carry):
        first = jnp.where(i < e0, 0, jnp.where(i < e1, e0, e1))
        q_at = pl.ds(pl.multiple_of(i * rows, rows), rows)
        for width in range(1, 5):

            @pl.when(i - first + 1 == width)
            def _():
                k_at = pl.ds(pl.multiple_of(first * rows, rows), width * rows)

                def attend(q, k, v):
                    scores = window_scores(q * BF(0.125), k, rows, width)
                    top = jnp.max(scores, axis=1, keepdims=True)
                    probs = jnp.exp(scores - top)
                    total = jnp.sum(probs, axis=1, keepdims=True)
                    return dot(probs.astype(BF), v, ((1,), (0,))) / total

                for tile in range(main // LANES):
                    lanes = slice(tile * LANES, (tile + 1) * LANES)
                    k_lanes = slice(main + lanes.start, main + lanes.stop)
                    v_lanes = slice(2 * main + lanes.start, 2 * main + lanes.stop)
                    q, k, v = perm[q_at, lanes], perm[k_at, k_lanes], perm[k_at, v_lanes]
                    low = head_lanes(rows, 0)
                    zero = jnp.zeros_like(q)
                    left = attend(jnp.where(low, q, zero), k, v)
                    right = attend(jnp.where(low, zero, q), k, v)
                    mixed[q_at, lanes] = jnp.where(low, left, right).astype(BF)
                if main % LANES:
                    lanes = main - HD
                    mixed[q_at, lanes:main] = attend(
                        perm[q_at, lanes:main],
                        perm[k_at, main + lanes : 2 * main],
                        perm[k_at, 2 * main + lanes : 3 * main],
                    ).astype(BF)
                base = 3 * main
                mixed[q_at, main : main + HD] = attend(
                    perm[q_at, base : base + HD],
                    perm[k_at, base + HD : base + 2 * HD],
                    perm[k_at, base + 2 * HD : base + 3 * HD],
                ).astype(BF)

        return carry

    lax.fori_loop(0, units, unit, 0)
    for src, dst in places:
        at = pl.ds(pl.multiple_of(dst * block, block), block)
        out_ref[src * block : (src + 1) * block, :] = mixed[at, :]


def bwd_kernel(
    shards, units, heads, info_ref, qkv_ref, dmix_ref, out_ref, perm, dperm, dq_acc, dk_acc, dv_acc
):
    block = UNIT
    rows = shards * block
    main = heads * HD
    places, e0, e1 = place_blocks(info_ref, shards, units)
    for src, dst in places:
        at = pl.ds(pl.multiple_of(dst * block, block), block)
        perm[at, :] = qkv_ref[src * block : (src + 1) * block, :]
        dperm[at, :] = dmix_ref[src * block : (src + 1) * block, :]
    dk_acc[...] = jnp.zeros_like(dk_acc)
    dv_acc[...] = jnp.zeros_like(dv_acc)

    def unit(i, carry):
        first = jnp.where(i < e0, 0, jnp.where(i < e1, e0, e1))
        q_at = pl.ds(pl.multiple_of(i * rows, rows), rows)
        for width in range(1, 5):

            @pl.when(i - first + 1 == width)
            def _():
                k_at = pl.ds(pl.multiple_of(first * rows, rows), width * rows)

                def pull(q, k, v, g):
                    q = q * BF(0.125)
                    scores = window_scores(q, k, rows, width)
                    top = jnp.max(scores, axis=1, keepdims=True)
                    probs = jnp.exp(scores - top)
                    total = jnp.sum(probs, axis=1, keepdims=True)
                    probs = probs * (1.0 / total)
                    d_probs = cols_dot(g, v)
                    delta = jnp.sum(probs * d_probs, axis=1, keepdims=True)
                    d_scores = (probs * (d_probs - delta)).astype(BF)
                    d_q = dot(d_scores, k, ((1,), (0,))) * 0.125
                    return d_q, rows_dot(d_scores, q), rows_dot(probs.astype(BF), g)

                for tile in range(main // LANES):
                    lanes = slice(tile * LANES, (tile + 1) * LANES)
                    k_lanes = slice(main + lanes.start, main + lanes.stop)
                    v_lanes = slice(2 * main + lanes.start, 2 * main + lanes.stop)
                    q, k, v = perm[q_at, lanes], perm[k_at, k_lanes], perm[k_at, v_lanes]
                    g = dperm[q_at, lanes]
                    low = head_lanes(rows, 0)
                    zero = jnp.zeros_like(q)
                    dq0, dk0, dv0 = pull(jnp.where(low, q, zero), k, v, jnp.where(low, g, zero))
                    dq1, dk1, dv1 = pull(jnp.where(low, zero, q), k, v, jnp.where(low, zero, g))
                    dq_acc[q_at, lanes] = jnp.where(low, dq0, dq1).astype(BF)
                    dk_acc[k_at, lanes] += dk0 + dk1
                    dv_acc[k_at, lanes] += dv0 + dv1
                extra = [(main, 3 * main, 3 * main + HD, 3 * main + 2 * HD)]
                if main % LANES:
                    extra.append((main - HD, main - HD, 2 * main - HD, 3 * main - HD))
                for own, q_lane, k_lane, v_lane in extra:
                    dq0, dk0, dv0 = pull(
                        perm[q_at, q_lane : q_lane + HD],
                        perm[k_at, k_lane : k_lane + HD],
                        perm[k_at, v_lane : v_lane + HD],
                        dperm[q_at, own : own + HD],
                    )
                    dq_acc[q_at, own : own + HD] = dq0.astype(BF)
                    dk_acc[k_at, own : own + HD] += dk0
                    dv_acc[k_at, own : own + HD] += dv0

        return carry

    lax.fori_loop(0, units, unit, 0)
    for src, dst in places:
        at = pl.ds(pl.multiple_of(dst * block, block), block)
        to = slice(src * block, (src + 1) * block)
        for part, acc in enumerate((dq_acc, dk_acc, dv_acc)):
            got = acc[at, :].astype(BF)
            out_ref[to, part * main : (part + 1) * main] = got[:, :main]
            lane = 3 * main + part * HD
            out_ref[to, lane : lane + HD] = got[:, main:]


def vmem_call(kernel, out_shape, scratch, cost, inputs):
    return pl.pallas_call(
        kernel,
        out_shape=out_shape,
        in_specs=[pl.BlockSpec(memory_space=pltpu.SMEM)]
        + [pl.BlockSpec(memory_space=pltpu.VMEM)] * (len(inputs) - 1),
        out_specs=pl.BlockSpec(memory_space=pltpu.VMEM),
        scratch_shapes=scratch,
        compiler_params=pltpu.CompilerParams(vmem_limit_bytes=48 << 20),
        cost_estimate=cost,
    )(*inputs)


def attention_fwd(info, qkv, shards, heads):
    total, width = qkv.shape
    units = total // (shards * UNIT)
    own = (heads + 1) * HD
    return vmem_call(
        functools.partial(fwd_kernel, shards, units, heads),
        jax.ShapeDtypeStruct((total, own), BF),
        [pltpu.VMEM((total, width), BF), pltpu.VMEM((total, own), BF)],
        pl.CostEstimate(flops=1, bytes_accessed=1, transcendentals=0),
        (info, qkv),
    )


def attention_bwd(info, qkv, d_mixed, shards, heads):
    total, width = qkv.shape
    units = total // (shards * UNIT)
    own = (heads + 1) * HD
    return vmem_call(
        functools.partial(bwd_kernel, shards, units, heads),
        jax.ShapeDtypeStruct((total, width), BF),
        [
            pltpu.VMEM((total, width), BF),
            pltpu.VMEM((total, own), BF),
            pltpu.VMEM((total, own), BF),
            pltpu.VMEM((total, own), F32),
            pltpu.VMEM((total, own), F32),
        ],
        pl.CostEstimate(flops=1, bytes_accessed=1, transcendentals=0),
        (info, qkv, d_mixed),
    )


def on_place(me, core, shards, run):
    for m in range(shards):
        for c in range(2):

            @pl.when((me == m) & (core == c))
            def _():
                run(m, c)


def attn_columns(value, j, heads):
    main = heads * HD
    first = D // main * main
    parts = [value[:, p * D + j * main : p * D + (j + 1) * main] for p in range(3)]
    parts += [value[:, p * D + first : (p + 1) * D] for p in range(3)]
    return jnp.concatenate(parts, axis=1)


def fc_columns(value, j, width):
    return value[:, j * width : (j + 1) * width]


def pack_kernel(shards, half, step, columns, at_ref, dep_ref, weight_ref, *outs):
    del dep_ref

    def run(m, c):
        outs[0][...] = columns(weight_ref, m)
        for d in range(1, shards):
            piece = columns(weight_ref.at[c * step : c * step + half], m ^ d)
            outs[d][...] = piece

    on_place(at_ref[0], at_ref[1], shards, run)


def pack_attn_kernel(shards, half, step, heads, at_ref, weight_ref, *refs):
    vectors, outs = refs[0], refs[1:]
    count, length = vectors.shape

    def run(m, c):
        outs[0][: shards_rows(outs[0]), :] = attn_columns(weight_ref, m, heads)
        for d in range(1, shards):
            outs[d][:half, :] = attn_columns(weight_ref.at[c * step : c * step + half], m ^ d, heads)

    def shards_rows(ref):
        return ref.shape[0] - VEC_ROWS

    on_place(at_ref[0], at_ref[1], shards, run)
    width = outs[0].shape[1]
    block = jnp.concatenate(
        [vectors[...].astype(F32), jnp.zeros((VEC_ROWS - count, length), F32)], axis=0
    )
    block = jnp.concatenate(
        [block, jnp.zeros((VEC_ROWS, width - length), F32)], axis=1
    ).astype(BF)
    for out in outs:
        out[out.shape[0] - VEC_ROWS :, :] = block


def place_attn_kernel(shards, half, step, rows, count, at_ref, *refs):
    own, mine, other = refs[0], refs[1:shards], refs[shards]
    out, vec = refs[shards + 1 :]

    def run(m, c):
        out[m * rows : (m + 1) * rows, :] = own[:rows]
        for d in range(1, shards):
            base = (m ^ d) * rows
            a, b = mine[d - 1][:half], other[d - 1]
            low, high = (a, b) if c == 0 else (b, a)
            out[base : base + step, :] = low[:step]
            out[base + step : base + rows, :] = high
        for j in range(shards):
            ref, at = (own, rows) if j == m else (mine[(j ^ m) - 1], half)
            vec[:, j * rows : (j + 1) * rows] = ref[at : at + VEC_ROWS, :rows].astype(F32)[:count]

    on_place(at_ref[0], at_ref[1], shards, run)


def place_kernel(shards, half, step, rows, at_ref, *refs):
    own, mine, other, out = refs[0], refs[1:shards], refs[shards], refs[shards + 1]

    def run(m, c):
        out[m * rows : (m + 1) * rows, :] = own[...]
        for d in range(1, shards):
            base = (m ^ d) * rows
            low, high = (mine[d - 1][...], other[d - 1]) if c == 0 else (other[d - 1], mine[d - 1][...])
            out[base : base + step, :] = low[:step]
            out[base + step : base + rows, :] = high

    on_place(at_ref[0], at_ref[1], shards, run)


def pack_part_kernel(shards, length, stride, columns, at_ref, weight_ref, *outs):
    part = pl.ds(pl.multiple_of(at_ref[2] * stride, 16), length)
    for m in range(shards):

        @pl.when(at_ref[0] == m)
        def _():
            outs[0][...] = columns(weight_ref, m)
            for d in range(1, shards):
                outs[d][...] = columns(weight_ref.at[part], m ^ d)


def place_part_kernel(shards, length, stride, rows, at_ref, own, mine, near, across, out):
    me, q = at_ref[0], at_ref[2]
    out[pl.ds(pl.multiple_of(me * rows, 16), rows), :] = own[...]
    size = (shards - 1) * length
    for d in range(1, shards):
        base = jnp.bitwise_xor(me, d) * rows
        for flip, ref, first in ((0, mine, 0), (2, near, 0), (1, across, 0), (3, across, size)):
            to = base + jnp.bitwise_xor(q, flip) * stride
            row = first + (d - 1) * length
            out[pl.ds(pl.multiple_of(to, 16), length), :] = ref[row : row + length, :]


def unpack_kernel(shards, half, step, places, at_ref, mine, other, *outs):
    def run(m, c):
        for d in range(shards):
            for index, where, row, low, high in places(m, d):
                out, width = outs[index], high - low
                a = mine[row : row + half, low:high]
                b = other[row : row + half, low:high]
                first, second = (a, b) if c == 0 else (b, a)
                out[:step, where : where + width] = first[:step].astype(F32)
                out[step:, where : where + width] = second.astype(F32)

    on_place(at_ref[0], at_ref[1], shards, run)


def spread_kernel(shards, places, at_ref, whole, *outs):
    for m in range(shards):

        @pl.when(at_ref[0] == m)
        def _():
            for d in range(shards):
                for index, where, row, low, high in places(m, d):
                    outs[index][:, where : where + high - low] = whole[:, low:high].astype(F32)


def local_call(kernel, out_shape, cost_bytes, at, *inputs, anywhere=()):
    vmem = pl.BlockSpec(memory_space=pltpu.VMEM)
    specs = [pl.BlockSpec(memory_space=pl.ANY) if i in anywhere else vmem for i in range(len(inputs))]
    return pl.pallas_call(
        kernel,
        out_shape=out_shape,
        in_specs=[pl.BlockSpec(memory_space=pltpu.SMEM)] + specs,
        out_specs=jax.tree.map(lambda _: vmem, out_shape),
        compiler_params=pltpu.CompilerParams(vmem_limit_bytes=48 << 20),
        cost_estimate=pl.CostEstimate(flops=1, bytes_accessed=1, transcendentals=0),
    )(at, *inputs)


def body(
    tokens,
    cotangent,
    lengths,
    attn_weight,
    query_bias,
    value_bias,
    proj_weight,
    proj_bias,
    ln1_gain,
    ln1_bias,
    ln2_gain,
    ln2_bias,
    fc_weight,
    fc_bias,
    out_weight,
    out_bias,
):
    n = lax.axis_size("shard")
    planes = lax.axis_size("plane")
    me = lax.axis_index("shard")
    core = lax.axis_index("core")
    heads = (HEADS - 1) // n
    main = heads * HD
    spare = D - n * main
    own_rows = attn_weight.shape[0]
    own_ff = fc_bias.shape[0]
    rows = tokens.shape[1]
    half = -(-own_rows // 32) * 16
    step = own_rows - half
    quarter = lax.axis_index("plane") % 2 * 2 + core
    at = jnp.stack([me, core, quarter]).astype(jnp.int32)

    def swap(value, d):
        return lax.ppermute(value, "shard", [(i, i ^ d) for i in range(n)])

    def swap_plane(value):
        return lax.ppermute(value, "plane", [(i, i ^ 1) for i in range(planes)])

    def swap_core(value):
        return lax.ppermute(value, "core", [(0, 1), (1, 0)])

    def gather_near(value):
        if n != 4:
            return [swap(value, d) for d in range(1, n)]
        return [swap(value, 1), swap(value, 2)]

    def gather_far(value, near):
        if n != 4:
            return [value] + near
        one, two = near
        cut = value.shape[0] // 32 * 16
        three = jnp.concatenate([swap(one[:cut], 2), swap(two[cut:], 1)], axis=0)
        return [value, one, two, three]

    def gather(value):
        return gather_far(value, gather_near(value))

    def pick(stacked, index):
        return lax.dynamic_index_in_dim(stacked, index, 0, keepdims=False)

    def natural(pieces):
        stacked = jnp.stack(pieces)
        return [pick(stacked, me ^ j) for j in range(n)]

    def after(value, *deps):
        return lax.optimization_barrier((value, deps))[0]

    def block(value, d):
        return value[d * rows : (d + 1) * rows]

    def place(own, mine):
        other = swap_core(jnp.stack(mine))
        return local_call(
            functools.partial(place_kernel, n, half, step, own_rows),
            jax.ShapeDtypeStruct((n * own_rows, own.shape[1]), BF),
            n * own.size * 4,
            at,
            own,
            *mine,
            other,
        )

    def pack(weight, columns, width, dep):
        shapes = [jax.ShapeDtypeStruct((own_rows, width), BF)]
        shapes += [jax.ShapeDtypeStruct((half, width), BF)] * (n - 1)
        return local_call(
            functools.partial(pack_kernel, n, half, step, columns),
            shapes,
            weight.size * 2,
            at,
            dep,
            weight,
            anywhere=(0,),
        )

    def reduce_rows(parts):
        total = parts[0].astype(F32)
        for d in range(1, n):
            total = total + swap(parts[d].astype(BF), d).astype(F32)
        return total

    def core_halves(parts):
        keep = lax.dynamic_slice_in_dim(parts, core * step, half, 1)
        give = lax.dynamic_slice_in_dim(parts, (1 - core) * step, half, 1)
        return (keep.astype(F32) + swap_core(give).astype(F32)).astype(BF)

    vectors = (
        query_bias, value_bias, proj_bias, ln1_gain, ln1_bias, ln2_gain, ln2_bias, out_bias
    )
    tokens_near = gather_near(tokens[0])
    attn_width = 3 * (main + spare)
    attn_sent = local_call(
        functools.partial(pack_attn_kernel, n, half, step, heads),
        [jax.ShapeDtypeStruct((own_rows + VEC_ROWS, attn_width), BF)]
        + [jax.ShapeDtypeStruct((half + VEC_ROWS, attn_width), BF)] * (n - 1),
        attn_weight.size * 2,
        at,
        attn_weight,
        jnp.concatenate(vectors).reshape(len(vectors), own_rows),
    )
    attn_got = [swap(attn_sent[d], d) for d in range(1, n)]
    attn_got, tokens_near = after((attn_got, tokens_near))
    attn_other = swap_core(jnp.stack([piece[:half] for piece in attn_got]))
    tokens_parts = gather_far(tokens[0], tokens_near)
    w_attn, small = local_call(
        functools.partial(place_attn_kernel, n, half, step, own_rows, len(vectors)),
        [
            jax.ShapeDtypeStruct((D, attn_width), BF),
            jax.ShapeDtypeStruct((len(vectors), D), F32),
        ],
        D * attn_width * 4,
        at,
        attn_sent[0],
        *attn_got,
        attn_other,
    )
    b_query, b_value, b_proj, gain_one, bias_one, gain_two, bias_two, b_out = [
        small[i] for i in range(8)
    ]

    def my_columns(vector):
        return lax.dynamic_slice_in_dim(vector, me * main, main, 0), vector[n * main :]

    q_main, q_spare = my_columns(b_query)
    v_main, v_spare = my_columns(b_value)
    qkv_bias = jnp.concatenate(
        [q_main, jnp.zeros_like(q_main), v_main, q_spare, jnp.zeros_like(q_spare), v_spare]
    )

    group_tokens = jnp.concatenate(tokens_parts, axis=0)
    proj_half = lax.dynamic_slice_in_dim(after(proj_weight, attn_got), core * step, half, 0)
    proj_near = gather_near(proj_half)
    own_cot = cotangent[0]
    cot_all = lax.all_gather(after(own_cot, attn_got, tokens_near), "shard", axis=0, tiled=True)
    late_fc = after(fc_weight, attn_got)
    stride = own_rows // 64 * 16
    length = own_rows - 3 * stride
    by_parts = own_rows % 16 == 0 and stride > 0 and planes % 2 == 0
    if by_parts:
        fc_sent = local_call(
            functools.partial(
                pack_part_kernel, n, length, stride, lambda ref, j: fc_columns(ref, j, own_ff)
            ),
            [jax.ShapeDtypeStruct((own_rows, own_ff), BF)]
            + [jax.ShapeDtypeStruct((length, own_ff), BF)] * (n - 1),
            fc_weight.size * 2,
            at,
            late_fc,
        )
    else:
        fc_sent = pack(late_fc, lambda ref, j: fc_columns(ref, j, own_ff), own_ff, lengths)
    xhat_one, _ = normalize(group_tokens.astype(F32))
    normed = (xhat_one * gain_one + bias_one).astype(BF)
    qkv = (jnp.dot(normed, w_attn, preferred_element_type=F32) + qkv_bias).astype(BF)
    qkv, proj_near, fc_sent = after((qkv, proj_near, fc_sent))
    proj_parts = gather_far(proj_half, proj_near)
    fc_got = [swap(fc_sent[d], d) for d in range(1, n)]
    info = jnp.concatenate([lengths[0], me.astype(jnp.int32)[None]])
    mixed_heads = attention_fwd(info, qkv, n, heads)
    mixed_heads, proj_parts, fc_got = after((mixed_heads, proj_parts, fc_got))
    got = [block(mixed_heads, 0)[:, :main]] + [
        swap(block(mixed_heads, d)[:, :main], d) for d in range(1, n)
    ]
    if by_parts:
        fc_mine = jnp.concatenate(fc_got)
        fc_near = swap_plane(fc_mine)
    w_proj = place(proj_weight, proj_parts[1:])
    got, w_proj = after((got, w_proj))
    got, cot_all = after((got, cot_all))
    mixed_low = jnp.concatenate(natural(got) + [block(mixed_heads, 0)[:, main:]], axis=1)
    own_tokens = tokens[0].astype(F32)
    middle = own_tokens + jnp.dot(mixed_low, w_proj, preferred_element_type=F32) + b_proj
    xhat_two, inv_two = normalize(middle)
    own_normed_two = (xhat_two * gain_two + bias_two).astype(BF)
    normed_near = gather_near(own_normed_two)
    normed_near_sent = own_normed_two
    if by_parts:
        w_fc = local_call(
            functools.partial(place_part_kernel, n, length, stride, own_rows),
            jax.ShapeDtypeStruct((D, own_ff), BF),
            D * own_ff * 4,
            at,
            fc_sent[0],
            fc_mine,
            fc_near,
            swap_core(jnp.concatenate(after([fc_mine, fc_near], normed_near_sent))),
        )
    else:
        w_fc = place(fc_sent[0], fc_got)
    normed_parts = gather_far(own_normed_two, normed_near)
    cot_parts = [own_cot] + [
        lax.dynamic_slice_in_dim(cot_all, (me ^ d) * rows, rows, 0) for d in range(1, n)
    ]
    group_cot = jnp.concatenate(cot_parts, axis=0)
    normed_two = jnp.concatenate(normed_parts, axis=0)

    def feed(part):
        hidden = jnp.dot(part, w_fc, preferred_element_type=F32) + fc_bias.astype(F32)
        inner = jnp.tanh(0.7978845608028654 * (hidden + 0.044715 * hidden * hidden * hidden))
        slope = 0.5 * (1.0 + inner) + 0.5 * hidden * (1.0 - inner * inner) * (
            0.7978845608028654 * (1.0 + 3 * 0.044715 * hidden * hidden)
        )
        return (0.5 * hidden * (1.0 + inner)).astype(BF), slope.astype(BF)

    fed = [feed(part) for part in normed_parts]
    active_parts = [a for a, _ in fed]
    active = jnp.concatenate(active_parts, axis=0)

    d_active = after(cols_dot(group_cot, out_weight).astype(BF))
    grad_out_weight = rows_dot(active, group_cot).astype(BF)
    sum_out_weight = lax.psum(grad_out_weight, ("plane", "core"))
    d_active = after(d_active, grad_out_weight)
    d_hidden_parts = [
        (block(d_active, d).astype(F32) * slope.astype(F32)).astype(BF)
        for d, (_, slope) in enumerate(fed)
    ]
    d_hidden = jnp.concatenate(d_hidden_parts, axis=0)
    e = reduce_rows([cols_dot(part, w_fc) for part in d_hidden_parts])
    e_gain = e * gain_two
    d_middle = own_cot.astype(F32) + inv_two * (
        e_gain
        - jnp.mean(e_gain, axis=-1, keepdims=True)
        - xhat_two * jnp.mean(e_gain * xhat_two, axis=-1, keepdims=True)
    )
    d_branch = d_middle.astype(BF)
    d_mixed = cols_dot(d_branch, w_proj).astype(BF)
    for_heads = jnp.stack([d_mixed[:, j * main : (j + 1) * main] for j in range(n)])
    last = d_mixed[:, n * main :]
    dmix_parts = [jnp.concatenate([pick(for_heads, me), last], axis=1)] + [
        swap(jnp.concatenate([pick(for_heads, me ^ d), last], axis=1), d) for d in range(1, n)
    ]

    grad_fc = rows_dot(normed_two, d_hidden).astype(BF).reshape(n, own_rows, own_ff)
    fc_halves = core_halves(grad_fc)
    grad_fc_bias = jnp.sum(d_hidden.astype(F32), axis=0)

    grad_proj = rows_dot(mixed_low, d_branch).astype(BF).reshape(n, own_rows, D)
    proj_halves = after(core_halves(grad_proj), dmix_parts)
    proj_part = reduce_rows([pick(proj_halves, me ^ d) for d in range(n)]).astype(BF)
    dmix_parts, fc_halves = after((dmix_parts, fc_halves))
    fc_sum = lax.psum(fc_halves.reshape(n * half, own_ff), "plane").reshape(n, half, own_ff)
    d_qkv = attention_bwd(info, qkv, jnp.concatenate(dmix_parts, axis=0), n, heads)
    d_qkv, proj_part = after((d_qkv, proj_part))
    proj_rows = jnp.where(
        core == 0,
        jnp.concatenate([proj_part[:step], jnp.zeros((half, D), BF)]),
        jnp.concatenate([jnp.zeros((step, D), BF), proj_part]),
    )

    grad_main = rows_dot(normed, d_qkv[:, : 3 * main]).astype(BF).reshape(n, own_rows, 3 * main)
    attn_got = [swap(pick(grad_main, me ^ d), d) for d in range(1, n)]
    grad_spare = rows_dot(normed, d_qkv[:, 3 * main :]).astype(BF).reshape(n, own_rows, 3 * spare)
    attn_parts = jnp.concatenate(
        [pick(grad_main, me)] + attn_got + [pick(grad_spare, me), proj_rows], axis=1
    )
    attn_sum = lax.psum(after(attn_parts, sum_out_weight), ("plane", "core"))

    counted = (lax.broadcasted_iota(jnp.int32, (n * rows, 1), 0) < rows) | (
        lax.broadcasted_iota(jnp.int32, (1, d_qkv.shape[1]), 1) < 3 * main
    )
    d_once = after(jnp.where(counted, d_qkv, BF(0)), attn_parts)
    f = reduce_rows([cols_dot(block(d_once, d), w_attn) for d in range(n)])
    xhat_own, inv_own = normalize(own_tokens)
    f_gain = f * gain_one
    d_tokens = inv_own * (
        f_gain
        - jnp.mean(f_gain, axis=-1, keepdims=True)
        - xhat_own * jnp.mean(f_gain * xhat_own, axis=-1, keepdims=True)
    )
    input_grad = (d_middle + d_tokens).astype(BF)[None]

    late_active = after(active, attn_parts)
    out_parts = [
        jnp.dot(block(late_active, d), out_weight, preferred_element_type=F32) for d in range(n)
    ]
    output = (middle + reduce_rows(out_parts) + b_out).astype(BF)[None]

    fc_sum = after(fc_sum, attn_parts)
    fc_parts = jnp.concatenate(
        [pick(fc_sum, me)] + [swap(pick(fc_sum, me ^ d), d) for d in range(1, n)]
    )
    sum_fc_weight = local_call(
        functools.partial(
            unpack_kernel,
            n,
            half,
            step,
            lambda m, d: [(0, (m ^ d) * own_ff, d * half, 0, own_ff)],
        ),
        [jax.ShapeDtypeStruct((own_rows, n * own_ff), F32)],
        own_rows * n * own_ff * 8,
        at,
        fc_parts,
        swap_core(fc_parts),
    )[0]
    sum_out_weight = sum_out_weight.astype(F32)

    def attn_places(m, d):
        base = d * 3 * main
        places = [
            (0, p * D + (m ^ d) * main, 0, base + p * main, base + (p + 1) * main)
            for p in range(3)
        ]
        if d == 0:
            base = n * 3 * main
            places += [
                (0, p * D + n * main, 0, base + p * spare, base + (p + 1) * spare)
                for p in range(3)
            ]
            places.append((1, 0, 0, 3 * D, 4 * D))
        return places

    d_once_sum = jnp.sum(d_once.astype(F32), axis=0)

    def vector_of(part):
        whole = jnp.zeros((D,), F32)
        whole = lax.dynamic_update_slice_in_dim(
            whole, d_once_sum[part * main : (part + 1) * main], me * main, 0
        )
        lane = 3 * main + part * spare
        return jnp.concatenate([whole[: n * main], d_once_sum[lane : lane + spare]])

    small_grads = jnp.stack(
        [
            vector_of(0),
            vector_of(2),
            jnp.sum(d_branch.astype(F32), axis=0),
            jnp.sum(f * xhat_own, axis=0),
            jnp.sum(f, axis=0),
            jnp.sum(e * xhat_two, axis=0),
            jnp.sum(e, axis=0),
            jnp.sum(own_cot.astype(F32), axis=0),
        ]
    )
    small_grads = small_grads.reshape(8, n, own_rows).transpose(1, 0, 2)
    small_own = pick(small_grads, me)
    for d in range(1, n):
        small_own = small_own + swap(pick(small_grads, me ^ d), d)
    small_own = jnp.concatenate([small_own, grad_fc_bias.reshape(-1, own_rows)], axis=0)
    small_own = small_own + swap_core(small_own)
    hop = 1
    while hop < planes:
        small_own = small_own + lax.ppermute(
            small_own, "plane", [(i, i ^ hop) for i in range(planes)]
        )
        hop *= 2
    attn_sum, small_own, output, input_grad, sum_fc_weight, sum_out_weight = after(
        (attn_sum, small_own, output, input_grad, sum_fc_weight, sum_out_weight)
    )
    sum_attn_weight, sum_proj_weight = local_call(
        functools.partial(spread_kernel, n, attn_places),
        [
            jax.ShapeDtypeStruct((own_rows, 3 * D), F32),
            jax.ShapeDtypeStruct((own_rows, D), F32),
        ],
        own_rows * 4 * D * 8,
        at,
        attn_sum,
    )
    s = small_own[:8]
    sum_fc_bias = small_own[8:].reshape(-1)
    return (
        output,
        input_grad,
        sum_attn_weight,
        s[0],
        s[1],
        sum_proj_weight,
        s[2],
        s[3],
        s[4],
        s[5],
        s[6],
        sum_fc_weight,
        sum_fc_bias,
        sum_out_weight,
        s[7],
    )


def solution(mesh):
    shards, reps = mesh.devices.shape
    split = jax.sharding.Mesh(
        mesh.devices.reshape(shards, reps // 2, 2), ("shard", "plane", "core")
    )
    rep = ("plane", "core")
    batch = P(rep, "shard", None)
    row, vec = P("shard", None), P("shard")
    return jax.shard_map(
        body,
        mesh=split,
        in_specs=(batch, batch, P(rep, None), row, vec, vec, row)
        + (vec,) * 5
        + (row, vec, row, vec),
        out_specs=(batch, batch, row, vec, vec, row) + (vec,) * 5 + (row, vec, row, vec),
        check_vma=False,
    )
```

```python
import functools
import math

import jax
import jax.numpy as jnp
from jax import lax
from jax.experimental import pallas as pl
from jax.experimental.pallas import tpu as pltpu
from jax.sharding import PartitionSpec as P

D = 1600
HEADS = 25
HD = 64
UNIT = 32
LANES = 128
NEG = -1e30
VEC_ROWS = 16
BF = jnp.bfloat16
F32 = jnp.float32


def dot(left, right, dims):
    return lax.dot_general(left, right, (dims, ((), ())), preferred_element_type=F32)


def rows_dot(left, right):
    return dot(left, right, ((0,), (0,)))


def cols_dot(left, right):
    return dot(left, right, ((1,), (1,)))


def normalize(values):
    center = values - jnp.mean(values, axis=-1, keepdims=True)
    spread = jnp.mean(center * center, axis=-1, keepdims=True)
    inv = lax.rsqrt(spread + 1e-05)
    return center * inv, inv


def place_blocks(info_ref, shards, units):
    b0, b1, b2, me = info_ref[0], info_ref[1], info_ref[2], info_ref[3]
    e0, e1 = b0, b0 + b1
    places = []
    for d in range(shards):
        s = jnp.bitwise_xor(me, d)
        for u in range(units):
            first = jnp.where(u < e0, 0, jnp.where(u < e1, e0, e1))
            span = jnp.where(u < e0, b0, jnp.where(u < e1, b1, b2))
            places.append((d * units + u, first * shards + s * span + (u - first)))
    return places, e0, e1


def head_lanes(tile_rows, half):
    lane = lax.broadcasted_iota(jnp.int32, (tile_rows, LANES), 1)
    return (lane < HD) if half == 0 else (lane >= HD)


def window_scores(q, k, rows, width):
    scores = cols_dot(q, k)
    row = lax.broadcasted_iota(jnp.int32, (rows, width * rows), 0)
    col = lax.broadcasted_iota(jnp.int32, (rows, width * rows), 1)
    return jnp.where(col <= row + (width - 1) * rows, scores, NEG)


def fwd_kernel(shards, units, heads, info_ref, qkv_ref, out_ref, perm, mixed):
    block = UNIT
    rows = shards * block
    main = heads * HD
    places, e0, e1 = place_blocks(info_ref, shards, units)
    for src, dst in places:
        at = pl.ds(pl.multiple_of(dst * block, block), block)
        perm[at, :] = qkv_ref[src * block : (src + 1) * block, :]

    def unit(i, carry):
        first = jnp.where(i < e0, 0, jnp.where(i < e1, e0, e1))
        q_at = pl.ds(pl.multiple_of(i * rows, rows), rows)
        for width in range(1, 5):

            @pl.when(i - first + 1 == width)
            def _():
                k_at = pl.ds(pl.multiple_of(first * rows, rows), width * rows)

                def attend(q, k, v):
                    scores = window_scores(q * BF(0.125), k, rows, width)
                    top = jnp.max(scores, axis=1, keepdims=True)
                    probs = jnp.exp(scores - top)
                    total = jnp.sum(probs, axis=1, keepdims=True)
                    return dot(probs.astype(BF), v, ((1,), (0,))) / total

                for tile in range(main // LANES):
                    lanes = slice(tile * LANES, (tile + 1) * LANES)
                    k_lanes = slice(main + lanes.start, main + lanes.stop)
                    v_lanes = slice(2 * main + lanes.start, 2 * main + lanes.stop)
                    q, k, v = perm[q_at, lanes], perm[k_at, k_lanes], perm[k_at, v_lanes]
                    low = head_lanes(rows, 0)
                    zero = jnp.zeros_like(q)
                    left = attend(jnp.where(low, q, zero), k, v)
                    right = attend(jnp.where(low, zero, q), k, v)
                    mixed[q_at, lanes] = jnp.where(low, left, right).astype(BF)
                if main % LANES:
                    lanes = main - HD
                    mixed[q_at, lanes:main] = attend(
                        perm[q_at, lanes:main],
                        perm[k_at, main + lanes : 2 * main],
                        perm[k_at, 2 * main + lanes : 3 * main],
                    ).astype(BF)
                base = 3 * main
                mixed[q_at, main : main + HD] = attend(
                    perm[q_at, base : base + HD],
                    perm[k_at, base + HD : base + 2 * HD],
                    perm[k_at, base + 2 * HD : base + 3 * HD],
                ).astype(BF)

        return carry

    lax.fori_loop(0, units, unit, 0)
    for src, dst in places:
        at = pl.ds(pl.multiple_of(dst * block, block), block)
        out_ref[src * block : (src + 1) * block, :] = mixed[at, :]


def bwd_kernel(
    shards, units, heads, info_ref, qkv_ref, dmix_ref, out_ref, perm, dperm, dq_acc, dk_acc, dv_acc
):
    block = UNIT
    rows = shards * block
    main = heads * HD
    places, e0, e1 = place_blocks(info_ref, shards, units)
    for src, dst in places:
        at = pl.ds(pl.multiple_of(dst * block, block), block)
        perm[at, :] = qkv_ref[src * block : (src + 1) * block, :]
        dperm[at, :] = dmix_ref[src * block : (src + 1) * block, :]
    dk_acc[...] = jnp.zeros_like(dk_acc)
    dv_acc[...] = jnp.zeros_like(dv_acc)

    def unit(i, carry):
        first = jnp.where(i < e0, 0, jnp.where(i < e1, e0, e1))
        q_at = pl.ds(pl.multiple_of(i * rows, rows), rows)
        for width in range(1, 5):

            @pl.when(i - first + 1 == width)
            def _():
                k_at = pl.ds(pl.multiple_of(first * rows, rows), width * rows)

                def pull(q, k, v, g):
                    q = q * BF(0.125)
                    scores = window_scores(q, k, rows, width)
                    top = jnp.max(scores, axis=1, keepdims=True)
                    probs = jnp.exp(scores - top)
                    total = jnp.sum(probs, axis=1, keepdims=True)
                    probs = probs * (1.0 / total)
                    d_probs = cols_dot(g, v)
                    delta = jnp.sum(probs * d_probs, axis=1, keepdims=True)
                    d_scores = (probs * (d_probs - delta)).astype(BF)
                    d_q = dot(d_scores, k, ((1,), (0,))) * 0.125
                    return d_q, rows_dot(d_scores, q), rows_dot(probs.astype(BF), g)

                for tile in range(main // LANES):
                    lanes = slice(tile * LANES, (tile + 1) * LANES)
                    k_lanes = slice(main + lanes.start, main + lanes.stop)
                    v_lanes = slice(2 * main + lanes.start, 2 * main + lanes.stop)
                    q, k, v = perm[q_at, lanes], perm[k_at, k_lanes], perm[k_at, v_lanes]
                    g = dperm[q_at, lanes]
                    low = head_lanes(rows, 0)
                    zero = jnp.zeros_like(q)
                    dq0, dk0, dv0 = pull(jnp.where(low, q, zero), k, v, jnp.where(low, g, zero))
                    dq1, dk1, dv1 = pull(jnp.where(low, zero, q), k, v, jnp.where(low, zero, g))
                    dq_acc[q_at, lanes] = jnp.where(low, dq0, dq1).astype(BF)
                    dk_acc[k_at, lanes] += dk0 + dk1
                    dv_acc[k_at, lanes] += dv0 + dv1
                extra = [(main, 3 * main, 3 * main + HD, 3 * main + 2 * HD)]
                if main % LANES:
                    extra.append((main - HD, main - HD, 2 * main - HD, 3 * main - HD))
                for own, q_lane, k_lane, v_lane in extra:
                    dq0, dk0, dv0 = pull(
                        perm[q_at, q_lane : q_lane + HD],
                        perm[k_at, k_lane : k_lane + HD],
                        perm[k_at, v_lane : v_lane + HD],
                        dperm[q_at, own : own + HD],
                    )
                    dq_acc[q_at, own : own + HD] = dq0.astype(BF)
                    dk_acc[k_at, own : own + HD] += dk0
                    dv_acc[k_at, own : own + HD] += dv0

        return carry

    lax.fori_loop(0, units, unit, 0)
    for src, dst in places:
        at = pl.ds(pl.multiple_of(dst * block, block), block)
        to = slice(src * block, (src + 1) * block)
        for part, acc in enumerate((dq_acc, dk_acc, dv_acc)):
            got = acc[at, :].astype(BF)
            out_ref[to, part * main : (part + 1) * main] = got[:, :main]
            lane = 3 * main + part * HD
            out_ref[to, lane : lane + HD] = got[:, main:]


def vmem_call(kernel, out_shape, scratch, cost, inputs):
    return pl.pallas_call(
        kernel,
        out_shape=out_shape,
        in_specs=[pl.BlockSpec(memory_space=pltpu.SMEM)]
        + [pl.BlockSpec(memory_space=pltpu.VMEM)] * (len(inputs) - 1),
        out_specs=pl.BlockSpec(memory_space=pltpu.VMEM),
        scratch_shapes=scratch,
        compiler_params=pltpu.CompilerParams(vmem_limit_bytes=48 << 20),
        cost_estimate=cost,
    )(*inputs)


def attention_fwd(info, qkv, shards, heads):
    total, width = qkv.shape
    units = total // (shards * UNIT)
    own = (heads + 1) * HD
    return vmem_call(
        functools.partial(fwd_kernel, shards, units, heads),
        jax.ShapeDtypeStruct((total, own), BF),
        [pltpu.VMEM((total, width), BF), pltpu.VMEM((total, own), BF)],
        pl.CostEstimate(flops=1, bytes_accessed=1, transcendentals=0),
        (info, qkv),
    )


def attention_bwd(info, qkv, d_mixed, shards, heads):
    total, width = qkv.shape
    units = total // (shards * UNIT)
    own = (heads + 1) * HD
    return vmem_call(
        functools.partial(bwd_kernel, shards, units, heads),
        jax.ShapeDtypeStruct((total, width), BF),
        [
            pltpu.VMEM((total, width), BF),
            pltpu.VMEM((total, own), BF),
            pltpu.VMEM((total, own), BF),
            pltpu.VMEM((total, own), F32),
            pltpu.VMEM((total, own), F32),
        ],
        pl.CostEstimate(flops=1, bytes_accessed=1, transcendentals=0),
        (info, qkv, d_mixed),
    )


def on_place(me, core, shards, run):
    for m in range(shards):
        for c in range(2):

            @pl.when((me == m) & (core == c))
            def _():
                run(m, c)


def attn_columns(value, j, heads):
    main = heads * HD
    first = D // main * main
    parts = [value[:, p * D + j * main : p * D + (j + 1) * main] for p in range(3)]
    parts += [value[:, p * D + first : (p + 1) * D] for p in range(3)]
    return jnp.concatenate(parts, axis=1)


def fc_columns(value, j, width):
    return value[:, j * width : (j + 1) * width]


def pack_kernel(shards, half, step, columns, at_ref, dep_ref, weight_ref, *outs):
    del dep_ref

    def run(m, c):
        outs[0][...] = columns(weight_ref, m)
        for d in range(1, shards):
            piece = columns(weight_ref.at[c * step : c * step + half], m ^ d)
            outs[d][...] = piece

    on_place(at_ref[0], at_ref[1], shards, run)


def pack_attn_kernel(shards, half, step, heads, count, at_ref, weight_ref, *refs):
    sources, outs = refs[:count], refs[count : count + shards]
    vectors, sems = refs[count + shards : 2 * count + shards], refs[2 * count + shards]
    length = vectors[0].shape[0]
    copies = [
        pltpu.make_async_copy(source, vector, sems.at[i])
        for i, (source, vector) in enumerate(zip(sources, vectors))
    ]
    for copy in copies:
        copy.start()

    def run(m, c):
        outs[0][: shards_rows(outs[0]), :] = attn_columns(weight_ref, m, heads)
        for d in range(1, shards):
            outs[d][:half, :] = attn_columns(weight_ref.at[c * step : c * step + half], m ^ d, heads)

    def shards_rows(ref):
        return ref.shape[0] - VEC_ROWS

    on_place(at_ref[0], at_ref[1], shards, run)
    for copy in copies:
        copy.wait()
    width = outs[0].shape[1]
    block = jnp.concatenate(
        [v[...].astype(F32).reshape(1, length) for v in vectors]
        + [jnp.zeros((VEC_ROWS - count, length), F32)],
        axis=0,
    )
    block = jnp.concatenate(
        [block, jnp.zeros((VEC_ROWS, width - length), F32)], axis=1
    ).astype(BF)
    for out in outs:
        out[out.shape[0] - VEC_ROWS :, :] = block


def place_attn_kernel(shards, half, step, rows, count, at_ref, *refs):
    own, mine, other = refs[0], refs[1:shards], refs[shards]
    out, vec = refs[shards + 1 :]

    def run(m, c):
        out[m * rows : (m + 1) * rows, :] = own[:rows]
        for d in range(1, shards):
            base = (m ^ d) * rows
            a, b = mine[d - 1][:half], other[d - 1]
            low, high = (a, b) if c == 0 else (b, a)
            out[base : base + step, :] = low[:step]
            out[base + step : base + rows, :] = high
        for j in range(shards):
            ref, at = (own, rows) if j == m else (mine[(j ^ m) - 1], half)
            vec[:, j * rows : (j + 1) * rows] = ref[at : at + VEC_ROWS, :rows].astype(F32)[:count]

    on_place(at_ref[0], at_ref[1], shards, run)


def place_kernel(shards, half, step, rows, at_ref, *refs):
    own, mine, other, out = refs[0], refs[1:shards], refs[shards], refs[shards + 1]

    def run(m, c):
        out[m * rows : (m + 1) * rows, :] = own[...]
        for d in range(1, shards):
            base = (m ^ d) * rows
            low, high = (mine[d - 1][...], other[d - 1]) if c == 0 else (other[d - 1], mine[d - 1][...])
            out[base : base + step, :] = low[:step]
            out[base + step : base + rows, :] = high

    on_place(at_ref[0], at_ref[1], shards, run)


def pack_part_kernel(shards, length, stride, columns, at_ref, weight_ref, *outs):
    part = pl.ds(pl.multiple_of(at_ref[2] * stride, 16), length)
    for m in range(shards):

        @pl.when(at_ref[0] == m)
        def _():
            outs[0][...] = columns(weight_ref, m)
            for d in range(1, shards):
                outs[d][...] = columns(weight_ref.at[part], m ^ d)


def place_part_kernel(shards, length, stride, rows, at_ref, own, mine, near, across, out):
    me, q = at_ref[0], at_ref[2]
    out[pl.ds(pl.multiple_of(me * rows, 16), rows), :] = own[...]
    size = (shards - 1) * length
    for d in range(1, shards):
        base = jnp.bitwise_xor(me, d) * rows
        for flip, ref, first in ((0, mine, 0), (2, near, 0), (1, across, 0), (3, across, size)):
            to = base + jnp.bitwise_xor(q, flip) * stride
            row = first + (d - 1) * length
            out[pl.ds(pl.multiple_of(to, 16), length), :] = ref[row : row + length, :]


def unpack_kernel(shards, half, step, places, at_ref, mine, other, *outs):
    def run(m, c):
        for d in range(shards):
            for index, where, row, low, high in places(m, d):
                out, width = outs[index], high - low
                a = mine[row : row + half, low:high]
                b = other[row : row + half, low:high]
                first, second = (a, b) if c == 0 else (b, a)
                out[:step, where : where + width] = first[:step].astype(F32)
                out[step:, where : where + width] = second.astype(F32)

    on_place(at_ref[0], at_ref[1], shards, run)


def spread_kernel(shards, places, at_ref, *refs):
    parts, outs = refs[: shards + 2], refs[shards + 2 :]
    for m in range(shards):

        @pl.when(at_ref[0] == m)
        def _():
            for d in range(shards):
                for index, where, part, low, high in places(m, d):
                    values = parts[part][:, low:high].astype(F32)
                    outs[index][:, where : where + high - low] = values


def local_call(kernel, out_shape, cost_bytes, at, *inputs, anywhere=(), scratch=()):
    vmem = pl.BlockSpec(memory_space=pltpu.VMEM)
    specs = [pl.BlockSpec(memory_space=pl.ANY) if i in anywhere else vmem for i in range(len(inputs))]
    return pl.pallas_call(
        kernel,
        out_shape=out_shape,
        in_specs=[pl.BlockSpec(memory_space=pltpu.SMEM)] + specs,
        out_specs=jax.tree.map(lambda _: vmem, out_shape),
        scratch_shapes=list(scratch),
        compiler_params=pltpu.CompilerParams(vmem_limit_bytes=48 << 20),
        cost_estimate=pl.CostEstimate(flops=1, bytes_accessed=1, transcendentals=0),
    )(at, *inputs)


def body(
    tokens,
    cotangent,
    lengths,
    attn_weight,
    query_bias,
    value_bias,
    proj_weight,
    proj_bias,
    ln1_gain,
    ln1_bias,
    ln2_gain,
    ln2_bias,
    fc_weight,
    fc_bias,
    out_weight,
    out_bias,
):
    n = lax.axis_size("shard")
    planes = lax.axis_size("plane")
    me = lax.axis_index("shard")
    core = lax.axis_index("core")
    heads = (HEADS - 1) // n
    main = heads * HD
    spare = D - n * main
    own_rows = attn_weight.shape[0]
    own_ff = fc_bias.shape[0]
    rows = tokens.shape[1]
    half = -(-own_rows // 32) * 16
    step = own_rows - half
    quarter = lax.axis_index("plane") % 2 * 2 + core
    at = jnp.stack([me, core, quarter]).astype(jnp.int32)

    def swap(value, d):
        return lax.ppermute(value, "shard", [(i, i ^ d) for i in range(n)])

    def swap_plane(value):
        return lax.ppermute(value, "plane", [(i, i ^ 1) for i in range(planes)])

    def swap_core(value):
        return lax.ppermute(value, "core", [(0, 1), (1, 0)])

    def gather_near(value):
        if n != 4:
            return [swap(value, d) for d in range(1, n)]
        return [swap(value, 1), swap(value, 2)]

    def gather_far(value, near):
        if n != 4:
            return [value] + near
        one, two = near
        cut = value.shape[0] // 32 * 16
        three = jnp.concatenate([swap(one[:cut], 2), swap(two[cut:], 1)], axis=0)
        return [value, one, two, three]

    def gather(value):
        return gather_far(value, gather_near(value))

    def pick(stacked, index):
        return lax.dynamic_index_in_dim(stacked, index, 0, keepdims=False)

    def natural(pieces):
        stacked = jnp.stack(pieces)
        return [pick(stacked, me ^ j) for j in range(n)]

    def after(value, *deps):
        return lax.optimization_barrier((value, deps))[0]

    def block(value, d):
        return value[d * rows : (d + 1) * rows]

    def place(own, mine):
        other = swap_core(jnp.stack(mine))
        return local_call(
            functools.partial(place_kernel, n, half, step, own_rows),
            jax.ShapeDtypeStruct((n * own_rows, own.shape[1]), BF),
            n * own.size * 4,
            at,
            own,
            *mine,
            other,
        )

    def pack(weight, columns, width, dep):
        shapes = [jax.ShapeDtypeStruct((own_rows, width), BF)]
        shapes += [jax.ShapeDtypeStruct((half, width), BF)] * (n - 1)
        return local_call(
            functools.partial(pack_kernel, n, half, step, columns),
            shapes,
            weight.size * 2,
            at,
            dep,
            weight,
            anywhere=(0,),
        )

    def reduce_rows(parts, *deps):
        got = after([swap(parts[d].astype(BF), d) for d in range(1, n)], *deps)
        total = parts[0].astype(F32)
        for part in got:
            total = total + part.astype(F32)
        return total

    def core_halves(parts):
        keep = lax.dynamic_slice_in_dim(parts, core * step, half, 1)
        give = lax.dynamic_slice_in_dim(parts, (1 - core) * step, half, 1)
        return (keep.astype(F32) + swap_core(give).astype(F32)).astype(BF)

    vectors = (
        query_bias, value_bias, proj_bias, ln1_gain, ln1_bias, ln2_gain, ln2_bias, out_bias
    )
    tokens_near = gather_near(tokens[0])
    attn_width = 3 * (main + spare)
    attn_sent = local_call(
        functools.partial(pack_attn_kernel, n, half, step, heads, len(vectors)),
        [jax.ShapeDtypeStruct((own_rows + VEC_ROWS, attn_width), BF)]
        + [jax.ShapeDtypeStruct((half + VEC_ROWS, attn_width), BF)] * (n - 1),
        attn_weight.size * 2,
        at,
        attn_weight,
        *vectors,
        anywhere=range(1, len(vectors) + 1),
        scratch=[pltpu.VMEM((own_rows,), BF)] * len(vectors)
        + [pltpu.SemaphoreType.DMA((len(vectors),))],
    )
    attn_got = [swap(attn_sent[d], d) for d in range(1, n)]
    attn_got, tokens_near = after((attn_got, tokens_near))
    attn_other = swap_core(jnp.stack([piece[:half] for piece in attn_got]))
    tokens_parts = gather_far(tokens[0], tokens_near)
    w_attn, small = local_call(
        functools.partial(place_attn_kernel, n, half, step, own_rows, len(vectors)),
        [
            jax.ShapeDtypeStruct((D, attn_width), BF),
            jax.ShapeDtypeStruct((len(vectors), D), F32),
        ],
        D * attn_width * 4,
        at,
        attn_sent[0],
        *attn_got,
        attn_other,
    )
    b_query, b_value, b_proj, gain_one, bias_one, gain_two, bias_two, b_out = [
        small[i] for i in range(8)
    ]

    def my_columns(vector):
        return lax.dynamic_slice_in_dim(vector, me * main, main, 0), vector[n * main :]

    q_main, q_spare = my_columns(b_query)
    v_main, v_spare = my_columns(b_value)
    qkv_bias = jnp.concatenate(
        [q_main, jnp.zeros_like(q_main), v_main, q_spare, jnp.zeros_like(q_spare), v_spare]
    )

    group_tokens = jnp.concatenate(tokens_parts, axis=0)
    proj_half = lax.dynamic_slice_in_dim(after(proj_weight, attn_got), core * step, half, 0)
    proj_near = gather_near(proj_half)
    own_cot = cotangent[0]
    cot_all = lax.all_gather(after(own_cot, attn_got, tokens_parts), "shard", axis=0, tiled=True)
    late_fc = after(fc_weight, attn_got)
    stride = own_rows // 64 * 16
    length = own_rows - 3 * stride
    by_parts = own_rows % 16 == 0 and stride > 0 and planes % 2 == 0
    if by_parts:
        fc_sent = local_call(
            functools.partial(
                pack_part_kernel, n, length, stride, lambda ref, j: fc_columns(ref, j, own_ff)
            ),
            [jax.ShapeDtypeStruct((own_rows, own_ff), BF)]
            + [jax.ShapeDtypeStruct((length, own_ff), BF)] * (n - 1),
            fc_weight.size * 2,
            at,
            late_fc,
        )
    else:
        fc_sent = pack(late_fc, lambda ref, j: fc_columns(ref, j, own_ff), own_ff, lengths)
    xhat_one, _ = normalize(group_tokens.astype(F32))
    normed = (xhat_one * gain_one + bias_one).astype(BF)
    qkv = (jnp.dot(normed, w_attn, preferred_element_type=F32) + qkv_bias).astype(BF)
    qkv, proj_near, fc_sent = after((qkv, proj_near, fc_sent))
    proj_parts = gather_far(proj_half, proj_near)
    fc_got = [swap(fc_sent[d], d) for d in range(1, n)]
    info = jnp.concatenate([lengths[0], me.astype(jnp.int32)[None]])
    mixed_heads = attention_fwd(info, qkv, n, heads)
    mixed_heads, proj_parts = after((mixed_heads, proj_parts))
    got = [block(mixed_heads, 0)[:, :main]] + [
        swap(block(mixed_heads, d)[:, :main], d) for d in range(1, n)
    ]
    w_proj = place(proj_weight, proj_parts[1:])
    got, w_proj, fc_got = after((got, w_proj, fc_got))
    if by_parts:
        fc_mine = jnp.concatenate(fc_got)
        fc_near = swap_plane(fc_mine)
    got, cot_all = after((got, cot_all))
    mixed_low = jnp.concatenate(natural(got) + [block(mixed_heads, 0)[:, main:]], axis=1)
    own_tokens = tokens[0].astype(F32)
    middle = own_tokens + jnp.dot(mixed_low, w_proj, preferred_element_type=F32) + b_proj
    xhat_two, inv_two = normalize(middle)
    own_normed_two = (xhat_two * gain_two + bias_two).astype(BF)
    normed_near = gather_near(own_normed_two)
    if by_parts:
        w_fc = local_call(
            functools.partial(place_part_kernel, n, length, stride, own_rows),
            jax.ShapeDtypeStruct((D, own_ff), BF),
            D * own_ff * 4,
            at,
            fc_sent[0],
            fc_mine,
            fc_near,
            swap_core(jnp.concatenate(after([fc_mine, fc_near], normed_near))),
        )
    else:
        w_fc = place(fc_sent[0], fc_got)
    normed_parts = gather_far(own_normed_two, normed_near)
    cot_parts = [own_cot] + [
        lax.dynamic_slice_in_dim(cot_all, (me ^ d) * rows, rows, 0) for d in range(1, n)
    ]
    group_cot = jnp.concatenate(cot_parts, axis=0)
    normed_two = jnp.concatenate(normed_parts, axis=0)

    def feed(part):
        hidden = jnp.dot(part, w_fc, preferred_element_type=F32) + fc_bias.astype(F32)
        inner = jnp.tanh(0.7978845608028654 * (hidden + 0.044715 * hidden * hidden * hidden))
        slope = 0.5 * (1.0 + inner) + 0.5 * hidden * (1.0 - inner * inner) * (
            0.7978845608028654 * (1.0 + 3 * 0.044715 * hidden * hidden)
        )
        return (0.5 * hidden * (1.0 + inner)).astype(BF), slope.astype(BF)

    fed = [feed(part) for part in normed_parts]
    active_parts = [a for a, _ in fed]
    active = jnp.concatenate(active_parts, axis=0)

    d_active = after(cols_dot(group_cot, out_weight).astype(BF))
    grad_out_weight = rows_dot(active, group_cot).astype(BF)
    sum_out_weight = lax.psum(grad_out_weight, ("plane", "core"))
    d_active = after(d_active, grad_out_weight)
    d_hidden_parts = [
        (block(d_active, d).astype(F32) * slope.astype(F32)).astype(BF)
        for d, (_, slope) in enumerate(fed)
    ]
    d_hidden = jnp.concatenate(d_hidden_parts, axis=0)
    grad_fc = rows_dot(normed_two, d_hidden).astype(BF).reshape(n, own_rows, own_ff)
    e = reduce_rows([cols_dot(part, w_fc) for part in d_hidden_parts], grad_fc)
    e_gain = e * gain_two
    d_middle = own_cot.astype(F32) + inv_two * (
        e_gain
        - jnp.mean(e_gain, axis=-1, keepdims=True)
        - xhat_two * jnp.mean(e_gain * xhat_two, axis=-1, keepdims=True)
    )
    d_branch = d_middle.astype(BF)
    d_mixed = cols_dot(d_branch, w_proj).astype(BF)
    for_heads = jnp.stack([d_mixed[:, j * main : (j + 1) * main] for j in range(n)])
    last = d_mixed[:, n * main :]
    dmix_parts = [jnp.concatenate([pick(for_heads, me), last], axis=1)] + [
        swap(jnp.concatenate([pick(for_heads, me ^ d), last], axis=1), d) for d in range(1, n)
    ]

    fc_halves = core_halves(grad_fc)
    grad_fc_bias = jnp.sum(d_hidden.astype(F32), axis=0)

    grad_proj = rows_dot(mixed_low, d_branch).astype(BF).reshape(n, own_rows, D)
    proj_halves = after(core_halves(grad_proj), dmix_parts)
    proj_part = reduce_rows([pick(proj_halves, me ^ d) for d in range(n)]).astype(BF)
    dmix_parts, fc_halves = after((dmix_parts, fc_halves))
    fc_sum = lax.psum(fc_halves.reshape(n * half, own_ff), "plane").reshape(n, half, own_ff)
    d_qkv = attention_bwd(info, qkv, jnp.concatenate(dmix_parts, axis=0), n, heads)
    d_qkv, proj_part = after((d_qkv, proj_part))
    proj_rows = jnp.where(
        core == 0,
        jnp.concatenate([proj_part[:step], jnp.zeros((half, D), BF)]),
        jnp.concatenate([jnp.zeros((step, D), BF), proj_part]),
    )

    grad_main = rows_dot(normed, d_qkv[:, : 3 * main]).astype(BF).reshape(n, own_rows, 3 * main)
    attn_got = [swap(pick(grad_main, me ^ d), d) for d in range(1, n)]
    grad_spare = rows_dot(normed, d_qkv[:, 3 * main :]).astype(BF).reshape(n, own_rows, 3 * spare)
    attn_parts = (pick(grad_main, me), *attn_got, pick(grad_spare, me), proj_rows)
    attn_sum = lax.psum(after(attn_parts, sum_out_weight), ("plane", "core"))

    counted = (lax.broadcasted_iota(jnp.int32, (n * rows, 1), 0) < rows) | (
        lax.broadcasted_iota(jnp.int32, (1, d_qkv.shape[1]), 1) < 3 * main
    )
    d_once = after(jnp.where(counted, d_qkv, BF(0)), attn_parts)
    f = reduce_rows([cols_dot(block(d_once, d), w_attn) for d in range(n)])
    xhat_own, inv_own = normalize(own_tokens)
    f_gain = f * gain_one
    d_tokens = inv_own * (
        f_gain
        - jnp.mean(f_gain, axis=-1, keepdims=True)
        - xhat_own * jnp.mean(f_gain * xhat_own, axis=-1, keepdims=True)
    )
    input_grad = (d_middle + d_tokens).astype(BF)[None]

    late_active = after(active, attn_parts)
    out_parts = [
        jnp.dot(block(late_active, d), out_weight, preferred_element_type=F32) for d in range(n)
    ]
    output = (middle + reduce_rows(out_parts) + b_out).astype(BF)[None]

    fc_sum = after(fc_sum, attn_parts)
    fc_parts = jnp.concatenate(
        [pick(fc_sum, me)] + [swap(pick(fc_sum, me ^ d), d) for d in range(1, n)]
    )
    sum_fc_weight = local_call(
        functools.partial(
            unpack_kernel,
            n,
            half,
            step,
            lambda m, d: [(0, (m ^ d) * own_ff, d * half, 0, own_ff)],
        ),
        [jax.ShapeDtypeStruct((own_rows, n * own_ff), F32)],
        own_rows * n * own_ff * 8,
        at,
        fc_parts,
        swap_core(fc_parts),
    )[0]
    sum_out_weight = after(sum_out_weight, attn_got).astype(F32)

    def attn_places(m, d):
        places = [(0, p * D + (m ^ d) * main, d, p * main, (p + 1) * main) for p in range(3)]
        if d == 0:
            places += [
                (0, p * D + n * main, n, p * spare, (p + 1) * spare) for p in range(3)
            ]
            places.append((1, 0, n + 1, 0, D))
        return places

    d_once_sum = jnp.sum(d_once.astype(F32), axis=0)

    def vector_of(part):
        whole = jnp.zeros((D,), F32)
        whole = lax.dynamic_update_slice_in_dim(
            whole, d_once_sum[part * main : (part + 1) * main], me * main, 0
        )
        lane = 3 * main + part * spare
        return jnp.concatenate([whole[: n * main], d_once_sum[lane : lane + spare]])

    small_grads = jnp.stack(
        [
            vector_of(0),
            vector_of(2),
            jnp.sum(d_branch.astype(F32), axis=0),
            jnp.sum(f * xhat_own, axis=0),
            jnp.sum(f, axis=0),
            jnp.sum(e * xhat_two, axis=0),
            jnp.sum(e, axis=0),
            jnp.sum(own_cot.astype(F32), axis=0),
        ]
    )
    small_grads = small_grads.reshape(8, n, own_rows).transpose(1, 0, 2)
    small_own = pick(small_grads, me)
    for d in range(1, n):
        small_own = small_own + swap(pick(small_grads, me ^ d), d)
    small_own = jnp.concatenate([small_own, grad_fc_bias.reshape(-1, own_rows)], axis=0)
    small_own = small_own + swap_core(small_own)
    hop = 1
    while hop < planes:
        small_own = small_own + lax.ppermute(
            small_own, "plane", [(i, i ^ hop) for i in range(planes)]
        )
        hop *= 2
    attn_sum, small_own, output, input_grad, sum_fc_weight, sum_out_weight = after(
        (attn_sum, small_own, output, input_grad, sum_fc_weight, sum_out_weight)
    )
    sum_attn_weight, sum_proj_weight = local_call(
        functools.partial(spread_kernel, n, attn_places),
        [
            jax.ShapeDtypeStruct((own_rows, 3 * D), F32),
            jax.ShapeDtypeStruct((own_rows, D), F32),
        ],
        own_rows * 4 * D * 8,
        at,
        *attn_sum,
    )
    s = small_own[:8]
    sum_fc_bias = small_own[8:].reshape(-1)
    return (
        output,
        input_grad,
        sum_attn_weight,
        s[0],
        s[1],
        sum_proj_weight,
        s[2],
        s[3],
        s[4],
        s[5],
        s[6],
        sum_fc_weight,
        sum_fc_bias,
        sum_out_weight,
        s[7],
    )


def solution(mesh):
    shards, reps = mesh.devices.shape
    split = jax.sharding.Mesh(
        mesh.devices.reshape(shards, reps // 2, 2), ("shard", "plane", "core")
    )
    rep = ("plane", "core")
    batch = P(rep, "shard", None)
    row, vec = P("shard", None), P("shard")
    return jax.shard_map(
        body,
        mesh=split,
        in_specs=(batch, batch, P(rep, None), row, vec, vec, row)
        + (vec,) * 5
        + (row, vec, row, vec),
        out_specs=(batch, batch, row, vec, vec, row) + (vec,) * 5 + (row, vec, row, vec),
        check_vma=False,
    )
```

```python
import functools
import math

import jax
import jax.numpy as jnp
from jax import lax
from jax.experimental import pallas as pl
from jax.experimental.pallas import tpu as pltpu
from jax.sharding import PartitionSpec as P

D = 1600
HEADS = 25
HD = 64
UNIT = 32
LANES = 128
NEG = -1e30
VEC_ROWS = 16
BF = jnp.bfloat16
F32 = jnp.float32


def dot(left, right, dims):
    return lax.dot_general(left, right, (dims, ((), ())), preferred_element_type=F32)


def rows_dot(left, right):
    return dot(left, right, ((0,), (0,)))


def cols_dot(left, right):
    return dot(left, right, ((1,), (1,)))


def normalize(values):
    center = values - jnp.mean(values, axis=-1, keepdims=True)
    spread = jnp.mean(center * center, axis=-1, keepdims=True)
    inv = lax.rsqrt(spread + 1e-05)
    return center * inv, inv


def place_blocks(info_ref, shards, units):
    b0, b1, b2, me = info_ref[0], info_ref[1], info_ref[2], info_ref[3]
    e0, e1 = b0, b0 + b1
    places = []
    for d in range(shards):
        s = jnp.bitwise_xor(me, d)
        for u in range(units):
            first = jnp.where(u < e0, 0, jnp.where(u < e1, e0, e1))
            span = jnp.where(u < e0, b0, jnp.where(u < e1, b1, b2))
            places.append((d * units + u, first * shards + s * span + (u - first)))
    return places, e0, e1


def head_lanes(tile_rows, half):
    lane = lax.broadcasted_iota(jnp.int32, (tile_rows, LANES), 1)
    return (lane < HD) if half == 0 else (lane >= HD)


def window_scores(q, k, rows, width):
    scores = cols_dot(q, k)
    row = lax.broadcasted_iota(jnp.int32, (rows, width * rows), 0)
    col = lax.broadcasted_iota(jnp.int32, (rows, width * rows), 1)
    return jnp.where(col <= row + (width - 1) * rows, scores, NEG)


def fwd_kernel(shards, units, heads, info_ref, qkv_ref, out_ref, perm, mixed):
    block = UNIT
    rows = shards * block
    main = heads * HD
    places, e0, e1 = place_blocks(info_ref, shards, units)
    for src, dst in places:
        at = pl.ds(pl.multiple_of(dst * block, block), block)
        perm[at, :] = qkv_ref[src * block : (src + 1) * block, :]

    def unit(i, carry):
        first = jnp.where(i < e0, 0, jnp.where(i < e1, e0, e1))
        q_at = pl.ds(pl.multiple_of(i * rows, rows), rows)
        for width in range(1, 5):

            @pl.when(i - first + 1 == width)
            def _():
                k_at = pl.ds(pl.multiple_of(first * rows, rows), width * rows)

                def attend(q, k, v):
                    scores = window_scores(q * BF(0.125), k, rows, width)
                    top = jnp.max(scores, axis=1, keepdims=True)
                    probs = jnp.exp(scores - top)
                    total = jnp.sum(probs, axis=1, keepdims=True)
                    return dot(probs.astype(BF), v, ((1,), (0,))) / total

                for tile in range(main // LANES):
                    lanes = slice(tile * LANES, (tile + 1) * LANES)
                    k_lanes = slice(main + lanes.start, main + lanes.stop)
                    v_lanes = slice(2 * main + lanes.start, 2 * main + lanes.stop)
                    q, k, v = perm[q_at, lanes], perm[k_at, k_lanes], perm[k_at, v_lanes]
                    low = head_lanes(rows, 0)
                    zero = jnp.zeros_like(q)
                    left = attend(jnp.where(low, q, zero), k, v)
                    right = attend(jnp.where(low, zero, q), k, v)
                    mixed[q_at, lanes] = jnp.where(low, left, right).astype(BF)
                if main % LANES:
                    lanes = main - HD
                    mixed[q_at, lanes:main] = attend(
                        perm[q_at, lanes:main],
                        perm[k_at, main + lanes : 2 * main],
                        perm[k_at, 2 * main + lanes : 3 * main],
                    ).astype(BF)
                base = 3 * main
                mixed[q_at, main : main + HD] = attend(
                    perm[q_at, base : base + HD],
                    perm[k_at, base + HD : base + 2 * HD],
                    perm[k_at, base + 2 * HD : base + 3 * HD],
                ).astype(BF)

        return carry

    lax.fori_loop(0, units, unit, 0)
    for src, dst in places:
        at = pl.ds(pl.multiple_of(dst * block, block), block)
        out_ref[src * block : (src + 1) * block, :] = mixed[at, :]


def bwd_kernel(
    shards, units, heads, info_ref, qkv_ref, dmix_ref, out_ref, perm, dperm, dq_acc, dk_acc, dv_acc
):
    block = UNIT
    rows = shards * block
    main = heads * HD
    places, e0, e1 = place_blocks(info_ref, shards, units)
    for src, dst in places:
        at = pl.ds(pl.multiple_of(dst * block, block), block)
        perm[at, :] = qkv_ref[src * block : (src + 1) * block, :]
        dperm[at, :] = dmix_ref[src * block : (src + 1) * block, :]
    dk_acc[...] = jnp.zeros_like(dk_acc)
    dv_acc[...] = jnp.zeros_like(dv_acc)

    def unit(i, carry):
        first = jnp.where(i < e0, 0, jnp.where(i < e1, e0, e1))
        q_at = pl.ds(pl.multiple_of(i * rows, rows), rows)
        for width in range(1, 5):

            @pl.when(i - first + 1 == width)
            def _():
                k_at = pl.ds(pl.multiple_of(first * rows, rows), width * rows)

                def pull(q, k, v, g):
                    q = q * BF(0.125)
                    scores = window_scores(q, k, rows, width)
                    top = jnp.max(scores, axis=1, keepdims=True)
                    probs = jnp.exp(scores - top)
                    total = jnp.sum(probs, axis=1, keepdims=True)
                    probs = probs * (1.0 / total)
                    d_probs = cols_dot(g, v)
                    delta = jnp.sum(probs * d_probs, axis=1, keepdims=True)
                    d_scores = (probs * (d_probs - delta)).astype(BF)
                    d_q = dot(d_scores, k, ((1,), (0,))) * 0.125
                    return d_q, rows_dot(d_scores, q), rows_dot(probs.astype(BF), g)

                for tile in range(main // LANES):
                    lanes = slice(tile * LANES, (tile + 1) * LANES)
                    k_lanes = slice(main + lanes.start, main + lanes.stop)
                    v_lanes = slice(2 * main + lanes.start, 2 * main + lanes.stop)
                    q, k, v = perm[q_at, lanes], perm[k_at, k_lanes], perm[k_at, v_lanes]
                    g = dperm[q_at, lanes]
                    low = head_lanes(rows, 0)
                    zero = jnp.zeros_like(q)
                    dq0, dk0, dv0 = pull(jnp.where(low, q, zero), k, v, jnp.where(low, g, zero))
                    dq1, dk1, dv1 = pull(jnp.where(low, zero, q), k, v, jnp.where(low, zero, g))
                    dq_acc[q_at, lanes] = jnp.where(low, dq0, dq1).astype(BF)
                    dk_acc[k_at, lanes] += dk0 + dk1
                    dv_acc[k_at, lanes] += dv0 + dv1
                extra = [(main, 3 * main, 3 * main + HD, 3 * main + 2 * HD)]
                if main % LANES:
                    extra.append((main - HD, main - HD, 2 * main - HD, 3 * main - HD))
                for own, q_lane, k_lane, v_lane in extra:
                    dq0, dk0, dv0 = pull(
                        perm[q_at, q_lane : q_lane + HD],
                        perm[k_at, k_lane : k_lane + HD],
                        perm[k_at, v_lane : v_lane + HD],
                        dperm[q_at, own : own + HD],
                    )
                    dq_acc[q_at, own : own + HD] = dq0.astype(BF)
                    dk_acc[k_at, own : own + HD] += dk0
                    dv_acc[k_at, own : own + HD] += dv0

        return carry

    lax.fori_loop(0, units, unit, 0)
    for src, dst in places:
        at = pl.ds(pl.multiple_of(dst * block, block), block)
        to = slice(src * block, (src + 1) * block)
        for part, acc in enumerate((dq_acc, dk_acc, dv_acc)):
            got = acc[at, :].astype(BF)
            out_ref[to, part * main : (part + 1) * main] = got[:, :main]
            lane = 3 * main + part * HD
            out_ref[to, lane : lane + HD] = got[:, main:]


def vmem_call(kernel, out_shape, scratch, cost, inputs):
    return pl.pallas_call(
        kernel,
        out_shape=out_shape,
        in_specs=[pl.BlockSpec(memory_space=pltpu.SMEM)]
        + [pl.BlockSpec(memory_space=pltpu.VMEM)] * (len(inputs) - 1),
        out_specs=pl.BlockSpec(memory_space=pltpu.VMEM),
        scratch_shapes=scratch,
        compiler_params=pltpu.CompilerParams(vmem_limit_bytes=48 << 20),
        cost_estimate=cost,
    )(*inputs)


def attention_fwd(info, qkv, shards, heads):
    total, width = qkv.shape
    units = total // (shards * UNIT)
    own = (heads + 1) * HD
    return vmem_call(
        functools.partial(fwd_kernel, shards, units, heads),
        jax.ShapeDtypeStruct((total, own), BF),
        [pltpu.VMEM((total, width), BF), pltpu.VMEM((total, own), BF)],
        pl.CostEstimate(flops=1, bytes_accessed=1, transcendentals=0),
        (info, qkv),
    )


def attention_bwd(info, qkv, d_mixed, shards, heads):
    total, width = qkv.shape
    units = total // (shards * UNIT)
    own = (heads + 1) * HD
    return vmem_call(
        functools.partial(bwd_kernel, shards, units, heads),
        jax.ShapeDtypeStruct((total, width), BF),
        [
            pltpu.VMEM((total, width), BF),
            pltpu.VMEM((total, own), BF),
            pltpu.VMEM((total, own), BF),
            pltpu.VMEM((total, own), F32),
            pltpu.VMEM((total, own), F32),
        ],
        pl.CostEstimate(flops=1, bytes_accessed=1, transcendentals=0),
        (info, qkv, d_mixed),
    )


def on_place(me, core, shards, run):
    for m in range(shards):
        for c in range(2):

            @pl.when((me == m) & (core == c))
            def _():
                run(m, c)


def attn_columns(value, j, heads):
    main = heads * HD
    first = D // main * main
    parts = [value[:, p * D + j * main : p * D + (j + 1) * main] for p in range(3)]
    parts += [value[:, p * D + first : (p + 1) * D] for p in range(3)]
    return jnp.concatenate(parts, axis=1)


def fc_columns(value, j, width):
    return value[:, j * width : (j + 1) * width]


def pack_kernel(shards, half, step, columns, at_ref, dep_ref, weight_ref, *outs):
    del dep_ref

    def run(m, c):
        outs[0][...] = columns(weight_ref, m)
        for d in range(1, shards):
            piece = columns(weight_ref.at[c * step : c * step + half], m ^ d)
            outs[d][...] = piece

    on_place(at_ref[0], at_ref[1], shards, run)


def pack_attn_kernel(shards, half, step, heads, count, at_ref, weight_ref, *refs):
    sources, outs = refs[:count], refs[count : count + shards]
    vectors, sems = refs[count + shards : 2 * count + shards], refs[2 * count + shards]
    length = vectors[0].shape[0]
    copies = [
        pltpu.make_async_copy(source, vector, sems.at[i])
        for i, (source, vector) in enumerate(zip(sources, vectors))
    ]
    for copy in copies:
        copy.start()

    def run(m, c):
        outs[0][: shards_rows(outs[0]), :] = attn_columns(weight_ref, m, heads)
        for d in range(1, shards):
            outs[d][:half, :] = attn_columns(weight_ref.at[c * step : c * step + half], m ^ d, heads)

    def shards_rows(ref):
        return ref.shape[0] - VEC_ROWS

    on_place(at_ref[0], at_ref[1], shards, run)
    for copy in copies:
        copy.wait()
    width = outs[0].shape[1]
    block = jnp.concatenate(
        [v[...].astype(F32).reshape(1, length) for v in vectors]
        + [jnp.zeros((VEC_ROWS - count, length), F32)],
        axis=0,
    )
    block = jnp.concatenate(
        [block, jnp.zeros((VEC_ROWS, width - length), F32)], axis=1
    ).astype(BF)
    for out in outs:
        out[out.shape[0] - VEC_ROWS :, :] = block


def place_attn_kernel(shards, half, step, rows, count, at_ref, *refs):
    own, mine, other = refs[0], refs[1:shards], refs[shards]
    out, vec = refs[shards + 1 :]

    def run(m, c):
        out[m * rows : (m + 1) * rows, :] = own[:rows]
        for d in range(1, shards):
            base = (m ^ d) * rows
            a, b = mine[d - 1][:half], other[d - 1]
            low, high = (a, b) if c == 0 else (b, a)
            out[base : base + step, :] = low[:step]
            out[base + step : base + rows, :] = high
        for j in range(shards):
            ref, at = (own, rows) if j == m else (mine[(j ^ m) - 1], half)
            vec[:, j * rows : (j + 1) * rows] = ref[at : at + VEC_ROWS, :rows].astype(F32)[:count]

    on_place(at_ref[0], at_ref[1], shards, run)


def place_kernel(shards, half, step, rows, at_ref, *refs):
    own, mine, other, out = refs[0], refs[1:shards], refs[shards], refs[shards + 1]

    def run(m, c):
        out[m * rows : (m + 1) * rows, :] = own[...]
        for d in range(1, shards):
            base = (m ^ d) * rows
            low, high = (mine[d - 1][...], other[d - 1]) if c == 0 else (other[d - 1], mine[d - 1][...])
            out[base : base + step, :] = low[:step]
            out[base + step : base + rows, :] = high

    on_place(at_ref[0], at_ref[1], shards, run)


def pack_part_kernel(shards, length, stride, columns, at_ref, weight_ref, *outs):
    part = pl.ds(pl.multiple_of(at_ref[2] * stride, 16), length)
    for m in range(shards):

        @pl.when(at_ref[0] == m)
        def _():
            outs[0][...] = columns(weight_ref, m)
            for d in range(1, shards):
                outs[d][...] = columns(weight_ref.at[part], m ^ d)


def place_part_kernel(shards, length, stride, rows, at_ref, own, mine, near, across, out):
    me, q = at_ref[0], at_ref[2]
    out[pl.ds(pl.multiple_of(me * rows, 16), rows), :] = own[...]
    size = (shards - 1) * length
    for d in range(1, shards):
        base = jnp.bitwise_xor(me, d) * rows
        for flip, ref, first in ((0, mine, 0), (2, near, 0), (1, across, 0), (3, across, size)):
            to = base + jnp.bitwise_xor(q, flip) * stride
            row = first + (d - 1) * length
            out[pl.ds(pl.multiple_of(to, 16), length), :] = ref[row : row + length, :]


def unpack_kernel(shards, half, step, places, count, at_ref, *refs):
    mine, other, outs = refs[:count], refs[count : 2 * count], refs[2 * count :]

    def run(m, c):
        for d in range(shards):
            for index, where, part, row, low, high in places(m, d):
                out, width = outs[index], high - low
                a = mine[part][row : row + half, low:high]
                b = other[part][row : row + half, low:high]
                first, second = (a, b) if c == 0 else (b, a)
                out[:step, where : where + width] = first[:step].astype(F32)
                out[step:, where : where + width] = second.astype(F32)

    on_place(at_ref[0], at_ref[1], shards, run)


def local_call(kernel, out_shape, cost_bytes, at, *inputs, anywhere=(), scratch=()):
    vmem = pl.BlockSpec(memory_space=pltpu.VMEM)
    hbm = pl.BlockSpec(memory_space=pltpu.HBM)
    specs = [hbm if i in anywhere else vmem for i in range(len(inputs))]
    return pl.pallas_call(
        kernel,
        out_shape=out_shape,
        in_specs=[pl.BlockSpec(memory_space=pltpu.SMEM)] + specs,
        out_specs=jax.tree.map(lambda _: vmem, out_shape),
        scratch_shapes=list(scratch),
        compiler_params=pltpu.CompilerParams(vmem_limit_bytes=48 << 20),
        cost_estimate=pl.CostEstimate(flops=1, bytes_accessed=1, transcendentals=0),
    )(at, *inputs)


def body(
    tokens,
    cotangent,
    lengths,
    attn_weight,
    query_bias,
    value_bias,
    proj_weight,
    proj_bias,
    ln1_gain,
    ln1_bias,
    ln2_gain,
    ln2_bias,
    fc_weight,
    fc_bias,
    out_weight,
    out_bias,
):
    n = lax.axis_size("shard")
    planes = lax.axis_size("plane")
    me = lax.axis_index("shard")
    core = lax.axis_index("core")
    heads = (HEADS - 1) // n
    main = heads * HD
    spare = D - n * main
    own_rows = attn_weight.shape[0]
    own_ff = fc_bias.shape[0]
    rows = tokens.shape[1]
    half = -(-own_rows // 32) * 16
    step = own_rows - half
    quarter = lax.axis_index("plane") % 2 * 2 + core
    at = jnp.stack([me, core, quarter]).astype(jnp.int32)

    def swap(value, d):
        return lax.ppermute(value, "shard", [(i, i ^ d) for i in range(n)])

    def swap_plane(value):
        return lax.ppermute(value, "plane", [(i, i ^ 1) for i in range(planes)])

    def swap_core(value):
        return lax.ppermute(value, "core", [(0, 1), (1, 0)])

    def gather_near(value):
        if n != 4:
            return [swap(value, d) for d in range(1, n)]
        return [swap(value, 1), swap(value, 2)]

    def gather_far(value, near):
        if n != 4:
            return [value] + near
        one, two = near
        cut = value.shape[0] // 32 * 16
        three = jnp.concatenate([swap(one[:cut], 2), swap(two[cut:], 1)], axis=0)
        return [value, one, two, three]

    def gather(value):
        return gather_far(value, gather_near(value))

    def pick(stacked, index):
        return lax.dynamic_index_in_dim(stacked, index, 0, keepdims=False)

    def natural(pieces):
        stacked = jnp.stack(pieces)
        return [pick(stacked, me ^ j) for j in range(n)]

    def after(value, *deps):
        return lax.optimization_barrier((value, deps))[0]

    def block(value, d):
        return value[d * rows : (d + 1) * rows]

    def place(own, mine):
        other = swap_core(jnp.stack(mine))
        return local_call(
            functools.partial(place_kernel, n, half, step, own_rows),
            jax.ShapeDtypeStruct((n * own_rows, own.shape[1]), BF),
            n * own.size * 4,
            at,
            own,
            *mine,
            other,
        )

    def pack(weight, columns, width, dep):
        shapes = [jax.ShapeDtypeStruct((own_rows, width), BF)]
        shapes += [jax.ShapeDtypeStruct((half, width), BF)] * (n - 1)
        return local_call(
            functools.partial(pack_kernel, n, half, step, columns),
            shapes,
            weight.size * 2,
            at,
            dep,
            weight,
            anywhere=(0,),
        )

    def reduce_rows(parts, *deps):
        got = after([swap(parts[d].astype(BF), d) for d in range(1, n)], *deps)
        total = parts[0].astype(F32)
        for part in got:
            total = total + part.astype(F32)
        return total

    def core_halves(parts):
        keep = lax.dynamic_slice_in_dim(parts, core * step, half, 1)
        give = lax.dynamic_slice_in_dim(parts, (1 - core) * step, half, 1)
        return (keep.astype(F32) + swap_core(give).astype(F32)).astype(BF)

    vectors = (
        query_bias, value_bias, proj_bias, ln1_gain, ln1_bias, ln2_gain, ln2_bias, out_bias
    )
    tokens_near = gather_near(tokens[0])
    attn_width = 3 * (main + spare)
    attn_sent = local_call(
        functools.partial(pack_attn_kernel, n, half, step, heads, len(vectors)),
        [jax.ShapeDtypeStruct((own_rows + VEC_ROWS, attn_width), BF)]
        + [jax.ShapeDtypeStruct((half + VEC_ROWS, attn_width), BF)] * (n - 1),
        attn_weight.size * 2,
        at,
        attn_weight,
        *vectors,
        anywhere=range(1, len(vectors) + 1),
        scratch=[pltpu.VMEM((own_rows,), BF)] * len(vectors)
        + [pltpu.SemaphoreType.DMA((len(vectors),))],
    )
    attn_got = [swap(attn_sent[d], d) for d in range(1, n)]
    attn_got, tokens_near = after((attn_got, tokens_near))
    attn_other = swap_core(jnp.stack([piece[:half] for piece in attn_got]))
    tokens_parts = gather_far(tokens[0], tokens_near)
    w_attn, small = local_call(
        functools.partial(place_attn_kernel, n, half, step, own_rows, len(vectors)),
        [
            jax.ShapeDtypeStruct((D, attn_width), BF),
            jax.ShapeDtypeStruct((len(vectors), D), F32),
        ],
        D * attn_width * 4,
        at,
        attn_sent[0],
        *attn_got,
        attn_other,
    )
    b_query, b_value, b_proj, gain_one, bias_one, gain_two, bias_two, b_out = [
        small[i] for i in range(8)
    ]

    def my_columns(vector):
        return lax.dynamic_slice_in_dim(vector, me * main, main, 0), vector[n * main :]

    q_main, q_spare = my_columns(b_query)
    v_main, v_spare = my_columns(b_value)
    qkv_bias = jnp.concatenate(
        [q_main, jnp.zeros_like(q_main), v_main, q_spare, jnp.zeros_like(q_spare), v_spare]
    )

    group_tokens = jnp.concatenate(tokens_parts, axis=0)
    proj_half = lax.dynamic_slice_in_dim(after(proj_weight, attn_got), core * step, half, 0)
    proj_near = gather_near(proj_half)
    own_cot = cotangent[0]
    cot_all = lax.all_gather(after(own_cot, attn_got, tokens_parts), "shard", axis=0, tiled=True)
    late_fc = after(fc_weight, attn_got)
    stride = own_rows // 64 * 16
    length = own_rows - 3 * stride
    by_parts = own_rows % 16 == 0 and stride > 0 and planes % 2 == 0
    if by_parts:
        fc_sent = local_call(
            functools.partial(
                pack_part_kernel, n, length, stride, lambda ref, j: fc_columns(ref, j, own_ff)
            ),
            [jax.ShapeDtypeStruct((own_rows, own_ff), BF)]
            + [jax.ShapeDtypeStruct((length, own_ff), BF)] * (n - 1),
            fc_weight.size * 2,
            at,
            late_fc,
        )
    else:
        fc_sent = pack(late_fc, lambda ref, j: fc_columns(ref, j, own_ff), own_ff, lengths)
    xhat_one, _ = normalize(group_tokens.astype(F32))
    normed = (xhat_one * gain_one + bias_one).astype(BF)
    qkv = (jnp.dot(normed, w_attn, preferred_element_type=F32) + qkv_bias).astype(BF)
    qkv, proj_near, fc_sent = after((qkv, proj_near, fc_sent))
    proj_parts = gather_far(proj_half, proj_near)
    fc_got = [swap(fc_sent[d], d) for d in range(1, n)]
    info = jnp.concatenate([lengths[0], me.astype(jnp.int32)[None]])
    mixed_heads = attention_fwd(info, qkv, n, heads)
    mixed_heads, proj_parts, fc_got = after((mixed_heads, proj_parts, fc_got))
    if by_parts:
        fc_mine = jnp.concatenate(fc_got)
        fc_near = swap_plane(fc_mine)
    got = [block(mixed_heads, 0)[:, :main]] + [
        swap(block(mixed_heads, d)[:, :main], d) for d in range(1, n)
    ]
    w_proj = place(proj_weight, proj_parts[1:])
    got, w_proj, cot_all = after((got, w_proj, cot_all))
    mixed_low = jnp.concatenate(natural(got) + [block(mixed_heads, 0)[:, main:]], axis=1)
    own_tokens = tokens[0].astype(F32)
    middle = own_tokens + jnp.dot(mixed_low, w_proj, preferred_element_type=F32) + b_proj
    xhat_two, inv_two = normalize(middle)
    own_normed_two = (xhat_two * gain_two + bias_two).astype(BF)
    normed_near = gather_near(own_normed_two)
    if by_parts:
        w_fc = local_call(
            functools.partial(place_part_kernel, n, length, stride, own_rows),
            jax.ShapeDtypeStruct((D, own_ff), BF),
            D * own_ff * 4,
            at,
            fc_sent[0],
            fc_mine,
            fc_near,
            swap_core(jnp.concatenate(after([fc_mine, fc_near], own_normed_two))),
        )
    else:
        w_fc = place(fc_sent[0], fc_got)
    cot_parts = [own_cot] + [
        lax.dynamic_slice_in_dim(cot_all, (me ^ d) * rows, rows, 0) for d in range(1, n)
    ]
    group_cot = jnp.concatenate(cot_parts, axis=0)
    d_active = cols_dot(group_cot, out_weight).astype(BF)
    normed_near, d_active = after((normed_near, d_active))
    normed_parts = gather_far(own_normed_two, normed_near)
    normed_two = jnp.concatenate(normed_parts, axis=0)

    def feed(part):
        hidden = jnp.dot(part, w_fc, preferred_element_type=F32) + fc_bias.astype(F32)
        inner = jnp.tanh(0.7978845608028654 * (hidden + 0.044715 * hidden * hidden * hidden))
        slope = 0.5 * (1.0 + inner) + 0.5 * hidden * (1.0 - inner * inner) * (
            0.7978845608028654 * (1.0 + 3 * 0.044715 * hidden * hidden)
        )
        return (0.5 * hidden * (1.0 + inner)).astype(BF), slope.astype(BF)

    fed = [feed(part) for part in normed_parts]
    active_parts = [a for a, _ in fed]
    active = jnp.concatenate(active_parts, axis=0)

    plane = lax.axis_index("plane")
    inner = (plane == 1) | (plane == 2)
    chained = planes == 4

    def add(one, two):
        return (one.astype(F32) + two.astype(F32)).astype(BF)

    def send_a(value):
        if chained:
            return lax.ppermute(value, "plane", [(0, 1), (3, 2)])
        return lax.psum(value, "plane")

    def send_b(value):
        return lax.ppermute(value, "plane", [(1, 2), (2, 1)]) if chained else value

    def send_c(value):
        return lax.ppermute(value, "plane", [(1, 0), (2, 3)]) if chained else value

    def merge(value, got):
        return add(value, got) if chained else got

    def last(value, got):
        return jnp.where(inner, value, got) if chained else got

    d_hidden_parts = [
        (block(d_active, d).astype(F32) * slope.astype(F32)).astype(BF)
        for d, (_, slope) in enumerate(fed)
    ]
    d_hidden = jnp.concatenate(d_hidden_parts, axis=0)
    e_parts = [cols_dot(part, w_fc) for part in d_hidden_parts]
    e_got = [swap(e_parts[d].astype(BF), d) for d in range(1, n)]
    late_active, late_cot = after((active, group_cot), d_hidden_parts)
    grad_out = rows_dot(late_active, late_cot).astype(BF)
    out_half = grad_out.shape[0] // 2
    out_give = lax.dynamic_slice_in_dim(grad_out, (1 - core) * out_half, out_half, 0)
    out_keep = lax.dynamic_slice_in_dim(grad_out, core * out_half, out_half, 0)
    x_out = add(out_keep, swap_core(out_give))
    a_out = send_a(x_out)
    late_normed, late_d = after((normed_two, d_hidden), out_give)
    grad_fc = rows_dot(late_normed, late_d).astype(BF).reshape(n, own_rows, own_ff)
    e_got, x_out, grad_fc = after((e_got, x_out, grad_fc))

    e = e_parts[0] + sum(part.astype(F32) for part in e_got)
    e_gain = e * gain_two
    d_middle = own_cot.astype(F32) + inv_two * (
        e_gain
        - jnp.mean(e_gain, axis=-1, keepdims=True)
        - xhat_two * jnp.mean(e_gain * xhat_two, axis=-1, keepdims=True)
    )
    d_branch = d_middle.astype(BF)
    d_mixed = cols_dot(d_branch, w_proj).astype(BF)
    for_heads = jnp.stack([d_mixed[:, j * main : (j + 1) * main] for j in range(n)])
    spare_cols = d_mixed[:, n * main :]
    dmix_parts = [jnp.concatenate([pick(for_heads, me), spare_cols], axis=1)] + [
        swap(jnp.concatenate([pick(for_heads, me ^ d), spare_cols], axis=1), d)
        for d in range(1, n)
    ]
    fc_halves = core_halves(grad_fc)
    grad_proj = rows_dot(mixed_low, d_branch).astype(BF).reshape(n, own_rows, D)
    dmix_parts, fc_halves, grad_proj, a_out = after((dmix_parts, fc_halves, grad_proj, a_out))

    y_out = merge(x_out, a_out)
    b_out_sum = send_b(y_out)
    fc_got = [swap(pick(fc_halves, me ^ d), d) for d in range(1, n)]
    proj_halves = core_halves(grad_proj)
    d_qkv = attention_bwd(info, qkv, jnp.concatenate(dmix_parts, axis=0), n, heads)
    d_qkv, fc_got, proj_halves = after((d_qkv, fc_got, proj_halves))

    fc_parts = [pick(fc_halves, me)] + fc_got
    x_fc = [jnp.concatenate(fc_parts[: n // 2]), jnp.concatenate(fc_parts[n // 2 :])]
    a_fc = send_a(x_fc[0])
    proj_part = lax.psum_scatter(
        proj_halves.reshape(n * half, D), "shard", scatter_dimension=0, tiled=True
    )
    grad_attn = rows_dot(normed, d_qkv).astype(BF).reshape(n, own_rows, d_qkv.shape[1])
    attn_halves = core_halves(grad_attn)
    attn_halves, a_fc, b_out_sum = after((attn_halves, a_fc, b_out_sum))

    t_out = merge(y_out, b_out_sum)
    c_out_sum = send_c(t_out)
    y_fc = [merge(x_fc[0], a_fc)]
    a_fc = send_a(x_fc[1])
    attn_own = pick(attn_halves, me)
    attn_got = [swap(pick(attn_halves, me ^ d)[:, : 3 * main], d) for d in range(1, n)]
    attn_got, a_fc = after((attn_got, a_fc))

    y_fc.append(merge(x_fc[1], a_fc))
    b_fc = [send_b(y) for y in y_fc]
    attn_all = [attn_own[:, : 3 * main]] + attn_got
    cut = n // 2 + 1
    x_attn = [jnp.concatenate(attn_all[:cut], axis=1)]
    a_attn = send_a(x_attn[0])
    proj_part, a_attn, b_fc[0] = after((proj_part, a_attn, b_fc[0]))

    x_attn.append(
        jnp.concatenate(attn_all[cut:] + [proj_part, attn_own[:, 3 * main :]], axis=1)
    )
    y_attn = [merge(x_attn[0], a_attn)]
    t_fc = [merge(y_fc[0], b_fc[0])]
    c_fc = [send_c(t_fc[0])]
    b_attn = [send_b(y_attn[0])]
    a_attn = send_a(x_attn[1])
    a_attn, b_attn[0], b_fc[1] = after((a_attn, b_attn[0], b_fc[1]))

    t_fc.append(merge(y_fc[1], b_fc[1]))
    c_fc.append(send_c(t_fc[1]))
    t_attn = [merge(y_attn[0], b_attn[0])]
    c_attn = [send_c(t_attn[0])]
    y_attn.append(merge(x_attn[1], a_attn))
    b_attn.append(send_b(y_attn[1]))
    c_out_sum, c_fc[0], b_attn[1] = after((c_out_sum, c_fc[0], b_attn[1]))

    t_attn.append(merge(y_attn[1], b_attn[1]))
    c_attn.append(send_c(t_attn[1]))
    out_mine = last(t_out, c_out_sum)
    grad_fc_bias = jnp.sum(d_hidden.astype(F32), axis=0)

    counted = (lax.broadcasted_iota(jnp.int32, (n * rows, 1), 0) < rows) | (
        lax.broadcasted_iota(jnp.int32, (1, d_qkv.shape[1]), 1) < 3 * main
    )
    def row_sums(parts):
        stacked = jnp.stack([part.astype(BF) for part in parts])
        ordered = jnp.concatenate([pick(stacked, me ^ j) for j in range(n)])
        return lax.psum_scatter(ordered, "shard", scatter_dimension=0, tiled=True).astype(F32)

    d_once = after(jnp.where(counted, d_qkv, BF(0)), attn_halves)
    f = row_sums([cols_dot(block(d_once, d), w_attn) for d in range(n)])
    xhat_own, inv_own = normalize(own_tokens)
    f_gain = f * gain_one
    d_tokens = inv_own * (
        f_gain
        - jnp.mean(f_gain, axis=-1, keepdims=True)
        - xhat_own * jnp.mean(f_gain * xhat_own, axis=-1, keepdims=True)
    )
    input_grad = (d_middle + d_tokens).astype(BF)[None]

    late_active = after(active, attn_got)
    output = row_sums(
        [jnp.dot(block(late_active, d), out_weight, preferred_element_type=F32) for d in range(n)]
    )
    output = (middle + output + b_out).astype(BF)[None]

    out_other = swap_core(out_mine)
    sum_out_weight = jnp.concatenate(
        [jnp.where(core == 0, out_mine, out_other), jnp.where(core == 0, out_other, out_mine)]
    ).astype(F32)
    fc_mine = [last(t, c) for t, c in zip(t_fc, c_fc)]
    first_fc = n // 2
    sum_fc_weight = local_call(
        functools.partial(
            unpack_kernel,
            n,
            half,
            step,
            lambda m, d: [
                (0, (m ^ d) * own_ff, d // first_fc, d % first_fc * half, 0, own_ff)
            ],
            2,
        ),
        [jax.ShapeDtypeStruct((own_rows, n * own_ff), F32)],
        own_rows * n * own_ff * 8,
        at,
        *fc_mine,
        *[swap_core(value) for value in fc_mine],
    )[0]

    def attn_places(m, d):
        part, base = (0, d * 3 * main) if d < cut else (1, (d - cut) * 3 * main)
        places = [
            (0, p * D + (m ^ d) * main, part, 0, base + p * main, base + (p + 1) * main)
            for p in range(3)
        ]
        if d == 0:
            base = (n - cut) * 3 * main
            places.append((1, 0, 1, 0, base, base + D))
            base += D
            places += [
                (0, p * D + n * main, 1, 0, base + p * spare, base + (p + 1) * spare)
                for p in range(3)
            ]
        return places

    d_once_sum = jnp.sum(d_once.astype(F32), axis=0)

    def vector_of(part):
        whole = jnp.zeros((D,), F32)
        whole = lax.dynamic_update_slice_in_dim(
            whole, d_once_sum[part * main : (part + 1) * main], me * main, 0
        )
        lane = 3 * main + part * spare
        return jnp.concatenate([whole[: n * main], d_once_sum[lane : lane + spare]])

    small_grads = jnp.stack(
        [
            vector_of(0),
            vector_of(2),
            jnp.sum(d_branch.astype(F32), axis=0),
            jnp.sum(f * xhat_own, axis=0),
            jnp.sum(f, axis=0),
            jnp.sum(e * xhat_two, axis=0),
            jnp.sum(e, axis=0),
            jnp.sum(own_cot.astype(F32), axis=0),
        ]
    )
    small_grads = small_grads.reshape(8, n, own_rows).transpose(1, 0, 2)
    small_own = pick(small_grads, me)
    for d in range(1, n):
        small_own = small_own + swap(pick(small_grads, me ^ d), d)
    small_own = jnp.concatenate([small_own, grad_fc_bias.reshape(-1, own_rows)], axis=0)
    small_own = small_own + swap_core(small_own)
    hop = 1
    while hop < planes:
        small_own = small_own + lax.ppermute(
            small_own, "plane", [(i, i ^ hop) for i in range(planes)]
        )
        hop *= 2
    attn_mine = [last(t, c) for t, c in zip(t_attn, c_attn)]
    attn_other = [swap_core(attn_mine[0])]
    attn_mine, attn_other, small_own, output, input_grad, sum_fc_weight, sum_out_weight = after(
        (attn_mine, attn_other, small_own, output, input_grad, sum_fc_weight, sum_out_weight)
    )
    attn_other.append(swap_core(attn_mine[1]))
    sum_attn_weight, sum_proj_weight = local_call(
        functools.partial(unpack_kernel, n, half, step, attn_places, 2),
        [
            jax.ShapeDtypeStruct((own_rows, 3 * D), F32),
            jax.ShapeDtypeStruct((own_rows, D), F32),
        ],
        own_rows * 4 * D * 8,
        at,
        *attn_mine,
        *attn_other,
    )
    s = small_own[:8]
    sum_fc_bias = small_own[8:].reshape(-1)
    return (
        output,
        input_grad,
        sum_attn_weight,
        s[0],
        s[1],
        sum_proj_weight,
        s[2],
        s[3],
        s[4],
        s[5],
        s[6],
        sum_fc_weight,
        sum_fc_bias,
        sum_out_weight,
        s[7],
    )


def solution(mesh):
    shards, reps = mesh.devices.shape
    split = jax.sharding.Mesh(
        mesh.devices.reshape(shards, reps // 2, 2), ("shard", "plane", "core")
    )
    rep = ("plane", "core")
    batch = P(rep, "shard", None)
    row, vec = P("shard", None), P("shard")
    return jax.shard_map(
        body,
        mesh=split,
        in_specs=(batch, batch, P(rep, None), row, vec, vec, row)
        + (vec,) * 5
        + (row, vec, row, vec),
        out_specs=(batch, batch, row, vec, vec, row) + (vec,) * 5 + (row, vec, row, vec),
        check_vma=False,
    )
```

```python
import functools
import math

import jax
import jax.numpy as jnp
from jax import lax
from jax.experimental import pallas as pl
from jax.experimental.pallas import tpu as pltpu
from jax.sharding import PartitionSpec as P

D = 1600
HEADS = 25
HD = 64
UNIT = 32
LANES = 128
NEG = -1e30
VEC_ROWS = 16
BF = jnp.bfloat16
F32 = jnp.float32


def dot(left, right, dims):
    return lax.dot_general(left, right, (dims, ((), ())), preferred_element_type=F32)


def rows_dot(left, right):
    return dot(left, right, ((0,), (0,)))


def cols_dot(left, right):
    return dot(left, right, ((1,), (1,)))


def normalize(values):
    center = values - jnp.mean(values, axis=-1, keepdims=True)
    spread = jnp.mean(center * center, axis=-1, keepdims=True)
    inv = lax.rsqrt(spread + 1e-05)
    return center * inv, inv


def place_blocks(info_ref, shards, units):
    b0, b1, b2, me = info_ref[0], info_ref[1], info_ref[2], info_ref[3]
    e0, e1 = b0, b0 + b1
    places = []
    for d in range(shards):
        s = jnp.bitwise_xor(me, d)
        for u in range(units):
            first = jnp.where(u < e0, 0, jnp.where(u < e1, e0, e1))
            span = jnp.where(u < e0, b0, jnp.where(u < e1, b1, b2))
            places.append((d * units + u, first * shards + s * span + (u - first)))
    return places, e0, e1


def head_lanes(tile_rows, half):
    lane = lax.broadcasted_iota(jnp.int32, (tile_rows, LANES), 1)
    return (lane < HD) if half == 0 else (lane >= HD)


def window_scores(q, k, rows, width):
    scores = cols_dot(q, k)
    row = lax.broadcasted_iota(jnp.int32, (rows, width * rows), 0)
    col = lax.broadcasted_iota(jnp.int32, (rows, width * rows), 1)
    return jnp.where(col <= row + (width - 1) * rows, scores, NEG)


def fwd_kernel(shards, units, heads, info_ref, qkv_ref, out_ref, perm, mixed):
    block = UNIT
    rows = shards * block
    main = heads * HD
    places, e0, e1 = place_blocks(info_ref, shards, units)
    for src, dst in places:
        at = pl.ds(pl.multiple_of(dst * block, block), block)
        perm[at, :] = qkv_ref[src * block : (src + 1) * block, :]

    def unit(i, carry):
        first = jnp.where(i < e0, 0, jnp.where(i < e1, e0, e1))
        q_at = pl.ds(pl.multiple_of(i * rows, rows), rows)
        for width in range(1, 5):

            @pl.when(i - first + 1 == width)
            def _():
                k_at = pl.ds(pl.multiple_of(first * rows, rows), width * rows)

                def attend(q, k, v):
                    scores = window_scores(q * BF(0.125), k, rows, width)
                    top = jnp.max(scores, axis=1, keepdims=True)
                    probs = jnp.exp(scores - top)
                    total = jnp.sum(probs, axis=1, keepdims=True)
                    return dot(probs.astype(BF), v, ((1,), (0,))) / total

                for tile in range(main // LANES):
                    lanes = slice(tile * LANES, (tile + 1) * LANES)
                    k_lanes = slice(main + lanes.start, main + lanes.stop)
                    v_lanes = slice(2 * main + lanes.start, 2 * main + lanes.stop)
                    q, k, v = perm[q_at, lanes], perm[k_at, k_lanes], perm[k_at, v_lanes]
                    low = head_lanes(rows, 0)
                    zero = jnp.zeros_like(q)
                    left = attend(jnp.where(low, q, zero), k, v)
                    right = attend(jnp.where(low, zero, q), k, v)
                    mixed[q_at, lanes] = jnp.where(low, left, right).astype(BF)
                if main % LANES:
                    lanes = main - HD
                    mixed[q_at, lanes:main] = attend(
                        perm[q_at, lanes:main],
                        perm[k_at, main + lanes : 2 * main],
                        perm[k_at, 2 * main + lanes : 3 * main],
                    ).astype(BF)
                base = 3 * main
                mixed[q_at, main : main + HD] = attend(
                    perm[q_at, base : base + HD],
                    perm[k_at, base + HD : base + 2 * HD],
                    perm[k_at, base + 2 * HD : base + 3 * HD],
                ).astype(BF)

        return carry

    lax.fori_loop(0, units, unit, 0)
    for src, dst in places:
        at = pl.ds(pl.multiple_of(dst * block, block), block)
        out_ref[src * block : (src + 1) * block, :] = mixed[at, :]


def bwd_kernel(
    shards, units, heads, info_ref, qkv_ref, dmix_ref, out_ref, perm, dperm, dq_acc, dk_acc, dv_acc
):
    block = UNIT
    rows = shards * block
    main = heads * HD
    places, e0, e1 = place_blocks(info_ref, shards, units)
    for src, dst in places:
        at = pl.ds(pl.multiple_of(dst * block, block), block)
        perm[at, :] = qkv_ref[src * block : (src + 1) * block, :]
        dperm[at, :] = dmix_ref[src * block : (src + 1) * block, :]
    dk_acc[...] = jnp.zeros_like(dk_acc)
    dv_acc[...] = jnp.zeros_like(dv_acc)

    def unit(i, carry):
        first = jnp.where(i < e0, 0, jnp.where(i < e1, e0, e1))
        q_at = pl.ds(pl.multiple_of(i * rows, rows), rows)
        for width in range(1, 5):

            @pl.when(i - first + 1 == width)
            def _():
                k_at = pl.ds(pl.multiple_of(first * rows, rows), width * rows)

                def pull(q, k, v, g):
                    q = q * BF(0.125)
                    scores = window_scores(q, k, rows, width)
                    top = jnp.max(scores, axis=1, keepdims=True)
                    probs = jnp.exp(scores - top)
                    total = jnp.sum(probs, axis=1, keepdims=True)
                    probs = probs * (1.0 / total)
                    d_probs = cols_dot(g, v)
                    delta = jnp.sum(probs * d_probs, axis=1, keepdims=True)
                    d_scores = (probs * (d_probs - delta)).astype(BF)
                    d_q = dot(d_scores, k, ((1,), (0,))) * 0.125
                    return d_q, rows_dot(d_scores, q), rows_dot(probs.astype(BF), g)

                for tile in range(main // LANES):
                    lanes = slice(tile * LANES, (tile + 1) * LANES)
                    k_lanes = slice(main + lanes.start, main + lanes.stop)
                    v_lanes = slice(2 * main + lanes.start, 2 * main + lanes.stop)
                    q, k, v = perm[q_at, lanes], perm[k_at, k_lanes], perm[k_at, v_lanes]
                    g = dperm[q_at, lanes]
                    low = head_lanes(rows, 0)
                    zero = jnp.zeros_like(q)
                    dq0, dk0, dv0 = pull(jnp.where(low, q, zero), k, v, jnp.where(low, g, zero))
                    dq1, dk1, dv1 = pull(jnp.where(low, zero, q), k, v, jnp.where(low, zero, g))
                    dq_acc[q_at, lanes] = jnp.where(low, dq0, dq1).astype(BF)
                    dk_acc[k_at, lanes] += dk0 + dk1
                    dv_acc[k_at, lanes] += dv0 + dv1
                extra = [(main, 3 * main, 3 * main + HD, 3 * main + 2 * HD)]
                if main % LANES:
                    extra.append((main - HD, main - HD, 2 * main - HD, 3 * main - HD))
                for own, q_lane, k_lane, v_lane in extra:
                    dq0, dk0, dv0 = pull(
                        perm[q_at, q_lane : q_lane + HD],
                        perm[k_at, k_lane : k_lane + HD],
                        perm[k_at, v_lane : v_lane + HD],
                        dperm[q_at, own : own + HD],
                    )
                    dq_acc[q_at, own : own + HD] = dq0.astype(BF)
                    dk_acc[k_at, own : own + HD] += dk0
                    dv_acc[k_at, own : own + HD] += dv0

        return carry

    lax.fori_loop(0, units, unit, 0)
    for src, dst in places:
        at = pl.ds(pl.multiple_of(dst * block, block), block)
        to = slice(src * block, (src + 1) * block)
        for part, acc in enumerate((dq_acc, dk_acc, dv_acc)):
            got = acc[at, :].astype(BF)
            out_ref[to, part * main : (part + 1) * main] = got[:, :main]
            lane = 3 * main + part * HD
            out_ref[to, lane : lane + HD] = got[:, main:]


def vmem_call(kernel, out_shape, scratch, cost, inputs):
    return pl.pallas_call(
        kernel,
        out_shape=out_shape,
        in_specs=[pl.BlockSpec(memory_space=pltpu.SMEM)]
        + [pl.BlockSpec(memory_space=pltpu.VMEM)] * (len(inputs) - 1),
        out_specs=pl.BlockSpec(memory_space=pltpu.VMEM),
        scratch_shapes=scratch,
        compiler_params=pltpu.CompilerParams(vmem_limit_bytes=48 << 20),
        cost_estimate=cost,
    )(*inputs)


def attention_fwd(info, qkv, shards, heads):
    total, width = qkv.shape
    units = total // (shards * UNIT)
    own = (heads + 1) * HD
    return vmem_call(
        functools.partial(fwd_kernel, shards, units, heads),
        jax.ShapeDtypeStruct((total, own), BF),
        [pltpu.VMEM((total, width), BF), pltpu.VMEM((total, own), BF)],
        pl.CostEstimate(flops=1, bytes_accessed=1, transcendentals=0),
        (info, qkv),
    )


def attention_bwd(info, qkv, d_mixed, shards, heads):
    total, width = qkv.shape
    units = total // (shards * UNIT)
    own = (heads + 1) * HD
    return vmem_call(
        functools.partial(bwd_kernel, shards, units, heads),
        jax.ShapeDtypeStruct((total, width), BF),
        [
            pltpu.VMEM((total, width), BF),
            pltpu.VMEM((total, own), BF),
            pltpu.VMEM((total, own), BF),
            pltpu.VMEM((total, own), F32),
            pltpu.VMEM((total, own), F32),
        ],
        pl.CostEstimate(flops=1, bytes_accessed=1, transcendentals=0),
        (info, qkv, d_mixed),
    )


def on_place(me, core, shards, run):
    for m in range(shards):
        for c in range(2):

            @pl.when((me == m) & (core == c))
            def _():
                run(m, c)


def attn_columns(value, j, heads):
    main = heads * HD
    first = D // main * main
    parts = [value[:, p * D + j * main : p * D + (j + 1) * main] for p in range(3)]
    parts += [value[:, p * D + first : (p + 1) * D] for p in range(3)]
    return jnp.concatenate(parts, axis=1)


def fc_columns(value, j, width):
    return value[:, j * width : (j + 1) * width]


def pack_kernel(shards, half, step, columns, at_ref, dep_ref, weight_ref, *outs):
    del dep_ref

    def run(m, c):
        outs[0][...] = columns(weight_ref, m)
        for d in range(1, shards):
            piece = columns(weight_ref.at[c * step : c * step + half], m ^ d)
            outs[d][...] = piece

    on_place(at_ref[0], at_ref[1], shards, run)


def pack_attn_kernel(shards, half, step, heads, count, at_ref, weight_ref, *refs):
    sources, outs = refs[:count], refs[count : count + shards]
    vectors, sems = refs[count + shards : 2 * count + shards], refs[2 * count + shards]
    length = vectors[0].shape[0]
    copies = [
        pltpu.make_async_copy(source, vector, sems.at[i])
        for i, (source, vector) in enumerate(zip(sources, vectors))
    ]
    for copy in copies:
        copy.start()

    def run(m, c):
        outs[0][: shards_rows(outs[0]), :] = attn_columns(weight_ref, m, heads)
        for d in range(1, shards):
            outs[d][:half, :] = attn_columns(weight_ref.at[c * step : c * step + half], m ^ d, heads)

    def shards_rows(ref):
        return ref.shape[0] - VEC_ROWS

    on_place(at_ref[0], at_ref[1], shards, run)
    for copy in copies:
        copy.wait()
    width = outs[0].shape[1]
    block = jnp.concatenate(
        [v[...].astype(F32).reshape(1, length) for v in vectors]
        + [jnp.zeros((VEC_ROWS - count, length), F32)],
        axis=0,
    )
    block = jnp.concatenate(
        [block, jnp.zeros((VEC_ROWS, width - length), F32)], axis=1
    ).astype(BF)
    for out in outs:
        out[out.shape[0] - VEC_ROWS :, :] = block


def place_attn_kernel(shards, half, step, rows, count, at_ref, *refs):
    own, mine, other = refs[0], refs[1:shards], refs[shards]
    out, vec = refs[shards + 1 :]

    def run(m, c):
        out[m * rows : (m + 1) * rows, :] = own[:rows]
        for d in range(1, shards):
            base = (m ^ d) * rows
            a, b = mine[d - 1][:half], other[d - 1]
            low, high = (a, b) if c == 0 else (b, a)
            out[base : base + step, :] = low[:step]
            out[base + step : base + rows, :] = high
        for j in range(shards):
            ref, at = (own, rows) if j == m else (mine[(j ^ m) - 1], half)
            vec[:, j * rows : (j + 1) * rows] = ref[at : at + VEC_ROWS, :rows].astype(F32)[:count]

    on_place(at_ref[0], at_ref[1], shards, run)


def place_kernel(shards, half, step, rows, at_ref, *refs):
    own, mine, other, out = refs[0], refs[1:shards], refs[shards], refs[shards + 1]

    def run(m, c):
        out[m * rows : (m + 1) * rows, :] = own[...]
        for d in range(1, shards):
            base = (m ^ d) * rows
            low, high = (mine[d - 1][...], other[d - 1]) if c == 0 else (other[d - 1], mine[d - 1][...])
            out[base : base + step, :] = low[:step]
            out[base + step : base + rows, :] = high

    on_place(at_ref[0], at_ref[1], shards, run)


def pack_part_kernel(shards, length, stride, columns, at_ref, weight_ref, *outs):
    part = pl.ds(pl.multiple_of(at_ref[2] * stride, 16), length)
    for m in range(shards):

        @pl.when(at_ref[0] == m)
        def _():
            outs[0][...] = columns(weight_ref, m)
            for d in range(1, shards):
                outs[d][...] = columns(weight_ref.at[part], m ^ d)


def place_part_kernel(shards, length, stride, rows, at_ref, own, mine, near, across, out):
    me, q = at_ref[0], at_ref[2]
    out[pl.ds(pl.multiple_of(me * rows, 16), rows), :] = own[...]
    size = (shards - 1) * length
    for d in range(1, shards):
        base = jnp.bitwise_xor(me, d) * rows
        for flip, ref, first in ((0, mine, 0), (2, near, 0), (1, across, 0), (3, across, size)):
            to = base + jnp.bitwise_xor(q, flip) * stride
            row = first + (d - 1) * length
            out[pl.ds(pl.multiple_of(to, 16), length), :] = ref[row : row + length, :]


def unpack_kernel(shards, half, step, places, count, at_ref, *refs):
    mine, other, outs = refs[:count], refs[count : 2 * count], refs[2 * count :]

    def run(m, c):
        for d in range(shards):
            for index, where, part, row, low, high in places(m, d):
                out, width = outs[index], high - low
                a = mine[part][row : row + half, low:high]
                b = other[part][row : row + half, low:high]
                first, second = (a, b) if c == 0 else (b, a)
                out[:step, where : where + width] = first[:step].astype(F32)
                out[step:, where : where + width] = second.astype(F32)

    on_place(at_ref[0], at_ref[1], shards, run)


def spread_kernel(shards, places, at_ref, *refs):
    parts, outs = refs[: shards + 2], refs[shards + 2 :]
    for m in range(shards):

        @pl.when(at_ref[0] == m)
        def _():
            for d in range(shards):
                for index, where, part, low, high in places(m, d):
                    values = parts[part][:, low:high].astype(F32)
                    outs[index][:, where : where + high - low] = values


def local_call(kernel, out_shape, cost_bytes, at, *inputs, anywhere=(), scratch=()):
    vmem = pl.BlockSpec(memory_space=pltpu.VMEM)
    hbm = pl.BlockSpec(memory_space=pltpu.HBM)
    specs = [hbm if i in anywhere else vmem for i in range(len(inputs))]
    return pl.pallas_call(
        kernel,
        out_shape=out_shape,
        in_specs=[pl.BlockSpec(memory_space=pltpu.SMEM)] + specs,
        out_specs=jax.tree.map(lambda _: vmem, out_shape),
        scratch_shapes=list(scratch),
        compiler_params=pltpu.CompilerParams(vmem_limit_bytes=48 << 20),
        cost_estimate=pl.CostEstimate(flops=1, bytes_accessed=1, transcendentals=0),
    )(at, *inputs)


def body(
    tokens,
    cotangent,
    lengths,
    attn_weight,
    query_bias,
    value_bias,
    proj_weight,
    proj_bias,
    ln1_gain,
    ln1_bias,
    ln2_gain,
    ln2_bias,
    fc_weight,
    fc_bias,
    out_weight,
    out_bias,
):
    n = lax.axis_size("shard")
    planes = lax.axis_size("plane")
    me = lax.axis_index("shard")
    core = lax.axis_index("core")
    heads = (HEADS - 1) // n
    main = heads * HD
    spare = D - n * main
    own_rows = attn_weight.shape[0]
    own_ff = fc_bias.shape[0]
    rows = tokens.shape[1]
    half = -(-own_rows // 32) * 16
    step = own_rows - half
    quarter = lax.axis_index("plane") % 2 * 2 + core
    at = jnp.stack([me, core, quarter]).astype(jnp.int32)

    def swap(value, d):
        return lax.ppermute(value, "shard", [(i, i ^ d) for i in range(n)])

    def swap_plane(value):
        return lax.ppermute(value, "plane", [(i, i ^ 1) for i in range(planes)])

    def swap_core(value):
        return lax.ppermute(value, "core", [(0, 1), (1, 0)])

    def gather_near(value):
        if n != 4:
            return [swap(value, d) for d in range(1, n)]
        return [swap(value, 1), swap(value, 2)]

    def gather_far(value, near):
        if n != 4:
            return [value] + near
        one, two = near
        cut = value.shape[0] // 32 * 16
        three = jnp.concatenate([swap(one[:cut], 2), swap(two[cut:], 1)], axis=0)
        return [value, one, two, three]

    def gather(value):
        return gather_far(value, gather_near(value))

    def pick(stacked, index):
        return lax.dynamic_index_in_dim(stacked, index, 0, keepdims=False)

    def natural(pieces):
        stacked = jnp.stack(pieces)
        return [pick(stacked, me ^ j) for j in range(n)]

    def after(value, *deps):
        return lax.optimization_barrier((value, deps))[0]

    def block(value, d):
        return value[d * rows : (d + 1) * rows]

    def place(own, mine):
        other = swap_core(jnp.stack(mine))
        return local_call(
            functools.partial(place_kernel, n, half, step, own_rows),
            jax.ShapeDtypeStruct((n * own_rows, own.shape[1]), BF),
            n * own.size * 4,
            at,
            own,
            *mine,
            other,
        )

    def pack(weight, columns, width, dep):
        shapes = [jax.ShapeDtypeStruct((own_rows, width), BF)]
        shapes += [jax.ShapeDtypeStruct((half, width), BF)] * (n - 1)
        return local_call(
            functools.partial(pack_kernel, n, half, step, columns),
            shapes,
            weight.size * 2,
            at,
            dep,
            weight,
            anywhere=(0,),
        )

    def reduce_rows(parts, *deps):
        got = after([swap(parts[d].astype(BF), d) for d in range(1, n)], *deps)
        total = parts[0].astype(F32)
        for part in got:
            total = total + part.astype(F32)
        return total

    def core_halves(parts):
        keep = lax.dynamic_slice_in_dim(parts, core * step, half, 1)
        give = lax.dynamic_slice_in_dim(parts, (1 - core) * step, half, 1)
        return (keep.astype(F32) + swap_core(give).astype(F32)).astype(BF)

    vectors = (
        query_bias, value_bias, proj_bias, ln1_gain, ln1_bias, ln2_gain, ln2_bias, out_bias
    )
    tokens_near = gather_near(tokens[0])
    attn_width = 3 * (main + spare)
    attn_sent = local_call(
        functools.partial(pack_attn_kernel, n, half, step, heads, len(vectors)),
        [jax.ShapeDtypeStruct((own_rows + VEC_ROWS, attn_width), BF)]
        + [jax.ShapeDtypeStruct((half + VEC_ROWS, attn_width), BF)] * (n - 1),
        attn_weight.size * 2,
        at,
        attn_weight,
        *vectors,
        anywhere=range(1, len(vectors) + 1),
        scratch=[pltpu.VMEM((own_rows,), BF)] * len(vectors)
        + [pltpu.SemaphoreType.DMA((len(vectors),))],
    )
    attn_got = [swap(attn_sent[d], d) for d in range(1, n)]
    attn_got, tokens_near = after((attn_got, tokens_near))
    attn_other = swap_core(jnp.stack([piece[:half] for piece in attn_got]))
    tokens_parts = gather_far(tokens[0], tokens_near)
    w_attn, small = local_call(
        functools.partial(place_attn_kernel, n, half, step, own_rows, len(vectors)),
        [
            jax.ShapeDtypeStruct((D, attn_width), BF),
            jax.ShapeDtypeStruct((len(vectors), D), F32),
        ],
        D * attn_width * 4,
        at,
        attn_sent[0],
        *attn_got,
        attn_other,
    )
    b_query, b_value, b_proj, gain_one, bias_one, gain_two, bias_two, b_out = [
        small[i] for i in range(8)
    ]

    def my_columns(vector):
        return lax.dynamic_slice_in_dim(vector, me * main, main, 0), vector[n * main :]

    q_main, q_spare = my_columns(b_query)
    v_main, v_spare = my_columns(b_value)
    qkv_bias = jnp.concatenate(
        [q_main, jnp.zeros_like(q_main), v_main, q_spare, jnp.zeros_like(q_spare), v_spare]
    )

    group_tokens = jnp.concatenate(tokens_parts, axis=0)
    proj_half = lax.dynamic_slice_in_dim(after(proj_weight, attn_got), core * step, half, 0)
    proj_near = gather_near(proj_half)
    own_cot = cotangent[0]
    cot_all = lax.all_gather(after(own_cot, attn_got, tokens_parts), "shard", axis=0, tiled=True)
    late_fc = after(fc_weight, attn_got)
    stride = own_rows // 64 * 16
    length = own_rows - 3 * stride
    by_parts = own_rows % 16 == 0 and stride > 0 and planes % 2 == 0
    if by_parts:
        fc_sent = local_call(
            functools.partial(
                pack_part_kernel, n, length, stride, lambda ref, j: fc_columns(ref, j, own_ff)
            ),
            [jax.ShapeDtypeStruct((own_rows, own_ff), BF)]
            + [jax.ShapeDtypeStruct((length, own_ff), BF)] * (n - 1),
            fc_weight.size * 2,
            at,
            late_fc,
        )
    else:
        fc_sent = pack(late_fc, lambda ref, j: fc_columns(ref, j, own_ff), own_ff, lengths)
    xhat_one, _ = normalize(group_tokens.astype(F32))
    normed = (xhat_one * gain_one + bias_one).astype(BF)
    qkv = (jnp.dot(normed, w_attn, preferred_element_type=F32) + qkv_bias).astype(BF)
    qkv, proj_near, fc_sent = after((qkv, proj_near, fc_sent))
    proj_parts = gather_far(proj_half, proj_near)
    fc_got = [swap(fc_sent[d], d) for d in range(1, n)]
    info = jnp.concatenate([lengths[0], me.astype(jnp.int32)[None]])
    mixed_heads = attention_fwd(info, qkv, n, heads)
    mixed_heads, proj_parts, fc_got = after((mixed_heads, proj_parts, fc_got))
    if by_parts:
        fc_mine = jnp.concatenate(fc_got)
        fc_near = swap_plane(fc_mine)
    got = [block(mixed_heads, 0)[:, :main]] + [
        swap(block(mixed_heads, d)[:, :main], d) for d in range(1, n)
    ]
    w_proj = place(proj_weight, proj_parts[1:])
    got, w_proj, cot_all = after((got, w_proj, cot_all))
    mixed_low = jnp.concatenate(natural(got) + [block(mixed_heads, 0)[:, main:]], axis=1)
    own_tokens = tokens[0].astype(F32)
    middle = own_tokens + jnp.dot(mixed_low, w_proj, preferred_element_type=F32) + b_proj
    xhat_two, inv_two = normalize(middle)
    own_normed_two = (xhat_two * gain_two + bias_two).astype(BF)
    normed_near = gather_near(own_normed_two)
    if by_parts:
        w_fc = local_call(
            functools.partial(place_part_kernel, n, length, stride, own_rows),
            jax.ShapeDtypeStruct((D, own_ff), BF),
            D * own_ff * 4,
            at,
            fc_sent[0],
            fc_mine,
            fc_near,
            swap_core(jnp.concatenate(after([fc_mine, fc_near], own_normed_two))),
        )
    else:
        w_fc = place(fc_sent[0], fc_got)
    cot_parts = [own_cot] + [
        lax.dynamic_slice_in_dim(cot_all, (me ^ d) * rows, rows, 0) for d in range(1, n)
    ]
    group_cot = jnp.concatenate(cot_parts, axis=0)
    d_active = cols_dot(group_cot, out_weight).astype(BF)
    normed_near, d_active = after((normed_near, d_active))
    normed_parts = gather_far(own_normed_two, normed_near)
    normed_two = jnp.concatenate(normed_parts, axis=0)

    def feed(part):
        hidden = jnp.dot(part, w_fc, preferred_element_type=F32) + fc_bias.astype(F32)
        inner = jnp.tanh(0.7978845608028654 * (hidden + 0.044715 * hidden * hidden * hidden))
        slope = 0.5 * (1.0 + inner) + 0.5 * hidden * (1.0 - inner * inner) * (
            0.7978845608028654 * (1.0 + 3 * 0.044715 * hidden * hidden)
        )
        return (0.5 * hidden * (1.0 + inner)).astype(BF), slope.astype(BF)

    fed = [feed(part) for part in normed_parts]
    active_parts = [a for a, _ in fed]
    active = jnp.concatenate(active_parts, axis=0)

    plane = lax.axis_index("plane")
    inner = (plane == 1) | (plane == 2)
    chained = planes == 4

    def add(one, two):
        return (one.astype(F32) + two.astype(F32)).astype(BF)

    def send_a(value):
        if chained:
            return lax.ppermute(value, "plane", [(0, 1), (3, 2)])
        return lax.psum(value, "plane")

    def send_b(value):
        return lax.ppermute(value, "plane", [(1, 2), (2, 1)]) if chained else value

    def send_c(value):
        return lax.ppermute(value, "plane", [(1, 0), (2, 3)]) if chained else value

    def merge(value, got):
        return add(value, got) if chained else got

    def last(value, got):
        return jnp.where(inner, value, got) if chained else got

    d_hidden_parts = [
        (block(d_active, d).astype(F32) * slope.astype(F32)).astype(BF)
        for d, (_, slope) in enumerate(fed)
    ]
    d_hidden = jnp.concatenate(d_hidden_parts, axis=0)
    e_parts = [cols_dot(part, w_fc) for part in d_hidden_parts]
    e_got = [swap(e_parts[d].astype(BF), d) for d in range(1, n)]
    late_normed, late_d = after((normed_two, d_hidden), e_parts)
    grad_fc = rows_dot(late_normed, late_d).astype(BF).reshape(n, own_rows, own_ff)
    fc_halves = core_halves(grad_fc)
    late_active, late_cot = after((active, group_cot), grad_fc)
    grad_out = rows_dot(late_active, late_cot).astype(BF)
    out_half = grad_out.shape[0] // 2
    out_give = lax.dynamic_slice_in_dim(grad_out, (1 - core) * out_half, out_half, 0)
    out_keep = lax.dynamic_slice_in_dim(grad_out, core * out_half, out_half, 0)
    e_got, fc_halves, out_give = after((e_got, fc_halves, out_give))
    fc_sum = lax.psum(fc_halves.reshape(n * half, own_ff), "plane").reshape(n, half, own_ff)

    e = e_parts[0] + sum(part.astype(F32) for part in e_got)
    e_gain = e * gain_two
    d_middle = own_cot.astype(F32) + inv_two * (
        e_gain
        - jnp.mean(e_gain, axis=-1, keepdims=True)
        - xhat_two * jnp.mean(e_gain * xhat_two, axis=-1, keepdims=True)
    )
    d_branch = d_middle.astype(BF)
    d_mixed = cols_dot(d_branch, w_proj).astype(BF)
    for_heads = jnp.stack([d_mixed[:, j * main : (j + 1) * main] for j in range(n)])
    spare_cols = d_mixed[:, n * main :]
    dmix_parts = [jnp.concatenate([pick(for_heads, me), spare_cols], axis=1)] + [
        swap(jnp.concatenate([pick(for_heads, me ^ d), spare_cols], axis=1), d)
        for d in range(1, n)
    ]
    x_out = add(out_keep, swap_core(out_give))
    grad_proj = rows_dot(mixed_low, d_branch).astype(BF).reshape(n, own_rows, D)
    proj_halves = core_halves(grad_proj)
    dmix_parts, x_out, proj_halves = after((dmix_parts, x_out, proj_halves))

    a_out = send_a(x_out)
    proj_got = [swap(pick(proj_halves, me ^ d), d) for d in range(1, n)]
    d_qkv = attention_bwd(info, qkv, jnp.concatenate(dmix_parts, axis=0), n, heads)
    d_qkv, proj_got = after((d_qkv, proj_got))

    proj_part = pick(proj_halves, me).astype(F32) + sum(part.astype(F32) for part in proj_got)
    proj_part = proj_part.astype(BF)
    proj_rows = jnp.where(
        core == 0,
        jnp.concatenate([proj_part[:step], jnp.zeros((half, D), BF)]),
        jnp.concatenate([jnp.zeros((step, D), BF), proj_part]),
    )
    grad_main = rows_dot(normed, d_qkv[:, : 3 * main]).astype(BF).reshape(n, own_rows, 3 * main)
    attn_got = [swap(pick(grad_main, me ^ d), d) for d in range(1, n)]
    grad_spare = rows_dot(normed, d_qkv[:, 3 * main :]).astype(BF).reshape(n, own_rows, 3 * spare)
    grad_spare = pick(grad_spare, me)
    attn_got, a_out, fc_sum, grad_spare, proj_rows = after(
        (attn_got, a_out, fc_sum, grad_spare, proj_rows)
    )

    attn_parts = (pick(grad_main, me), *attn_got, grad_spare, proj_rows)
    attn_sum = lax.psum(attn_parts, ("plane", "core"))
    y_out = merge(x_out, a_out)
    b_out_sum = send_b(y_out)
    grad_fc_bias = jnp.sum(d_hidden.astype(F32), axis=0)

    counted = (lax.broadcasted_iota(jnp.int32, (n * rows, 1), 0) < rows) | (
        lax.broadcasted_iota(jnp.int32, (1, d_qkv.shape[1]), 1) < 3 * main
    )
    d_once = after(jnp.where(counted, d_qkv, BF(0)), attn_got)
    f = reduce_rows([cols_dot(block(d_once, d), w_attn) for d in range(n)])
    f, b_out_sum = after((f, b_out_sum))
    t_out = merge(y_out, b_out_sum)
    c_out_sum = send_c(t_out)
    xhat_own, inv_own = normalize(own_tokens)
    f_gain = f * gain_one
    d_tokens = inv_own * (
        f_gain
        - jnp.mean(f_gain, axis=-1, keepdims=True)
        - xhat_own * jnp.mean(f_gain * xhat_own, axis=-1, keepdims=True)
    )
    input_grad = (d_middle + d_tokens).astype(BF)[None]

    late_active = after(active, f)
    output = reduce_rows(
        [jnp.dot(block(late_active, d), out_weight, preferred_element_type=F32) for d in range(n)]
    )
    output = (middle + output + b_out).astype(BF)[None]

    out_mine = last(t_out, c_out_sum)
    out_other = swap_core(out_mine)
    sum_out_weight = jnp.concatenate(
        [jnp.where(core == 0, out_mine, out_other), jnp.where(core == 0, out_other, out_mine)]
    ).astype(F32)
    fc_sum = after(fc_sum, f)
    fc_parts = jnp.concatenate(
        [pick(fc_sum, me)] + [swap(pick(fc_sum, me ^ d), d) for d in range(1, n)]
    )
    sum_fc_weight = local_call(
        functools.partial(
            unpack_kernel,
            n,
            half,
            step,
            lambda m, d: [(0, (m ^ d) * own_ff, 0, d * half, 0, own_ff)],
            1,
        ),
        [jax.ShapeDtypeStruct((own_rows, n * own_ff), F32)],
        own_rows * n * own_ff * 8,
        at,
        fc_parts,
        swap_core(fc_parts),
    )[0]

    def attn_places(m, d):
        places = [(0, p * D + (m ^ d) * main, d, p * main, (p + 1) * main) for p in range(3)]
        if d == 0:
            places += [
                (0, p * D + n * main, n, p * spare, (p + 1) * spare) for p in range(3)
            ]
            places.append((1, 0, n + 1, 0, D))
        return places

    d_once_sum = jnp.sum(d_once.astype(F32), axis=0)

    def vector_of(part):
        whole = jnp.zeros((D,), F32)
        whole = lax.dynamic_update_slice_in_dim(
            whole, d_once_sum[part * main : (part + 1) * main], me * main, 0
        )
        lane = 3 * main + part * spare
        return jnp.concatenate([whole[: n * main], d_once_sum[lane : lane + spare]])

    small_grads = jnp.stack(
        [
            vector_of(0),
            vector_of(2),
            jnp.sum(d_branch.astype(F32), axis=0),
            jnp.sum(f * xhat_own, axis=0),
            jnp.sum(f, axis=0),
            jnp.sum(e * xhat_two, axis=0),
            jnp.sum(e, axis=0),
            jnp.sum(own_cot.astype(F32), axis=0),
        ]
    )
    small_grads = small_grads.reshape(8, n, own_rows).transpose(1, 0, 2)
    small_own = pick(small_grads, me)
    for d in range(1, n):
        small_own = small_own + swap(pick(small_grads, me ^ d), d)
    small_own = jnp.concatenate([small_own, grad_fc_bias.reshape(-1, own_rows)], axis=0)
    small_own = small_own + swap_core(small_own)
    hop = 1
    while hop < planes:
        small_own = small_own + lax.ppermute(
            small_own, "plane", [(i, i ^ hop) for i in range(planes)]
        )
        hop *= 2
    attn_sum, small_own, output, input_grad, sum_fc_weight, sum_out_weight = after(
        (attn_sum, small_own, output, input_grad, sum_fc_weight, sum_out_weight)
    )
    sum_attn_weight, sum_proj_weight = local_call(
        functools.partial(spread_kernel, n, attn_places),
        [
            jax.ShapeDtypeStruct((own_rows, 3 * D), F32),
            jax.ShapeDtypeStruct((own_rows, D), F32),
        ],
        own_rows * 4 * D * 8,
        at,
        *attn_sum,
    )
    s = small_own[:8]
    sum_fc_bias = small_own[8:].reshape(-1)
    return (
        output,
        input_grad,
        sum_attn_weight,
        s[0],
        s[1],
        sum_proj_weight,
        s[2],
        s[3],
        s[4],
        s[5],
        s[6],
        sum_fc_weight,
        sum_fc_bias,
        sum_out_weight,
        s[7],
    )


def solution(mesh):
    shards, reps = mesh.devices.shape
    split = jax.sharding.Mesh(
        mesh.devices.reshape(shards, reps // 2, 2), ("shard", "plane", "core")
    )
    rep = ("plane", "core")
    batch = P(rep, "shard", None)
    row, vec = P("shard", None), P("shard")
    return jax.shard_map(
        body,
        mesh=split,
        in_specs=(batch, batch, P(rep, None), row, vec, vec, row)
        + (vec,) * 5
        + (row, vec, row, vec),
        out_specs=(batch, batch, row, vec, vec, row) + (vec,) * 5 + (row, vec, row, vec),
        check_vma=False,
    )
```

```python
import functools
import math

import jax
import jax.numpy as jnp
from jax import lax
from jax.experimental import pallas as pl
from jax.experimental.pallas import tpu as pltpu
from jax.sharding import PartitionSpec as P

D = 1600
HEADS = 25
HD = 64
UNIT = 32
LANES = 128
NEG = -1e30
VEC_ROWS = 16
BF = jnp.bfloat16
F32 = jnp.float32


def dot(left, right, dims):
    return lax.dot_general(left, right, (dims, ((), ())), preferred_element_type=F32)


def rows_dot(left, right):
    return dot(left, right, ((0,), (0,)))


def cols_dot(left, right):
    return dot(left, right, ((1,), (1,)))


def normalize(values):
    center = values - jnp.mean(values, axis=-1, keepdims=True)
    spread = jnp.mean(center * center, axis=-1, keepdims=True)
    inv = lax.rsqrt(spread + 1e-05)
    return center * inv, inv


def place_blocks(info_ref, shards, units):
    b0, b1, b2, me = info_ref[0], info_ref[1], info_ref[2], info_ref[3]
    e0, e1 = b0, b0 + b1
    places = []
    for d in range(shards):
        s = jnp.bitwise_xor(me, d)
        for u in range(units):
            first = jnp.where(u < e0, 0, jnp.where(u < e1, e0, e1))
            span = jnp.where(u < e0, b0, jnp.where(u < e1, b1, b2))
            places.append((d * units + u, first * shards + s * span + (u - first)))
    return places, e0, e1


def head_lanes(tile_rows, half):
    lane = lax.broadcasted_iota(jnp.int32, (tile_rows, LANES), 1)
    return (lane < HD) if half == 0 else (lane >= HD)


def window_scores(q, k, rows, width):
    scores = cols_dot(q, k)
    row = lax.broadcasted_iota(jnp.int32, (rows, width * rows), 0)
    col = lax.broadcasted_iota(jnp.int32, (rows, width * rows), 1)
    return jnp.where(col <= row + (width - 1) * rows, scores, NEG)


def fwd_kernel(shards, units, heads, info_ref, qkv_ref, out_ref, perm, mixed):
    block = UNIT
    rows = shards * block
    main = heads * HD
    places, e0, e1 = place_blocks(info_ref, shards, units)
    for src, dst in places:
        at = pl.ds(pl.multiple_of(dst * block, block), block)
        perm[at, :] = qkv_ref[src * block : (src + 1) * block, :]

    def unit(i, carry):
        first = jnp.where(i < e0, 0, jnp.where(i < e1, e0, e1))
        q_at = pl.ds(pl.multiple_of(i * rows, rows), rows)
        for width in range(1, 5):

            @pl.when(i - first + 1 == width)
            def _():
                k_at = pl.ds(pl.multiple_of(first * rows, rows), width * rows)

                def attend(q, k, v):
                    scores = window_scores(q * BF(0.125), k, rows, width)
                    top = jnp.max(scores, axis=1, keepdims=True)
                    probs = jnp.exp(scores - top)
                    total = jnp.sum(probs, axis=1, keepdims=True)
                    return dot(probs.astype(BF), v, ((1,), (0,))) / total

                for tile in range(main // LANES):
                    lanes = slice(tile * LANES, (tile + 1) * LANES)
                    k_lanes = slice(main + lanes.start, main + lanes.stop)
                    v_lanes = slice(2 * main + lanes.start, 2 * main + lanes.stop)
                    q, k, v = perm[q_at, lanes], perm[k_at, k_lanes], perm[k_at, v_lanes]
                    low = head_lanes(rows, 0)
                    zero = jnp.zeros_like(q)
                    left = attend(jnp.where(low, q, zero), k, v)
                    right = attend(jnp.where(low, zero, q), k, v)
                    mixed[q_at, lanes] = jnp.where(low, left, right).astype(BF)
                if main % LANES:
                    lanes = main - HD
                    mixed[q_at, lanes:main] = attend(
                        perm[q_at, lanes:main],
                        perm[k_at, main + lanes : 2 * main],
                        perm[k_at, 2 * main + lanes : 3 * main],
                    ).astype(BF)
                base = 3 * main
                mixed[q_at, main : main + HD] = attend(
                    perm[q_at, base : base + HD],
                    perm[k_at, base + HD : base + 2 * HD],
                    perm[k_at, base + 2 * HD : base + 3 * HD],
                ).astype(BF)

        return carry

    lax.fori_loop(0, units, unit, 0)
    for src, dst in places:
        at = pl.ds(pl.multiple_of(dst * block, block), block)
        out_ref[src * block : (src + 1) * block, :] = mixed[at, :]


def bwd_kernel(
    shards, units, heads, info_ref, qkv_ref, dmix_ref, out_ref, perm, dperm, dq_acc, dk_acc, dv_acc
):
    block = UNIT
    rows = shards * block
    main = heads * HD
    places, e0, e1 = place_blocks(info_ref, shards, units)
    for src, dst in places:
        at = pl.ds(pl.multiple_of(dst * block, block), block)
        perm[at, :] = qkv_ref[src * block : (src + 1) * block, :]
        dperm[at, :] = dmix_ref[src * block : (src + 1) * block, :]
    dk_acc[...] = jnp.zeros_like(dk_acc)
    dv_acc[...] = jnp.zeros_like(dv_acc)

    def unit(i, carry):
        first = jnp.where(i < e0, 0, jnp.where(i < e1, e0, e1))
        q_at = pl.ds(pl.multiple_of(i * rows, rows), rows)
        for width in range(1, 5):

            @pl.when(i - first + 1 == width)
            def _():
                k_at = pl.ds(pl.multiple_of(first * rows, rows), width * rows)

                def pull(q, k, v, g):
                    q = q * BF(0.125)
                    scores = window_scores(q, k, rows, width)
                    top = jnp.max(scores, axis=1, keepdims=True)
                    probs = jnp.exp(scores - top)
                    total = jnp.sum(probs, axis=1, keepdims=True)
                    probs = probs * (1.0 / total)
                    d_probs = cols_dot(g, v)
                    delta = jnp.sum(probs * d_probs, axis=1, keepdims=True)
                    d_scores = (probs * (d_probs - delta)).astype(BF)
                    d_q = dot(d_scores, k, ((1,), (0,))) * 0.125
                    return d_q, rows_dot(d_scores, q), rows_dot(probs.astype(BF), g)

                for tile in range(main // LANES):
                    lanes = slice(tile * LANES, (tile + 1) * LANES)
                    k_lanes = slice(main + lanes.start, main + lanes.stop)
                    v_lanes = slice(2 * main + lanes.start, 2 * main + lanes.stop)
                    q, k, v = perm[q_at, lanes], perm[k_at, k_lanes], perm[k_at, v_lanes]
                    g = dperm[q_at, lanes]
                    low = head_lanes(rows, 0)
                    zero = jnp.zeros_like(q)
                    dq0, dk0, dv0 = pull(jnp.where(low, q, zero), k, v, jnp.where(low, g, zero))
                    dq1, dk1, dv1 = pull(jnp.where(low, zero, q), k, v, jnp.where(low, zero, g))
                    dq_acc[q_at, lanes] = jnp.where(low, dq0, dq1).astype(BF)
                    dk_acc[k_at, lanes] += dk0 + dk1
                    dv_acc[k_at, lanes] += dv0 + dv1
                extra = [(main, 3 * main, 3 * main + HD, 3 * main + 2 * HD)]
                if main % LANES:
                    extra.append((main - HD, main - HD, 2 * main - HD, 3 * main - HD))
                for own, q_lane, k_lane, v_lane in extra:
                    dq0, dk0, dv0 = pull(
                        perm[q_at, q_lane : q_lane + HD],
                        perm[k_at, k_lane : k_lane + HD],
                        perm[k_at, v_lane : v_lane + HD],
                        dperm[q_at, own : own + HD],
                    )
                    dq_acc[q_at, own : own + HD] = dq0.astype(BF)
                    dk_acc[k_at, own : own + HD] += dk0
                    dv_acc[k_at, own : own + HD] += dv0

        return carry

    lax.fori_loop(0, units, unit, 0)
    for src, dst in places:
        at = pl.ds(pl.multiple_of(dst * block, block), block)
        to = slice(src * block, (src + 1) * block)
        for part, acc in enumerate((dq_acc, dk_acc, dv_acc)):
            got = acc[at, :].astype(BF)
            out_ref[to, part * main : (part + 1) * main] = got[:, :main]
            lane = 3 * main + part * HD
            out_ref[to, lane : lane + HD] = got[:, main:]


def vmem_call(kernel, out_shape, scratch, cost, inputs):
    return pl.pallas_call(
        kernel,
        out_shape=out_shape,
        in_specs=[pl.BlockSpec(memory_space=pltpu.SMEM)]
        + [pl.BlockSpec(memory_space=pltpu.VMEM)] * (len(inputs) - 1),
        out_specs=pl.BlockSpec(memory_space=pltpu.VMEM),
        scratch_shapes=scratch,
        compiler_params=pltpu.CompilerParams(vmem_limit_bytes=48 << 20),
        cost_estimate=cost,
    )(*inputs)


def attention_fwd(info, qkv, shards, heads):
    total, width = qkv.shape
    units = total // (shards * UNIT)
    own = (heads + 1) * HD
    return vmem_call(
        functools.partial(fwd_kernel, shards, units, heads),
        jax.ShapeDtypeStruct((total, own), BF),
        [pltpu.VMEM((total, width), BF), pltpu.VMEM((total, own), BF)],
        pl.CostEstimate(flops=1, bytes_accessed=1, transcendentals=0),
        (info, qkv),
    )


def attention_bwd(info, qkv, d_mixed, shards, heads):
    total, width = qkv.shape
    units = total // (shards * UNIT)
    own = (heads + 1) * HD
    return vmem_call(
        functools.partial(bwd_kernel, shards, units, heads),
        jax.ShapeDtypeStruct((total, width), BF),
        [
            pltpu.VMEM((total, width), BF),
            pltpu.VMEM((total, own), BF),
            pltpu.VMEM((total, own), BF),
            pltpu.VMEM((total, own), F32),
            pltpu.VMEM((total, own), F32),
        ],
        pl.CostEstimate(flops=1, bytes_accessed=1, transcendentals=0),
        (info, qkv, d_mixed),
    )


def on_place(me, core, shards, run):
    for m in range(shards):
        for c in range(2):

            @pl.when((me == m) & (core == c))
            def _():
                run(m, c)


def attn_columns(value, j, heads):
    main = heads * HD
    first = D // main * main
    parts = [value[:, p * D + j * main : p * D + (j + 1) * main] for p in range(3)]
    parts += [value[:, p * D + first : (p + 1) * D] for p in range(3)]
    return jnp.concatenate(parts, axis=1)


def fc_columns(value, j, width):
    return value[:, j * width : (j + 1) * width]


def pack_kernel(shards, half, step, columns, at_ref, dep_ref, weight_ref, *outs):
    del dep_ref

    def run(m, c):
        outs[0][...] = columns(weight_ref, m)
        for d in range(1, shards):
            piece = columns(weight_ref.at[c * step : c * step + half], m ^ d)
            outs[d][...] = piece

    on_place(at_ref[0], at_ref[1], shards, run)


def pack_attn_kernel(shards, half, step, heads, count, at_ref, weight_ref, *refs):
    sources, outs = refs[:count], refs[count : count + shards]
    vectors, sems = refs[count + shards : 2 * count + shards], refs[2 * count + shards]
    length = vectors[0].shape[0]
    copies = [
        pltpu.make_async_copy(source, vector, sems.at[i])
        for i, (source, vector) in enumerate(zip(sources, vectors))
    ]
    for copy in copies:
        copy.start()

    def run(m, c):
        outs[0][: shards_rows(outs[0]), :] = attn_columns(weight_ref, m, heads)
        for d in range(1, shards):
            outs[d][:half, :] = attn_columns(weight_ref.at[c * step : c * step + half], m ^ d, heads)

    def shards_rows(ref):
        return ref.shape[0] - VEC_ROWS

    on_place(at_ref[0], at_ref[1], shards, run)
    for copy in copies:
        copy.wait()
    width = outs[0].shape[1]
    block = jnp.concatenate(
        [v[...].astype(F32).reshape(1, length) for v in vectors]
        + [jnp.zeros((VEC_ROWS - count, length), F32)],
        axis=0,
    )
    block = jnp.concatenate(
        [block, jnp.zeros((VEC_ROWS, width - length), F32)], axis=1
    ).astype(BF)
    for out in outs:
        out[out.shape[0] - VEC_ROWS :, :] = block


def place_attn_kernel(shards, half, step, rows, count, at_ref, *refs):
    own, mine, other = refs[0], refs[1:shards], refs[shards]
    out, vec = refs[shards + 1 :]

    def run(m, c):
        out[m * rows : (m + 1) * rows, :] = own[:rows]
        for d in range(1, shards):
            base = (m ^ d) * rows
            a, b = mine[d - 1][:half], other[d - 1]
            low, high = (a, b) if c == 0 else (b, a)
            out[base : base + step, :] = low[:step]
            out[base + step : base + rows, :] = high
        for j in range(shards):
            ref, at = (own, rows) if j == m else (mine[(j ^ m) - 1], half)
            vec[:, j * rows : (j + 1) * rows] = ref[at : at + VEC_ROWS, :rows].astype(F32)[:count]

    on_place(at_ref[0], at_ref[1], shards, run)


def place_kernel(shards, half, step, rows, at_ref, *refs):
    own, mine, other, out = refs[0], refs[1:shards], refs[shards], refs[shards + 1]

    def run(m, c):
        out[m * rows : (m + 1) * rows, :] = own[...]
        for d in range(1, shards):
            base = (m ^ d) * rows
            low, high = (mine[d - 1][...], other[d - 1]) if c == 0 else (other[d - 1], mine[d - 1][...])
            out[base : base + step, :] = low[:step]
            out[base + step : base + rows, :] = high

    on_place(at_ref[0], at_ref[1], shards, run)


def pack_part_kernel(shards, length, stride, columns, at_ref, weight_ref, *outs):
    part = pl.ds(pl.multiple_of(at_ref[2] * stride, 16), length)
    for m in range(shards):

        @pl.when(at_ref[0] == m)
        def _():
            outs[0][...] = columns(weight_ref, m)
            for d in range(1, shards):
                outs[d][...] = columns(weight_ref.at[part], m ^ d)


def place_part_kernel(shards, length, stride, rows, at_ref, own, mine, near, across, out):
    me, q = at_ref[0], at_ref[2]
    out[pl.ds(pl.multiple_of(me * rows, 16), rows), :] = own[...]
    size = (shards - 1) * length
    for d in range(1, shards):
        base = jnp.bitwise_xor(me, d) * rows
        for flip, ref, first in ((0, mine, 0), (2, near, 0), (1, across, 0), (3, across, size)):
            to = base + jnp.bitwise_xor(q, flip) * stride
            row = first + (d - 1) * length
            out[pl.ds(pl.multiple_of(to, 16), length), :] = ref[row : row + length, :]


def unpack_kernel(shards, half, step, places, count, at_ref, *refs):
    mine, other, outs = refs[:count], refs[count : 2 * count], refs[2 * count :]

    def run(m, c):
        for d in range(shards):
            for index, where, part, row, low, high in places(m, d):
                out, width = outs[index], high - low
                a = mine[part][row : row + half, low:high]
                b = other[part][row : row + half, low:high]
                first, second = (a, b) if c == 0 else (b, a)
                out[:step, where : where + width] = first[:step].astype(F32)
                out[step:, where : where + width] = second.astype(F32)

    on_place(at_ref[0], at_ref[1], shards, run)


def local_call(kernel, out_shape, cost_bytes, at, *inputs, anywhere=(), scratch=()):
    vmem = pl.BlockSpec(memory_space=pltpu.VMEM)
    hbm = pl.BlockSpec(memory_space=pltpu.HBM)
    specs = [hbm if i in anywhere else vmem for i in range(len(inputs))]
    return pl.pallas_call(
        kernel,
        out_shape=out_shape,
        in_specs=[pl.BlockSpec(memory_space=pltpu.SMEM)] + specs,
        out_specs=jax.tree.map(lambda _: vmem, out_shape),
        scratch_shapes=list(scratch),
        compiler_params=pltpu.CompilerParams(vmem_limit_bytes=48 << 20),
        cost_estimate=pl.CostEstimate(flops=1, bytes_accessed=1, transcendentals=0),
    )(at, *inputs)


def body(
    tokens,
    cotangent,
    lengths,
    attn_weight,
    query_bias,
    value_bias,
    proj_weight,
    proj_bias,
    ln1_gain,
    ln1_bias,
    ln2_gain,
    ln2_bias,
    fc_weight,
    fc_bias,
    out_weight,
    out_bias,
):
    n = lax.axis_size("shard")
    planes = lax.axis_size("plane")
    me = lax.axis_index("shard")
    core = lax.axis_index("core")
    heads = (HEADS - 1) // n
    main = heads * HD
    spare = D - n * main
    own_rows = attn_weight.shape[0]
    own_ff = fc_bias.shape[0]
    rows = tokens.shape[1]
    half = -(-own_rows // 32) * 16
    step = own_rows - half
    quarter = lax.axis_index("plane") % 2 * 2 + core
    at = jnp.stack([me, core, quarter]).astype(jnp.int32)

    def swap(value, d):
        return lax.ppermute(value, "shard", [(i, i ^ d) for i in range(n)])

    def swap_plane(value):
        return lax.ppermute(value, "plane", [(i, i ^ 1) for i in range(planes)])

    def swap_core(value):
        return lax.ppermute(value, "core", [(0, 1), (1, 0)])

    def gather_near(value):
        if n != 4:
            return [swap(value, d) for d in range(1, n)]
        return [swap(value, 1), swap(value, 2)]

    def gather_far(value, near):
        if n != 4:
            return [value] + near
        one, two = near
        cut = value.shape[0] // 32 * 16
        three = jnp.concatenate([swap(one[:cut], 2), swap(two[cut:], 1)], axis=0)
        return [value, one, two, three]

    def gather(value):
        return gather_far(value, gather_near(value))

    def pick(stacked, index):
        return lax.dynamic_index_in_dim(stacked, index, 0, keepdims=False)

    def natural(pieces):
        stacked = jnp.stack(pieces)
        return [pick(stacked, me ^ j) for j in range(n)]

    def after(value, *deps):
        return lax.optimization_barrier((value, deps))[0]

    def block(value, d):
        return value[d * rows : (d + 1) * rows]

    def place(own, mine):
        other = swap_core(jnp.stack(mine))
        return local_call(
            functools.partial(place_kernel, n, half, step, own_rows),
            jax.ShapeDtypeStruct((n * own_rows, own.shape[1]), BF),
            n * own.size * 4,
            at,
            own,
            *mine,
            other,
        )

    def pack(weight, columns, width, dep):
        shapes = [jax.ShapeDtypeStruct((own_rows, width), BF)]
        shapes += [jax.ShapeDtypeStruct((half, width), BF)] * (n - 1)
        return local_call(
            functools.partial(pack_kernel, n, half, step, columns),
            shapes,
            weight.size * 2,
            at,
            dep,
            weight,
            anywhere=(0,),
        )

    def reduce_rows(parts, *deps):
        got = after([swap(parts[d].astype(BF), d) for d in range(1, n)], *deps)
        total = parts[0].astype(F32)
        for part in got:
            total = total + part.astype(F32)
        return total

    def core_halves(parts):
        keep = lax.dynamic_slice_in_dim(parts, core * step, half, 1)
        give = lax.dynamic_slice_in_dim(parts, (1 - core) * step, half, 1)
        return (keep.astype(F32) + swap_core(give).astype(F32)).astype(BF)

    vectors = (
        query_bias, value_bias, proj_bias, ln1_gain, ln1_bias, ln2_gain, ln2_bias, out_bias
    )
    tokens_near = gather_near(tokens[0])
    attn_width = 3 * (main + spare)
    attn_sent = local_call(
        functools.partial(pack_attn_kernel, n, half, step, heads, len(vectors)),
        [jax.ShapeDtypeStruct((own_rows + VEC_ROWS, attn_width), BF)]
        + [jax.ShapeDtypeStruct((half + VEC_ROWS, attn_width), BF)] * (n - 1),
        attn_weight.size * 2,
        at,
        attn_weight,
        *vectors,
        anywhere=range(1, len(vectors) + 1),
        scratch=[pltpu.VMEM((own_rows,), BF)] * len(vectors)
        + [pltpu.SemaphoreType.DMA((len(vectors),))],
    )
    attn_got = [swap(attn_sent[d], d) for d in range(1, n)]
    attn_got, tokens_near = after((attn_got, tokens_near))
    attn_other = swap_core(jnp.stack([piece[:half] for piece in attn_got]))
    tokens_parts = gather_far(tokens[0], tokens_near)
    w_attn, small = local_call(
        functools.partial(place_attn_kernel, n, half, step, own_rows, len(vectors)),
        [
            jax.ShapeDtypeStruct((D, attn_width), BF),
            jax.ShapeDtypeStruct((len(vectors), D), F32),
        ],
        D * attn_width * 4,
        at,
        attn_sent[0],
        *attn_got,
        attn_other,
    )
    b_query, b_value, b_proj, gain_one, bias_one, gain_two, bias_two, b_out = [
        small[i] for i in range(8)
    ]

    def my_columns(vector):
        return lax.dynamic_slice_in_dim(vector, me * main, main, 0), vector[n * main :]

    q_main, q_spare = my_columns(b_query)
    v_main, v_spare = my_columns(b_value)
    qkv_bias = jnp.concatenate(
        [q_main, jnp.zeros_like(q_main), v_main, q_spare, jnp.zeros_like(q_spare), v_spare]
    )

    group_tokens = jnp.concatenate(tokens_parts, axis=0)
    proj_half = lax.dynamic_slice_in_dim(after(proj_weight, attn_got), core * step, half, 0)
    proj_near = gather_near(proj_half)
    own_cot = cotangent[0]
    cot_all = lax.all_gather(after(own_cot, attn_got, tokens_parts), "shard", axis=0, tiled=True)
    late_fc = after(fc_weight, attn_got)
    stride = own_rows // 64 * 16
    length = own_rows - 3 * stride
    by_parts = own_rows % 16 == 0 and stride > 0 and planes % 2 == 0
    if by_parts:
        fc_sent = local_call(
            functools.partial(
                pack_part_kernel, n, length, stride, lambda ref, j: fc_columns(ref, j, own_ff)
            ),
            [jax.ShapeDtypeStruct((own_rows, own_ff), BF)]
            + [jax.ShapeDtypeStruct((length, own_ff), BF)] * (n - 1),
            fc_weight.size * 2,
            at,
            late_fc,
        )
    else:
        fc_sent = pack(late_fc, lambda ref, j: fc_columns(ref, j, own_ff), own_ff, lengths)
    xhat_one, _ = normalize(group_tokens.astype(F32))
    normed = (xhat_one * gain_one + bias_one).astype(BF)
    qkv = (jnp.dot(normed, w_attn, preferred_element_type=F32) + qkv_bias).astype(BF)
    qkv, proj_near, fc_sent = after((qkv, proj_near, fc_sent))
    proj_parts = gather_far(proj_half, proj_near)
    fc_got = [swap(fc_sent[d], d) for d in range(1, n)]
    info = jnp.concatenate([lengths[0], me.astype(jnp.int32)[None]])
    mixed_heads = attention_fwd(info, qkv, n, heads)
    mixed_heads, proj_parts, fc_got = after((mixed_heads, proj_parts, fc_got))
    if by_parts:
        fc_mine = jnp.concatenate(fc_got)
        fc_near = swap_plane(fc_mine)
    got = [block(mixed_heads, 0)[:, :main]] + [
        swap(block(mixed_heads, d)[:, :main], d) for d in range(1, n)
    ]
    w_proj = place(proj_weight, proj_parts[1:])
    got, w_proj, cot_all = after((got, w_proj, cot_all))
    mixed_low = jnp.concatenate(natural(got) + [block(mixed_heads, 0)[:, main:]], axis=1)
    own_tokens = tokens[0].astype(F32)
    middle = own_tokens + jnp.dot(mixed_low, w_proj, preferred_element_type=F32) + b_proj
    xhat_two, inv_two = normalize(middle)
    own_normed_two = (xhat_two * gain_two + bias_two).astype(BF)
    normed_near = gather_near(own_normed_two)
    if by_parts:
        w_fc = local_call(
            functools.partial(place_part_kernel, n, length, stride, own_rows),
            jax.ShapeDtypeStruct((D, own_ff), BF),
            D * own_ff * 4,
            at,
            fc_sent[0],
            fc_mine,
            fc_near,
            swap_core(jnp.concatenate(after([fc_mine, fc_near], own_normed_two))),
        )
    else:
        w_fc = place(fc_sent[0], fc_got)
    cot_parts = [own_cot] + [
        lax.dynamic_slice_in_dim(cot_all, (me ^ d) * rows, rows, 0) for d in range(1, n)
    ]
    group_cot = jnp.concatenate(cot_parts, axis=0)
    d_active = cols_dot(group_cot, out_weight).astype(BF)
    normed_near, d_active = after((normed_near, d_active))
    normed_parts = gather_far(own_normed_two, normed_near)
    normed_two = jnp.concatenate(normed_parts, axis=0)

    def feed(part):
        hidden = jnp.dot(part, w_fc, preferred_element_type=F32) + fc_bias.astype(F32)
        inner = jnp.tanh(0.7978845608028654 * (hidden + 0.044715 * hidden * hidden * hidden))
        slope = 0.5 * (1.0 + inner) + 0.5 * hidden * (1.0 - inner * inner) * (
            0.7978845608028654 * (1.0 + 3 * 0.044715 * hidden * hidden)
        )
        return (0.5 * hidden * (1.0 + inner)).astype(BF), slope.astype(BF)

    fed = [feed(part) for part in normed_parts]
    active_parts = [a for a, _ in fed]
    active = jnp.concatenate(active_parts, axis=0)

    plane = lax.axis_index("plane")
    inner = (plane == 1) | (plane == 2)
    chained = planes == 4

    def add(one, two):
        return (one.astype(F32) + two.astype(F32)).astype(BF)

    def send_a(value):
        if chained:
            return lax.ppermute(value, "plane", [(0, 1), (3, 2)])
        return lax.psum(value, "plane")

    def send_b(value):
        return lax.ppermute(value, "plane", [(1, 2), (2, 1)]) if chained else value

    def send_c(value):
        return lax.ppermute(value, "plane", [(1, 0), (2, 3)]) if chained else value

    def merge(value, got):
        return add(value, got) if chained else got

    def last(value, got):
        return jnp.where(inner, value, got) if chained else got

    d_hidden_parts = [
        (block(d_active, d).astype(F32) * slope.astype(F32)).astype(BF)
        for d, (_, slope) in enumerate(fed)
    ]
    d_hidden = jnp.concatenate(d_hidden_parts, axis=0)
    e_parts = [cols_dot(part, w_fc) for part in d_hidden_parts]
    e_got = [swap(e_parts[d].astype(BF), d) for d in range(1, n)]
    late_active, late_cot = after((active, group_cot), e_parts)
    grad_out = rows_dot(late_active, late_cot).astype(BF)
    out_half = grad_out.shape[0] // 2
    out_give = lax.dynamic_slice_in_dim(grad_out, (1 - core) * out_half, out_half, 0)
    out_keep = lax.dynamic_slice_in_dim(grad_out, core * out_half, out_half, 0)
    late_normed, late_d = after((normed_two, d_hidden), out_give, e_got[0])
    grad_fc = rows_dot(late_normed, late_d).astype(BF).reshape(n, own_rows, own_ff)
    x_out = add(out_keep, swap_core(out_give))
    a_out = send_a(x_out)
    e_got, x_out, grad_fc = after((e_got, x_out, grad_fc))

    e = e_parts[0] + sum(part.astype(F32) for part in e_got)
    e_gain = e * gain_two
    d_middle = own_cot.astype(F32) + inv_two * (
        e_gain
        - jnp.mean(e_gain, axis=-1, keepdims=True)
        - xhat_two * jnp.mean(e_gain * xhat_two, axis=-1, keepdims=True)
    )
    d_branch = d_middle.astype(BF)
    d_mixed = cols_dot(d_branch, w_proj).astype(BF)
    for_heads = jnp.stack([d_mixed[:, j * main : (j + 1) * main] for j in range(n)])
    spare_cols = d_mixed[:, n * main :]
    dmix_parts = [jnp.concatenate([pick(for_heads, me), spare_cols], axis=1)] + [
        swap(jnp.concatenate([pick(for_heads, me ^ d), spare_cols], axis=1), d)
        for d in range(1, n)
    ]
    x_fc = core_halves(grad_fc)
    a_fc = send_a(x_fc)
    grad_proj = rows_dot(mixed_low, d_branch).astype(BF).reshape(n, own_rows, D)
    dmix_parts, x_fc, grad_proj, a_out = after((dmix_parts, x_fc, grad_proj, a_out))

    y_out = merge(x_out, a_out)
    b_out_sum = send_b(y_out)
    proj_halves = core_halves(grad_proj)
    d_qkv = attention_bwd(info, qkv, jnp.concatenate(dmix_parts, axis=0), n, heads)
    d_qkv, proj_halves = after((d_qkv, proj_halves))

    grad_main = rows_dot(normed, d_qkv[:, : 3 * main]).astype(BF).reshape(n, own_rows, 3 * main)
    grad_spare = rows_dot(normed, d_qkv[:, 3 * main :]).astype(BF).reshape(n, own_rows, 3 * spare)
    main_halves = core_halves(grad_main)
    spare_half = core_halves(pick(grad_spare, me)[None])[0]
    main_halves, spare_half, a_fc, b_out_sum = after((main_halves, spare_half, a_fc, b_out_sum))
    attn_got = [swap(pick(main_halves, me ^ d), d) for d in range(1, n)]
    y_fc = merge(x_fc, a_fc)
    b_fc = send_b(y_fc)
    t_out = merge(y_out, b_out_sum)
    c_out_sum = send_c(t_out)
    counted = (lax.broadcasted_iota(jnp.int32, (n * rows, 1), 0) < rows) | (
        lax.broadcasted_iota(jnp.int32, (1, d_qkv.shape[1]), 1) < 3 * main
    )
    d_once = jnp.where(counted, after(d_qkv, main_halves), BF(0))
    f_parts = [cols_dot(block(d_once, d), w_attn) for d in range(n)]
    attn_got, f_parts = after((attn_got, f_parts))

    attn_all = [pick(main_halves, me)] + attn_got
    cut = n // 2 + 1
    x_attn = [jnp.concatenate(attn_all[:cut], axis=1)]
    a_attn = send_a(x_attn[0])
    proj_part = pick(proj_halves, me).astype(F32)
    proj_got = [swap(pick(proj_halves, me ^ d), d) for d in range(1, n)]
    proj_got, a_attn, b_fc, c_out_sum = after((proj_got, a_attn, b_fc, c_out_sum))
    for part in proj_got:
        proj_part = proj_part + part.astype(F32)

    x_attn.append(jnp.concatenate(attn_all[cut:] + [proj_part.astype(BF), spare_half], axis=1))
    a_next = send_a(x_attn[1])
    y_attn = [merge(x_attn[0], a_attn)]
    b_attn = [send_b(y_attn[0])]
    t_fc = merge(y_fc, b_fc)
    c_fc = send_c(t_fc)
    a_next, b_attn[0] = after((a_next, b_attn[0]))

    y_attn.append(merge(x_attn[1], a_next))
    b_attn.append(send_b(y_attn[1]))
    t_attn = [merge(y_attn[0], b_attn[0])]
    c_attn = [send_c(t_attn[0])]
    f = reduce_rows(after(f_parts, a_next, b_attn[0]))
    b_attn[1], c_fc = after((b_attn[1], c_fc))

    t_attn.append(merge(y_attn[1], b_attn[1]))
    c_attn.append(send_c(t_attn[1]))
    grad_fc_bias = jnp.sum(d_hidden.astype(F32), axis=0)

    xhat_own, inv_own = normalize(own_tokens)
    f_gain = f * gain_one
    d_tokens = inv_own * (
        f_gain
        - jnp.mean(f_gain, axis=-1, keepdims=True)
        - xhat_own * jnp.mean(f_gain * xhat_own, axis=-1, keepdims=True)
    )
    input_grad = (d_middle + d_tokens).astype(BF)[None]

    late_active = after(active, attn_got)
    out_parts = [
        jnp.dot(block(late_active, d), out_weight, preferred_element_type=F32) for d in range(n)
    ]
    out_parts = after(out_parts, b_attn)
    output = (middle + reduce_rows(out_parts) + b_out).astype(BF)[None]

    out_mine = after(last(t_out, c_out_sum), b_attn)
    out_other = swap_core(out_mine)
    sum_out_weight = jnp.concatenate(
        [jnp.where(core == 0, out_mine, out_other), jnp.where(core == 0, out_other, out_mine)]
    ).astype(F32)
    fc_sum = last(t_fc, c_fc)
    fc_parts = jnp.concatenate(
        [pick(fc_sum, me)] + [swap(pick(fc_sum, me ^ d), d) for d in range(1, n)]
    )
    sum_fc_weight = local_call(
        functools.partial(
            unpack_kernel,
            n,
            half,
            step,
            lambda m, d: [(0, (m ^ d) * own_ff, 0, d * half, 0, own_ff)],
            1,
        ),
        [jax.ShapeDtypeStruct((own_rows, n * own_ff), F32)],
        own_rows * n * own_ff * 8,
        at,
        fc_parts,
        swap_core(fc_parts),
    )[0]

    def attn_places(m, d):
        part, base = (0, d * 3 * main) if d < cut else (1, (d - cut) * 3 * main)
        places = [
            (0, p * D + (m ^ d) * main, part, 0, base + p * main, base + (p + 1) * main)
            for p in range(3)
        ]
        if d == 0:
            base = (n - cut) * 3 * main
            places.append((1, 0, 1, 0, base, base + D))
            base += D
            places += [
                (0, p * D + n * main, 1, 0, base + p * spare, base + (p + 1) * spare)
                for p in range(3)
            ]
        return places

    d_once_sum = jnp.sum(d_once.astype(F32), axis=0)

    def vector_of(part):
        whole = jnp.zeros((D,), F32)
        whole = lax.dynamic_update_slice_in_dim(
            whole, d_once_sum[part * main : (part + 1) * main], me * main, 0
        )
        lane = 3 * main + part * spare
        return jnp.concatenate([whole[: n * main], d_once_sum[lane : lane + spare]])

    small_grads = jnp.stack(
        [
            vector_of(0),
            vector_of(2),
            jnp.sum(d_branch.astype(F32), axis=0),
            jnp.sum(f * xhat_own, axis=0),
            jnp.sum(f, axis=0),
            jnp.sum(e * xhat_two, axis=0),
            jnp.sum(e, axis=0),
            jnp.sum(own_cot.astype(F32), axis=0),
        ]
    )
    small_grads = small_grads.reshape(8, n, own_rows).transpose(1, 0, 2)
    small_own = pick(small_grads, me)
    for d in range(1, n):
        small_own = small_own + swap(pick(small_grads, me ^ d), d)
    small_own = jnp.concatenate([small_own, grad_fc_bias.reshape(-1, own_rows)], axis=0)
    small_own = small_own + swap_core(small_own)
    hop = 1
    while hop < planes:
        small_own = small_own + lax.ppermute(
            small_own, "plane", [(i, i ^ hop) for i in range(planes)]
        )
        hop *= 2
    attn_mine = [last(t, c) for t, c in zip(t_attn, c_attn)]
    attn_other = [swap_core(attn_mine[0])]
    attn_mine, attn_other, small_own, output, input_grad, sum_fc_weight, sum_out_weight = after(
        (attn_mine, attn_other, small_own, output, input_grad, sum_fc_weight, sum_out_weight)
    )
    attn_other.append(swap_core(attn_mine[1]))
    sum_attn_weight, sum_proj_weight = local_call(
        functools.partial(unpack_kernel, n, half, step, attn_places, 2),
        [
            jax.ShapeDtypeStruct((own_rows, 3 * D), F32),
            jax.ShapeDtypeStruct((own_rows, D), F32),
        ],
        own_rows * 4 * D * 8,
        at,
        *attn_mine,
        *attn_other,
    )
    s = small_own[:8]
    sum_fc_bias = small_own[8:].reshape(-1)
    return (
        output,
        input_grad,
        sum_attn_weight,
        s[0],
        s[1],
        sum_proj_weight,
        s[2],
        s[3],
        s[4],
        s[5],
        s[6],
        sum_fc_weight,
        sum_fc_bias,
        sum_out_weight,
        s[7],
    )


def solution(mesh):
    shards, reps = mesh.devices.shape
    split = jax.sharding.Mesh(
        mesh.devices.reshape(shards, reps // 2, 2), ("shard", "plane", "core")
    )
    rep = ("plane", "core")
    batch = P(rep, "shard", None)
    row, vec = P("shard", None), P("shard")
    return jax.shard_map(
        body,
        mesh=split,
        in_specs=(batch, batch, P(rep, None), row, vec, vec, row)
        + (vec,) * 5
        + (row, vec, row, vec),
        out_specs=(batch, batch, row, vec, vec, row) + (vec,) * 5 + (row, vec, row, vec),
        check_vma=False,
    )
```

```python
import functools
import math

import jax
import jax.numpy as jnp
from jax import lax
from jax.experimental import pallas as pl
from jax.experimental.pallas import tpu as pltpu
from jax.sharding import PartitionSpec as P

D = 1600
HEADS = 25
HD = 64
UNIT = 32
LANES = 128
NEG = -1e30
VEC_ROWS = 16
BF = jnp.bfloat16
F32 = jnp.float32


def dot(left, right, dims):
    return lax.dot_general(left, right, (dims, ((), ())), preferred_element_type=F32)


def rows_dot(left, right):
    return dot(left, right, ((0,), (0,)))


def cols_dot(left, right):
    return dot(left, right, ((1,), (1,)))


def normalize(values):
    center = values - jnp.mean(values, axis=-1, keepdims=True)
    spread = jnp.mean(center * center, axis=-1, keepdims=True)
    inv = lax.rsqrt(spread + 1e-05)
    return center * inv, inv


def place_blocks(info_ref, shards, units):
    b0, b1, b2, me = info_ref[0], info_ref[1], info_ref[2], info_ref[3]
    e0, e1 = b0, b0 + b1
    places = []
    for d in range(shards):
        s = jnp.bitwise_xor(me, d)
        for u in range(units):
            first = jnp.where(u < e0, 0, jnp.where(u < e1, e0, e1))
            span = jnp.where(u < e0, b0, jnp.where(u < e1, b1, b2))
            places.append((d * units + u, first * shards + s * span + (u - first)))
    return places, e0, e1


def head_lanes(tile_rows, half):
    lane = lax.broadcasted_iota(jnp.int32, (tile_rows, LANES), 1)
    return (lane < HD) if half == 0 else (lane >= HD)


def window_scores(q, k, rows, width):
    scores = cols_dot(q, k)
    row = lax.broadcasted_iota(jnp.int32, (rows, width * rows), 0)
    col = lax.broadcasted_iota(jnp.int32, (rows, width * rows), 1)
    return jnp.where(col <= row + (width - 1) * rows, scores, NEG)


def fwd_kernel(shards, units, heads, info_ref, qkv_ref, out_ref, perm, mixed):
    block = UNIT
    rows = shards * block
    main = heads * HD
    places, e0, e1 = place_blocks(info_ref, shards, units)
    for src, dst in places:
        at = pl.ds(pl.multiple_of(dst * block, block), block)
        perm[at, :] = qkv_ref[src * block : (src + 1) * block, :]

    def unit(i, carry):
        first = jnp.where(i < e0, 0, jnp.where(i < e1, e0, e1))
        q_at = pl.ds(pl.multiple_of(i * rows, rows), rows)
        for width in range(1, 5):

            @pl.when(i - first + 1 == width)
            def _():
                k_at = pl.ds(pl.multiple_of(first * rows, rows), width * rows)

                def attend(q, k, v):
                    scores = window_scores(q * BF(0.125), k, rows, width)
                    top = jnp.max(scores, axis=1, keepdims=True)
                    probs = jnp.exp(scores - top)
                    total = jnp.sum(probs, axis=1, keepdims=True)
                    return dot(probs.astype(BF), v, ((1,), (0,))) / total

                for tile in range(main // LANES):
                    lanes = slice(tile * LANES, (tile + 1) * LANES)
                    k_lanes = slice(main + lanes.start, main + lanes.stop)
                    v_lanes = slice(2 * main + lanes.start, 2 * main + lanes.stop)
                    q, k, v = perm[q_at, lanes], perm[k_at, k_lanes], perm[k_at, v_lanes]
                    low = head_lanes(rows, 0)
                    zero = jnp.zeros_like(q)
                    left = attend(jnp.where(low, q, zero), k, v)
                    right = attend(jnp.where(low, zero, q), k, v)
                    mixed[q_at, lanes] = jnp.where(low, left, right).astype(BF)
                if main % LANES:
                    lanes = main - HD
                    mixed[q_at, lanes:main] = attend(
                        perm[q_at, lanes:main],
                        perm[k_at, main + lanes : 2 * main],
                        perm[k_at, 2 * main + lanes : 3 * main],
                    ).astype(BF)
                base = 3 * main
                mixed[q_at, main : main + HD] = attend(
                    perm[q_at, base : base + HD],
                    perm[k_at, base + HD : base + 2 * HD],
                    perm[k_at, base + 2 * HD : base + 3 * HD],
                ).astype(BF)

        return carry

    lax.fori_loop(0, units, unit, 0)
    for src, dst in places:
        at = pl.ds(pl.multiple_of(dst * block, block), block)
        out_ref[src * block : (src + 1) * block, :] = mixed[at, :]


def bwd_kernel(
    shards, units, heads, info_ref, qkv_ref, dmix_ref, out_ref, perm, dperm, dq_acc, dk_acc, dv_acc
):
    block = UNIT
    rows = shards * block
    main = heads * HD
    places, e0, e1 = place_blocks(info_ref, shards, units)
    for src, dst in places:
        at = pl.ds(pl.multiple_of(dst * block, block), block)
        perm[at, :] = qkv_ref[src * block : (src + 1) * block, :]
        dperm[at, :] = dmix_ref[src * block : (src + 1) * block, :]
    dk_acc[...] = jnp.zeros_like(dk_acc)
    dv_acc[...] = jnp.zeros_like(dv_acc)

    def unit(i, carry):
        first = jnp.where(i < e0, 0, jnp.where(i < e1, e0, e1))
        q_at = pl.ds(pl.multiple_of(i * rows, rows), rows)
        for width in range(1, 5):

            @pl.when(i - first + 1 == width)
            def _():
                k_at = pl.ds(pl.multiple_of(first * rows, rows), width * rows)

                def pull(q, k, v, g):
                    q = q * BF(0.125)
                    scores = window_scores(q, k, rows, width)
                    top = jnp.max(scores, axis=1, keepdims=True)
                    probs = jnp.exp(scores - top)
                    total = jnp.sum(probs, axis=1, keepdims=True)
                    probs = probs * (1.0 / total)
                    d_probs = cols_dot(g, v)
                    delta = jnp.sum(probs * d_probs, axis=1, keepdims=True)
                    d_scores = (probs * (d_probs - delta)).astype(BF)
                    d_q = dot(d_scores, k, ((1,), (0,))) * 0.125
                    return d_q, rows_dot(d_scores, q), rows_dot(probs.astype(BF), g)

                for tile in range(main // LANES):
                    lanes = slice(tile * LANES, (tile + 1) * LANES)
                    k_lanes = slice(main + lanes.start, main + lanes.stop)
                    v_lanes = slice(2 * main + lanes.start, 2 * main + lanes.stop)
                    q, k, v = perm[q_at, lanes], perm[k_at, k_lanes], perm[k_at, v_lanes]
                    g = dperm[q_at, lanes]
                    low = head_lanes(rows, 0)
                    zero = jnp.zeros_like(q)
                    dq0, dk0, dv0 = pull(jnp.where(low, q, zero), k, v, jnp.where(low, g, zero))
                    dq1, dk1, dv1 = pull(jnp.where(low, zero, q), k, v, jnp.where(low, zero, g))
                    dq_acc[q_at, lanes] = jnp.where(low, dq0, dq1).astype(BF)
                    dk_acc[k_at, lanes] += dk0 + dk1
                    dv_acc[k_at, lanes] += dv0 + dv1
                extra = [(main, 3 * main, 3 * main + HD, 3 * main + 2 * HD)]
                if main % LANES:
                    extra.append((main - HD, main - HD, 2 * main - HD, 3 * main - HD))
                for own, q_lane, k_lane, v_lane in extra:
                    dq0, dk0, dv0 = pull(
                        perm[q_at, q_lane : q_lane + HD],
                        perm[k_at, k_lane : k_lane + HD],
                        perm[k_at, v_lane : v_lane + HD],
                        dperm[q_at, own : own + HD],
                    )
                    dq_acc[q_at, own : own + HD] = dq0.astype(BF)
                    dk_acc[k_at, own : own + HD] += dk0
                    dv_acc[k_at, own : own + HD] += dv0

        return carry

    lax.fori_loop(0, units, unit, 0)
    for src, dst in places:
        at = pl.ds(pl.multiple_of(dst * block, block), block)
        to = slice(src * block, (src + 1) * block)
        for part, acc in enumerate((dq_acc, dk_acc, dv_acc)):
            got = acc[at, :].astype(BF)
            out_ref[to, part * main : (part + 1) * main] = got[:, :main]
            lane = 3 * main + part * HD
            out_ref[to, lane : lane + HD] = got[:, main:]


def vmem_call(kernel, out_shape, scratch, cost, inputs):
    return pl.pallas_call(
        kernel,
        out_shape=out_shape,
        in_specs=[pl.BlockSpec(memory_space=pltpu.SMEM)]
        + [pl.BlockSpec(memory_space=pltpu.VMEM)] * (len(inputs) - 1),
        out_specs=pl.BlockSpec(memory_space=pltpu.VMEM),
        scratch_shapes=scratch,
        compiler_params=pltpu.CompilerParams(vmem_limit_bytes=48 << 20),
        cost_estimate=cost,
    )(*inputs)


def attention_fwd(info, qkv, shards, heads):
    total, width = qkv.shape
    units = total // (shards * UNIT)
    own = (heads + 1) * HD
    return vmem_call(
        functools.partial(fwd_kernel, shards, units, heads),
        jax.ShapeDtypeStruct((total, own), BF),
        [pltpu.VMEM((total, width), BF), pltpu.VMEM((total, own), BF)],
        pl.CostEstimate(flops=1, bytes_accessed=1, transcendentals=0),
        (info, qkv),
    )


def attention_bwd(info, qkv, d_mixed, shards, heads):
    total, width = qkv.shape
    units = total // (shards * UNIT)
    own = (heads + 1) * HD
    return vmem_call(
        functools.partial(bwd_kernel, shards, units, heads),
        jax.ShapeDtypeStruct((total, width), BF),
        [
            pltpu.VMEM((total, width), BF),
            pltpu.VMEM((total, own), BF),
            pltpu.VMEM((total, own), BF),
            pltpu.VMEM((total, own), F32),
            pltpu.VMEM((total, own), F32),
        ],
        pl.CostEstimate(flops=1, bytes_accessed=1, transcendentals=0),
        (info, qkv, d_mixed),
    )


def on_place(me, core, shards, run):
    for m in range(shards):
        for c in range(2):

            @pl.when((me == m) & (core == c))
            def _():
                run(m, c)


def attn_columns(value, j, heads):
    main = heads * HD
    first = D // main * main
    parts = [value[:, p * D + j * main : p * D + (j + 1) * main] for p in range(3)]
    parts += [value[:, p * D + first : (p + 1) * D] for p in range(3)]
    return jnp.concatenate(parts, axis=1)


def fc_columns(value, j, width):
    return value[:, j * width : (j + 1) * width]


def pack_kernel(shards, half, step, columns, at_ref, dep_ref, weight_ref, *outs):
    del dep_ref

    def run(m, c):
        outs[0][...] = columns(weight_ref, m)
        for d in range(1, shards):
            piece = columns(weight_ref.at[c * step : c * step + half], m ^ d)
            outs[d][...] = piece

    on_place(at_ref[0], at_ref[1], shards, run)


def pack_attn_kernel(shards, half, step, heads, count, at_ref, weight_ref, *refs):
    sources, outs = refs[:count], refs[count : count + shards]
    vectors, sems = refs[count + shards : 2 * count + shards], refs[2 * count + shards]
    length = vectors[0].shape[0]
    copies = [
        pltpu.make_async_copy(source, vector, sems.at[i])
        for i, (source, vector) in enumerate(zip(sources, vectors))
    ]
    for copy in copies:
        copy.start()

    def run(m, c):
        outs[0][: shards_rows(outs[0]), :] = attn_columns(weight_ref, m, heads)
        for d in range(1, shards):
            outs[d][:half, :] = attn_columns(weight_ref.at[c * step : c * step + half], m ^ d, heads)

    def shards_rows(ref):
        return ref.shape[0] - VEC_ROWS

    on_place(at_ref[0], at_ref[1], shards, run)
    for copy in copies:
        copy.wait()
    width = outs[0].shape[1]
    block = jnp.concatenate(
        [v[...].astype(F32).reshape(1, length) for v in vectors]
        + [jnp.zeros((VEC_ROWS - count, length), F32)],
        axis=0,
    )
    block = jnp.concatenate(
        [block, jnp.zeros((VEC_ROWS, width - length), F32)], axis=1
    ).astype(BF)
    for out in outs:
        out[out.shape[0] - VEC_ROWS :, :] = block


def place_attn_kernel(shards, half, step, rows, count, at_ref, *refs):
    own, mine, other = refs[0], refs[1:shards], refs[shards]
    out, vec = refs[shards + 1 :]

    def run(m, c):
        out[m * rows : (m + 1) * rows, :] = own[:rows]
        for d in range(1, shards):
            base = (m ^ d) * rows
            a, b = mine[d - 1][:half], other[d - 1]
            low, high = (a, b) if c == 0 else (b, a)
            out[base : base + step, :] = low[:step]
            out[base + step : base + rows, :] = high
        for j in range(shards):
            ref, at = (own, rows) if j == m else (mine[(j ^ m) - 1], half)
            vec[:, j * rows : (j + 1) * rows] = ref[at : at + VEC_ROWS, :rows].astype(F32)[:count]

    on_place(at_ref[0], at_ref[1], shards, run)


def place_kernel(shards, half, step, rows, at_ref, *refs):
    own, mine, other, out = refs[0], refs[1:shards], refs[shards], refs[shards + 1]

    def run(m, c):
        out[m * rows : (m + 1) * rows, :] = own[...]
        for d in range(1, shards):
            base = (m ^ d) * rows
            low, high = (mine[d - 1][...], other[d - 1]) if c == 0 else (other[d - 1], mine[d - 1][...])
            out[base : base + step, :] = low[:step]
            out[base + step : base + rows, :] = high

    on_place(at_ref[0], at_ref[1], shards, run)


def pack_part_kernel(shards, length, stride, columns, at_ref, weight_ref, *outs):
    part = pl.ds(pl.multiple_of(at_ref[2] * stride, 16), length)
    for m in range(shards):

        @pl.when(at_ref[0] == m)
        def _():
            outs[0][...] = columns(weight_ref, m)
            for d in range(1, shards):
                outs[d][...] = columns(weight_ref.at[part], m ^ d)


def place_part_kernel(shards, length, stride, rows, at_ref, own, mine, near, across, out):
    me, q = at_ref[0], at_ref[2]
    out[pl.ds(pl.multiple_of(me * rows, 16), rows), :] = own[...]
    size = (shards - 1) * length
    for d in range(1, shards):
        base = jnp.bitwise_xor(me, d) * rows
        for flip, ref, first in ((0, mine, 0), (2, near, 0), (1, across, 0), (3, across, size)):
            to = base + jnp.bitwise_xor(q, flip) * stride
            row = first + (d - 1) * length
            out[pl.ds(pl.multiple_of(to, 16), length), :] = ref[row : row + length, :]


def unpack_kernel(shards, half, step, places, count, at_ref, *refs):
    mine, other, outs = refs[:count], refs[count : 2 * count], refs[2 * count :]

    def run(m, c):
        for d in range(shards):
            for index, where, part, row, low, high in places(m, d):
                out, width = outs[index], high - low
                a = mine[part][row : row + half, low:high]
                b = other[part][row : row + half, low:high]
                first, second = (a, b) if c == 0 else (b, a)
                out[:step, where : where + width] = first[:step].astype(F32)
                out[step:, where : where + width] = second.astype(F32)

    on_place(at_ref[0], at_ref[1], shards, run)


def spread_kernel(shards, places, at_ref, *refs):
    parts, outs = refs[: shards + 2], refs[shards + 2 :]
    for m in range(shards):

        @pl.when(at_ref[0] == m)
        def _():
            for d in range(shards):
                for index, where, part, low, high in places(m, d):
                    values = parts[part][:, low:high].astype(F32)
                    outs[index][:, where : where + high - low] = values


def local_call(kernel, out_shape, cost_bytes, at, *inputs, anywhere=(), scratch=()):
    vmem = pl.BlockSpec(memory_space=pltpu.VMEM)
    hbm = pl.BlockSpec(memory_space=pltpu.HBM)
    specs = [hbm if i in anywhere else vmem for i in range(len(inputs))]
    return pl.pallas_call(
        kernel,
        out_shape=out_shape,
        in_specs=[pl.BlockSpec(memory_space=pltpu.SMEM)] + specs,
        out_specs=jax.tree.map(lambda _: vmem, out_shape),
        scratch_shapes=list(scratch),
        compiler_params=pltpu.CompilerParams(vmem_limit_bytes=48 << 20),
        cost_estimate=pl.CostEstimate(flops=1, bytes_accessed=1, transcendentals=0),
    )(at, *inputs)


def body(
    tokens,
    cotangent,
    lengths,
    attn_weight,
    query_bias,
    value_bias,
    proj_weight,
    proj_bias,
    ln1_gain,
    ln1_bias,
    ln2_gain,
    ln2_bias,
    fc_weight,
    fc_bias,
    out_weight,
    out_bias,
):
    n = lax.axis_size("shard")
    planes = lax.axis_size("plane")
    me = lax.axis_index("shard")
    core = lax.axis_index("core")
    heads = (HEADS - 1) // n
    main = heads * HD
    spare = D - n * main
    own_rows = attn_weight.shape[0]
    own_ff = fc_bias.shape[0]
    rows = tokens.shape[1]
    half = -(-own_rows // 32) * 16
    step = own_rows - half
    quarter = lax.axis_index("plane") % 2 * 2 + core
    at = jnp.stack([me, core, quarter]).astype(jnp.int32)

    def swap(value, d):
        return lax.ppermute(value, "shard", [(i, i ^ d) for i in range(n)])

    def swap_plane(value):
        return lax.ppermute(value, "plane", [(i, i ^ 1) for i in range(planes)])

    def swap_core(value):
        return lax.ppermute(value, "core", [(0, 1), (1, 0)])

    def gather_near(value):
        if n != 4:
            return [swap(value, d) for d in range(1, n)]
        return [swap(value, 1), swap(value, 2)]

    def gather_far(value, near):
        if n != 4:
            return [value] + near
        one, two = near
        cut = value.shape[0] // 32 * 16
        three = jnp.concatenate([swap(one[:cut], 2), swap(two[cut:], 1)], axis=0)
        return [value, one, two, three]

    def gather(value):
        return gather_far(value, gather_near(value))

    def pick(stacked, index):
        return lax.dynamic_index_in_dim(stacked, index, 0, keepdims=False)

    def natural(pieces):
        stacked = jnp.stack(pieces)
        return [pick(stacked, me ^ j) for j in range(n)]

    def after(value, *deps):
        return lax.optimization_barrier((value, deps))[0]

    def block(value, d):
        return value[d * rows : (d + 1) * rows]

    def place(own, mine):
        other = swap_core(jnp.stack(mine))
        return local_call(
            functools.partial(place_kernel, n, half, step, own_rows),
            jax.ShapeDtypeStruct((n * own_rows, own.shape[1]), BF),
            n * own.size * 4,
            at,
            own,
            *mine,
            other,
        )

    def pack(weight, columns, width, dep):
        shapes = [jax.ShapeDtypeStruct((own_rows, width), BF)]
        shapes += [jax.ShapeDtypeStruct((half, width), BF)] * (n - 1)
        return local_call(
            functools.partial(pack_kernel, n, half, step, columns),
            shapes,
            weight.size * 2,
            at,
            dep,
            weight,
            anywhere=(0,),
        )

    def reduce_rows(parts, *deps):
        got = after([swap(parts[d].astype(BF), d) for d in range(1, n)], *deps)
        total = parts[0].astype(F32)
        for part in got:
            total = total + part.astype(F32)
        return total

    def core_halves(parts):
        keep = lax.dynamic_slice_in_dim(parts, core * step, half, 1)
        give = lax.dynamic_slice_in_dim(parts, (1 - core) * step, half, 1)
        return (keep.astype(F32) + swap_core(give).astype(F32)).astype(BF)

    vectors = (
        query_bias, value_bias, proj_bias, ln1_gain, ln1_bias, ln2_gain, ln2_bias, out_bias
    )
    tokens_near = gather_near(tokens[0])
    attn_width = 3 * (main + spare)
    attn_sent = local_call(
        functools.partial(pack_attn_kernel, n, half, step, heads, len(vectors)),
        [jax.ShapeDtypeStruct((own_rows + VEC_ROWS, attn_width), BF)]
        + [jax.ShapeDtypeStruct((half + VEC_ROWS, attn_width), BF)] * (n - 1),
        attn_weight.size * 2,
        at,
        attn_weight,
        *vectors,
        anywhere=range(1, len(vectors) + 1),
        scratch=[pltpu.VMEM((own_rows,), BF)] * len(vectors)
        + [pltpu.SemaphoreType.DMA((len(vectors),))],
    )
    attn_got = [swap(attn_sent[d], d) for d in range(1, n)]
    attn_got, tokens_near = after((attn_got, tokens_near))
    attn_other = swap_core(jnp.stack([piece[:half] for piece in attn_got]))
    tokens_parts = gather_far(tokens[0], tokens_near)
    w_attn, small = local_call(
        functools.partial(place_attn_kernel, n, half, step, own_rows, len(vectors)),
        [
            jax.ShapeDtypeStruct((D, attn_width), BF),
            jax.ShapeDtypeStruct((len(vectors), D), F32),
        ],
        D * attn_width * 4,
        at,
        attn_sent[0],
        *attn_got,
        attn_other,
    )
    b_query, b_value, b_proj, gain_one, bias_one, gain_two, bias_two, b_out = [
        small[i] for i in range(8)
    ]

    def my_columns(vector):
        return lax.dynamic_slice_in_dim(vector, me * main, main, 0), vector[n * main :]

    q_main, q_spare = my_columns(b_query)
    v_main, v_spare = my_columns(b_value)
    qkv_bias = jnp.concatenate(
        [q_main, jnp.zeros_like(q_main), v_main, q_spare, jnp.zeros_like(q_spare), v_spare]
    )

    group_tokens = jnp.concatenate(tokens_parts, axis=0)
    proj_half = lax.dynamic_slice_in_dim(after(proj_weight, attn_got), core * step, half, 0)
    proj_near = gather_near(proj_half)
    own_cot = cotangent[0]
    cot_all = lax.all_gather(after(own_cot, attn_got, tokens_parts), "shard", axis=0, tiled=True)
    late_fc = after(fc_weight, attn_got)
    stride = own_rows // 64 * 16
    length = own_rows - 3 * stride
    by_parts = own_rows % 16 == 0 and stride > 0 and planes % 2 == 0
    if by_parts:
        fc_sent = local_call(
            functools.partial(
                pack_part_kernel, n, length, stride, lambda ref, j: fc_columns(ref, j, own_ff)
            ),
            [jax.ShapeDtypeStruct((own_rows, own_ff), BF)]
            + [jax.ShapeDtypeStruct((length, own_ff), BF)] * (n - 1),
            fc_weight.size * 2,
            at,
            late_fc,
        )
    else:
        fc_sent = pack(late_fc, lambda ref, j: fc_columns(ref, j, own_ff), own_ff, lengths)
    xhat_one, _ = normalize(group_tokens.astype(F32))
    normed = (xhat_one * gain_one + bias_one).astype(BF)
    qkv = (jnp.dot(normed, w_attn, preferred_element_type=F32) + qkv_bias).astype(BF)
    qkv, proj_near, fc_sent = after((qkv, proj_near, fc_sent))
    proj_parts = gather_far(proj_half, proj_near)
    fc_got = [swap(fc_sent[d], d) for d in range(1, n)]
    info = jnp.concatenate([lengths[0], me.astype(jnp.int32)[None]])
    mixed_heads = attention_fwd(info, qkv, n, heads)
    mixed_heads, proj_parts, fc_got = after((mixed_heads, proj_parts, fc_got))
    if by_parts:
        fc_mine = jnp.concatenate(fc_got)
        fc_near = swap_plane(fc_mine)
    got = [block(mixed_heads, 0)[:, :main]] + [
        swap(block(mixed_heads, d)[:, :main], d) for d in range(1, n)
    ]
    w_proj = place(proj_weight, proj_parts[1:])
    got, w_proj, cot_all = after((got, w_proj, cot_all))
    mixed_low = jnp.concatenate(natural(got) + [block(mixed_heads, 0)[:, main:]], axis=1)
    own_tokens = tokens[0].astype(F32)
    middle = own_tokens + jnp.dot(mixed_low, w_proj, preferred_element_type=F32) + b_proj
    xhat_two, inv_two = normalize(middle)
    own_normed_two = (xhat_two * gain_two + bias_two).astype(BF)
    normed_near = gather_near(own_normed_two)
    if by_parts:
        w_fc = local_call(
            functools.partial(place_part_kernel, n, length, stride, own_rows),
            jax.ShapeDtypeStruct((D, own_ff), BF),
            D * own_ff * 4,
            at,
            fc_sent[0],
            fc_mine,
            fc_near,
            swap_core(jnp.concatenate(after([fc_mine, fc_near], own_normed_two))),
        )
    else:
        w_fc = place(fc_sent[0], fc_got)
    cot_parts = [own_cot] + [
        lax.dynamic_slice_in_dim(cot_all, (me ^ d) * rows, rows, 0) for d in range(1, n)
    ]
    group_cot = jnp.concatenate(cot_parts, axis=0)
    d_active = cols_dot(group_cot, out_weight).astype(BF)
    normed_near, d_active = after((normed_near, d_active))
    normed_parts = gather_far(own_normed_two, normed_near)
    normed_two = jnp.concatenate(normed_parts, axis=0)

    def feed(part):
        hidden = jnp.dot(part, w_fc, preferred_element_type=F32) + fc_bias.astype(F32)
        inner = jnp.tanh(0.7978845608028654 * (hidden + 0.044715 * hidden * hidden * hidden))
        slope = 0.5 * (1.0 + inner) + 0.5 * hidden * (1.0 - inner * inner) * (
            0.7978845608028654 * (1.0 + 3 * 0.044715 * hidden * hidden)
        )
        return (0.5 * hidden * (1.0 + inner)).astype(BF), slope.astype(BF)

    fed = [feed(part) for part in normed_parts]
    active_parts = [a for a, _ in fed]
    active = jnp.concatenate(active_parts, axis=0)

    d_hidden_parts = [
        (block(d_active, d).astype(F32) * slope.astype(F32)).astype(BF)
        for d, (_, slope) in enumerate(fed)
    ]
    d_hidden = jnp.concatenate(d_hidden_parts, axis=0)
    e_parts = [cols_dot(part, w_fc) for part in d_hidden_parts]
    e_got = [swap(e_parts[d].astype(BF), d) for d in range(1, n)]
    late_active, late_cot = after((active, group_cot), e_parts)
    grad_out = rows_dot(late_active, late_cot).astype(BF)
    sum_out_weight = lax.psum(grad_out, ("plane", "core"))
    late_normed, late_d = after((normed_two, d_hidden), grad_out, e_got[0])
    grad_fc = rows_dot(late_normed, late_d).astype(BF).reshape(n, own_rows, own_ff)
    e_got, grad_fc = after((e_got, grad_fc))

    e = e_parts[0] + sum(part.astype(F32) for part in e_got)
    e_gain = e * gain_two
    d_middle = own_cot.astype(F32) + inv_two * (
        e_gain
        - jnp.mean(e_gain, axis=-1, keepdims=True)
        - xhat_two * jnp.mean(e_gain * xhat_two, axis=-1, keepdims=True)
    )
    d_branch = d_middle.astype(BF)
    d_mixed = cols_dot(d_branch, w_proj).astype(BF)
    for_heads = jnp.stack([d_mixed[:, j * main : (j + 1) * main] for j in range(n)])
    spare_cols = d_mixed[:, n * main :]
    dmix_parts = [jnp.concatenate([pick(for_heads, me), spare_cols], axis=1)] + [
        swap(jnp.concatenate([pick(for_heads, me ^ d), spare_cols], axis=1), d)
        for d in range(1, n)
    ]
    fc_halves = core_halves(grad_fc)
    grad_proj = rows_dot(mixed_low, d_branch).astype(BF).reshape(n, own_rows, D)
    proj_halves = core_halves(grad_proj)
    dmix_parts, fc_halves, proj_halves = after((dmix_parts, fc_halves, proj_halves))
    fc_sum = lax.psum(fc_halves.reshape(n * half, own_ff), "plane").reshape(n, half, own_ff)

    proj_got = [swap(pick(proj_halves, me ^ d), d) for d in range(1, n)]
    d_qkv = attention_bwd(info, qkv, jnp.concatenate(dmix_parts, axis=0), n, heads)
    d_qkv, proj_got, sum_out_weight = after((d_qkv, proj_got, sum_out_weight))

    grad_main = rows_dot(normed, d_qkv[:, : 3 * main]).astype(BF).reshape(n, own_rows, 3 * main)
    attn_got = [swap(pick(grad_main, me ^ d), d) for d in range(1, n)]
    grad_spare = rows_dot(normed, d_qkv[:, 3 * main :]).astype(BF).reshape(n, own_rows, 3 * spare)
    grad_spare = pick(grad_spare, me)
    proj_part = pick(proj_halves, me).astype(F32) + sum(part.astype(F32) for part in proj_got)
    proj_part = proj_part.astype(BF)
    proj_rows = jnp.where(
        core == 0,
        jnp.concatenate([proj_part[:step], jnp.zeros((half, D), BF)]),
        jnp.concatenate([jnp.zeros((step, D), BF), proj_part]),
    )
    counted = (lax.broadcasted_iota(jnp.int32, (n * rows, 1), 0) < rows) | (
        lax.broadcasted_iota(jnp.int32, (1, d_qkv.shape[1]), 1) < 3 * main
    )
    d_once = jnp.where(counted, after(d_qkv, grad_main, grad_spare), BF(0))
    f_parts = [cols_dot(block(d_once, d), w_attn) for d in range(n)]
    sum_out_weight = after(sum_out_weight, f_parts).astype(F32)
    attn_got, grad_spare, proj_rows, f_parts, sum_out_weight = after(
        (attn_got, grad_spare, proj_rows, f_parts, sum_out_weight)
    )

    attn_parts = (pick(grad_main, me), *attn_got, grad_spare, proj_rows)
    attn_sum = lax.psum(attn_parts, ("plane", "core"))
    f_got = [swap(f_parts[d].astype(BF), d) for d in range(1, n)]
    late_active = after(active, attn_got)
    out_parts = [
        jnp.dot(block(late_active, d), out_weight, preferred_element_type=F32) for d in range(n)
    ]
    f_got, out_parts = after((f_got, out_parts))
    out_got = [swap(out_parts[d].astype(BF), d) for d in range(1, n)]
    f = f_parts[0] + sum(part.astype(F32) for part in f_got)
    grad_fc_bias = jnp.sum(d_hidden.astype(F32), axis=0)
    out_got, fc_sum = after((out_got, fc_sum))
    output = middle + out_parts[0] + sum(part.astype(F32) for part in out_got) + b_out
    output = output.astype(BF)[None]

    xhat_own, inv_own = normalize(own_tokens)
    f_gain = f * gain_one
    d_tokens = inv_own * (
        f_gain
        - jnp.mean(f_gain, axis=-1, keepdims=True)
        - xhat_own * jnp.mean(f_gain * xhat_own, axis=-1, keepdims=True)
    )
    input_grad = (d_middle + d_tokens).astype(BF)[None]

    fc_parts = jnp.concatenate(
        [pick(fc_sum, me)] + [swap(pick(fc_sum, me ^ d), d) for d in range(1, n)]
    )
    sum_fc_weight = local_call(
        functools.partial(
            unpack_kernel,
            n,
            half,
            step,
            lambda m, d: [(0, (m ^ d) * own_ff, 0, d * half, 0, own_ff)],
            1,
        ),
        [jax.ShapeDtypeStruct((own_rows, n * own_ff), F32)],
        own_rows * n * own_ff * 8,
        at,
        fc_parts,
        swap_core(fc_parts),
    )[0]

    def attn_places(m, d):
        places = [(0, p * D + (m ^ d) * main, d, p * main, (p + 1) * main) for p in range(3)]
        if d == 0:
            places += [
                (0, p * D + n * main, n, p * spare, (p + 1) * spare) for p in range(3)
            ]
            places.append((1, 0, n + 1, 0, D))
        return places

    d_once_sum = jnp.sum(d_once.astype(F32), axis=0)

    def vector_of(part):
        whole = jnp.zeros((D,), F32)
        whole = lax.dynamic_update_slice_in_dim(
            whole, d_once_sum[part * main : (part + 1) * main], me * main, 0
        )
        lane = 3 * main + part * spare
        return jnp.concatenate([whole[: n * main], d_once_sum[lane : lane + spare]])

    small_grads = jnp.stack(
        [
            vector_of(0),
            vector_of(2),
            jnp.sum(d_branch.astype(F32), axis=0),
            jnp.sum(f * xhat_own, axis=0),
            jnp.sum(f, axis=0),
            jnp.sum(e * xhat_two, axis=0),
            jnp.sum(e, axis=0),
            jnp.sum(own_cot.astype(F32), axis=0),
        ]
    )
    small_grads = small_grads.reshape(8, n, own_rows).transpose(1, 0, 2)
    small_own = pick(small_grads, me)
    for d in range(1, n):
        small_own = small_own + swap(pick(small_grads, me ^ d), d)
    small_own = jnp.concatenate([small_own, grad_fc_bias.reshape(-1, own_rows)], axis=0)
    small_own = small_own + swap_core(small_own)
    hop = 1
    while hop < planes:
        small_own = small_own + lax.ppermute(
            small_own, "plane", [(i, i ^ hop) for i in range(planes)]
        )
        hop *= 2
    attn_sum, small_own, output, input_grad, sum_fc_weight = after(
        (attn_sum, small_own, output, input_grad, sum_fc_weight)
    )
    sum_attn_weight, sum_proj_weight = local_call(
        functools.partial(spread_kernel, n, attn_places),
        [
            jax.ShapeDtypeStruct((own_rows, 3 * D), F32),
            jax.ShapeDtypeStruct((own_rows, D), F32),
        ],
        own_rows * 4 * D * 8,
        at,
        *attn_sum,
    )
    s = small_own[:8]
    sum_fc_bias = small_own[8:].reshape(-1)
    return (
        output,
        input_grad,
        sum_attn_weight,
        s[0],
        s[1],
        sum_proj_weight,
        s[2],
        s[3],
        s[4],
        s[5],
        s[6],
        sum_fc_weight,
        sum_fc_bias,
        sum_out_weight,
        s[7],
    )


def solution(mesh):
    shards, reps = mesh.devices.shape
    split = jax.sharding.Mesh(
        mesh.devices.reshape(shards, reps // 2, 2), ("shard", "plane", "core")
    )
    rep = ("plane", "core")
    batch = P(rep, "shard", None)
    row, vec = P("shard", None), P("shard")
    return jax.shard_map(
        body,
        mesh=split,
        in_specs=(batch, batch, P(rep, None), row, vec, vec, row)
        + (vec,) * 5
        + (row, vec, row, vec),
        out_specs=(batch, batch, row, vec, vec, row) + (vec,) * 5 + (row, vec, row, vec),
        check_vma=False,
    )
```

```python
import functools
import math

import jax
import jax.numpy as jnp
from jax import lax
from jax.experimental import pallas as pl
from jax.experimental.pallas import tpu as pltpu
from jax.sharding import PartitionSpec as P

D = 1600
HEADS = 25
HD = 64
UNIT = 32
LANES = 128
NEG = -1e30
VEC_ROWS = 16
BF = jnp.bfloat16
F32 = jnp.float32


def dot(left, right, dims):
    return lax.dot_general(left, right, (dims, ((), ())), preferred_element_type=F32)


def rows_dot(left, right):
    return dot(left, right, ((0,), (0,)))


def cols_dot(left, right):
    return dot(left, right, ((1,), (1,)))


def normalize(values):
    center = values - jnp.mean(values, axis=-1, keepdims=True)
    spread = jnp.mean(center * center, axis=-1, keepdims=True)
    inv = lax.rsqrt(spread + 1e-05)
    return center * inv, inv


def place_blocks(info_ref, shards, units):
    b0, b1, b2, me = info_ref[0], info_ref[1], info_ref[2], info_ref[3]
    e0, e1 = b0, b0 + b1
    places = []
    for d in range(shards):
        s = jnp.bitwise_xor(me, d)
        for u in range(units):
            first = jnp.where(u < e0, 0, jnp.where(u < e1, e0, e1))
            span = jnp.where(u < e0, b0, jnp.where(u < e1, b1, b2))
            places.append((d * units + u, first * shards + s * span + (u - first)))
    return places, e0, e1


def head_lanes(tile_rows, half):
    lane = lax.broadcasted_iota(jnp.int32, (tile_rows, LANES), 1)
    return (lane < HD) if half == 0 else (lane >= HD)


def window_scores(q, k, rows, width):
    scores = cols_dot(q, k)
    row = lax.broadcasted_iota(jnp.int32, (rows, width * rows), 0)
    col = lax.broadcasted_iota(jnp.int32, (rows, width * rows), 1)
    return jnp.where(col <= row + (width - 1) * rows, scores, NEG)


def fwd_kernel(shards, units, heads, info_ref, qkv_ref, out_ref, perm, mixed):
    block = UNIT
    rows = shards * block
    main = heads * HD
    places, e0, e1 = place_blocks(info_ref, shards, units)
    for src, dst in places:
        at = pl.ds(pl.multiple_of(dst * block, block), block)
        perm[at, :] = qkv_ref[src * block : (src + 1) * block, :]

    def unit(i, carry):
        first = jnp.where(i < e0, 0, jnp.where(i < e1, e0, e1))
        q_at = pl.ds(pl.multiple_of(i * rows, rows), rows)
        for width in range(1, 5):

            @pl.when(i - first + 1 == width)
            def _():
                k_at = pl.ds(pl.multiple_of(first * rows, rows), width * rows)

                def attend(q, k, v):
                    scores = window_scores(q * BF(0.125), k, rows, width)
                    top = jnp.max(scores, axis=1, keepdims=True)
                    probs = jnp.exp(scores - top)
                    total = jnp.sum(probs, axis=1, keepdims=True)
                    return dot(probs.astype(BF), v, ((1,), (0,))) / total

                for tile in range(main // LANES):
                    lanes = slice(tile * LANES, (tile + 1) * LANES)
                    k_lanes = slice(main + lanes.start, main + lanes.stop)
                    v_lanes = slice(2 * main + lanes.start, 2 * main + lanes.stop)
                    q, k, v = perm[q_at, lanes], perm[k_at, k_lanes], perm[k_at, v_lanes]
                    low = head_lanes(rows, 0)
                    zero = jnp.zeros_like(q)
                    left = attend(jnp.where(low, q, zero), k, v)
                    right = attend(jnp.where(low, zero, q), k, v)
                    mixed[q_at, lanes] = jnp.where(low, left, right).astype(BF)
                if main % LANES:
                    lanes = main - HD
                    mixed[q_at, lanes:main] = attend(
                        perm[q_at, lanes:main],
                        perm[k_at, main + lanes : 2 * main],
                        perm[k_at, 2 * main + lanes : 3 * main],
                    ).astype(BF)
                base = 3 * main
                mixed[q_at, main : main + HD] = attend(
                    perm[q_at, base : base + HD],
                    perm[k_at, base + HD : base + 2 * HD],
                    perm[k_at, base + 2 * HD : base + 3 * HD],
                ).astype(BF)

        return carry

    lax.fori_loop(0, units, unit, 0)
    for src, dst in places:
        at = pl.ds(pl.multiple_of(dst * block, block), block)
        out_ref[src * block : (src + 1) * block, :] = mixed[at, :]


def bwd_kernel(
    shards, units, heads, info_ref, qkv_ref, dmix_ref, out_ref, perm, dperm, dq_acc, dk_acc, dv_acc
):
    block = UNIT
    rows = shards * block
    main = heads * HD
    places, e0, e1 = place_blocks(info_ref, shards, units)
    for src, dst in places:
        at = pl.ds(pl.multiple_of(dst * block, block), block)
        perm[at, :] = qkv_ref[src * block : (src + 1) * block, :]
        dperm[at, :] = dmix_ref[src * block : (src + 1) * block, :]
    dk_acc[...] = jnp.zeros_like(dk_acc)
    dv_acc[...] = jnp.zeros_like(dv_acc)

    def unit(i, carry):
        first = jnp.where(i < e0, 0, jnp.where(i < e1, e0, e1))
        q_at = pl.ds(pl.multiple_of(i * rows, rows), rows)
        for width in range(1, 5):

            @pl.when(i - first + 1 == width)
            def _():
                k_at = pl.ds(pl.multiple_of(first * rows, rows), width * rows)

                def pull(q, k, v, g):
                    q = q * BF(0.125)
                    scores = window_scores(q, k, rows, width)
                    top = jnp.max(scores, axis=1, keepdims=True)
                    probs = jnp.exp(scores - top)
                    total = jnp.sum(probs, axis=1, keepdims=True)
                    probs = probs * (1.0 / total)
                    d_probs = cols_dot(g, v)
                    delta = jnp.sum(probs * d_probs, axis=1, keepdims=True)
                    d_scores = (probs * (d_probs - delta)).astype(BF)
                    d_q = dot(d_scores, k, ((1,), (0,))) * 0.125
                    return d_q, rows_dot(d_scores, q), rows_dot(probs.astype(BF), g)

                for tile in range(main // LANES):
                    lanes = slice(tile * LANES, (tile + 1) * LANES)
                    k_lanes = slice(main + lanes.start, main + lanes.stop)
                    v_lanes = slice(2 * main + lanes.start, 2 * main + lanes.stop)
                    q, k, v = perm[q_at, lanes], perm[k_at, k_lanes], perm[k_at, v_lanes]
                    g = dperm[q_at, lanes]
                    low = head_lanes(rows, 0)
                    zero = jnp.zeros_like(q)
                    dq0, dk0, dv0 = pull(jnp.where(low, q, zero), k, v, jnp.where(low, g, zero))
                    dq1, dk1, dv1 = pull(jnp.where(low, zero, q), k, v, jnp.where(low, zero, g))
                    dq_acc[q_at, lanes] = jnp.where(low, dq0, dq1).astype(BF)
                    dk_acc[k_at, lanes] += dk0 + dk1
                    dv_acc[k_at, lanes] += dv0 + dv1
                extra = [(main, 3 * main, 3 * main + HD, 3 * main + 2 * HD)]
                if main % LANES:
                    extra.append((main - HD, main - HD, 2 * main - HD, 3 * main - HD))
                for own, q_lane, k_lane, v_lane in extra:
                    dq0, dk0, dv0 = pull(
                        perm[q_at, q_lane : q_lane + HD],
                        perm[k_at, k_lane : k_lane + HD],
                        perm[k_at, v_lane : v_lane + HD],
                        dperm[q_at, own : own + HD],
                    )
                    dq_acc[q_at, own : own + HD] = dq0.astype(BF)
                    dk_acc[k_at, own : own + HD] += dk0
                    dv_acc[k_at, own : own + HD] += dv0

        return carry

    lax.fori_loop(0, units, unit, 0)
    for src, dst in places:
        at = pl.ds(pl.multiple_of(dst * block, block), block)
        to = slice(src * block, (src + 1) * block)
        for part, acc in enumerate((dq_acc, dk_acc, dv_acc)):
            got = acc[at, :].astype(BF)
            out_ref[to, part * main : (part + 1) * main] = got[:, :main]
            lane = 3 * main + part * HD
            out_ref[to, lane : lane + HD] = got[:, main:]


def vmem_call(kernel, out_shape, scratch, cost, inputs):
    return pl.pallas_call(
        kernel,
        out_shape=out_shape,
        in_specs=[pl.BlockSpec(memory_space=pltpu.SMEM)]
        + [pl.BlockSpec(memory_space=pltpu.VMEM)] * (len(inputs) - 1),
        out_specs=pl.BlockSpec(memory_space=pltpu.VMEM),
        scratch_shapes=scratch,
        compiler_params=pltpu.CompilerParams(vmem_limit_bytes=48 << 20),
        cost_estimate=cost,
    )(*inputs)


def attention_fwd(info, qkv, shards, heads):
    total, width = qkv.shape
    units = total // (shards * UNIT)
    own = (heads + 1) * HD
    return vmem_call(
        functools.partial(fwd_kernel, shards, units, heads),
        jax.ShapeDtypeStruct((total, own), BF),
        [pltpu.VMEM((total, width), BF), pltpu.VMEM((total, own), BF)],
        pl.CostEstimate(flops=1, bytes_accessed=1, transcendentals=0),
        (info, qkv),
    )


def attention_bwd(info, qkv, d_mixed, shards, heads):
    total, width = qkv.shape
    units = total // (shards * UNIT)
    own = (heads + 1) * HD
    return vmem_call(
        functools.partial(bwd_kernel, shards, units, heads),
        jax.ShapeDtypeStruct((total, width), BF),
        [
            pltpu.VMEM((total, width), BF),
            pltpu.VMEM((total, own), BF),
            pltpu.VMEM((total, own), BF),
            pltpu.VMEM((total, own), F32),
            pltpu.VMEM((total, own), F32),
        ],
        pl.CostEstimate(flops=1, bytes_accessed=1, transcendentals=0),
        (info, qkv, d_mixed),
    )


def on_place(me, core, shards, run):
    for m in range(shards):
        for c in range(2):

            @pl.when((me == m) & (core == c))
            def _():
                run(m, c)


def attn_columns(value, j, heads):
    main = heads * HD
    first = D // main * main
    parts = [value[:, p * D + j * main : p * D + (j + 1) * main] for p in range(3)]
    parts += [value[:, p * D + first : (p + 1) * D] for p in range(3)]
    return jnp.concatenate(parts, axis=1)


def fc_columns(value, j, width):
    return value[:, j * width : (j + 1) * width]


def pack_kernel(shards, half, step, columns, at_ref, dep_ref, weight_ref, *outs):
    del dep_ref

    def run(m, c):
        outs[0][...] = columns(weight_ref, m)
        for d in range(1, shards):
            piece = columns(weight_ref.at[c * step : c * step + half], m ^ d)
            outs[d][...] = piece

    on_place(at_ref[0], at_ref[1], shards, run)


def pack_attn_kernel(shards, half, step, heads, count, at_ref, weight_ref, *refs):
    sources, outs = refs[:count], refs[count : count + shards]
    vectors, sems = refs[count + shards : 2 * count + shards], refs[2 * count + shards]
    length = vectors[0].shape[0]
    copies = [
        pltpu.make_async_copy(source, vector, sems.at[i])
        for i, (source, vector) in enumerate(zip(sources, vectors))
    ]
    for copy in copies:
        copy.start()

    def run(m, c):
        outs[0][: shards_rows(outs[0]), :] = attn_columns(weight_ref, m, heads)
        for d in range(1, shards):
            outs[d][:half, :] = attn_columns(weight_ref.at[c * step : c * step + half], m ^ d, heads)

    def shards_rows(ref):
        return ref.shape[0] - VEC_ROWS

    on_place(at_ref[0], at_ref[1], shards, run)
    for copy in copies:
        copy.wait()
    width = outs[0].shape[1]
    block = jnp.concatenate(
        [v[...].astype(F32).reshape(1, length) for v in vectors]
        + [jnp.zeros((VEC_ROWS - count, length), F32)],
        axis=0,
    )
    block = jnp.concatenate(
        [block, jnp.zeros((VEC_ROWS, width - length), F32)], axis=1
    ).astype(BF)
    for out in outs:
        out[out.shape[0] - VEC_ROWS :, :] = block


def place_attn_kernel(shards, half, step, rows, count, at_ref, *refs):
    own, mine, other = refs[0], refs[1:shards], refs[shards]
    out, vec = refs[shards + 1 :]

    def run(m, c):
        out[m * rows : (m + 1) * rows, :] = own[:rows]
        for d in range(1, shards):
            base = (m ^ d) * rows
            a, b = mine[d - 1][:half], other[d - 1]
            low, high = (a, b) if c == 0 else (b, a)
            out[base : base + step, :] = low[:step]
            out[base + step : base + rows, :] = high
        for j in range(shards):
            ref, at = (own, rows) if j == m else (mine[(j ^ m) - 1], half)
            vec[:, j * rows : (j + 1) * rows] = ref[at : at + VEC_ROWS, :rows].astype(F32)[:count]

    on_place(at_ref[0], at_ref[1], shards, run)


def place_kernel(shards, half, step, rows, at_ref, *refs):
    own, mine, other, out = refs[0], refs[1:shards], refs[shards], refs[shards + 1]

    def run(m, c):
        out[m * rows : (m + 1) * rows, :] = own[...]
        for d in range(1, shards):
            base = (m ^ d) * rows
            low, high = (mine[d - 1][...], other[d - 1]) if c == 0 else (other[d - 1], mine[d - 1][...])
            out[base : base + step, :] = low[:step]
            out[base + step : base + rows, :] = high

    on_place(at_ref[0], at_ref[1], shards, run)


def pack_part_kernel(shards, length, stride, columns, at_ref, weight_ref, *outs):
    part = pl.ds(pl.multiple_of(at_ref[2] * stride, 16), length)
    for m in range(shards):

        @pl.when(at_ref[0] == m)
        def _():
            outs[0][...] = columns(weight_ref, m)
            for d in range(1, shards):
                outs[d][...] = columns(weight_ref.at[part], m ^ d)


def place_part_kernel(shards, length, stride, rows, at_ref, own, mine, near, across, out):
    me, q = at_ref[0], at_ref[2]
    out[pl.ds(pl.multiple_of(me * rows, 16), rows), :] = own[...]
    size = (shards - 1) * length
    for d in range(1, shards):
        base = jnp.bitwise_xor(me, d) * rows
        for flip, ref, first in ((0, mine, 0), (2, near, 0), (1, across, 0), (3, across, size)):
            to = base + jnp.bitwise_xor(q, flip) * stride
            row = first + (d - 1) * length
            out[pl.ds(pl.multiple_of(to, 16), length), :] = ref[row : row + length, :]


def unpack_kernel(shards, half, step, places, count, at_ref, *refs):
    mine, other, outs = refs[:count], refs[count : 2 * count], refs[2 * count :]

    def run(m, c):
        for d in range(shards):
            for index, where, part, row, low, high in places(m, d):
                out, width = outs[index], high - low
                a = mine[part][row : row + half, low:high]
                b = other[part][row : row + half, low:high]
                first, second = (a, b) if c == 0 else (b, a)
                out[:step, where : where + width] = first[:step].astype(F32)
                out[step:, where : where + width] = second.astype(F32)

    on_place(at_ref[0], at_ref[1], shards, run)


def local_call(kernel, out_shape, cost_bytes, at, *inputs, anywhere=(), scratch=()):
    vmem = pl.BlockSpec(memory_space=pltpu.VMEM)
    hbm = pl.BlockSpec(memory_space=pltpu.HBM)
    specs = [hbm if i in anywhere else vmem for i in range(len(inputs))]
    return pl.pallas_call(
        kernel,
        out_shape=out_shape,
        in_specs=[pl.BlockSpec(memory_space=pltpu.SMEM)] + specs,
        out_specs=jax.tree.map(lambda _: vmem, out_shape),
        scratch_shapes=list(scratch),
        compiler_params=pltpu.CompilerParams(vmem_limit_bytes=48 << 20),
        cost_estimate=pl.CostEstimate(flops=1, bytes_accessed=1, transcendentals=0),
    )(at, *inputs)


def body(
    tokens,
    cotangent,
    lengths,
    attn_weight,
    query_bias,
    value_bias,
    proj_weight,
    proj_bias,
    ln1_gain,
    ln1_bias,
    ln2_gain,
    ln2_bias,
    fc_weight,
    fc_bias,
    out_weight,
    out_bias,
):
    n = lax.axis_size("shard")
    planes = lax.axis_size("plane")
    me = lax.axis_index("shard")
    core = lax.axis_index("core")
    heads = (HEADS - 1) // n
    main = heads * HD
    spare = D - n * main
    own_rows = attn_weight.shape[0]
    own_ff = fc_bias.shape[0]
    rows = tokens.shape[1]
    half = -(-own_rows // 32) * 16
    step = own_rows - half
    quarter = lax.axis_index("plane") % 2 * 2 + core
    at = jnp.stack([me, core, quarter]).astype(jnp.int32)

    def swap(value, d):
        return lax.ppermute(value, "shard", [(i, i ^ d) for i in range(n)])

    def swap_plane(value):
        return lax.ppermute(value, "plane", [(i, i ^ 1) for i in range(planes)])

    def swap_core(value):
        return lax.ppermute(value, "core", [(0, 1), (1, 0)])

    def gather_near(value):
        if n != 4:
            return [swap(value, d) for d in range(1, n)]
        return [swap(value, 1), swap(value, 2)]

    def gather_far(value, near):
        if n != 4:
            return [value] + near
        one, two = near
        cut = value.shape[0] // 32 * 16
        three = jnp.concatenate([swap(one[:cut], 2), swap(two[cut:], 1)], axis=0)
        return [value, one, two, three]

    def gather(value):
        return gather_far(value, gather_near(value))

    def pick(stacked, index):
        return lax.dynamic_index_in_dim(stacked, index, 0, keepdims=False)

    def natural(pieces):
        stacked = jnp.stack(pieces)
        return [pick(stacked, me ^ j) for j in range(n)]

    def after(value, *deps):
        return lax.optimization_barrier((value, deps))[0]

    def block(value, d):
        return value[d * rows : (d + 1) * rows]

    def place(own, mine):
        other = swap_core(jnp.stack(mine))
        return local_call(
            functools.partial(place_kernel, n, half, step, own_rows),
            jax.ShapeDtypeStruct((n * own_rows, own.shape[1]), BF),
            n * own.size * 4,
            at,
            own,
            *mine,
            other,
        )

    def pack(weight, columns, width, dep):
        shapes = [jax.ShapeDtypeStruct((own_rows, width), BF)]
        shapes += [jax.ShapeDtypeStruct((half, width), BF)] * (n - 1)
        return local_call(
            functools.partial(pack_kernel, n, half, step, columns),
            shapes,
            weight.size * 2,
            at,
            dep,
            weight,
            anywhere=(0,),
        )

    def reduce_rows(parts, *deps):
        got = after([swap(parts[d].astype(BF), d) for d in range(1, n)], *deps)
        total = parts[0].astype(F32)
        for part in got:
            total = total + part.astype(F32)
        return total

    def core_halves(parts):
        keep = lax.dynamic_slice_in_dim(parts, core * step, half, 1)
        give = lax.dynamic_slice_in_dim(parts, (1 - core) * step, half, 1)
        return (keep.astype(F32) + swap_core(give).astype(F32)).astype(BF)

    vectors = (
        query_bias, value_bias, proj_bias, ln1_gain, ln1_bias, ln2_gain, ln2_bias, out_bias
    )
    tokens_near = gather_near(tokens[0])
    attn_width = 3 * (main + spare)
    attn_sent = local_call(
        functools.partial(pack_attn_kernel, n, half, step, heads, len(vectors)),
        [jax.ShapeDtypeStruct((own_rows + VEC_ROWS, attn_width), BF)]
        + [jax.ShapeDtypeStruct((half + VEC_ROWS, attn_width), BF)] * (n - 1),
        attn_weight.size * 2,
        at,
        attn_weight,
        *vectors,
        anywhere=range(1, len(vectors) + 1),
        scratch=[pltpu.VMEM((own_rows,), BF)] * len(vectors)
        + [pltpu.SemaphoreType.DMA((len(vectors),))],
    )
    attn_got = [swap(attn_sent[d], d) for d in range(1, n)]
    attn_got, tokens_near = after((attn_got, tokens_near))
    attn_other = swap_core(jnp.stack([piece[:half] for piece in attn_got]))
    tokens_parts = gather_far(tokens[0], tokens_near)
    w_attn, small = local_call(
        functools.partial(place_attn_kernel, n, half, step, own_rows, len(vectors)),
        [
            jax.ShapeDtypeStruct((D, attn_width), BF),
            jax.ShapeDtypeStruct((len(vectors), D), F32),
        ],
        D * attn_width * 4,
        at,
        attn_sent[0],
        *attn_got,
        attn_other,
    )
    b_query, b_value, b_proj, gain_one, bias_one, gain_two, bias_two, b_out = [
        small[i] for i in range(8)
    ]

    def my_columns(vector):
        return lax.dynamic_slice_in_dim(vector, me * main, main, 0), vector[n * main :]

    q_main, q_spare = my_columns(b_query)
    v_main, v_spare = my_columns(b_value)
    qkv_bias = jnp.concatenate(
        [q_main, jnp.zeros_like(q_main), v_main, q_spare, jnp.zeros_like(q_spare), v_spare]
    )

    group_tokens = jnp.concatenate(tokens_parts, axis=0)
    proj_half = lax.dynamic_slice_in_dim(after(proj_weight, attn_got), core * step, half, 0)
    proj_near = gather_near(proj_half)
    own_cot = cotangent[0]
    cot_all = lax.all_gather(after(own_cot, attn_got, tokens_parts), "shard", axis=0, tiled=True)
    late_fc = after(fc_weight, attn_got)
    stride = own_rows // 64 * 16
    length = own_rows - 3 * stride
    by_parts = own_rows % 16 == 0 and stride > 0 and planes % 2 == 0
    if by_parts:
        fc_sent = local_call(
            functools.partial(
                pack_part_kernel, n, length, stride, lambda ref, j: fc_columns(ref, j, own_ff)
            ),
            [jax.ShapeDtypeStruct((own_rows, own_ff), BF)]
            + [jax.ShapeDtypeStruct((length, own_ff), BF)] * (n - 1),
            fc_weight.size * 2,
            at,
            late_fc,
        )
    else:
        fc_sent = pack(late_fc, lambda ref, j: fc_columns(ref, j, own_ff), own_ff, lengths)
    xhat_one, _ = normalize(group_tokens.astype(F32))
    normed = (xhat_one * gain_one + bias_one).astype(BF)
    qkv = (jnp.dot(normed, w_attn, preferred_element_type=F32) + qkv_bias).astype(BF)
    qkv, proj_near, fc_sent = after((qkv, proj_near, fc_sent))
    proj_parts = gather_far(proj_half, proj_near)
    fc_got = [swap(fc_sent[d], d) for d in range(1, n)]
    info = jnp.concatenate([lengths[0], me.astype(jnp.int32)[None]])
    mixed_heads = attention_fwd(info, qkv, n, heads)
    mixed_heads, proj_parts, fc_got = after((mixed_heads, proj_parts, fc_got))
    if by_parts:
        fc_mine = jnp.concatenate(fc_got)
        fc_near = swap_plane(fc_mine)
    got = [block(mixed_heads, 0)[:, :main]] + [
        swap(block(mixed_heads, d)[:, :main], d) for d in range(1, n)
    ]
    w_proj = place(proj_weight, proj_parts[1:])
    got, w_proj, cot_all = after((got, w_proj, cot_all))
    mixed_low = jnp.concatenate(natural(got) + [block(mixed_heads, 0)[:, main:]], axis=1)
    own_tokens = tokens[0].astype(F32)
    middle = own_tokens + jnp.dot(mixed_low, w_proj, preferred_element_type=F32) + b_proj
    xhat_two, inv_two = normalize(middle)
    own_normed_two = (xhat_two * gain_two + bias_two).astype(BF)
    normed_near = gather_near(own_normed_two)
    if by_parts:
        w_fc = local_call(
            functools.partial(place_part_kernel, n, length, stride, own_rows),
            jax.ShapeDtypeStruct((D, own_ff), BF),
            D * own_ff * 4,
            at,
            fc_sent[0],
            fc_mine,
            fc_near,
            swap_core(jnp.concatenate(after([fc_mine, fc_near], own_normed_two))),
        )
    else:
        w_fc = place(fc_sent[0], fc_got)
    cot_parts = [own_cot] + [
        lax.dynamic_slice_in_dim(cot_all, (me ^ d) * rows, rows, 0) for d in range(1, n)
    ]
    group_cot = jnp.concatenate(cot_parts, axis=0)
    d_active = cols_dot(group_cot, out_weight).astype(BF)
    normed_near, d_active = after((normed_near, d_active))
    normed_parts = gather_far(own_normed_two, normed_near)
    normed_two = jnp.concatenate(normed_parts, axis=0)

    def feed(part):
        hidden = jnp.dot(part, w_fc, preferred_element_type=F32) + fc_bias.astype(F32)
        inner = jnp.tanh(0.7978845608028654 * (hidden + 0.044715 * hidden * hidden * hidden))
        slope = 0.5 * (1.0 + inner) + 0.5 * hidden * (1.0 - inner * inner) * (
            0.7978845608028654 * (1.0 + 3 * 0.044715 * hidden * hidden)
        )
        return (0.5 * hidden * (1.0 + inner)).astype(BF), slope.astype(BF)

    fed = [feed(part) for part in normed_parts]
    active_parts = [a for a, _ in fed]
    active = jnp.concatenate(active_parts, axis=0)

    grad_out_weight = rows_dot(active, group_cot).astype(BF)
    sum_out_weight = lax.psum(grad_out_weight, ("plane", "core"))
    d_active = after(d_active, grad_out_weight)
    d_hidden_parts = [
        (block(d_active, d).astype(F32) * slope.astype(F32)).astype(BF)
        for d, (_, slope) in enumerate(fed)
    ]
    d_hidden = jnp.concatenate(d_hidden_parts, axis=0)
    e = reduce_rows([cols_dot(part, w_fc) for part in d_hidden_parts])
    e_gain = e * gain_two
    d_middle = own_cot.astype(F32) + inv_two * (
        e_gain
        - jnp.mean(e_gain, axis=-1, keepdims=True)
        - xhat_two * jnp.mean(e_gain * xhat_two, axis=-1, keepdims=True)
    )
    d_branch = d_middle.astype(BF)
    d_mixed = cols_dot(d_branch, w_proj).astype(BF)
    for_heads = jnp.stack([d_mixed[:, j * main : (j + 1) * main] for j in range(n)])
    last = d_mixed[:, n * main :]
    dmix_parts = [jnp.concatenate([pick(for_heads, me), last], axis=1)] + [
        swap(jnp.concatenate([pick(for_heads, me ^ d), last], axis=1), d) for d in range(1, n)
    ]

    grad_fc = rows_dot(normed_two, d_hidden).astype(BF).reshape(n, own_rows, own_ff)
    fc_halves = after(core_halves(grad_fc), dmix_parts)
    fc_parts = jnp.concatenate(
        [pick(fc_halves, me)] + [swap(pick(fc_halves, me ^ d), d) for d in range(1, n)]
    )
    fc_sum = lax.psum(fc_parts, "plane")
    grad_fc_bias = jnp.sum(d_hidden.astype(F32), axis=0)

    d_qkv = attention_bwd(info, qkv, jnp.concatenate(dmix_parts, axis=0), n, heads)
    d_qkv, fc_parts = after((d_qkv, fc_parts))

    grad_proj = rows_dot(mixed_low, d_branch).astype(BF).reshape(n, own_rows, D)
    proj_halves = after(core_halves(grad_proj), fc_parts)
    proj_part = reduce_rows([pick(proj_halves, me ^ d) for d in range(n)]).astype(BF)

    grad_main = rows_dot(normed, d_qkv[:, : 3 * main]).astype(BF).reshape(n, own_rows, 3 * main)
    grad_spare = rows_dot(normed, d_qkv[:, 3 * main :]).astype(BF).reshape(n, own_rows, 3 * spare)
    main_halves = core_halves(grad_main)
    spare_halves = core_halves(pick(grad_spare, me)[None])[0]
    attn_parts = jnp.concatenate(
        [pick(main_halves, me)]
        + [swap(pick(main_halves, me ^ d), d) for d in range(1, n)]
        + [spare_halves, proj_part],
        axis=1,
    )
    attn_sum = lax.psum(after(attn_parts, fc_sum), "plane")

    counted = (lax.broadcasted_iota(jnp.int32, (n * rows, 1), 0) < rows) | (
        lax.broadcasted_iota(jnp.int32, (1, d_qkv.shape[1]), 1) < 3 * main
    )
    d_once = after(jnp.where(counted, d_qkv, BF(0)), attn_parts)
    f = reduce_rows([cols_dot(block(d_once, d), w_attn) for d in range(n)])
    xhat_own, inv_own = normalize(own_tokens)
    f_gain = f * gain_one
    d_tokens = inv_own * (
        f_gain
        - jnp.mean(f_gain, axis=-1, keepdims=True)
        - xhat_own * jnp.mean(f_gain * xhat_own, axis=-1, keepdims=True)
    )
    input_grad = (d_middle + d_tokens).astype(BF)[None]

    late_active = after(active, attn_parts)
    out_parts = [
        jnp.dot(block(late_active, d), out_weight, preferred_element_type=F32) for d in range(n)
    ]
    output = (middle + reduce_rows(out_parts) + b_out).astype(BF)[None]

    sum_fc_weight = local_call(
        functools.partial(
            unpack_kernel,
            n,
            half,
            step,
            lambda m, d: [(0, (m ^ d) * own_ff, 0, d * half, 0, own_ff)],
            1,
        ),
        [jax.ShapeDtypeStruct((own_rows, n * own_ff), F32)],
        own_rows * n * own_ff * 8,
        at,
        fc_sum,
        swap_core(fc_sum),
    )[0]

    def attn_places(m, d):
        base = d * 3 * main
        places = [
            (0, p * D + (m ^ d) * main, 0, 0, base + p * main, base + (p + 1) * main)
            for p in range(3)
        ]
        if d == 0:
            base = n * 3 * main
            places += [
                (0, p * D + n * main, 0, 0, base + p * spare, base + (p + 1) * spare)
                for p in range(3)
            ]
            places.append((1, 0, 0, 0, 3 * D, 4 * D))
        return places

    d_once_sum = jnp.sum(d_once.astype(F32), axis=0)

    def vector_of(part):
        whole = jnp.zeros((D,), F32)
        whole = lax.dynamic_update_slice_in_dim(
            whole, d_once_sum[part * main : (part + 1) * main], me * main, 0
        )
        lane = 3 * main + part * spare
        return jnp.concatenate([whole[: n * main], d_once_sum[lane : lane + spare]])

    small_grads = jnp.stack(
        [
            vector_of(0),
            vector_of(2),
            jnp.sum(d_branch.astype(F32), axis=0),
            jnp.sum(f * xhat_own, axis=0),
            jnp.sum(f, axis=0),
            jnp.sum(e * xhat_two, axis=0),
            jnp.sum(e, axis=0),
            jnp.sum(own_cot.astype(F32), axis=0),
        ]
    )
    small_grads = small_grads.reshape(8, n, own_rows).transpose(1, 0, 2)
    small_own = pick(small_grads, me)
    for d in range(1, n):
        small_own = small_own + swap(pick(small_grads, me ^ d), d)
    small_own = jnp.concatenate([small_own, grad_fc_bias.reshape(-1, own_rows)], axis=0)
    small_own = small_own + swap_core(small_own)
    hop = 1
    while hop < planes:
        small_own = small_own + lax.ppermute(
            small_own, "plane", [(i, i ^ hop) for i in range(planes)]
        )
        hop *= 2
    sum_out_weight = sum_out_weight.astype(F32)
    attn_sum, small_own, output, input_grad, sum_fc_weight, sum_out_weight = after(
        (attn_sum, small_own, output, input_grad, sum_fc_weight, sum_out_weight)
    )
    sum_attn_weight, sum_proj_weight = local_call(
        functools.partial(unpack_kernel, n, half, step, attn_places, 1),
        [
            jax.ShapeDtypeStruct((own_rows, 3 * D), F32),
            jax.ShapeDtypeStruct((own_rows, D), F32),
        ],
        own_rows * 4 * D * 8,
        at,
        attn_sum,
        swap_core(attn_sum),
    )
    s = small_own[:8]
    sum_fc_bias = small_own[8:].reshape(-1)
    return (
        output,
        input_grad,
        sum_attn_weight,
        s[0],
        s[1],
        sum_proj_weight,
        s[2],
        s[3],
        s[4],
        s[5],
        s[6],
        sum_fc_weight,
        sum_fc_bias,
        sum_out_weight,
        s[7],
    )


def solution(mesh):
    shards, reps = mesh.devices.shape
    split = jax.sharding.Mesh(
        mesh.devices.reshape(shards, reps // 2, 2), ("shard", "plane", "core")
    )
    rep = ("plane", "core")
    batch = P(rep, "shard", None)
    row, vec = P("shard", None), P("shard")
    return jax.shard_map(
        body,
        mesh=split,
        in_specs=(batch, batch, P(rep, None), row, vec, vec, row)
        + (vec,) * 5
        + (row, vec, row, vec),
        out_specs=(batch, batch, row, vec, vec, row) + (vec,) * 5 + (row, vec, row, vec),
        check_vma=False,
    )
```

```python
import functools
import math

import jax
import jax.numpy as jnp
from jax import lax
from jax.experimental import pallas as pl
from jax.experimental.pallas import tpu as pltpu
from jax.sharding import PartitionSpec as P

D = 1600
HEADS = 25
HD = 64
UNIT = 32
LANES = 128
NEG = -1e30
VEC_ROWS = 16
BF = jnp.bfloat16
F32 = jnp.float32


def dot(left, right, dims):
    return lax.dot_general(left, right, (dims, ((), ())), preferred_element_type=F32)


def rows_dot(left, right):
    return dot(left, right, ((0,), (0,)))


def cols_dot(left, right):
    return dot(left, right, ((1,), (1,)))


def normalize(values):
    center = values - jnp.mean(values, axis=-1, keepdims=True)
    spread = jnp.mean(center * center, axis=-1, keepdims=True)
    inv = lax.rsqrt(spread + 1e-05)
    return center * inv, inv


def place_blocks(info_ref, shards, units):
    b0, b1, b2, me = info_ref[0], info_ref[1], info_ref[2], info_ref[3]
    e0, e1 = b0, b0 + b1
    places = []
    for d in range(shards):
        s = jnp.bitwise_xor(me, d)
        for u in range(units):
            first = jnp.where(u < e0, 0, jnp.where(u < e1, e0, e1))
            span = jnp.where(u < e0, b0, jnp.where(u < e1, b1, b2))
            places.append((d * units + u, first * shards + s * span + (u - first)))
    return places, e0, e1


def head_lanes(tile_rows, half):
    lane = lax.broadcasted_iota(jnp.int32, (tile_rows, LANES), 1)
    return (lane < HD) if half == 0 else (lane >= HD)


def window_scores(q, k, rows, width):
    scores = cols_dot(q, k)
    row = lax.broadcasted_iota(jnp.int32, (rows, width * rows), 0)
    col = lax.broadcasted_iota(jnp.int32, (rows, width * rows), 1)
    return jnp.where(col <= row + (width - 1) * rows, scores, NEG)


def fwd_kernel(shards, units, heads, info_ref, qkv_ref, out_ref, perm, mixed):
    block = UNIT
    rows = shards * block
    main = heads * HD
    places, e0, e1 = place_blocks(info_ref, shards, units)
    for src, dst in places:
        at = pl.ds(pl.multiple_of(dst * block, block), block)
        perm[at, :] = qkv_ref[src * block : (src + 1) * block, :]

    def unit(i, carry):
        first = jnp.where(i < e0, 0, jnp.where(i < e1, e0, e1))
        q_at = pl.ds(pl.multiple_of(i * rows, rows), rows)
        for width in range(1, 5):

            @pl.when(i - first + 1 == width)
            def _():
                k_at = pl.ds(pl.multiple_of(first * rows, rows), width * rows)

                def attend(q, k, v):
                    scores = window_scores(q * BF(0.125), k, rows, width)
                    top = jnp.max(scores, axis=1, keepdims=True)
                    probs = jnp.exp(scores - top)
                    total = jnp.sum(probs, axis=1, keepdims=True)
                    return dot(probs.astype(BF), v, ((1,), (0,))) / total

                for tile in range(main // LANES):
                    lanes = slice(tile * LANES, (tile + 1) * LANES)
                    k_lanes = slice(main + lanes.start, main + lanes.stop)
                    v_lanes = slice(2 * main + lanes.start, 2 * main + lanes.stop)
                    q, k, v = perm[q_at, lanes], perm[k_at, k_lanes], perm[k_at, v_lanes]
                    low = head_lanes(rows, 0)
                    zero = jnp.zeros_like(q)
                    left = attend(jnp.where(low, q, zero), k, v)
                    right = attend(jnp.where(low, zero, q), k, v)
                    mixed[q_at, lanes] = jnp.where(low, left, right).astype(BF)
                if main % LANES:
                    lanes = main - HD
                    mixed[q_at, lanes:main] = attend(
                        perm[q_at, lanes:main],
                        perm[k_at, main + lanes : 2 * main],
                        perm[k_at, 2 * main + lanes : 3 * main],
                    ).astype(BF)
                base = 3 * main
                mixed[q_at, main : main + HD] = attend(
                    perm[q_at, base : base + HD],
                    perm[k_at, base + HD : base + 2 * HD],
                    perm[k_at, base + 2 * HD : base + 3 * HD],
                ).astype(BF)

        return carry

    lax.fori_loop(0, units, unit, 0)
    for src, dst in places:
        at = pl.ds(pl.multiple_of(dst * block, block), block)
        out_ref[src * block : (src + 1) * block, :] = mixed[at, :]


def bwd_kernel(
    shards, units, heads, info_ref, qkv_ref, dmix_ref, out_ref, perm, dperm, dq_acc, dk_acc, dv_acc
):
    block = UNIT
    rows = shards * block
    main = heads * HD
    places, e0, e1 = place_blocks(info_ref, shards, units)
    for src, dst in places:
        at = pl.ds(pl.multiple_of(dst * block, block), block)
        perm[at, :] = qkv_ref[src * block : (src + 1) * block, :]
        dperm[at, :] = dmix_ref[src * block : (src + 1) * block, :]
    dk_acc[...] = jnp.zeros_like(dk_acc)
    dv_acc[...] = jnp.zeros_like(dv_acc)

    def unit(i, carry):
        first = jnp.where(i < e0, 0, jnp.where(i < e1, e0, e1))
        q_at = pl.ds(pl.multiple_of(i * rows, rows), rows)
        for width in range(1, 5):

            @pl.when(i - first + 1 == width)
            def _():
                k_at = pl.ds(pl.multiple_of(first * rows, rows), width * rows)

                def pull(q, k, v, g):
                    q = q * BF(0.125)
                    scores = window_scores(q, k, rows, width)
                    top = jnp.max(scores, axis=1, keepdims=True)
                    probs = jnp.exp(scores - top)
                    total = jnp.sum(probs, axis=1, keepdims=True)
                    probs = probs * (1.0 / total)
                    d_probs = cols_dot(g, v)
                    delta = jnp.sum(probs * d_probs, axis=1, keepdims=True)
                    d_scores = (probs * (d_probs - delta)).astype(BF)
                    d_q = dot(d_scores, k, ((1,), (0,))) * 0.125
                    return d_q, rows_dot(d_scores, q), rows_dot(probs.astype(BF), g)

                for tile in range(main // LANES):
                    lanes = slice(tile * LANES, (tile + 1) * LANES)
                    k_lanes = slice(main + lanes.start, main + lanes.stop)
                    v_lanes = slice(2 * main + lanes.start, 2 * main + lanes.stop)
                    q, k, v = perm[q_at, lanes], perm[k_at, k_lanes], perm[k_at, v_lanes]
                    g = dperm[q_at, lanes]
                    low = head_lanes(rows, 0)
                    zero = jnp.zeros_like(q)
                    dq0, dk0, dv0 = pull(jnp.where(low, q, zero), k, v, jnp.where(low, g, zero))
                    dq1, dk1, dv1 = pull(jnp.where(low, zero, q), k, v, jnp.where(low, zero, g))
                    dq_acc[q_at, lanes] = jnp.where(low, dq0, dq1).astype(BF)
                    dk_acc[k_at, lanes] += dk0 + dk1
                    dv_acc[k_at, lanes] += dv0 + dv1
                extra = [(main, 3 * main, 3 * main + HD, 3 * main + 2 * HD)]
                if main % LANES:
                    extra.append((main - HD, main - HD, 2 * main - HD, 3 * main - HD))
                for own, q_lane, k_lane, v_lane in extra:
                    dq0, dk0, dv0 = pull(
                        perm[q_at, q_lane : q_lane + HD],
                        perm[k_at, k_lane : k_lane + HD],
                        perm[k_at, v_lane : v_lane + HD],
                        dperm[q_at, own : own + HD],
                    )
                    dq_acc[q_at, own : own + HD] = dq0.astype(BF)
                    dk_acc[k_at, own : own + HD] += dk0
                    dv_acc[k_at, own : own + HD] += dv0

        return carry

    lax.fori_loop(0, units, unit, 0)
    for src, dst in places:
        at = pl.ds(pl.multiple_of(dst * block, block), block)
        to = slice(src * block, (src + 1) * block)
        for part, acc in enumerate((dq_acc, dk_acc, dv_acc)):
            got = acc[at, :].astype(BF)
            out_ref[to, part * main : (part + 1) * main] = got[:, :main]
            lane = 3 * main + part * HD
            out_ref[to, lane : lane + HD] = got[:, main:]


def vmem_call(kernel, out_shape, scratch, cost, inputs):
    return pl.pallas_call(
        kernel,
        out_shape=out_shape,
        in_specs=[pl.BlockSpec(memory_space=pltpu.SMEM)]
        + [pl.BlockSpec(memory_space=pltpu.VMEM)] * (len(inputs) - 1),
        out_specs=pl.BlockSpec(memory_space=pltpu.VMEM),
        scratch_shapes=scratch,
        compiler_params=pltpu.CompilerParams(vmem_limit_bytes=48 << 20),
        cost_estimate=cost,
    )(*inputs)


def attention_fwd(info, qkv, shards, heads):
    total, width = qkv.shape
    units = total // (shards * UNIT)
    own = (heads + 1) * HD
    return vmem_call(
        functools.partial(fwd_kernel, shards, units, heads),
        jax.ShapeDtypeStruct((total, own), BF),
        [pltpu.VMEM((total, width), BF), pltpu.VMEM((total, own), BF)],
        pl.CostEstimate(flops=1, bytes_accessed=1, transcendentals=0),
        (info, qkv),
    )


def attention_bwd(info, qkv, d_mixed, shards, heads):
    total, width = qkv.shape
    units = total // (shards * UNIT)
    own = (heads + 1) * HD
    return vmem_call(
        functools.partial(bwd_kernel, shards, units, heads),
        jax.ShapeDtypeStruct((total, width), BF),
        [
            pltpu.VMEM((total, width), BF),
            pltpu.VMEM((total, own), BF),
            pltpu.VMEM((total, own), BF),
            pltpu.VMEM((total, own), F32),
            pltpu.VMEM((total, own), F32),
        ],
        pl.CostEstimate(flops=1, bytes_accessed=1, transcendentals=0),
        (info, qkv, d_mixed),
    )


def on_place(me, core, shards, run):
    for m in range(shards):
        for c in range(2):

            @pl.when((me == m) & (core == c))
            def _():
                run(m, c)


def attn_columns(value, j, heads):
    main = heads * HD
    first = D // main * main
    parts = [value[:, p * D + j * main : p * D + (j + 1) * main] for p in range(3)]
    parts += [value[:, p * D + first : (p + 1) * D] for p in range(3)]
    return jnp.concatenate(parts, axis=1)


def fc_columns(value, j, width):
    return value[:, j * width : (j + 1) * width]


def pack_kernel(shards, half, step, columns, at_ref, dep_ref, weight_ref, *outs):
    del dep_ref

    def run(m, c):
        outs[0][...] = columns(weight_ref, m)
        for d in range(1, shards):
            piece = columns(weight_ref.at[c * step : c * step + half], m ^ d)
            outs[d][...] = piece

    on_place(at_ref[0], at_ref[1], shards, run)


def pack_attn_kernel(shards, half, step, heads, count, at_ref, weight_ref, *refs):
    sources, outs = refs[:count], refs[count : count + shards]
    vectors, sems = refs[count + shards : 2 * count + shards], refs[2 * count + shards]
    length = vectors[0].shape[0]
    copies = [
        pltpu.make_async_copy(source, vector, sems.at[i])
        for i, (source, vector) in enumerate(zip(sources, vectors))
    ]
    for copy in copies:
        copy.start()

    def run(m, c):
        outs[0][: shards_rows(outs[0]), :] = attn_columns(weight_ref, m, heads)
        for d in range(1, shards):
            outs[d][:half, :] = attn_columns(weight_ref.at[c * step : c * step + half], m ^ d, heads)

    def shards_rows(ref):
        return ref.shape[0] - VEC_ROWS

    on_place(at_ref[0], at_ref[1], shards, run)
    for copy in copies:
        copy.wait()
    width = outs[0].shape[1]
    block = jnp.concatenate(
        [v[...].astype(F32).reshape(1, length) for v in vectors]
        + [jnp.zeros((VEC_ROWS - count, length), F32)],
        axis=0,
    )
    block = jnp.concatenate(
        [block, jnp.zeros((VEC_ROWS, width - length), F32)], axis=1
    ).astype(BF)
    for out in outs:
        out[out.shape[0] - VEC_ROWS :, :] = block


def place_attn_kernel(shards, half, step, rows, count, at_ref, *refs):
    own, mine, other = refs[0], refs[1:shards], refs[shards]
    out, vec = refs[shards + 1 :]

    def run(m, c):
        out[m * rows : (m + 1) * rows, :] = own[:rows]
        for d in range(1, shards):
            base = (m ^ d) * rows
            a, b = mine[d - 1][:half], other[d - 1]
            low, high = (a, b) if c == 0 else (b, a)
            out[base : base + step, :] = low[:step]
            out[base + step : base + rows, :] = high
        for j in range(shards):
            ref, at = (own, rows) if j == m else (mine[(j ^ m) - 1], half)
            vec[:, j * rows : (j + 1) * rows] = ref[at : at + VEC_ROWS, :rows].astype(F32)[:count]

    on_place(at_ref[0], at_ref[1], shards, run)


def place_kernel(shards, half, step, rows, at_ref, *refs):
    own, mine, other, out = refs[0], refs[1:shards], refs[shards], refs[shards + 1]

    def run(m, c):
        out[m * rows : (m + 1) * rows, :] = own[...]
        for d in range(1, shards):
            base = (m ^ d) * rows
            low, high = (mine[d - 1][...], other[d - 1]) if c == 0 else (other[d - 1], mine[d - 1][...])
            out[base : base + step, :] = low[:step]
            out[base + step : base + rows, :] = high

    on_place(at_ref[0], at_ref[1], shards, run)


def pack_part_kernel(shards, length, stride, columns, at_ref, weight_ref, *outs):
    part = pl.ds(pl.multiple_of(at_ref[2] * stride, 16), length)
    for m in range(shards):

        @pl.when(at_ref[0] == m)
        def _():
            outs[0][...] = columns(weight_ref, m)
            for d in range(1, shards):
                outs[d][...] = columns(weight_ref.at[part], m ^ d)


def place_part_kernel(shards, length, stride, rows, at_ref, own, mine, near, across, out):
    me, q = at_ref[0], at_ref[2]
    out[pl.ds(pl.multiple_of(me * rows, 16), rows), :] = own[...]
    size = (shards - 1) * length
    for d in range(1, shards):
        base = jnp.bitwise_xor(me, d) * rows
        for flip, ref, first in ((0, mine, 0), (2, near, 0), (1, across, 0), (3, across, size)):
            to = base + jnp.bitwise_xor(q, flip) * stride
            row = first + (d - 1) * length
            out[pl.ds(pl.multiple_of(to, 16), length), :] = ref[row : row + length, :]


def unpack_kernel(shards, half, step, places, count, at_ref, *refs):
    mine, other, outs = refs[:count], refs[count : 2 * count], refs[2 * count :]

    def run(m, c):
        for d in range(shards):
            for index, where, part, row, low, high in places(m, d):
                out, width = outs[index], high - low
                a = mine[part][row : row + half, low:high]
                b = other[part][row : row + half, low:high]
                first, second = (a, b) if c == 0 else (b, a)
                out[:step, where : where + width] = first[:step].astype(F32)
                out[step:, where : where + width] = second.astype(F32)

    on_place(at_ref[0], at_ref[1], shards, run)


def local_call(kernel, out_shape, cost_bytes, at, *inputs, anywhere=(), scratch=()):
    vmem = pl.BlockSpec(memory_space=pltpu.VMEM)
    hbm = pl.BlockSpec(memory_space=pltpu.HBM)
    specs = [hbm if i in anywhere else vmem for i in range(len(inputs))]
    return pl.pallas_call(
        kernel,
        out_shape=out_shape,
        in_specs=[pl.BlockSpec(memory_space=pltpu.SMEM)] + specs,
        out_specs=jax.tree.map(lambda _: vmem, out_shape),
        scratch_shapes=list(scratch),
        compiler_params=pltpu.CompilerParams(vmem_limit_bytes=48 << 20),
        cost_estimate=pl.CostEstimate(flops=1, bytes_accessed=1, transcendentals=0),
    )(at, *inputs)


def body(
    tokens,
    cotangent,
    lengths,
    attn_weight,
    query_bias,
    value_bias,
    proj_weight,
    proj_bias,
    ln1_gain,
    ln1_bias,
    ln2_gain,
    ln2_bias,
    fc_weight,
    fc_bias,
    out_weight,
    out_bias,
):
    n = lax.axis_size("shard")
    planes = lax.axis_size("plane")
    me = lax.axis_index("shard")
    core = lax.axis_index("core")
    heads = (HEADS - 1) // n
    main = heads * HD
    spare = D - n * main
    own_rows = attn_weight.shape[0]
    own_ff = fc_bias.shape[0]
    rows = tokens.shape[1]
    half = -(-own_rows // 32) * 16
    step = own_rows - half
    quarter = lax.axis_index("plane") % 2 * 2 + core
    at = jnp.stack([me, core, quarter]).astype(jnp.int32)

    def swap(value, d):
        return lax.ppermute(value, "shard", [(i, i ^ d) for i in range(n)])

    def swap_plane(value):
        return lax.ppermute(value, "plane", [(i, i ^ 1) for i in range(planes)])

    def swap_core(value):
        return lax.ppermute(value, "core", [(0, 1), (1, 0)])

    def gather_near(value):
        if n != 4:
            return [swap(value, d) for d in range(1, n)]
        return [swap(value, 1), swap(value, 2)]

    def gather_far(value, near):
        if n != 4:
            return [value] + near
        one, two = near
        cut = value.shape[0] // 32 * 16
        three = jnp.concatenate([swap(one[:cut], 2), swap(two[cut:], 1)], axis=0)
        return [value, one, two, three]

    def gather(value):
        return gather_far(value, gather_near(value))

    def pick(stacked, index):
        return lax.dynamic_index_in_dim(stacked, index, 0, keepdims=False)

    def natural(pieces):
        stacked = jnp.stack(pieces)
        return [pick(stacked, me ^ j) for j in range(n)]

    def after(value, *deps):
        return lax.optimization_barrier((value, deps))[0]

    def block(value, d):
        return value[d * rows : (d + 1) * rows]

    def place(own, mine):
        other = swap_core(jnp.stack(mine))
        return local_call(
            functools.partial(place_kernel, n, half, step, own_rows),
            jax.ShapeDtypeStruct((n * own_rows, own.shape[1]), BF),
            n * own.size * 4,
            at,
            own,
            *mine,
            other,
        )

    def pack(weight, columns, width, dep):
        shapes = [jax.ShapeDtypeStruct((own_rows, width), BF)]
        shapes += [jax.ShapeDtypeStruct((half, width), BF)] * (n - 1)
        return local_call(
            functools.partial(pack_kernel, n, half, step, columns),
            shapes,
            weight.size * 2,
            at,
            dep,
            weight,
            anywhere=(0,),
        )

    def reduce_rows(parts, *deps):
        got = after([swap(parts[d].astype(BF), d) for d in range(1, n)], *deps)
        total = parts[0].astype(F32)
        for part in got:
            total = total + part.astype(F32)
        return total

    def core_halves(parts):
        keep = lax.dynamic_slice_in_dim(parts, core * step, half, 1)
        give = lax.dynamic_slice_in_dim(parts, (1 - core) * step, half, 1)
        return (keep.astype(F32) + swap_core(give).astype(F32)).astype(BF)

    vectors = (
        query_bias, value_bias, proj_bias, ln1_gain, ln1_bias, ln2_gain, ln2_bias, out_bias
    )
    tokens_near = gather_near(tokens[0])
    attn_width = 3 * (main + spare)
    attn_sent = local_call(
        functools.partial(pack_attn_kernel, n, half, step, heads, len(vectors)),
        [jax.ShapeDtypeStruct((own_rows + VEC_ROWS, attn_width), BF)]
        + [jax.ShapeDtypeStruct((half + VEC_ROWS, attn_width), BF)] * (n - 1),
        attn_weight.size * 2,
        at,
        attn_weight,
        *vectors,
        anywhere=range(1, len(vectors) + 1),
        scratch=[pltpu.VMEM((own_rows,), BF)] * len(vectors)
        + [pltpu.SemaphoreType.DMA((len(vectors),))],
    )
    attn_got = [swap(attn_sent[d], d) for d in range(1, n)]
    attn_got, tokens_near = after((attn_got, tokens_near))
    attn_other = swap_core(jnp.stack([piece[:half] for piece in attn_got]))
    tokens_parts = gather_far(tokens[0], tokens_near)
    w_attn, small = local_call(
        functools.partial(place_attn_kernel, n, half, step, own_rows, len(vectors)),
        [
            jax.ShapeDtypeStruct((D, attn_width), BF),
            jax.ShapeDtypeStruct((len(vectors), D), F32),
        ],
        D * attn_width * 4,
        at,
        attn_sent[0],
        *attn_got,
        attn_other,
    )
    b_query, b_value, b_proj, gain_one, bias_one, gain_two, bias_two, b_out = [
        small[i] for i in range(8)
    ]

    def my_columns(vector):
        return lax.dynamic_slice_in_dim(vector, me * main, main, 0), vector[n * main :]

    q_main, q_spare = my_columns(b_query)
    v_main, v_spare = my_columns(b_value)
    qkv_bias = jnp.concatenate(
        [q_main, jnp.zeros_like(q_main), v_main, q_spare, jnp.zeros_like(q_spare), v_spare]
    )

    group_tokens = jnp.concatenate(tokens_parts, axis=0)
    proj_half = lax.dynamic_slice_in_dim(after(proj_weight, attn_got), core * step, half, 0)
    proj_near = gather_near(proj_half)
    own_cot = cotangent[0]
    cot_all = lax.all_gather(after(own_cot, attn_got, tokens_parts), "shard", axis=0, tiled=True)
    late_fc = after(fc_weight, attn_got)
    stride = own_rows // 64 * 16
    length = own_rows - 3 * stride
    by_parts = own_rows % 16 == 0 and stride > 0 and planes % 2 == 0
    if by_parts:
        fc_sent = local_call(
            functools.partial(
                pack_part_kernel, n, length, stride, lambda ref, j: fc_columns(ref, j, own_ff)
            ),
            [jax.ShapeDtypeStruct((own_rows, own_ff), BF)]
            + [jax.ShapeDtypeStruct((length, own_ff), BF)] * (n - 1),
            fc_weight.size * 2,
            at,
            late_fc,
        )
    else:
        fc_sent = pack(late_fc, lambda ref, j: fc_columns(ref, j, own_ff), own_ff, lengths)
    xhat_one, _ = normalize(group_tokens.astype(F32))
    normed = (xhat_one * gain_one + bias_one).astype(BF)
    qkv = (jnp.dot(normed, w_attn, preferred_element_type=F32) + qkv_bias).astype(BF)
    qkv, proj_near, fc_sent = after((qkv, proj_near, fc_sent))
    proj_parts = gather_far(proj_half, proj_near)
    fc_got = [swap(fc_sent[d], d) for d in range(1, n)]
    info = jnp.concatenate([lengths[0], me.astype(jnp.int32)[None]])
    mixed_heads = attention_fwd(info, qkv, n, heads)
    mixed_heads, proj_parts, fc_first = after((mixed_heads, proj_parts, fc_got[:-1]))
    fc_got = list(fc_first) + fc_got[-1:]
    if by_parts:
        fc_mine = jnp.concatenate(fc_got)
        fc_near = swap_plane(fc_mine)
    got = [block(mixed_heads, 0)[:, :main]] + [
        swap(block(mixed_heads, d)[:, :main], d) for d in range(1, n)
    ]
    w_proj = place(proj_weight, proj_parts[1:])
    got, w_proj, cot_all = after((got, w_proj, cot_all))
    mixed_low = jnp.concatenate(natural(got) + [block(mixed_heads, 0)[:, main:]], axis=1)
    own_tokens = tokens[0].astype(F32)
    middle = own_tokens + jnp.dot(mixed_low, w_proj, preferred_element_type=F32) + b_proj
    xhat_two, inv_two = normalize(middle)
    own_normed_two = (xhat_two * gain_two + bias_two).astype(BF)
    normed_near = gather_near(own_normed_two)
    cot_parts = [own_cot] + [
        lax.dynamic_slice_in_dim(cot_all, (me ^ d) * rows, rows, 0) for d in range(1, n)
    ]
    group_cot = jnp.concatenate(cot_parts, axis=0)
    d_active = cols_dot(group_cot, out_weight).astype(BF)
    if by_parts:
        fc_mine, fc_near, d_active = after((fc_mine, fc_near, d_active), own_normed_two)
        w_fc = local_call(
            functools.partial(place_part_kernel, n, length, stride, own_rows),
            jax.ShapeDtypeStruct((D, own_ff), BF),
            D * own_ff * 4,
            at,
            fc_sent[0],
            fc_mine,
            fc_near,
            swap_core(jnp.concatenate([fc_mine, fc_near])),
        )
    else:
        w_fc = place(fc_sent[0], fc_got)
    normed_near, d_active = after((normed_near, d_active))

    def feed(part):
        hidden = jnp.dot(part, w_fc, preferred_element_type=F32) + fc_bias.astype(F32)
        inner = jnp.tanh(0.7978845608028654 * (hidden + 0.044715 * hidden * hidden * hidden))
        slope = 0.5 * (1.0 + inner) + 0.5 * hidden * (1.0 - inner * inner) * (
            0.7978845608028654 * (1.0 + 3 * 0.044715 * hidden * hidden)
        )
        return (0.5 * hidden * (1.0 + inner)).astype(BF), slope.astype(BF)

    if n == 4:
        one, two = normed_near
        cut = rows // 32 * 16
        far = [swap(one[:cut], 2), swap(two[cut:], 1)]
        fed = [feed(part) for part in (own_normed_two, one, two)]
        far, fed = after((far, fed))
        normed_parts = [own_normed_two, one, two, jnp.concatenate(far, axis=0)]
        fed.append(feed(normed_parts[3]))
    else:
        normed_parts = gather_far(own_normed_two, normed_near)
        fed = [feed(part) for part in normed_parts]
    normed_two = jnp.concatenate(normed_parts, axis=0)
    active_parts = [a for a, _ in fed]
    active = jnp.concatenate(active_parts, axis=0)

    grad_out_weight = rows_dot(active, group_cot).astype(BF)
    sum_out_weight = lax.psum(grad_out_weight, ("plane", "core"))
    d_active = after(d_active, grad_out_weight)
    d_hidden_parts = [
        (block(d_active, d).astype(F32) * slope.astype(F32)).astype(BF)
        for d, (_, slope) in enumerate(fed)
    ]
    d_hidden = jnp.concatenate(d_hidden_parts, axis=0)
    e = reduce_rows([cols_dot(part, w_fc) for part in d_hidden_parts])
    e_gain = e * gain_two
    d_middle = own_cot.astype(F32) + inv_two * (
        e_gain
        - jnp.mean(e_gain, axis=-1, keepdims=True)
        - xhat_two * jnp.mean(e_gain * xhat_two, axis=-1, keepdims=True)
    )
    d_branch = d_middle.astype(BF)
    d_mixed = cols_dot(d_branch, w_proj).astype(BF)
    for_heads = jnp.stack([d_mixed[:, j * main : (j + 1) * main] for j in range(n)])
    last = d_mixed[:, n * main :]
    dmix_parts = [jnp.concatenate([pick(for_heads, me), last], axis=1)] + [
        swap(jnp.concatenate([pick(for_heads, me ^ d), last], axis=1), d) for d in range(1, n)
    ]

    grad_fc = rows_dot(normed_two, d_hidden).astype(BF).reshape(n, own_rows, own_ff)
    fc_halves = after(core_halves(grad_fc), dmix_parts)
    fc_parts = jnp.concatenate(
        [pick(fc_halves, me)] + [swap(pick(fc_halves, me ^ d), d) for d in range(1, n)]
    )
    fc_sum = lax.psum(fc_parts, "plane")
    sum_out_weight = after(sum_out_weight, fc_parts).astype(F32)
    grad_fc_bias = jnp.sum(d_hidden.astype(F32), axis=0)

    d_qkv = attention_bwd(info, qkv, jnp.concatenate(dmix_parts, axis=0), n, heads)
    d_qkv, fc_parts = after((d_qkv, fc_parts))

    grad_proj = rows_dot(mixed_low, d_branch).astype(BF).reshape(n, own_rows, D)
    proj_halves = after(core_halves(grad_proj), fc_parts)
    proj_part = reduce_rows([pick(proj_halves, me ^ d) for d in range(n)]).astype(BF)

    grad_main = rows_dot(normed, d_qkv[:, : 3 * main]).astype(BF).reshape(n, own_rows, 3 * main)
    grad_spare = rows_dot(normed, d_qkv[:, 3 * main :]).astype(BF).reshape(n, own_rows, 3 * spare)
    main_halves = core_halves(grad_main)
    spare_halves = core_halves(pick(grad_spare, me)[None])[0]
    attn_parts = jnp.concatenate(
        [pick(main_halves, me)]
        + [swap(pick(main_halves, me ^ d), d) for d in range(1, n)]
        + [spare_halves, proj_part],
        axis=1,
    )
    attn_sum = lax.psum(after(attn_parts, fc_sum), "plane")

    counted = (lax.broadcasted_iota(jnp.int32, (n * rows, 1), 0) < rows) | (
        lax.broadcasted_iota(jnp.int32, (1, d_qkv.shape[1]), 1) < 3 * main
    )
    d_once = after(jnp.where(counted, d_qkv, BF(0)), attn_parts)
    f = reduce_rows([cols_dot(block(d_once, d), w_attn) for d in range(n)])
    xhat_own, inv_own = normalize(own_tokens)
    f_gain = f * gain_one
    d_tokens = inv_own * (
        f_gain
        - jnp.mean(f_gain, axis=-1, keepdims=True)
        - xhat_own * jnp.mean(f_gain * xhat_own, axis=-1, keepdims=True)
    )
    input_grad = (d_middle + d_tokens).astype(BF)[None]

    late_active = after(active, attn_parts)
    out_parts = [
        jnp.dot(block(late_active, d), out_weight, preferred_element_type=F32) for d in range(n)
    ]
    output = (middle + reduce_rows(out_parts) + b_out).astype(BF)[None]

    sum_fc_weight = local_call(
        functools.partial(
            unpack_kernel,
            n,
            half,
            step,
            lambda m, d: [(0, (m ^ d) * own_ff, 0, d * half, 0, own_ff)],
            1,
        ),
        [jax.ShapeDtypeStruct((own_rows, n * own_ff), F32)],
        own_rows * n * own_ff * 8,
        at,
        fc_sum,
        swap_core(fc_sum),
    )[0]

    def attn_places(m, d):
        base = d * 3 * main
        places = [
            (0, p * D + (m ^ d) * main, 0, 0, base + p * main, base + (p + 1) * main)
            for p in range(3)
        ]
        if d == 0:
            base = n * 3 * main
            places += [
                (0, p * D + n * main, 0, 0, base + p * spare, base + (p + 1) * spare)
                for p in range(3)
            ]
            places.append((1, 0, 0, 0, 3 * D, 4 * D))
        return places

    d_once_sum = jnp.sum(d_once.astype(F32), axis=0)

    def vector_of(part):
        whole = jnp.zeros((D,), F32)
        whole = lax.dynamic_update_slice_in_dim(
            whole, d_once_sum[part * main : (part + 1) * main], me * main, 0
        )
        lane = 3 * main + part * spare
        return jnp.concatenate([whole[: n * main], d_once_sum[lane : lane + spare]])

    early = after(
        (
            jnp.sum(d_branch.astype(F32), axis=0),
            jnp.sum(e * xhat_two, axis=0),
            jnp.sum(e, axis=0),
            jnp.sum(own_cot.astype(F32), axis=0),
        ),
        attn_parts,
    )
    small_grads = jnp.stack(
        [
            vector_of(0),
            vector_of(2),
            early[0],
            jnp.sum(f * xhat_own, axis=0),
            jnp.sum(f, axis=0),
            early[1],
            early[2],
            early[3],
        ]
    )
    small_grads = small_grads.reshape(8, n, own_rows).transpose(1, 0, 2)
    small_own = pick(small_grads, me)
    for d in range(1, n):
        small_own = small_own + swap(pick(small_grads, me ^ d), d)
    small_own = jnp.concatenate([small_own, grad_fc_bias.reshape(-1, own_rows)], axis=0)
    small_own = small_own + swap_core(small_own)
    hop = 1
    while hop < planes:
        small_own = small_own + lax.ppermute(
            small_own, "plane", [(i, i ^ hop) for i in range(planes)]
        )
        hop *= 2
    attn_sum, small_own, output, input_grad, sum_fc_weight, sum_out_weight = after(
        (attn_sum, small_own, output, input_grad, sum_fc_weight, sum_out_weight)
    )
    sum_attn_weight, sum_proj_weight = local_call(
        functools.partial(unpack_kernel, n, half, step, attn_places, 1),
        [
            jax.ShapeDtypeStruct((own_rows, 3 * D), F32),
            jax.ShapeDtypeStruct((own_rows, D), F32),
        ],
        own_rows * 4 * D * 8,
        at,
        attn_sum,
        swap_core(attn_sum),
    )
    s = small_own[:8]
    sum_fc_bias = small_own[8:].reshape(-1)
    return (
        output,
        input_grad,
        sum_attn_weight,
        s[0],
        s[1],
        sum_proj_weight,
        s[2],
        s[3],
        s[4],
        s[5],
        s[6],
        sum_fc_weight,
        sum_fc_bias,
        sum_out_weight,
        s[7],
    )


def solution(mesh):
    shards, reps = mesh.devices.shape
    split = jax.sharding.Mesh(
        mesh.devices.reshape(shards, reps // 2, 2), ("shard", "plane", "core")
    )
    rep = ("plane", "core")
    batch = P(rep, "shard", None)
    row, vec = P("shard", None), P("shard")
    return jax.shard_map(
        body,
        mesh=split,
        in_specs=(batch, batch, P(rep, None), row, vec, vec, row)
        + (vec,) * 5
        + (row, vec, row, vec),
        out_specs=(batch, batch, row, vec, vec, row) + (vec,) * 5 + (row, vec, row, vec),
        check_vma=False,
    )
```

```python
import functools
import math

import jax
import jax.numpy as jnp
from jax import lax
from jax.experimental import pallas as pl
from jax.experimental.pallas import tpu as pltpu
from jax.sharding import PartitionSpec as P

D = 1600
HEADS = 25
HD = 64
UNIT = 32
LANES = 128
NEG = -1e30
VEC_ROWS = 16
BF = jnp.bfloat16
F32 = jnp.float32


def dot(left, right, dims):
    return lax.dot_general(left, right, (dims, ((), ())), preferred_element_type=F32)


def rows_dot(left, right):
    return dot(left, right, ((0,), (0,)))


def cols_dot(left, right):
    return dot(left, right, ((1,), (1,)))


def normalize(values):
    center = values - jnp.mean(values, axis=-1, keepdims=True)
    spread = jnp.mean(center * center, axis=-1, keepdims=True)
    inv = lax.rsqrt(spread + 1e-05)
    return center * inv, inv


def place_blocks(info_ref, shards, units):
    b0, b1, b2, me = info_ref[0], info_ref[1], info_ref[2], info_ref[3]
    e0, e1 = b0, b0 + b1
    places = []
    for d in range(shards):
        s = jnp.bitwise_xor(me, d)
        for u in range(units):
            first = jnp.where(u < e0, 0, jnp.where(u < e1, e0, e1))
            span = jnp.where(u < e0, b0, jnp.where(u < e1, b1, b2))
            places.append((d * units + u, first * shards + s * span + (u - first)))
    return places, e0, e1


def head_lanes(tile_rows, half):
    lane = lax.broadcasted_iota(jnp.int32, (tile_rows, LANES), 1)
    return (lane < HD) if half == 0 else (lane >= HD)


def window_scores(q, k, rows, width):
    scores = cols_dot(q, k)
    row = lax.broadcasted_iota(jnp.int32, (rows, width * rows), 0)
    col = lax.broadcasted_iota(jnp.int32, (rows, width * rows), 1)
    return jnp.where(col <= row + (width - 1) * rows, scores, NEG)


def fwd_kernel(shards, units, heads, info_ref, qkv_ref, out_ref, perm, mixed):
    block = UNIT
    rows = shards * block
    main = heads * HD
    places, e0, e1 = place_blocks(info_ref, shards, units)
    for src, dst in places:
        at = pl.ds(pl.multiple_of(dst * block, block), block)
        perm[at, :] = qkv_ref[src * block : (src + 1) * block, :]

    def unit(i, carry):
        first = jnp.where(i < e0, 0, jnp.where(i < e1, e0, e1))
        q_at = pl.ds(pl.multiple_of(i * rows, rows), rows)
        for width in range(1, 5):

            @pl.when(i - first + 1 == width)
            def _():
                k_at = pl.ds(pl.multiple_of(first * rows, rows), width * rows)

                def attend(q, k, v):
                    scores = window_scores(q * BF(0.125), k, rows, width)
                    top = jnp.max(scores, axis=1, keepdims=True)
                    probs = jnp.exp(scores - top)
                    total = jnp.sum(probs, axis=1, keepdims=True)
                    return dot(probs.astype(BF), v, ((1,), (0,))) / total

                for tile in range(main // LANES):
                    lanes = slice(tile * LANES, (tile + 1) * LANES)
                    k_lanes = slice(main + lanes.start, main + lanes.stop)
                    v_lanes = slice(2 * main + lanes.start, 2 * main + lanes.stop)
                    q, k, v = perm[q_at, lanes], perm[k_at, k_lanes], perm[k_at, v_lanes]
                    low = head_lanes(rows, 0)
                    zero = jnp.zeros_like(q)
                    left = attend(jnp.where(low, q, zero), k, v)
                    right = attend(jnp.where(low, zero, q), k, v)
                    mixed[q_at, lanes] = jnp.where(low, left, right).astype(BF)
                if main % LANES:
                    lanes = main - HD
                    mixed[q_at, lanes:main] = attend(
                        perm[q_at, lanes:main],
                        perm[k_at, main + lanes : 2 * main],
                        perm[k_at, 2 * main + lanes : 3 * main],
                    ).astype(BF)
                base = 3 * main
                mixed[q_at, main : main + HD] = attend(
                    perm[q_at, base : base + HD],
                    perm[k_at, base + HD : base + 2 * HD],
                    perm[k_at, base + 2 * HD : base + 3 * HD],
                ).astype(BF)

        return carry

    lax.fori_loop(0, units, unit, 0)
    for src, dst in places:
        at = pl.ds(pl.multiple_of(dst * block, block), block)
        out_ref[src * block : (src + 1) * block, :] = mixed[at, :]


def bwd_kernel(
    shards, units, heads, info_ref, qkv_ref, dmix_ref, out_ref, perm, dperm, dq_acc, dk_acc, dv_acc
):
    block = UNIT
    rows = shards * block
    main = heads * HD
    places, e0, e1 = place_blocks(info_ref, shards, units)
    for src, dst in places:
        at = pl.ds(pl.multiple_of(dst * block, block), block)
        perm[at, :] = qkv_ref[src * block : (src + 1) * block, :]
        dperm[at, :] = dmix_ref[src * block : (src + 1) * block, :]
    dk_acc[...] = jnp.zeros_like(dk_acc)
    dv_acc[...] = jnp.zeros_like(dv_acc)

    def unit(i, carry):
        first = jnp.where(i < e0, 0, jnp.where(i < e1, e0, e1))
        q_at = pl.ds(pl.multiple_of(i * rows, rows), rows)
        for width in range(1, 5):

            @pl.when(i - first + 1 == width)
            def _():
                k_at = pl.ds(pl.multiple_of(first * rows, rows), width * rows)

                def pull(q, k, v, g):
                    q = q * BF(0.125)
                    scores = window_scores(q, k, rows, width)
                    top = jnp.max(scores, axis=1, keepdims=True)
                    probs = jnp.exp(scores - top)
                    total = jnp.sum(probs, axis=1, keepdims=True)
                    probs = probs * (1.0 / total)
                    d_probs = cols_dot(g, v)
                    delta = jnp.sum(probs * d_probs, axis=1, keepdims=True)
                    d_scores = (probs * (d_probs - delta)).astype(BF)
                    d_q = dot(d_scores, k, ((1,), (0,))) * 0.125
                    return d_q, rows_dot(d_scores, q), rows_dot(probs.astype(BF), g)

                for tile in range(main // LANES):
                    lanes = slice(tile * LANES, (tile + 1) * LANES)
                    k_lanes = slice(main + lanes.start, main + lanes.stop)
                    v_lanes = slice(2 * main + lanes.start, 2 * main + lanes.stop)
                    q, k, v = perm[q_at, lanes], perm[k_at, k_lanes], perm[k_at, v_lanes]
                    g = dperm[q_at, lanes]
                    low = head_lanes(rows, 0)
                    zero = jnp.zeros_like(q)
                    dq0, dk0, dv0 = pull(jnp.where(low, q, zero), k, v, jnp.where(low, g, zero))
                    dq1, dk1, dv1 = pull(jnp.where(low, zero, q), k, v, jnp.where(low, zero, g))
                    dq_acc[q_at, lanes] = jnp.where(low, dq0, dq1).astype(BF)
                    dk_acc[k_at, lanes] += dk0 + dk1
                    dv_acc[k_at, lanes] += dv0 + dv1
                extra = [(main, 3 * main, 3 * main + HD, 3 * main + 2 * HD)]
                if main % LANES:
                    extra.append((main - HD, main - HD, 2 * main - HD, 3 * main - HD))
                for own, q_lane, k_lane, v_lane in extra:
                    dq0, dk0, dv0 = pull(
                        perm[q_at, q_lane : q_lane + HD],
                        perm[k_at, k_lane : k_lane + HD],
                        perm[k_at, v_lane : v_lane + HD],
                        dperm[q_at, own : own + HD],
                    )
                    dq_acc[q_at, own : own + HD] = dq0.astype(BF)
                    dk_acc[k_at, own : own + HD] += dk0
                    dv_acc[k_at, own : own + HD] += dv0

        return carry

    lax.fori_loop(0, units, unit, 0)
    for src, dst in places:
        at = pl.ds(pl.multiple_of(dst * block, block), block)
        to = slice(src * block, (src + 1) * block)
        for part, acc in enumerate((dq_acc, dk_acc, dv_acc)):
            got = acc[at, :].astype(BF)
            out_ref[to, part * main : (part + 1) * main] = got[:, :main]
            lane = 3 * main + part * HD
            out_ref[to, lane : lane + HD] = got[:, main:]


def vmem_call(kernel, out_shape, scratch, cost, inputs):
    return pl.pallas_call(
        kernel,
        out_shape=out_shape,
        in_specs=[pl.BlockSpec(memory_space=pltpu.SMEM)]
        + [pl.BlockSpec(memory_space=pltpu.VMEM)] * (len(inputs) - 1),
        out_specs=pl.BlockSpec(memory_space=pltpu.VMEM),
        scratch_shapes=scratch,
        compiler_params=pltpu.CompilerParams(vmem_limit_bytes=48 << 20),
        cost_estimate=cost,
    )(*inputs)


def attention_fwd(info, qkv, shards, heads):
    total, width = qkv.shape
    units = total // (shards * UNIT)
    own = (heads + 1) * HD
    return vmem_call(
        functools.partial(fwd_kernel, shards, units, heads),
        jax.ShapeDtypeStruct((total, own), BF),
        [pltpu.VMEM((total, width), BF), pltpu.VMEM((total, own), BF)],
        pl.CostEstimate(flops=1, bytes_accessed=1, transcendentals=0),
        (info, qkv),
    )


def attention_bwd(info, qkv, d_mixed, shards, heads):
    total, width = qkv.shape
    units = total // (shards * UNIT)
    own = (heads + 1) * HD
    return vmem_call(
        functools.partial(bwd_kernel, shards, units, heads),
        jax.ShapeDtypeStruct((total, width), BF),
        [
            pltpu.VMEM((total, width), BF),
            pltpu.VMEM((total, own), BF),
            pltpu.VMEM((total, own), BF),
            pltpu.VMEM((total, own), F32),
            pltpu.VMEM((total, own), F32),
        ],
        pl.CostEstimate(flops=1, bytes_accessed=1, transcendentals=0),
        (info, qkv, d_mixed),
    )


def on_place(me, core, shards, run):
    for m in range(shards):
        for c in range(2):

            @pl.when((me == m) & (core == c))
            def _():
                run(m, c)


def attn_columns(value, j, heads):
    main = heads * HD
    first = D // main * main
    parts = [value[:, p * D + j * main : p * D + (j + 1) * main] for p in range(3)]
    parts += [value[:, p * D + first : (p + 1) * D] for p in range(3)]
    return jnp.concatenate(parts, axis=1)


def fc_columns(value, j, width):
    return value[:, j * width : (j + 1) * width]


def pack_kernel(shards, half, step, columns, at_ref, dep_ref, weight_ref, *outs):
    del dep_ref

    def run(m, c):
        outs[0][...] = columns(weight_ref, m)
        for d in range(1, shards):
            piece = columns(weight_ref.at[c * step : c * step + half], m ^ d)
            outs[d][...] = piece

    on_place(at_ref[0], at_ref[1], shards, run)


def pack_attn_kernel(shards, half, step, heads, count, at_ref, weight_ref, *refs):
    sources, outs = refs[:count], refs[count : count + shards]
    vectors, sems = refs[count + shards : 2 * count + shards], refs[2 * count + shards]
    length = vectors[0].shape[0]
    copies = [
        pltpu.make_async_copy(source, vector, sems.at[i])
        for i, (source, vector) in enumerate(zip(sources, vectors))
    ]
    for copy in copies:
        copy.start()

    def run(m, c):
        outs[0][: shards_rows(outs[0]), :] = attn_columns(weight_ref, m, heads)
        for d in range(1, shards):
            outs[d][:half, :] = attn_columns(weight_ref.at[c * step : c * step + half], m ^ d, heads)

    def shards_rows(ref):
        return ref.shape[0] - VEC_ROWS

    on_place(at_ref[0], at_ref[1], shards, run)
    for copy in copies:
        copy.wait()
    width = outs[0].shape[1]
    block = jnp.concatenate(
        [v[...].astype(F32).reshape(1, length) for v in vectors]
        + [jnp.zeros((VEC_ROWS - count, length), F32)],
        axis=0,
    )
    block = jnp.concatenate(
        [block, jnp.zeros((VEC_ROWS, width - length), F32)], axis=1
    ).astype(BF)
    for out in outs:
        out[out.shape[0] - VEC_ROWS :, :] = block


def hold_kernel(at_ref, dep_ref, value_ref, out_ref):
    del at_ref, dep_ref
    out_ref[...] = value_ref[...]


def place_attn_kernel(shards, half, step, rows, count, at_ref, *refs):
    own, mine, other = refs[0], refs[1:shards], refs[shards]
    out, vec = refs[shards + 1 :]

    def run(m, c):
        out[m * rows : (m + 1) * rows, :] = own[:rows]
        for d in range(1, shards):
            base = (m ^ d) * rows
            a, b = mine[d - 1][:half], other[d - 1]
            low, high = (a, b) if c == 0 else (b, a)
            out[base : base + step, :] = low[:step]
            out[base + step : base + rows, :] = high
        for j in range(shards):
            ref, at = (own, rows) if j == m else (mine[(j ^ m) - 1], half)
            vec[:, j * rows : (j + 1) * rows] = ref[at : at + VEC_ROWS, :rows].astype(F32)[:count]

    on_place(at_ref[0], at_ref[1], shards, run)


def place_kernel(shards, half, step, rows, at_ref, *refs):
    own, mine, other, out = refs[0], refs[1:shards], refs[shards], refs[shards + 1]

    def run(m, c):
        out[m * rows : (m + 1) * rows, :] = own[...]
        for d in range(1, shards):
            base = (m ^ d) * rows
            low, high = (mine[d - 1][...], other[d - 1]) if c == 0 else (other[d - 1], mine[d - 1][...])
            out[base : base + step, :] = low[:step]
            out[base + step : base + rows, :] = high

    on_place(at_ref[0], at_ref[1], shards, run)


def pack_part_kernel(shards, length, stride, columns, at_ref, weight_ref, *outs):
    part = pl.ds(pl.multiple_of(at_ref[2] * stride, 16), length)
    for m in range(shards):

        @pl.when(at_ref[0] == m)
        def _():
            outs[0][...] = columns(weight_ref, m)
            for d in range(1, shards):
                outs[d][...] = columns(weight_ref.at[part], m ^ d)


def place_part_kernel(shards, length, stride, rows, at_ref, own, mine, near, across, out):
    me, q = at_ref[0], at_ref[2]
    out[pl.ds(pl.multiple_of(me * rows, 16), rows), :] = own[...]
    size = (shards - 1) * length
    for d in range(1, shards):
        base = jnp.bitwise_xor(me, d) * rows
        for flip, ref, first in ((0, mine, 0), (2, near, 0), (1, across, 0), (3, across, size)):
            to = base + jnp.bitwise_xor(q, flip) * stride
            row = first + (d - 1) * length
            out[pl.ds(pl.multiple_of(to, 16), length), :] = ref[row : row + length, :]


def unpack_kernel(shards, half, step, places, count, at_ref, *refs):
    mine, other, outs = refs[:count], refs[count : 2 * count], refs[2 * count :]

    def run(m, c):
        for d in range(shards):
            for index, where, part, row, low, high in places(m, d):
                out, width = outs[index], high - low
                a = mine[part][row : row + half, low:high]
                b = other[part][row : row + half, low:high]
                first, second = (a, b) if c == 0 else (b, a)
                out[:step, where : where + width] = first[:step].astype(F32)
                out[step:, where : where + width] = second.astype(F32)

    on_place(at_ref[0], at_ref[1], shards, run)


def local_call(kernel, out_shape, cost_bytes, at, *inputs, anywhere=(), scratch=()):
    vmem = pl.BlockSpec(memory_space=pltpu.VMEM)
    hbm = pl.BlockSpec(memory_space=pltpu.HBM)
    specs = [hbm if i in anywhere else vmem for i in range(len(inputs))]
    return pl.pallas_call(
        kernel,
        out_shape=out_shape,
        in_specs=[pl.BlockSpec(memory_space=pltpu.SMEM)] + specs,
        out_specs=jax.tree.map(lambda _: vmem, out_shape),
        scratch_shapes=list(scratch),
        compiler_params=pltpu.CompilerParams(vmem_limit_bytes=48 << 20),
        cost_estimate=pl.CostEstimate(flops=1, bytes_accessed=1, transcendentals=0),
    )(at, *inputs)


def body(
    tokens,
    cotangent,
    lengths,
    attn_weight,
    query_bias,
    value_bias,
    proj_weight,
    proj_bias,
    ln1_gain,
    ln1_bias,
    ln2_gain,
    ln2_bias,
    fc_weight,
    fc_bias,
    out_weight,
    out_bias,
):
    n = lax.axis_size("shard")
    planes = lax.axis_size("plane")
    me = lax.axis_index("shard")
    core = lax.axis_index("core")
    heads = (HEADS - 1) // n
    main = heads * HD
    spare = D - n * main
    own_rows = attn_weight.shape[0]
    own_ff = fc_bias.shape[0]
    rows = tokens.shape[1]
    half = -(-own_rows // 32) * 16
    step = own_rows - half
    quarter = lax.axis_index("plane") % 2 * 2 + core
    at = jnp.stack([me, core, quarter]).astype(jnp.int32)

    def swap(value, d):
        return lax.ppermute(value, "shard", [(i, i ^ d) for i in range(n)])

    def swap_plane(value):
        return lax.ppermute(value, "plane", [(i, i ^ 1) for i in range(planes)])

    def swap_core(value):
        return lax.ppermute(value, "core", [(0, 1), (1, 0)])

    def gather_near(value):
        if n != 4:
            return [swap(value, d) for d in range(1, n)]
        return [swap(value, 1), swap(value, 2)]

    def gather_far(value, near):
        if n != 4:
            return [value] + near
        one, two = near
        cut = value.shape[0] // 32 * 16
        three = jnp.concatenate([swap(one[:cut], 2), swap(two[cut:], 1)], axis=0)
        return [value, one, two, three]

    def gather(value):
        return gather_far(value, gather_near(value))

    def pick(stacked, index):
        return lax.dynamic_index_in_dim(stacked, index, 0, keepdims=False)

    def natural(pieces):
        stacked = jnp.stack(pieces)
        return [pick(stacked, me ^ j) for j in range(n)]

    def after(value, *deps):
        return lax.optimization_barrier((value, deps))[0]

    def block(value, d):
        return value[d * rows : (d + 1) * rows]

    def place(own, mine):
        other = swap_core(jnp.stack(mine))
        return local_call(
            functools.partial(place_kernel, n, half, step, own_rows),
            jax.ShapeDtypeStruct((n * own_rows, own.shape[1]), BF),
            n * own.size * 4,
            at,
            own,
            *mine,
            other,
        )

    def pack(weight, columns, width, dep):
        shapes = [jax.ShapeDtypeStruct((own_rows, width), BF)]
        shapes += [jax.ShapeDtypeStruct((half, width), BF)] * (n - 1)
        return local_call(
            functools.partial(pack_kernel, n, half, step, columns),
            shapes,
            weight.size * 2,
            at,
            dep,
            weight,
            anywhere=(0,),
        )

    def reduce_rows(parts, *deps):
        got = after([swap(parts[d].astype(BF), d) for d in range(1, n)], *deps)
        total = parts[0].astype(F32)
        for part in got:
            total = total + part.astype(F32)
        return total

    def core_halves(parts):
        keep = lax.dynamic_slice_in_dim(parts, core * step, half, 1)
        give = lax.dynamic_slice_in_dim(parts, (1 - core) * step, half, 1)
        return (keep.astype(F32) + swap_core(give).astype(F32)).astype(BF)

    vectors = (
        query_bias, value_bias, proj_bias, ln1_gain, ln1_bias, ln2_gain, ln2_bias, out_bias
    )
    tokens_near = gather_near(tokens[0])
    attn_width = 3 * (main + spare)
    attn_sent = local_call(
        functools.partial(pack_attn_kernel, n, half, step, heads, len(vectors)),
        [jax.ShapeDtypeStruct((own_rows + VEC_ROWS, attn_width), BF)]
        + [jax.ShapeDtypeStruct((half + VEC_ROWS, attn_width), BF)] * (n - 1),
        attn_weight.size * 2,
        at,
        attn_weight,
        *vectors,
        anywhere=range(1, len(vectors) + 1),
        scratch=[pltpu.VMEM((own_rows,), BF)] * len(vectors)
        + [pltpu.SemaphoreType.DMA((len(vectors),))],
    )
    attn_got = [swap(attn_sent[d], d) for d in range(1, n)]
    attn_got, tokens_near = after((attn_got, tokens_near))
    attn_other = swap_core(jnp.stack([piece[:half] for piece in attn_got]))
    tokens_parts = gather_far(tokens[0], tokens_near)
    w_attn, small = local_call(
        functools.partial(place_attn_kernel, n, half, step, own_rows, len(vectors)),
        [
            jax.ShapeDtypeStruct((D, attn_width), BF),
            jax.ShapeDtypeStruct((len(vectors), D), F32),
        ],
        D * attn_width * 4,
        at,
        attn_sent[0],
        *attn_got,
        attn_other,
    )
    b_query, b_value, b_proj, gain_one, bias_one, gain_two, bias_two, b_out = [
        small[i] for i in range(8)
    ]

    def my_columns(vector):
        return lax.dynamic_slice_in_dim(vector, me * main, main, 0), vector[n * main :]

    q_main, q_spare = my_columns(b_query)
    v_main, v_spare = my_columns(b_value)
    qkv_bias = jnp.concatenate(
        [q_main, jnp.zeros_like(q_main), v_main, q_spare, jnp.zeros_like(q_spare), v_spare]
    )

    group_tokens = jnp.concatenate(tokens_parts, axis=0)
    proj_half = lax.dynamic_slice_in_dim(after(proj_weight, attn_got), core * step, half, 0)
    proj_near = gather_near(proj_half)
    own_cot = cotangent[0]
    late_fc = after(fc_weight, attn_got)
    stride = own_rows // 64 * 16
    length = own_rows - 3 * stride
    by_parts = own_rows % 16 == 0 and stride > 0 and planes % 2 == 0
    if by_parts:
        fc_sent = local_call(
            functools.partial(
                pack_part_kernel, n, length, stride, lambda ref, j: fc_columns(ref, j, own_ff)
            ),
            [jax.ShapeDtypeStruct((own_rows, own_ff), BF)]
            + [jax.ShapeDtypeStruct((length, own_ff), BF)] * (n - 1),
            fc_weight.size * 2,
            at,
            late_fc,
        )
    else:
        fc_sent = pack(late_fc, lambda ref, j: fc_columns(ref, j, own_ff), own_ff, lengths)
    xhat_one, _ = normalize(group_tokens.astype(F32))
    normed = (xhat_one * gain_one + bias_one).astype(BF)
    qkv = (jnp.dot(normed, w_attn, preferred_element_type=F32) + qkv_bias).astype(BF)
    late_cot = local_call(
        hold_kernel,
        jax.ShapeDtypeStruct(own_cot.shape, BF),
        own_cot.size * 4,
        at,
        small,
        own_cot,
    )
    qkv, proj_near, fc_sent = after((qkv, proj_near, fc_sent))
    cot_all = lax.all_gather(late_cot, "shard", axis=0, tiled=True)
    proj_parts = gather_far(proj_half, proj_near)
    fc_got = [swap(fc_sent[d], d) for d in range(1, n)]
    info = jnp.concatenate([lengths[0], me.astype(jnp.int32)[None]])
    mixed_heads = attention_fwd(info, qkv, n, heads)
    mixed_heads, proj_parts, fc_first = after((mixed_heads, proj_parts, fc_got[:-1]))
    fc_got = list(fc_first) + fc_got[-1:]
    if by_parts:
        fc_mine = jnp.concatenate(fc_got)
        fc_near = swap_plane(fc_mine)
    got = [block(mixed_heads, 0)[:, :main]] + [
        swap(block(mixed_heads, d)[:, :main], d) for d in range(1, n)
    ]
    w_proj = place(proj_weight, proj_parts[1:])
    got, w_proj, cot_all = after((got, w_proj, cot_all))
    mixed_low = jnp.concatenate(natural(got) + [block(mixed_heads, 0)[:, main:]], axis=1)
    own_tokens = tokens[0].astype(F32)
    middle = own_tokens + jnp.dot(mixed_low, w_proj, preferred_element_type=F32) + b_proj
    xhat_two, inv_two = normalize(middle)
    own_normed_two = (xhat_two * gain_two + bias_two).astype(BF)
    normed_near = gather_near(own_normed_two)
    cot_parts = [own_cot] + [
        lax.dynamic_slice_in_dim(cot_all, (me ^ d) * rows, rows, 0) for d in range(1, n)
    ]
    group_cot = jnp.concatenate(cot_parts, axis=0)
    d_active = cols_dot(group_cot, out_weight).astype(BF)
    if by_parts:
        fc_mine, fc_near = after((fc_mine, fc_near), own_normed_two)
        w_fc = local_call(
            functools.partial(place_part_kernel, n, length, stride, own_rows),
            jax.ShapeDtypeStruct((D, own_ff), BF),
            D * own_ff * 4,
            at,
            fc_sent[0],
            fc_mine,
            fc_near,
            swap_core(jnp.concatenate([fc_mine, fc_near])),
        )
    else:
        w_fc = place(fc_sent[0], fc_got)
    normed_near, d_active = after((normed_near, d_active))

    def feed(part):
        hidden = jnp.dot(part, w_fc, preferred_element_type=F32) + fc_bias.astype(F32)
        inner = jnp.tanh(0.7978845608028654 * (hidden + 0.044715 * hidden * hidden * hidden))
        slope = 0.5 * (1.0 + inner) + 0.5 * hidden * (1.0 - inner * inner) * (
            0.7978845608028654 * (1.0 + 3 * 0.044715 * hidden * hidden)
        )
        return (0.5 * hidden * (1.0 + inner)).astype(BF), slope.astype(BF)

    if n == 4:
        one, two = normed_near
        cut = rows // 32 * 16
        far = [swap(one[:cut], 2), swap(two[cut:], 1)]
        fed = [feed(part) for part in (own_normed_two, one, two)]
        far, fed = after((far, fed))
        normed_parts = [own_normed_two, one, two, jnp.concatenate(far, axis=0)]
        fed.append(feed(normed_parts[3]))
    else:
        normed_parts = gather_far(own_normed_two, normed_near)
        fed = [feed(part) for part in normed_parts]
    active_parts = [a for a, _ in fed]
    active = jnp.concatenate(active_parts, axis=0)

    grad_out_weight = rows_dot(active, group_cot).astype(BF)
    sum_out_weight = lax.psum(grad_out_weight, ("plane", "core"))
    d_active = after(d_active, grad_out_weight)
    d_hidden_parts = [
        (block(d_active, d).astype(F32) * slope.astype(F32)).astype(BF)
        for d, (_, slope) in enumerate(fed)
    ]
    d_hidden = jnp.concatenate(d_hidden_parts, axis=0)
    normed_two = jnp.concatenate(after(normed_parts, d_hidden_parts), axis=0)
    e = reduce_rows([cols_dot(part, w_fc) for part in d_hidden_parts])
    e_gain = e * gain_two
    d_middle = own_cot.astype(F32) + inv_two * (
        e_gain
        - jnp.mean(e_gain, axis=-1, keepdims=True)
        - xhat_two * jnp.mean(e_gain * xhat_two, axis=-1, keepdims=True)
    )
    d_branch = d_middle.astype(BF)
    d_mixed = cols_dot(d_branch, w_proj).astype(BF)
    for_heads = jnp.stack([d_mixed[:, j * main : (j + 1) * main] for j in range(n)])
    last = d_mixed[:, n * main :]
    dmix_parts = [jnp.concatenate([pick(for_heads, me), last], axis=1)] + [
        swap(jnp.concatenate([pick(for_heads, me ^ d), last], axis=1), d) for d in range(1, n)
    ]

    grad_fc = rows_dot(normed_two, d_hidden).astype(BF).reshape(n, own_rows, own_ff)
    fc_halves = after(core_halves(grad_fc), dmix_parts)
    fc_parts = jnp.concatenate(
        [pick(fc_halves, me)] + [swap(pick(fc_halves, me ^ d), d) for d in range(1, n)]
    )
    fc_sum = lax.psum(fc_parts, "plane")
    sum_out_weight = after(sum_out_weight, fc_parts).astype(F32)
    grad_fc_bias = jnp.sum(d_hidden.astype(F32), axis=0)

    d_qkv = attention_bwd(info, qkv, jnp.concatenate(dmix_parts, axis=0), n, heads)
    d_qkv, fc_parts = after((d_qkv, fc_parts))

    grad_proj = rows_dot(mixed_low, d_branch).astype(BF).reshape(n, own_rows, D)
    proj_halves = after(core_halves(grad_proj), fc_parts)
    proj_part = reduce_rows([pick(proj_halves, me ^ d) for d in range(n)]).astype(BF)

    grad_main = rows_dot(normed, d_qkv[:, : 3 * main]).astype(BF).reshape(n, own_rows, 3 * main)
    grad_spare = rows_dot(normed, d_qkv[:, 3 * main :]).astype(BF).reshape(n, own_rows, 3 * spare)
    main_halves = core_halves(grad_main)
    spare_halves = core_halves(pick(grad_spare, me)[None])[0]
    attn_parts = jnp.concatenate(
        [pick(main_halves, me)]
        + [swap(pick(main_halves, me ^ d), d) for d in range(1, n)]
        + [spare_halves, proj_part],
        axis=1,
    )
    attn_sum = lax.psum(after(attn_parts, fc_sum), "plane")

    counted = (lax.broadcasted_iota(jnp.int32, (n * rows, 1), 0) < rows) | (
        lax.broadcasted_iota(jnp.int32, (1, d_qkv.shape[1]), 1) < 3 * main
    )
    d_once = after(jnp.where(counted, d_qkv, BF(0)), attn_parts)
    f = reduce_rows([cols_dot(block(d_once, d), w_attn) for d in range(n)])
    xhat_own, inv_own = normalize(own_tokens)
    f_gain = f * gain_one
    d_tokens = inv_own * (
        f_gain
        - jnp.mean(f_gain, axis=-1, keepdims=True)
        - xhat_own * jnp.mean(f_gain * xhat_own, axis=-1, keepdims=True)
    )
    input_grad = (d_middle + d_tokens).astype(BF)[None]

    late_active = after(active, attn_parts)
    out_parts = [
        jnp.dot(block(late_active, d), out_weight, preferred_element_type=F32) for d in range(n)
    ]
    output = (middle + reduce_rows(out_parts) + b_out).astype(BF)[None]

    sum_fc_weight = local_call(
        functools.partial(
            unpack_kernel,
            n,
            half,
            step,
            lambda m, d: [(0, (m ^ d) * own_ff, 0, d * half, 0, own_ff)],
            1,
        ),
        [jax.ShapeDtypeStruct((own_rows, n * own_ff), F32)],
        own_rows * n * own_ff * 8,
        at,
        fc_sum,
        swap_core(fc_sum),
    )[0]

    def attn_places(m, d):
        base = d * 3 * main
        places = [
            (0, p * D + (m ^ d) * main, 0, 0, base + p * main, base + (p + 1) * main)
            for p in range(3)
        ]
        if d == 0:
            base = n * 3 * main
            places += [
                (0, p * D + n * main, 0, 0, base + p * spare, base + (p + 1) * spare)
                for p in range(3)
            ]
            places.append((1, 0, 0, 0, 3 * D, 4 * D))
        return places

    d_once_sum = jnp.sum(d_once.astype(F32), axis=0)

    def vector_of(part):
        whole = jnp.zeros((D,), F32)
        whole = lax.dynamic_update_slice_in_dim(
            whole, d_once_sum[part * main : (part + 1) * main], me * main, 0
        )
        lane = 3 * main + part * spare
        return jnp.concatenate([whole[: n * main], d_once_sum[lane : lane + spare]])

    early = after(
        (
            jnp.sum(d_branch.astype(F32), axis=0),
            jnp.sum(e * xhat_two, axis=0),
            jnp.sum(e, axis=0),
            jnp.sum(own_cot.astype(F32), axis=0),
        ),
        attn_parts,
    )
    small_grads = jnp.stack(
        [
            vector_of(0),
            vector_of(2),
            early[0],
            jnp.sum(f * xhat_own, axis=0),
            jnp.sum(f, axis=0),
            early[1],
            early[2],
            early[3],
        ]
    )
    small_grads = small_grads.reshape(8, n, own_rows).transpose(1, 0, 2)
    small_own = pick(small_grads, me)
    for d in range(1, n):
        small_own = small_own + swap(pick(small_grads, me ^ d), d)
    small_own = jnp.concatenate([small_own, grad_fc_bias.reshape(-1, own_rows)], axis=0)
    small_own = small_own + swap_core(small_own)
    hop = 1
    while hop < planes:
        small_own = small_own + lax.ppermute(
            small_own, "plane", [(i, i ^ hop) for i in range(planes)]
        )
        hop *= 2
    attn_sum, small_own, output, input_grad, sum_fc_weight, sum_out_weight = after(
        (attn_sum, small_own, output, input_grad, sum_fc_weight, sum_out_weight)
    )
    sum_attn_weight, sum_proj_weight = local_call(
        functools.partial(unpack_kernel, n, half, step, attn_places, 1),
        [
            jax.ShapeDtypeStruct((own_rows, 3 * D), F32),
            jax.ShapeDtypeStruct((own_rows, D), F32),
        ],
        own_rows * 4 * D * 8,
        at,
        attn_sum,
        swap_core(attn_sum),
    )
    s = small_own[:8]
    sum_fc_bias = small_own[8:].reshape(-1)
    return (
        output,
        input_grad,
        sum_attn_weight,
        s[0],
        s[1],
        sum_proj_weight,
        s[2],
        s[3],
        s[4],
        s[5],
        s[6],
        sum_fc_weight,
        sum_fc_bias,
        sum_out_weight,
        s[7],
    )


def solution(mesh):
    shards, reps = mesh.devices.shape
    split = jax.sharding.Mesh(
        mesh.devices.reshape(shards, reps // 2, 2), ("shard", "plane", "core")
    )
    rep = ("plane", "core")
    batch = P(rep, "shard", None)
    row, vec = P("shard", None), P("shard")
    return jax.shard_map(
        body,
        mesh=split,
        in_specs=(batch, batch, P(rep, None), row, vec, vec, row)
        + (vec,) * 5
        + (row, vec, row, vec),
        out_specs=(batch, batch, row, vec, vec, row) + (vec,) * 5 + (row, vec, row, vec),
        check_vma=False,
    )
```

```python
import functools
import math

import jax
import jax.numpy as jnp
from jax import lax
from jax.experimental import pallas as pl
from jax.experimental.pallas import tpu as pltpu
from jax.sharding import PartitionSpec as P

D = 1600
HEADS = 25
HD = 64
UNIT = 32
LANES = 128
NEG = -1e30
VEC_ROWS = 16
BF = jnp.bfloat16
F32 = jnp.float32


def dot(left, right, dims):
    return lax.dot_general(left, right, (dims, ((), ())), preferred_element_type=F32)


def rows_dot(left, right):
    return dot(left, right, ((0,), (0,)))


def cols_dot(left, right):
    return dot(left, right, ((1,), (1,)))


def normalize(values):
    center = values - jnp.mean(values, axis=-1, keepdims=True)
    spread = jnp.mean(center * center, axis=-1, keepdims=True)
    inv = lax.rsqrt(spread + 1e-05)
    return center * inv, inv


def place_blocks(info_ref, shards, units):
    b0, b1, b2, me = info_ref[0], info_ref[1], info_ref[2], info_ref[3]
    e0, e1 = b0, b0 + b1
    places = []
    for d in range(shards):
        s = jnp.bitwise_xor(me, d)
        for u in range(units):
            first = jnp.where(u < e0, 0, jnp.where(u < e1, e0, e1))
            span = jnp.where(u < e0, b0, jnp.where(u < e1, b1, b2))
            places.append((d * units + u, first * shards + s * span + (u - first)))
    return places, e0, e1


def head_lanes(tile_rows, half):
    lane = lax.broadcasted_iota(jnp.int32, (tile_rows, LANES), 1)
    return (lane < HD) if half == 0 else (lane >= HD)


def window_scores(q, k, rows, width):
    scores = cols_dot(q, k)
    row = lax.broadcasted_iota(jnp.int32, (rows, width * rows), 0)
    col = lax.broadcasted_iota(jnp.int32, (rows, width * rows), 1)
    return jnp.where(col <= row + (width - 1) * rows, scores, NEG)


def fwd_kernel(shards, units, heads, info_ref, qkv_ref, out_ref, perm, mixed):
    block = UNIT
    rows = shards * block
    main = heads * HD
    places, e0, e1 = place_blocks(info_ref, shards, units)
    for src, dst in places:
        at = pl.ds(pl.multiple_of(dst * block, block), block)
        perm[at, :] = qkv_ref[src * block : (src + 1) * block, :]

    def unit(i, carry):
        first = jnp.where(i < e0, 0, jnp.where(i < e1, e0, e1))
        q_at = pl.ds(pl.multiple_of(i * rows, rows), rows)
        for width in range(1, 5):

            @pl.when(i - first + 1 == width)
            def _():
                k_at = pl.ds(pl.multiple_of(first * rows, rows), width * rows)

                def attend(q, k, v):
                    scores = window_scores(q * BF(0.125), k, rows, width)
                    top = jnp.max(scores, axis=1, keepdims=True)
                    probs = jnp.exp(scores - top)
                    total = jnp.sum(probs, axis=1, keepdims=True)
                    return dot(probs.astype(BF), v, ((1,), (0,))) / total

                for tile in range(main // LANES):
                    lanes = slice(tile * LANES, (tile + 1) * LANES)
                    k_lanes = slice(main + lanes.start, main + lanes.stop)
                    v_lanes = slice(2 * main + lanes.start, 2 * main + lanes.stop)
                    q, k, v = perm[q_at, lanes], perm[k_at, k_lanes], perm[k_at, v_lanes]
                    low = head_lanes(rows, 0)
                    zero = jnp.zeros_like(q)
                    left = attend(jnp.where(low, q, zero), k, v)
                    right = attend(jnp.where(low, zero, q), k, v)
                    mixed[q_at, lanes] = jnp.where(low, left, right).astype(BF)
                if main % LANES:
                    lanes = main - HD
                    mixed[q_at, lanes:main] = attend(
                        perm[q_at, lanes:main],
                        perm[k_at, main + lanes : 2 * main],
                        perm[k_at, 2 * main + lanes : 3 * main],
                    ).astype(BF)
                base = 3 * main
                mixed[q_at, main : main + HD] = attend(
                    perm[q_at, base : base + HD],
                    perm[k_at, base + HD : base + 2 * HD],
                    perm[k_at, base + 2 * HD : base + 3 * HD],
                ).astype(BF)

        return carry

    lax.fori_loop(0, units, unit, 0)
    for src, dst in places:
        at = pl.ds(pl.multiple_of(dst * block, block), block)
        out_ref[src * block : (src + 1) * block, :] = mixed[at, :]


def bwd_kernel(
    shards, units, heads, info_ref, qkv_ref, dmix_ref, out_ref, perm, dperm, dq_acc, dk_acc, dv_acc
):
    block = UNIT
    rows = shards * block
    main = heads * HD
    places, e0, e1 = place_blocks(info_ref, shards, units)
    for src, dst in places:
        at = pl.ds(pl.multiple_of(dst * block, block), block)
        perm[at, :] = qkv_ref[src * block : (src + 1) * block, :]
        dperm[at, :] = dmix_ref[src * block : (src + 1) * block, :]
    dk_acc[...] = jnp.zeros_like(dk_acc)
    dv_acc[...] = jnp.zeros_like(dv_acc)

    def unit(i, carry):
        first = jnp.where(i < e0, 0, jnp.where(i < e1, e0, e1))
        q_at = pl.ds(pl.multiple_of(i * rows, rows), rows)
        for width in range(1, 5):

            @pl.when(i - first + 1 == width)
            def _():
                k_at = pl.ds(pl.multiple_of(first * rows, rows), width * rows)

                def pull(q, k, v, g):
                    q = q * BF(0.125)
                    scores = window_scores(q, k, rows, width)
                    top = jnp.max(scores, axis=1, keepdims=True)
                    probs = jnp.exp(scores - top)
                    total = jnp.sum(probs, axis=1, keepdims=True)
                    probs = probs * (1.0 / total)
                    d_probs = cols_dot(g, v)
                    delta = jnp.sum(probs * d_probs, axis=1, keepdims=True)
                    d_scores = (probs * (d_probs - delta)).astype(BF)
                    d_q = dot(d_scores, k, ((1,), (0,))) * 0.125
                    return d_q, rows_dot(d_scores, q), rows_dot(probs.astype(BF), g)

                for tile in range(main // LANES):
                    lanes = slice(tile * LANES, (tile + 1) * LANES)
                    k_lanes = slice(main + lanes.start, main + lanes.stop)
                    v_lanes = slice(2 * main + lanes.start, 2 * main + lanes.stop)
                    q, k, v = perm[q_at, lanes], perm[k_at, k_lanes], perm[k_at, v_lanes]
                    g = dperm[q_at, lanes]
                    low = head_lanes(rows, 0)
                    zero = jnp.zeros_like(q)
                    dq0, dk0, dv0 = pull(jnp.where(low, q, zero), k, v, jnp.where(low, g, zero))
                    dq1, dk1, dv1 = pull(jnp.where(low, zero, q), k, v, jnp.where(low, zero, g))
                    dq_acc[q_at, lanes] = jnp.where(low, dq0, dq1).astype(BF)
                    dk_acc[k_at, lanes] += dk0 + dk1
                    dv_acc[k_at, lanes] += dv0 + dv1
                extra = [(main, 3 * main, 3 * main + HD, 3 * main + 2 * HD)]
                if main % LANES:
                    extra.append((main - HD, main - HD, 2 * main - HD, 3 * main - HD))
                for own, q_lane, k_lane, v_lane in extra:
                    dq0, dk0, dv0 = pull(
                        perm[q_at, q_lane : q_lane + HD],
                        perm[k_at, k_lane : k_lane + HD],
                        perm[k_at, v_lane : v_lane + HD],
                        dperm[q_at, own : own + HD],
                    )
                    dq_acc[q_at, own : own + HD] = dq0.astype(BF)
                    dk_acc[k_at, own : own + HD] += dk0
                    dv_acc[k_at, own : own + HD] += dv0

        return carry

    lax.fori_loop(0, units, unit, 0)
    for src, dst in places:
        at = pl.ds(pl.multiple_of(dst * block, block), block)
        to = slice(src * block, (src + 1) * block)
        for part, acc in enumerate((dq_acc, dk_acc, dv_acc)):
            got = acc[at, :].astype(BF)
            out_ref[to, part * main : (part + 1) * main] = got[:, :main]
            lane = 3 * main + part * HD
            out_ref[to, lane : lane + HD] = got[:, main:]


def vmem_call(kernel, out_shape, scratch, cost, inputs):
    return pl.pallas_call(
        kernel,
        out_shape=out_shape,
        in_specs=[pl.BlockSpec(memory_space=pltpu.SMEM)]
        + [pl.BlockSpec(memory_space=pltpu.VMEM)] * (len(inputs) - 1),
        out_specs=pl.BlockSpec(memory_space=pltpu.VMEM),
        scratch_shapes=scratch,
        compiler_params=pltpu.CompilerParams(vmem_limit_bytes=48 << 20),
        cost_estimate=cost,
    )(*inputs)


def attention_fwd(info, qkv, shards, heads):
    total, width = qkv.shape
    units = total // (shards * UNIT)
    own = (heads + 1) * HD
    return vmem_call(
        functools.partial(fwd_kernel, shards, units, heads),
        jax.ShapeDtypeStruct((total, own), BF),
        [pltpu.VMEM((total, width), BF), pltpu.VMEM((total, own), BF)],
        pl.CostEstimate(flops=1, bytes_accessed=1, transcendentals=0),
        (info, qkv),
    )


def attention_bwd(info, qkv, d_mixed, shards, heads):
    total, width = qkv.shape
    units = total // (shards * UNIT)
    own = (heads + 1) * HD
    return vmem_call(
        functools.partial(bwd_kernel, shards, units, heads),
        jax.ShapeDtypeStruct((total, width), BF),
        [
            pltpu.VMEM((total, width), BF),
            pltpu.VMEM((total, own), BF),
            pltpu.VMEM((total, own), BF),
            pltpu.VMEM((total, own), F32),
            pltpu.VMEM((total, own), F32),
        ],
        pl.CostEstimate(flops=1, bytes_accessed=1, transcendentals=0),
        (info, qkv, d_mixed),
    )


def on_place(me, core, shards, run):
    for m in range(shards):
        for c in range(2):

            @pl.when((me == m) & (core == c))
            def _():
                run(m, c)


def attn_columns(value, j, heads):
    main = heads * HD
    first = D // main * main
    parts = [value[:, p * D + j * main : p * D + (j + 1) * main] for p in range(3)]
    parts += [value[:, p * D + first : (p + 1) * D] for p in range(3)]
    return jnp.concatenate(parts, axis=1)


def fc_columns(value, j, width):
    return value[:, j * width : (j + 1) * width]


def pack_kernel(shards, half, step, columns, at_ref, dep_ref, weight_ref, *outs):
    del dep_ref

    def run(m, c):
        outs[0][...] = columns(weight_ref, m)
        for d in range(1, shards):
            piece = columns(weight_ref.at[c * step : c * step + half], m ^ d)
            outs[d][...] = piece

    on_place(at_ref[0], at_ref[1], shards, run)


def pack_attn_kernel(shards, half, step, heads, count, at_ref, weight_ref, *refs):
    sources, outs = refs[:count], refs[count : count + shards]
    vectors, sems = refs[count + shards : 2 * count + shards], refs[2 * count + shards]
    length = vectors[0].shape[0]
    copies = [
        pltpu.make_async_copy(source, vector, sems.at[i])
        for i, (source, vector) in enumerate(zip(sources, vectors))
    ]
    for copy in copies:
        copy.start()

    def run(m, c):
        outs[0][: shards_rows(outs[0]), :] = attn_columns(weight_ref, m, heads)
        for d in range(1, shards):
            outs[d][:half, :] = attn_columns(weight_ref.at[c * step : c * step + half], m ^ d, heads)

    def shards_rows(ref):
        return ref.shape[0] - VEC_ROWS

    on_place(at_ref[0], at_ref[1], shards, run)
    for copy in copies:
        copy.wait()
    width = outs[0].shape[1]
    block = jnp.concatenate(
        [v[...].astype(F32).reshape(1, length) for v in vectors]
        + [jnp.zeros((VEC_ROWS - count, length), F32)],
        axis=0,
    )
    block = jnp.concatenate(
        [block, jnp.zeros((VEC_ROWS, width - length), F32)], axis=1
    ).astype(BF)
    for out in outs:
        out[out.shape[0] - VEC_ROWS :, :] = block


def place_attn_kernel(shards, half, step, rows, count, at_ref, *refs):
    own, mine, other = refs[0], refs[1:shards], refs[shards]
    out, vec = refs[shards + 1 :]

    def run(m, c):
        out[m * rows : (m + 1) * rows, :] = own[:rows]
        for d in range(1, shards):
            base = (m ^ d) * rows
            a, b = mine[d - 1][:half], other[d - 1]
            low, high = (a, b) if c == 0 else (b, a)
            out[base : base + step, :] = low[:step]
            out[base + step : base + rows, :] = high
        for j in range(shards):
            ref, at = (own, rows) if j == m else (mine[(j ^ m) - 1], half)
            vec[:, j * rows : (j + 1) * rows] = ref[at : at + VEC_ROWS, :rows].astype(F32)[:count]

    on_place(at_ref[0], at_ref[1], shards, run)


def place_kernel(shards, half, step, rows, at_ref, *refs):
    own, mine, other, out = refs[0], refs[1:shards], refs[shards], refs[shards + 1]

    def run(m, c):
        out[m * rows : (m + 1) * rows, :] = own[...]
        for d in range(1, shards):
            base = (m ^ d) * rows
            low, high = (mine[d - 1][...], other[d - 1]) if c == 0 else (other[d - 1], mine[d - 1][...])
            out[base : base + step, :] = low[:step]
            out[base + step : base + rows, :] = high

    on_place(at_ref[0], at_ref[1], shards, run)


def pack_part_kernel(shards, length, stride, columns, at_ref, weight_ref, *outs):
    part = pl.ds(pl.multiple_of(at_ref[2] * stride, 16), length)
    for m in range(shards):

        @pl.when(at_ref[0] == m)
        def _():
            outs[0][...] = columns(weight_ref, m)
            for d in range(1, shards):
                outs[d][...] = columns(weight_ref.at[part], m ^ d)


def place_part_kernel(shards, length, stride, rows, at_ref, own, mine, near, across, out):
    me, q = at_ref[0], at_ref[2]
    out[pl.ds(pl.multiple_of(me * rows, 16), rows), :] = own[...]
    size = (shards - 1) * length
    for d in range(1, shards):
        base = jnp.bitwise_xor(me, d) * rows
        for flip, ref, first in ((0, mine, 0), (2, near, 0), (1, across, 0), (3, across, size)):
            to = base + jnp.bitwise_xor(q, flip) * stride
            row = first + (d - 1) * length
            out[pl.ds(pl.multiple_of(to, 16), length), :] = ref[row : row + length, :]


def unpack_kernel(shards, half, step, places, count, at_ref, *refs):
    mine, other, outs = refs[:count], refs[count : 2 * count], refs[2 * count :]

    def run(m, c):
        for d in range(shards):
            for index, where, part, row, low, high in places(m, d):
                out, width = outs[index], high - low
                a = mine[part][row : row + half, low:high]
                b = other[part][row : row + half, low:high]
                first, second = (a, b) if c == 0 else (b, a)
                out[:step, where : where + width] = first[:step].astype(F32)
                out[step:, where : where + width] = second.astype(F32)

    on_place(at_ref[0], at_ref[1], shards, run)


def local_call(kernel, out_shape, cost_bytes, at, *inputs, anywhere=(), scratch=()):
    vmem = pl.BlockSpec(memory_space=pltpu.VMEM)
    hbm = pl.BlockSpec(memory_space=pltpu.HBM)
    specs = [hbm if i in anywhere else vmem for i in range(len(inputs))]
    return pl.pallas_call(
        kernel,
        out_shape=out_shape,
        in_specs=[pl.BlockSpec(memory_space=pltpu.SMEM)] + specs,
        out_specs=jax.tree.map(lambda _: vmem, out_shape),
        scratch_shapes=list(scratch),
        compiler_params=pltpu.CompilerParams(vmem_limit_bytes=48 << 20),
        cost_estimate=pl.CostEstimate(flops=1, bytes_accessed=1, transcendentals=0),
    )(at, *inputs)


def body(
    tokens,
    cotangent,
    lengths,
    attn_weight,
    query_bias,
    value_bias,
    proj_weight,
    proj_bias,
    ln1_gain,
    ln1_bias,
    ln2_gain,
    ln2_bias,
    fc_weight,
    fc_bias,
    out_weight,
    out_bias,
):
    n = lax.axis_size("shard")
    planes = lax.axis_size("plane")
    me = lax.axis_index("shard")
    core = lax.axis_index("core")
    heads = (HEADS - 1) // n
    main = heads * HD
    spare = D - n * main
    own_rows = attn_weight.shape[0]
    own_ff = fc_bias.shape[0]
    rows = tokens.shape[1]
    half = -(-own_rows // 32) * 16
    step = own_rows - half
    quarter = lax.axis_index("plane") % 2 * 2 + core
    at = jnp.stack([me, core, quarter]).astype(jnp.int32)

    def swap(value, d):
        return lax.ppermute(value, "shard", [(i, i ^ d) for i in range(n)])

    def swap_plane(value):
        return lax.ppermute(value, "plane", [(i, i ^ 1) for i in range(planes)])

    def swap_core(value):
        return lax.ppermute(value, "core", [(0, 1), (1, 0)])

    def gather_near(value):
        if n != 4:
            return [swap(value, d) for d in range(1, n)]
        return [swap(value, 1), swap(value, 2)]

    def gather_far(value, near):
        if n != 4:
            return [value] + near
        one, two = near
        cut = value.shape[0] // 32 * 16
        three = jnp.concatenate([swap(one[:cut], 2), swap(two[cut:], 1)], axis=0)
        return [value, one, two, three]

    def gather(value):
        return gather_far(value, gather_near(value))

    def pick(stacked, index):
        return lax.dynamic_index_in_dim(stacked, index, 0, keepdims=False)

    def natural(pieces):
        stacked = jnp.stack(pieces)
        return [pick(stacked, me ^ j) for j in range(n)]

    def after(value, *deps):
        return lax.optimization_barrier((value, deps))[0]

    def block(value, d):
        return value[d * rows : (d + 1) * rows]

    def place(own, mine):
        other = swap_core(jnp.stack(mine))
        return local_call(
            functools.partial(place_kernel, n, half, step, own_rows),
            jax.ShapeDtypeStruct((n * own_rows, own.shape[1]), BF),
            n * own.size * 4,
            at,
            own,
            *mine,
            other,
        )

    def pack(weight, columns, width, dep):
        shapes = [jax.ShapeDtypeStruct((own_rows, width), BF)]
        shapes += [jax.ShapeDtypeStruct((half, width), BF)] * (n - 1)
        return local_call(
            functools.partial(pack_kernel, n, half, step, columns),
            shapes,
            weight.size * 2,
            at,
            dep,
            weight,
            anywhere=(0,),
        )

    def reduce_rows(parts, *deps):
        got = after([swap(parts[d].astype(BF), d) for d in range(1, n)], *deps)
        total = parts[0].astype(F32)
        for part in got:
            total = total + part.astype(F32)
        return total

    def core_halves(parts):
        keep = lax.dynamic_slice_in_dim(parts, core * step, half, 1)
        give = lax.dynamic_slice_in_dim(parts, (1 - core) * step, half, 1)
        return (keep.astype(F32) + swap_core(give).astype(F32)).astype(BF)

    vectors = (
        query_bias, value_bias, proj_bias, ln1_gain, ln1_bias, ln2_gain, ln2_bias, out_bias
    )
    tokens_near = gather_near(tokens[0])
    attn_width = 3 * (main + spare)
    attn_sent = local_call(
        functools.partial(pack_attn_kernel, n, half, step, heads, len(vectors)),
        [jax.ShapeDtypeStruct((own_rows + VEC_ROWS, attn_width), BF)]
        + [jax.ShapeDtypeStruct((half + VEC_ROWS, attn_width), BF)] * (n - 1),
        attn_weight.size * 2,
        at,
        attn_weight,
        *vectors,
        anywhere=range(1, len(vectors) + 1),
        scratch=[pltpu.VMEM((own_rows,), BF)] * len(vectors)
        + [pltpu.SemaphoreType.DMA((len(vectors),))],
    )
    attn_got = [swap(attn_sent[d], d) for d in range(1, n)]
    attn_got, tokens_near = after((attn_got, tokens_near))
    attn_other = swap_core(jnp.stack([piece[:half] for piece in attn_got]))
    tokens_parts = gather_far(tokens[0], tokens_near)
    w_attn, small = local_call(
        functools.partial(place_attn_kernel, n, half, step, own_rows, len(vectors)),
        [
            jax.ShapeDtypeStruct((D, attn_width), BF),
            jax.ShapeDtypeStruct((len(vectors), D), F32),
        ],
        D * attn_width * 4,
        at,
        attn_sent[0],
        *attn_got,
        attn_other,
    )
    b_query, b_value, b_proj, gain_one, bias_one, gain_two, bias_two, b_out = [
        small[i] for i in range(8)
    ]

    def my_columns(vector):
        return lax.dynamic_slice_in_dim(vector, me * main, main, 0), vector[n * main :]

    q_main, q_spare = my_columns(b_query)
    v_main, v_spare = my_columns(b_value)
    qkv_bias = jnp.concatenate(
        [q_main, jnp.zeros_like(q_main), v_main, q_spare, jnp.zeros_like(q_spare), v_spare]
    )

    group_tokens = jnp.concatenate(tokens_parts, axis=0)
    proj_half = lax.dynamic_slice_in_dim(after(proj_weight, attn_got), core * step, half, 0)
    proj_near = gather_near(proj_half)
    own_cot = cotangent[0]
    cot_all = lax.all_gather(after(own_cot, attn_got, tokens_parts), "shard", axis=0, tiled=True)
    late_fc = after(fc_weight, attn_got)
    stride = own_rows // 64 * 16
    length = own_rows - 3 * stride
    by_parts = own_rows % 16 == 0 and stride > 0 and planes % 2 == 0
    if by_parts:
        fc_sent = local_call(
            functools.partial(
                pack_part_kernel, n, length, stride, lambda ref, j: fc_columns(ref, j, own_ff)
            ),
            [jax.ShapeDtypeStruct((own_rows, own_ff), BF)]
            + [jax.ShapeDtypeStruct((length, own_ff), BF)] * (n - 1),
            fc_weight.size * 2,
            at,
            late_fc,
        )
    else:
        fc_sent = pack(late_fc, lambda ref, j: fc_columns(ref, j, own_ff), own_ff, lengths)
    xhat_one, _ = normalize(group_tokens.astype(F32))
    normed = (xhat_one * gain_one + bias_one).astype(BF)
    qkv = (jnp.dot(normed, w_attn, preferred_element_type=F32) + qkv_bias).astype(BF)
    qkv, proj_near, fc_sent = after((qkv, proj_near, fc_sent))
    proj_parts = gather_far(proj_half, proj_near)
    fc_got = [swap(fc_sent[d], d) for d in range(1, n)]
    info = jnp.concatenate([lengths[0], me.astype(jnp.int32)[None]])
    mixed_heads = attention_fwd(info, qkv, n, heads)
    mixed_heads, proj_parts, fc_first = after((mixed_heads, proj_parts, fc_got[:-1]))
    fc_got = list(fc_first) + fc_got[-1:]
    if by_parts:
        fc_mine = jnp.concatenate(fc_got)
        fc_near = swap_plane(fc_mine)
    got = [block(mixed_heads, 0)[:, :main]] + [
        swap(block(mixed_heads, d)[:, :main], d) for d in range(1, n)
    ]
    w_proj = place(proj_weight, proj_parts[1:])
    got, w_proj, cot_all = after((got, w_proj, cot_all))
    mixed_low = jnp.concatenate(natural(got) + [block(mixed_heads, 0)[:, main:]], axis=1)
    own_tokens = tokens[0].astype(F32)
    middle = own_tokens + jnp.dot(mixed_low, w_proj, preferred_element_type=F32) + b_proj
    xhat_two, inv_two = normalize(middle)
    own_normed_two = (xhat_two * gain_two + bias_two).astype(BF)
    normed_near = gather_near(own_normed_two)
    if by_parts:
        w_fc = local_call(
            functools.partial(place_part_kernel, n, length, stride, own_rows),
            jax.ShapeDtypeStruct((D, own_ff), BF),
            D * own_ff * 4,
            at,
            fc_sent[0],
            fc_mine,
            fc_near,
            swap_core(jnp.concatenate(after([fc_mine, fc_near], own_normed_two))),
        )
    else:
        w_fc = place(fc_sent[0], fc_got)
    cot_parts = [own_cot] + [
        lax.dynamic_slice_in_dim(cot_all, (me ^ d) * rows, rows, 0) for d in range(1, n)
    ]
    group_cot = jnp.concatenate(cot_parts, axis=0)
    d_active = cols_dot(group_cot, out_weight).astype(BF)
    normed_near, d_active = after((normed_near, d_active))
    normed_parts = gather_far(own_normed_two, normed_near)
    normed_two = jnp.concatenate(normed_parts, axis=0)

    def feed(part):
        hidden = jnp.dot(part, w_fc, preferred_element_type=F32) + fc_bias.astype(F32)
        inner = jnp.tanh(0.7978845608028654 * (hidden + 0.044715 * hidden * hidden * hidden))
        slope = 0.5 * (1.0 + inner) + 0.5 * hidden * (1.0 - inner * inner) * (
            0.7978845608028654 * (1.0 + 3 * 0.044715 * hidden * hidden)
        )
        return (0.5 * hidden * (1.0 + inner)).astype(BF), slope.astype(BF)

    fed = [feed(part) for part in normed_parts]
    active_parts = [a for a, _ in fed]
    active = jnp.concatenate(active_parts, axis=0)

    grad_out_weight = rows_dot(active, group_cot).astype(BF)
    sum_out_weight = lax.psum(grad_out_weight, ("plane", "core"))
    d_active = after(d_active, grad_out_weight)
    d_hidden_parts = [
        (block(d_active, d).astype(F32) * slope.astype(F32)).astype(BF)
        for d, (_, slope) in enumerate(fed)
    ]
    d_hidden = jnp.concatenate(d_hidden_parts, axis=0)
    e = reduce_rows([cols_dot(part, w_fc) for part in d_hidden_parts])
    e_gain = e * gain_two
    d_middle = own_cot.astype(F32) + inv_two * (
        e_gain
        - jnp.mean(e_gain, axis=-1, keepdims=True)
        - xhat_two * jnp.mean(e_gain * xhat_two, axis=-1, keepdims=True)
    )
    d_branch = d_middle.astype(BF)
    d_mixed = cols_dot(d_branch, w_proj).astype(BF)
    for_heads = jnp.stack([d_mixed[:, j * main : (j + 1) * main] for j in range(n)])
    last = d_mixed[:, n * main :]
    dmix_parts = [jnp.concatenate([pick(for_heads, me), last], axis=1)] + [
        swap(jnp.concatenate([pick(for_heads, me ^ d), last], axis=1), d) for d in range(1, n)
    ]

    grad_fc = rows_dot(normed_two, d_hidden).astype(BF).reshape(n, own_rows, own_ff)
    fc_halves = after(core_halves(grad_fc), dmix_parts)
    fc_parts = jnp.concatenate(
        [pick(fc_halves, me)] + [swap(pick(fc_halves, me ^ d), d) for d in range(1, n)]
    )
    fc_sum = lax.psum(fc_parts, "plane")
    sum_out_weight = after(sum_out_weight, fc_parts).astype(F32)
    grad_fc_bias = jnp.sum(d_hidden.astype(F32), axis=0)

    d_qkv = attention_bwd(info, qkv, jnp.concatenate(dmix_parts, axis=0), n, heads)
    d_qkv, fc_parts = after((d_qkv, fc_parts))

    grad_proj = rows_dot(mixed_low, d_branch).astype(BF).reshape(n, own_rows, D)
    proj_halves = after(core_halves(grad_proj), fc_parts)
    proj_part = reduce_rows([pick(proj_halves, me ^ d) for d in range(n)]).astype(BF)

    grad_main = rows_dot(normed, d_qkv[:, : 3 * main]).astype(BF).reshape(n, own_rows, 3 * main)
    grad_spare = rows_dot(normed, d_qkv[:, 3 * main :]).astype(BF).reshape(n, own_rows, 3 * spare)
    main_halves = core_halves(grad_main)
    spare_halves = core_halves(pick(grad_spare, me)[None])[0]
    attn_parts = jnp.concatenate(
        [pick(main_halves, me)]
        + [swap(pick(main_halves, me ^ d), d) for d in range(1, n)]
        + [spare_halves, proj_part],
        axis=1,
    )
    attn_sum = lax.psum(after(attn_parts, fc_sum), "plane")

    counted = (lax.broadcasted_iota(jnp.int32, (n * rows, 1), 0) < rows) | (
        lax.broadcasted_iota(jnp.int32, (1, d_qkv.shape[1]), 1) < 3 * main
    )
    d_once = after(jnp.where(counted, d_qkv, BF(0)), attn_parts)
    f = reduce_rows([cols_dot(block(d_once, d), w_attn) for d in range(n)])
    xhat_own, inv_own = normalize(own_tokens)
    f_gain = f * gain_one
    d_tokens = inv_own * (
        f_gain
        - jnp.mean(f_gain, axis=-1, keepdims=True)
        - xhat_own * jnp.mean(f_gain * xhat_own, axis=-1, keepdims=True)
    )
    input_grad = (d_middle + d_tokens).astype(BF)[None]

    late_active = after(active, attn_parts)
    out_parts = [
        jnp.dot(block(late_active, d), out_weight, preferred_element_type=F32) for d in range(n)
    ]
    output = (middle + reduce_rows(out_parts) + b_out).astype(BF)[None]

    sum_fc_weight = local_call(
        functools.partial(
            unpack_kernel,
            n,
            half,
            step,
            lambda m, d: [(0, (m ^ d) * own_ff, 0, d * half, 0, own_ff)],
            1,
        ),
        [jax.ShapeDtypeStruct((own_rows, n * own_ff), F32)],
        own_rows * n * own_ff * 8,
        at,
        fc_sum,
        swap_core(fc_sum),
    )[0]

    def attn_places(m, d):
        base = d * 3 * main
        places = [
            (0, p * D + (m ^ d) * main, 0, 0, base + p * main, base + (p + 1) * main)
            for p in range(3)
        ]
        if d == 0:
            base = n * 3 * main
            places += [
                (0, p * D + n * main, 0, 0, base + p * spare, base + (p + 1) * spare)
                for p in range(3)
            ]
            places.append((1, 0, 0, 0, 3 * D, 4 * D))
        return places

    d_once_sum = jnp.sum(d_once.astype(F32), axis=0)

    def vector_of(part):
        whole = jnp.zeros((D,), F32)
        whole = lax.dynamic_update_slice_in_dim(
            whole, d_once_sum[part * main : (part + 1) * main], me * main, 0
        )
        lane = 3 * main + part * spare
        return jnp.concatenate([whole[: n * main], d_once_sum[lane : lane + spare]])

    early = after(
        (
            jnp.sum(d_branch.astype(F32), axis=0),
            jnp.sum(e * xhat_two, axis=0),
            jnp.sum(e, axis=0),
            jnp.sum(own_cot.astype(F32), axis=0),
        ),
        attn_parts,
    )
    small_grads = jnp.stack(
        [
            vector_of(0),
            vector_of(2),
            early[0],
            jnp.sum(f * xhat_own, axis=0),
            jnp.sum(f, axis=0),
            early[1],
            early[2],
            early[3],
        ]
    )
    small_grads = small_grads.reshape(8, n, own_rows).transpose(1, 0, 2)
    small_own = pick(small_grads, me)
    for d in range(1, n):
        small_own = small_own + swap(pick(small_grads, me ^ d), d)
    small_own = jnp.concatenate([small_own, grad_fc_bias.reshape(-1, own_rows)], axis=0)
    small_own = small_own + swap_core(small_own)
    hop = 1
    while hop < planes:
        small_own = small_own + lax.ppermute(
            small_own, "plane", [(i, i ^ hop) for i in range(planes)]
        )
        hop *= 2
    attn_sum, small_own, output, input_grad, sum_fc_weight, sum_out_weight = after(
        (attn_sum, small_own, output, input_grad, sum_fc_weight, sum_out_weight)
    )
    sum_attn_weight, sum_proj_weight = local_call(
        functools.partial(unpack_kernel, n, half, step, attn_places, 1),
        [
            jax.ShapeDtypeStruct((own_rows, 3 * D), F32),
            jax.ShapeDtypeStruct((own_rows, D), F32),
        ],
        own_rows * 4 * D * 8,
        at,
        attn_sum,
        swap_core(attn_sum),
    )
    s = small_own[:8]
    sum_fc_bias = small_own[8:].reshape(-1)
    return (
        output,
        input_grad,
        sum_attn_weight,
        s[0],
        s[1],
        sum_proj_weight,
        s[2],
        s[3],
        s[4],
        s[5],
        s[6],
        sum_fc_weight,
        sum_fc_bias,
        sum_out_weight,
        s[7],
    )


def solution(mesh):
    shards, reps = mesh.devices.shape
    split = jax.sharding.Mesh(
        mesh.devices.reshape(shards, reps // 2, 2), ("shard", "plane", "core")
    )
    rep = ("plane", "core")
    batch = P(rep, "shard", None)
    row, vec = P("shard", None), P("shard")
    return jax.shard_map(
        body,
        mesh=split,
        in_specs=(batch, batch, P(rep, None), row, vec, vec, row)
        + (vec,) * 5
        + (row, vec, row, vec),
        out_specs=(batch, batch, row, vec, vec, row) + (vec,) * 5 + (row, vec, row, vec),
        check_vma=False,
    )
```

```python
import functools
import math

import jax
import jax.numpy as jnp
from jax import lax
from jax.experimental import pallas as pl
from jax.experimental.pallas import tpu as pltpu
from jax.sharding import PartitionSpec as P

D = 1600
HEADS = 25
HD = 64
UNIT = 32
LANES = 128
NEG = -1e30
VEC_ROWS = 16
BF = jnp.bfloat16
F32 = jnp.float32


def dot(left, right, dims):
    return lax.dot_general(left, right, (dims, ((), ())), preferred_element_type=F32)


def rows_dot(left, right):
    return dot(left, right, ((0,), (0,)))


def cols_dot(left, right):
    return dot(left, right, ((1,), (1,)))


def normalize(values):
    center = values - jnp.mean(values, axis=-1, keepdims=True)
    spread = jnp.mean(center * center, axis=-1, keepdims=True)
    inv = lax.rsqrt(spread + 1e-05)
    return center * inv, inv


def place_blocks(info_ref, shards, units):
    b0, b1, b2, me = info_ref[0], info_ref[1], info_ref[2], info_ref[3]
    e0, e1 = b0, b0 + b1
    places = []
    for d in range(shards):
        s = jnp.bitwise_xor(me, d)
        for u in range(units):
            first = jnp.where(u < e0, 0, jnp.where(u < e1, e0, e1))
            span = jnp.where(u < e0, b0, jnp.where(u < e1, b1, b2))
            places.append((d * units + u, first * shards + s * span + (u - first)))
    return places, e0, e1


def head_lanes(tile_rows, half):
    lane = lax.broadcasted_iota(jnp.int32, (tile_rows, LANES), 1)
    return (lane < HD) if half == 0 else (lane >= HD)


def window_scores(q, k, rows, width):
    scores = cols_dot(q, k)
    row = lax.broadcasted_iota(jnp.int32, (rows, width * rows), 0)
    col = lax.broadcasted_iota(jnp.int32, (rows, width * rows), 1)
    return jnp.where(col <= row + (width - 1) * rows, scores, NEG)


def fwd_kernel(shards, units, heads, info_ref, qkv_ref, out_ref, perm, mixed):
    block = UNIT
    rows = shards * block
    main = heads * HD
    places, e0, e1 = place_blocks(info_ref, shards, units)
    for src, dst in places:
        at = pl.ds(pl.multiple_of(dst * block, block), block)
        perm[at, :] = qkv_ref[src * block : (src + 1) * block, :]

    def unit(i, carry):
        first = jnp.where(i < e0, 0, jnp.where(i < e1, e0, e1))
        q_at = pl.ds(pl.multiple_of(i * rows, rows), rows)
        for width in range(1, 5):

            @pl.when(i - first + 1 == width)
            def _():
                k_at = pl.ds(pl.multiple_of(first * rows, rows), width * rows)

                def attend(q, k, v):
                    scores = window_scores(q * BF(0.125), k, rows, width)
                    top = jnp.max(scores, axis=1, keepdims=True)
                    probs = jnp.exp(scores - top)
                    total = jnp.sum(probs, axis=1, keepdims=True)
                    return dot(probs.astype(BF), v, ((1,), (0,))) / total

                for tile in range(main // LANES):
                    lanes = slice(tile * LANES, (tile + 1) * LANES)
                    k_lanes = slice(main + lanes.start, main + lanes.stop)
                    v_lanes = slice(2 * main + lanes.start, 2 * main + lanes.stop)
                    q, k, v = perm[q_at, lanes], perm[k_at, k_lanes], perm[k_at, v_lanes]
                    low = head_lanes(rows, 0)
                    zero = jnp.zeros_like(q)
                    left = attend(jnp.where(low, q, zero), k, v)
                    right = attend(jnp.where(low, zero, q), k, v)
                    mixed[q_at, lanes] = jnp.where(low, left, right).astype(BF)
                if main % LANES:
                    lanes = main - HD
                    mixed[q_at, lanes:main] = attend(
                        perm[q_at, lanes:main],
                        perm[k_at, main + lanes : 2 * main],
                        perm[k_at, 2 * main + lanes : 3 * main],
                    ).astype(BF)
                base = 3 * main
                mixed[q_at, main : main + HD] = attend(
                    perm[q_at, base : base + HD],
                    perm[k_at, base + HD : base + 2 * HD],
                    perm[k_at, base + 2 * HD : base + 3 * HD],
                ).astype(BF)

        return carry

    lax.fori_loop(0, units, unit, 0)
    for src, dst in places:
        at = pl.ds(pl.multiple_of(dst * block, block), block)
        out_ref[src * block : (src + 1) * block, :] = mixed[at, :]


def bwd_kernel(
    shards, units, heads, info_ref, qkv_ref, dmix_ref, out_ref, perm, dperm, dq_acc, dk_acc, dv_acc
):
    block = UNIT
    rows = shards * block
    main = heads * HD
    places, e0, e1 = place_blocks(info_ref, shards, units)
    for src, dst in places:
        at = pl.ds(pl.multiple_of(dst * block, block), block)
        perm[at, :] = qkv_ref[src * block : (src + 1) * block, :]
        dperm[at, :] = dmix_ref[src * block : (src + 1) * block, :]
    dk_acc[...] = jnp.zeros_like(dk_acc)
    dv_acc[...] = jnp.zeros_like(dv_acc)

    def unit(i, carry):
        first = jnp.where(i < e0, 0, jnp.where(i < e1, e0, e1))
        q_at = pl.ds(pl.multiple_of(i * rows, rows), rows)
        for width in range(1, 5):

            @pl.when(i - first + 1 == width)
            def _():
                k_at = pl.ds(pl.multiple_of(first * rows, rows), width * rows)

                def pull(q, k, v, g):
                    q = q * BF(0.125)
                    scores = window_scores(q, k, rows, width)
                    top = jnp.max(scores, axis=1, keepdims=True)
                    probs = jnp.exp(scores - top)
                    total = jnp.sum(probs, axis=1, keepdims=True)
                    probs = probs * (1.0 / total)
                    d_probs = cols_dot(g, v)
                    delta = jnp.sum(probs * d_probs, axis=1, keepdims=True)
                    d_scores = (probs * (d_probs - delta)).astype(BF)
                    d_q = dot(d_scores, k, ((1,), (0,))) * 0.125
                    return d_q, rows_dot(d_scores, q), rows_dot(probs.astype(BF), g)

                for tile in range(main // LANES):
                    lanes = slice(tile * LANES, (tile + 1) * LANES)
                    k_lanes = slice(main + lanes.start, main + lanes.stop)
                    v_lanes = slice(2 * main + lanes.start, 2 * main + lanes.stop)
                    q, k, v = perm[q_at, lanes], perm[k_at, k_lanes], perm[k_at, v_lanes]
                    g = dperm[q_at, lanes]
                    low = head_lanes(rows, 0)
                    zero = jnp.zeros_like(q)
                    dq0, dk0, dv0 = pull(jnp.where(low, q, zero), k, v, jnp.where(low, g, zero))
                    dq1, dk1, dv1 = pull(jnp.where(low, zero, q), k, v, jnp.where(low, zero, g))
                    dq_acc[q_at, lanes] = jnp.where(low, dq0, dq1).astype(BF)
                    dk_acc[k_at, lanes] += dk0 + dk1
                    dv_acc[k_at, lanes] += dv0 + dv1
                extra = [(main, 3 * main, 3 * main + HD, 3 * main + 2 * HD)]
                if main % LANES:
                    extra.append((main - HD, main - HD, 2 * main - HD, 3 * main - HD))
                for own, q_lane, k_lane, v_lane in extra:
                    dq0, dk0, dv0 = pull(
                        perm[q_at, q_lane : q_lane + HD],
                        perm[k_at, k_lane : k_lane + HD],
                        perm[k_at, v_lane : v_lane + HD],
                        dperm[q_at, own : own + HD],
                    )
                    dq_acc[q_at, own : own + HD] = dq0.astype(BF)
                    dk_acc[k_at, own : own + HD] += dk0
                    dv_acc[k_at, own : own + HD] += dv0

        return carry

    lax.fori_loop(0, units, unit, 0)
    for src, dst in places:
        at = pl.ds(pl.multiple_of(dst * block, block), block)
        to = slice(src * block, (src + 1) * block)
        for part, acc in enumerate((dq_acc, dk_acc, dv_acc)):
            got = acc[at, :].astype(BF)
            out_ref[to, part * main : (part + 1) * main] = got[:, :main]
            lane = 3 * main + part * HD
            out_ref[to, lane : lane + HD] = got[:, main:]


def vmem_call(kernel, out_shape, scratch, cost, inputs):
    return pl.pallas_call(
        kernel,
        out_shape=out_shape,
        in_specs=[pl.BlockSpec(memory_space=pltpu.SMEM)]
        + [pl.BlockSpec(memory_space=pltpu.VMEM)] * (len(inputs) - 1),
        out_specs=pl.BlockSpec(memory_space=pltpu.VMEM),
        scratch_shapes=scratch,
        compiler_params=pltpu.CompilerParams(vmem_limit_bytes=48 << 20),
        cost_estimate=cost,
    )(*inputs)


def attention_fwd(info, qkv, shards, heads):
    total, width = qkv.shape
    units = total // (shards * UNIT)
    own = (heads + 1) * HD
    return vmem_call(
        functools.partial(fwd_kernel, shards, units, heads),
        jax.ShapeDtypeStruct((total, own), BF),
        [pltpu.VMEM((total, width), BF), pltpu.VMEM((total, own), BF)],
        pl.CostEstimate(flops=1, bytes_accessed=1, transcendentals=0),
        (info, qkv),
    )


def attention_bwd(info, qkv, d_mixed, shards, heads):
    total, width = qkv.shape
    units = total // (shards * UNIT)
    own = (heads + 1) * HD
    return vmem_call(
        functools.partial(bwd_kernel, shards, units, heads),
        jax.ShapeDtypeStruct((total, width), BF),
        [
            pltpu.VMEM((total, width), BF),
            pltpu.VMEM((total, own), BF),
            pltpu.VMEM((total, own), BF),
            pltpu.VMEM((total, own), F32),
            pltpu.VMEM((total, own), F32),
        ],
        pl.CostEstimate(flops=1, bytes_accessed=1, transcendentals=0),
        (info, qkv, d_mixed),
    )


def on_place(me, core, shards, run):
    for m in range(shards):
        for c in range(2):

            @pl.when((me == m) & (core == c))
            def _():
                run(m, c)


def attn_columns(value, j, heads):
    main = heads * HD
    first = D // main * main
    parts = [value[:, p * D + j * main : p * D + (j + 1) * main] for p in range(3)]
    parts += [value[:, p * D + first : (p + 1) * D] for p in range(3)]
    return jnp.concatenate(parts, axis=1)


def fc_columns(value, j, width):
    return value[:, j * width : (j + 1) * width]


def pack_kernel(shards, half, step, columns, at_ref, dep_ref, weight_ref, *outs):
    del dep_ref

    def run(m, c):
        outs[0][...] = columns(weight_ref, m)
        for d in range(1, shards):
            piece = columns(weight_ref.at[c * step : c * step + half], m ^ d)
            outs[d][...] = piece

    on_place(at_ref[0], at_ref[1], shards, run)


def pack_attn_kernel(shards, half, step, heads, count, at_ref, weight_ref, *refs):
    sources, outs = refs[:count], refs[count : count + shards]
    vectors, sems = refs[count + shards : 2 * count + shards], refs[2 * count + shards]
    length = vectors[0].shape[0]
    copies = [
        pltpu.make_async_copy(source, vector, sems.at[i])
        for i, (source, vector) in enumerate(zip(sources, vectors))
    ]
    for copy in copies:
        copy.start()

    def run(m, c):
        outs[0][: shards_rows(outs[0]), :] = attn_columns(weight_ref, m, heads)
        for d in range(1, shards):
            outs[d][:half, :] = attn_columns(weight_ref.at[c * step : c * step + half], m ^ d, heads)

    def shards_rows(ref):
        return ref.shape[0] - VEC_ROWS

    on_place(at_ref[0], at_ref[1], shards, run)
    for copy in copies:
        copy.wait()
    width = outs[0].shape[1]
    block = jnp.concatenate(
        [v[...].astype(F32).reshape(1, length) for v in vectors]
        + [jnp.zeros((VEC_ROWS - count, length), F32)],
        axis=0,
    )
    block = jnp.concatenate(
        [block, jnp.zeros((VEC_ROWS, width - length), F32)], axis=1
    ).astype(BF)
    for out in outs:
        out[out.shape[0] - VEC_ROWS :, :] = block


def place_attn_kernel(shards, half, step, rows, count, at_ref, *refs):
    own, mine, other = refs[0], refs[1:shards], refs[shards]
    out, vec = refs[shards + 1 :]

    def run(m, c):
        out[m * rows : (m + 1) * rows, :] = own[:rows]
        for d in range(1, shards):
            base = (m ^ d) * rows
            a, b = mine[d - 1][:half], other[d - 1]
            low, high = (a, b) if c == 0 else (b, a)
            out[base : base + step, :] = low[:step]
            out[base + step : base + rows, :] = high
        for j in range(shards):
            ref, at = (own, rows) if j == m else (mine[(j ^ m) - 1], half)
            vec[:, j * rows : (j + 1) * rows] = ref[at : at + VEC_ROWS, :rows].astype(F32)[:count]

    on_place(at_ref[0], at_ref[1], shards, run)


def place_kernel(shards, half, step, rows, at_ref, *refs):
    own, mine, other, out = refs[0], refs[1:shards], refs[shards], refs[shards + 1]

    def run(m, c):
        out[m * rows : (m + 1) * rows, :] = own[...]
        for d in range(1, shards):
            base = (m ^ d) * rows
            low, high = (mine[d - 1][...], other[d - 1]) if c == 0 else (other[d - 1], mine[d - 1][...])
            out[base : base + step, :] = low[:step]
            out[base + step : base + rows, :] = high

    on_place(at_ref[0], at_ref[1], shards, run)


def pack_part_kernel(shards, length, stride, columns, at_ref, weight_ref, *outs):
    part = pl.ds(pl.multiple_of(at_ref[2] * stride, 16), length)
    for m in range(shards):

        @pl.when(at_ref[0] == m)
        def _():
            outs[0][...] = columns(weight_ref, m)
            for d in range(1, shards):
                outs[d][...] = columns(weight_ref.at[part], m ^ d)


def place_part_kernel(shards, length, stride, rows, at_ref, own, mine, near, across, out):
    me, q = at_ref[0], at_ref[2]
    out[pl.ds(pl.multiple_of(me * rows, 16), rows), :] = own[...]
    size = (shards - 1) * length
    for d in range(1, shards):
        base = jnp.bitwise_xor(me, d) * rows
        for flip, ref, first in ((0, mine, 0), (2, near, 0), (1, across, 0), (3, across, size)):
            to = base + jnp.bitwise_xor(q, flip) * stride
            row = first + (d - 1) * length
            out[pl.ds(pl.multiple_of(to, 16), length), :] = ref[row : row + length, :]


def unpack_kernel(shards, half, step, places, count, at_ref, *refs):
    mine, other, outs = refs[:count], refs[count : 2 * count], refs[2 * count :]

    def run(m, c):
        for d in range(shards):
            for index, where, part, row, low, high in places(m, d):
                out, width = outs[index], high - low
                a = mine[part][row : row + half, low:high]
                b = other[part][row : row + half, low:high]
                first, second = (a, b) if c == 0 else (b, a)
                out[:step, where : where + width] = first[:step].astype(F32)
                out[step:, where : where + width] = second.astype(F32)

    on_place(at_ref[0], at_ref[1], shards, run)


def local_call(kernel, out_shape, cost_bytes, at, *inputs, anywhere=(), scratch=()):
    vmem = pl.BlockSpec(memory_space=pltpu.VMEM)
    hbm = pl.BlockSpec(memory_space=pltpu.HBM)
    specs = [hbm if i in anywhere else vmem for i in range(len(inputs))]
    return pl.pallas_call(
        kernel,
        out_shape=out_shape,
        in_specs=[pl.BlockSpec(memory_space=pltpu.SMEM)] + specs,
        out_specs=jax.tree.map(lambda _: vmem, out_shape),
        scratch_shapes=list(scratch),
        compiler_params=pltpu.CompilerParams(vmem_limit_bytes=48 << 20),
        cost_estimate=pl.CostEstimate(flops=1, bytes_accessed=1, transcendentals=0),
    )(at, *inputs)


def body(
    tokens,
    cotangent,
    lengths,
    attn_weight,
    query_bias,
    value_bias,
    proj_weight,
    proj_bias,
    ln1_gain,
    ln1_bias,
    ln2_gain,
    ln2_bias,
    fc_weight,
    fc_bias,
    out_weight,
    out_bias,
):
    n = lax.axis_size("shard")
    planes = lax.axis_size("plane")
    me = lax.axis_index("shard")
    core = lax.axis_index("core")
    heads = (HEADS - 1) // n
    main = heads * HD
    spare = D - n * main
    own_rows = attn_weight.shape[0]
    own_ff = fc_bias.shape[0]
    rows = tokens.shape[1]
    half = -(-own_rows // 32) * 16
    step = own_rows - half
    quarter = lax.axis_index("plane") % 2 * 2 + core
    at = jnp.stack([me, core, quarter]).astype(jnp.int32)

    def swap(value, d):
        return lax.ppermute(value, "shard", [(i, i ^ d) for i in range(n)])

    def swap_plane(value):
        return lax.ppermute(value, "plane", [(i, i ^ 1) for i in range(planes)])

    def swap_core(value):
        return lax.ppermute(value, "core", [(0, 1), (1, 0)])

    def gather_near(value):
        if n != 4:
            return [swap(value, d) for d in range(1, n)]
        return [swap(value, 1), swap(value, 2)]

    def gather_far(value, near):
        if n != 4:
            return [value] + near
        one, two = near
        cut = value.shape[0] // 32 * 16
        three = jnp.concatenate([swap(one[:cut], 2), swap(two[cut:], 1)], axis=0)
        return [value, one, two, three]

    def gather(value):
        return gather_far(value, gather_near(value))

    def pick(stacked, index):
        return lax.dynamic_index_in_dim(stacked, index, 0, keepdims=False)

    def natural(pieces):
        stacked = jnp.stack(pieces)
        return [pick(stacked, me ^ j) for j in range(n)]

    def after(value, *deps):
        return lax.optimization_barrier((value, deps))[0]

    def block(value, d):
        return value[d * rows : (d + 1) * rows]

    def place(own, mine):
        other = swap_core(jnp.stack(mine))
        return local_call(
            functools.partial(place_kernel, n, half, step, own_rows),
            jax.ShapeDtypeStruct((n * own_rows, own.shape[1]), BF),
            n * own.size * 4,
            at,
            own,
            *mine,
            other,
        )

    def pack(weight, columns, width, dep):
        shapes = [jax.ShapeDtypeStruct((own_rows, width), BF)]
        shapes += [jax.ShapeDtypeStruct((half, width), BF)] * (n - 1)
        return local_call(
            functools.partial(pack_kernel, n, half, step, columns),
            shapes,
            weight.size * 2,
            at,
            dep,
            weight,
            anywhere=(0,),
        )

    def reduce_rows(parts, *deps):
        got = after([swap(parts[d].astype(BF), d) for d in range(1, n)], *deps)
        total = parts[0].astype(F32)
        for part in got:
            total = total + part.astype(F32)
        return total

    def core_halves(parts):
        keep = lax.dynamic_slice_in_dim(parts, core * step, half, 1)
        give = lax.dynamic_slice_in_dim(parts, (1 - core) * step, half, 1)
        return (keep.astype(F32) + swap_core(give).astype(F32)).astype(BF)

    vectors = (
        query_bias, value_bias, proj_bias, ln1_gain, ln1_bias, ln2_gain, ln2_bias, out_bias
    )
    tokens_near = gather_near(tokens[0])
    attn_width = 3 * (main + spare)
    attn_sent = local_call(
        functools.partial(pack_attn_kernel, n, half, step, heads, len(vectors)),
        [jax.ShapeDtypeStruct((own_rows + VEC_ROWS, attn_width), BF)]
        + [jax.ShapeDtypeStruct((half + VEC_ROWS, attn_width), BF)] * (n - 1),
        attn_weight.size * 2,
        at,
        attn_weight,
        *vectors,
        anywhere=range(1, len(vectors) + 1),
        scratch=[pltpu.VMEM((own_rows,), BF)] * len(vectors)
        + [pltpu.SemaphoreType.DMA((len(vectors),))],
    )
    attn_got = [swap(attn_sent[d], d) for d in range(1, n)]
    attn_got, tokens_near = after((attn_got, tokens_near))
    attn_other = swap_core(jnp.stack([piece[:half] for piece in attn_got]))
    tokens_parts = gather_far(tokens[0], tokens_near)
    w_attn, small = local_call(
        functools.partial(place_attn_kernel, n, half, step, own_rows, len(vectors)),
        [
            jax.ShapeDtypeStruct((D, attn_width), BF),
            jax.ShapeDtypeStruct((len(vectors), D), F32),
        ],
        D * attn_width * 4,
        at,
        attn_sent[0],
        *attn_got,
        attn_other,
    )
    b_query, b_value, b_proj, gain_one, bias_one, gain_two, bias_two, b_out = [
        small[i] for i in range(8)
    ]

    def my_columns(vector):
        return lax.dynamic_slice_in_dim(vector, me * main, main, 0), vector[n * main :]

    q_main, q_spare = my_columns(b_query)
    v_main, v_spare = my_columns(b_value)
    qkv_bias = jnp.concatenate(
        [q_main, jnp.zeros_like(q_main), v_main, q_spare, jnp.zeros_like(q_spare), v_spare]
    )

    group_tokens = jnp.concatenate(tokens_parts, axis=0)
    proj_half = lax.dynamic_slice_in_dim(after(proj_weight, attn_got), core * step, half, 0)
    proj_near = gather_near(proj_half)
    own_cot = cotangent[0]
    cot_all = lax.all_gather(after(own_cot, attn_got, tokens_parts), "shard", axis=0, tiled=True)
    late_fc = after(fc_weight, attn_got)
    stride = own_rows // 64 * 16
    length = own_rows - 3 * stride
    by_parts = own_rows % 16 == 0 and stride > 0 and planes % 2 == 0
    if by_parts:
        fc_sent = local_call(
            functools.partial(
                pack_part_kernel, n, length, stride, lambda ref, j: fc_columns(ref, j, own_ff)
            ),
            [jax.ShapeDtypeStruct((own_rows, own_ff), BF)]
            + [jax.ShapeDtypeStruct((length, own_ff), BF)] * (n - 1),
            fc_weight.size * 2,
            at,
            late_fc,
        )
    else:
        fc_sent = pack(late_fc, lambda ref, j: fc_columns(ref, j, own_ff), own_ff, lengths)
    xhat_one, _ = normalize(group_tokens.astype(F32))
    normed = (xhat_one * gain_one + bias_one).astype(BF)
    qkv = (jnp.dot(normed, w_attn, preferred_element_type=F32) + qkv_bias).astype(BF)
    qkv, proj_near, fc_sent = after((qkv, proj_near, fc_sent))
    proj_parts = gather_far(proj_half, proj_near)
    fc_got = [swap(fc_sent[d], d) for d in range(1, n)]
    info = jnp.concatenate([lengths[0], me.astype(jnp.int32)[None]])
    mixed_heads = attention_fwd(info, qkv, n, heads)
    mixed_heads, proj_parts, fc_first = after((mixed_heads, proj_parts, fc_got[:-1]))
    fc_got = list(fc_first) + fc_got[-1:]
    if by_parts:
        fc_mine = jnp.concatenate(fc_got)
        fc_near = swap_plane(fc_mine)
    got = [block(mixed_heads, 0)[:, :main]] + [
        swap(block(mixed_heads, d)[:, :main], d) for d in range(1, n)
    ]
    w_proj = place(proj_weight, proj_parts[1:])
    got, w_proj, cot_all = after((got, w_proj, cot_all))
    mixed_low = jnp.concatenate(natural(got) + [block(mixed_heads, 0)[:, main:]], axis=1)
    own_tokens = tokens[0].astype(F32)
    middle = own_tokens + jnp.dot(mixed_low, w_proj, preferred_element_type=F32) + b_proj
    xhat_two, inv_two = normalize(middle)
    own_normed_two = (xhat_two * gain_two + bias_two).astype(BF)
    normed_near = gather_near(own_normed_two)
    if by_parts:
        w_fc = local_call(
            functools.partial(place_part_kernel, n, length, stride, own_rows),
            jax.ShapeDtypeStruct((D, own_ff), BF),
            D * own_ff * 4,
            at,
            fc_sent[0],
            fc_mine,
            fc_near,
            swap_core(jnp.concatenate(after([fc_mine, fc_near], own_normed_two))),
        )
    else:
        w_fc = place(fc_sent[0], fc_got)
    cot_parts = [own_cot] + [
        lax.dynamic_slice_in_dim(cot_all, (me ^ d) * rows, rows, 0) for d in range(1, n)
    ]
    group_cot = jnp.concatenate(cot_parts, axis=0)
    d_active = cols_dot(group_cot, out_weight).astype(BF)
    normed_near, d_active = after((normed_near, d_active))
    normed_parts = gather_far(own_normed_two, normed_near)
    normed_two = jnp.concatenate(normed_parts, axis=0)

    def feed(part):
        hidden = jnp.dot(part, w_fc, preferred_element_type=F32) + fc_bias.astype(F32)
        inner = jnp.tanh(0.7978845608028654 * (hidden + 0.044715 * hidden * hidden * hidden))
        slope = 0.5 * (1.0 + inner) + 0.5 * hidden * (1.0 - inner * inner) * (
            0.7978845608028654 * (1.0 + 3 * 0.044715 * hidden * hidden)
        )
        return (0.5 * hidden * (1.0 + inner)).astype(BF), slope.astype(BF)

    fed = [feed(part) for part in normed_parts]
    active_parts = [a for a, _ in fed]
    active = jnp.concatenate(active_parts, axis=0)

    grad_out_weight = rows_dot(active, group_cot).astype(BF)
    sum_out_weight = lax.psum(grad_out_weight, ("plane", "core"))
    d_active = after(d_active, grad_out_weight)
    d_hidden_parts = [
        (block(d_active, d).astype(F32) * slope.astype(F32)).astype(BF)
        for d, (_, slope) in enumerate(fed)
    ]
    d_hidden = jnp.concatenate(d_hidden_parts, axis=0)
    e = reduce_rows([cols_dot(part, w_fc) for part in d_hidden_parts])
    e_gain = e * gain_two
    d_middle = own_cot.astype(F32) + inv_two * (
        e_gain
        - jnp.mean(e_gain, axis=-1, keepdims=True)
        - xhat_two * jnp.mean(e_gain * xhat_two, axis=-1, keepdims=True)
    )
    d_branch = d_middle.astype(BF)
    d_mixed = cols_dot(d_branch, w_proj).astype(BF)
    for_heads = jnp.stack([d_mixed[:, j * main : (j + 1) * main] for j in range(n)])
    last = d_mixed[:, n * main :]
    dmix_parts = [jnp.concatenate([pick(for_heads, me), last], axis=1)] + [
        swap(jnp.concatenate([pick(for_heads, me ^ d), last], axis=1), d) for d in range(1, n)
    ]

    grad_fc = rows_dot(normed_two, d_hidden).astype(BF).reshape(n, own_rows, own_ff)
    fc_halves = after(core_halves(grad_fc), dmix_parts)
    fc_parts = jnp.concatenate(
        [pick(fc_halves, me)] + [swap(pick(fc_halves, me ^ d), d) for d in range(1, n)]
    )
    fc_sum = lax.psum(fc_parts, "plane")
    sum_out_weight = after(sum_out_weight, fc_parts).astype(F32)
    grad_fc_bias = jnp.sum(d_hidden.astype(F32), axis=0)

    d_qkv = attention_bwd(info, qkv, jnp.concatenate(dmix_parts, axis=0), n, heads)
    d_qkv, fc_parts, sum_out_weight = after((d_qkv, fc_parts, sum_out_weight))

    grad_proj = rows_dot(mixed_low, d_branch).astype(BF).reshape(n, own_rows, D)
    proj_halves = after(core_halves(grad_proj), fc_parts)
    proj_part = reduce_rows([pick(proj_halves, me ^ d) for d in range(n)]).astype(BF)

    grad_main = rows_dot(normed, d_qkv[:, : 3 * main]).astype(BF).reshape(n, own_rows, 3 * main)
    grad_spare = rows_dot(normed, d_qkv[:, 3 * main :]).astype(BF).reshape(n, own_rows, 3 * spare)
    main_halves = core_halves(grad_main)
    spare_halves = core_halves(pick(grad_spare, me)[None])[0]
    attn_parts = jnp.concatenate(
        [pick(main_halves, me)]
        + [swap(pick(main_halves, me ^ d), d) for d in range(1, n)]
        + [spare_halves, proj_part],
        axis=1,
    )
    attn_sum = lax.psum(after(attn_parts, fc_sum), "plane")

    counted = (lax.broadcasted_iota(jnp.int32, (n * rows, 1), 0) < rows) | (
        lax.broadcasted_iota(jnp.int32, (1, d_qkv.shape[1]), 1) < 3 * main
    )
    d_once = after(jnp.where(counted, d_qkv, BF(0)), attn_parts)
    f = reduce_rows([cols_dot(block(d_once, d), w_attn) for d in range(n)])
    xhat_own, inv_own = normalize(own_tokens)
    f_gain = f * gain_one
    d_tokens = inv_own * (
        f_gain
        - jnp.mean(f_gain, axis=-1, keepdims=True)
        - xhat_own * jnp.mean(f_gain * xhat_own, axis=-1, keepdims=True)
    )
    input_grad = (d_middle + d_tokens).astype(BF)[None]

    late_active = after(active, attn_parts)
    out_parts = [
        jnp.dot(block(late_active, d), out_weight, preferred_element_type=F32) for d in range(n)
    ]
    output = (middle + reduce_rows(out_parts) + b_out).astype(BF)[None]

    sum_fc_weight = local_call(
        functools.partial(
            unpack_kernel,
            n,
            half,
            step,
            lambda m, d: [(0, (m ^ d) * own_ff, 0, d * half, 0, own_ff)],
            1,
        ),
        [jax.ShapeDtypeStruct((own_rows, n * own_ff), F32)],
        own_rows * n * own_ff * 8,
        at,
        fc_sum,
        swap_core(fc_sum),
    )[0]

    def attn_places(m, d):
        base = d * 3 * main
        places = [
            (0, p * D + (m ^ d) * main, 0, 0, base + p * main, base + (p + 1) * main)
            for p in range(3)
        ]
        if d == 0:
            base = n * 3 * main
            places += [
                (0, p * D + n * main, 0, 0, base + p * spare, base + (p + 1) * spare)
                for p in range(3)
            ]
            places.append((1, 0, 0, 0, 3 * D, 4 * D))
        return places

    d_once_sum = jnp.sum(d_once.astype(F32), axis=0)

    def vector_of(part):
        whole = jnp.zeros((D,), F32)
        whole = lax.dynamic_update_slice_in_dim(
            whole, d_once_sum[part * main : (part + 1) * main], me * main, 0
        )
        lane = 3 * main + part * spare
        return jnp.concatenate([whole[: n * main], d_once_sum[lane : lane + spare]])

    early = after(
        (
            jnp.sum(d_branch.astype(F32), axis=0),
            jnp.sum(e * xhat_two, axis=0),
            jnp.sum(e, axis=0),
            jnp.sum(own_cot.astype(F32), axis=0),
        ),
        attn_parts,
    )
    small_grads = jnp.stack(
        [
            vector_of(0),
            vector_of(2),
            early[0],
            jnp.sum(f * xhat_own, axis=0),
            jnp.sum(f, axis=0),
            early[1],
            early[2],
            early[3],
        ]
    )
    small_grads = small_grads.reshape(8, n, own_rows).transpose(1, 0, 2)
    small_own = pick(small_grads, me)
    for d in range(1, n):
        small_own = small_own + swap(pick(small_grads, me ^ d), d)
    small_own = jnp.concatenate([small_own, grad_fc_bias.reshape(-1, own_rows)], axis=0)
    small_own = small_own + swap_core(small_own)
    hop = 1
    while hop < planes:
        small_own = small_own + lax.ppermute(
            small_own, "plane", [(i, i ^ hop) for i in range(planes)]
        )
        hop *= 2
    attn_sum, small_own, output, input_grad, sum_fc_weight, sum_out_weight = after(
        (attn_sum, small_own, output, input_grad, sum_fc_weight, sum_out_weight)
    )
    sum_attn_weight, sum_proj_weight = local_call(
        functools.partial(unpack_kernel, n, half, step, attn_places, 1),
        [
            jax.ShapeDtypeStruct((own_rows, 3 * D), F32),
            jax.ShapeDtypeStruct((own_rows, D), F32),
        ],
        own_rows * 4 * D * 8,
        at,
        attn_sum,
        swap_core(attn_sum),
    )
    s = small_own[:8]
    sum_fc_bias = small_own[8:].reshape(-1)
    return (
        output,
        input_grad,
        sum_attn_weight,
        s[0],
        s[1],
        sum_proj_weight,
        s[2],
        s[3],
        s[4],
        s[5],
        s[6],
        sum_fc_weight,
        sum_fc_bias,
        sum_out_weight,
        s[7],
    )


def solution(mesh):
    shards, reps = mesh.devices.shape
    split = jax.sharding.Mesh(
        mesh.devices.reshape(shards, reps // 2, 2), ("shard", "plane", "core")
    )
    rep = ("plane", "core")
    batch = P(rep, "shard", None)
    row, vec = P("shard", None), P("shard")
    return jax.shard_map(
        body,
        mesh=split,
        in_specs=(batch, batch, P(rep, None), row, vec, vec, row)
        + (vec,) * 5
        + (row, vec, row, vec),
        out_specs=(batch, batch, row, vec, vec, row) + (vec,) * 5 + (row, vec, row, vec),
        check_vma=False,
    )
```
